32 devices in a mesh: wide: 4 (over y, x), narrow: 8 (over z, core).
Axes of the slice: x: 2, y: 2, z: 4, core: 2. Of those that a mesh axis runs over, the one named last changes fastest.
Arguments:
- x_in: bfloat16 [64, 640, 768], P(('wide', 'narrow'))
- cotangent: bfloat16 [64, 640, 768], P(('wide', 'narrow')), may hold values from -6 to 6
- segment_ids: int32 [64, 640], P(('wide', 'narrow')), may hold values from 0 to 7, never falling along the last dimension, each value on 1 to 320 neighbouring positions
- type_ids: int32 [64, 640], P(('wide', 'narrow')), may hold values 0 or 1
- projection: float32 [768, 4608], P('narrow'), may hold values from -0.21875 to 0.21875
- context_out: float32 [768, 768], P('narrow'), may hold values from -2 to 2
- expand_weight: float32 [768, 3072], P('narrow'), may hold values from -0.21875 to 0.21875
- reduce_weight: float32 [3072, 768], P('narrow'), may hold values from -0.109375 to 0.109375
- vector_params: float32 [15, 768], P(None, 'narrow')
- first_projection: float32 [768, 4608], P('narrow'), may hold values from -0.00048828125 to 0.00048828125
- first_context: float32 [768, 768], P('narrow'), may hold values from -0.00048828125 to 0.00048828125
- first_expand: float32 [768, 3072], P('narrow'), may hold values from -0.00048828125 to 0.00048828125
- first_reduce: float32 [3072, 768], P('narrow'), may hold values from -0.00048828125 to 0.00048828125
- first_vectors: float32 [15, 768], P(None, 'narrow'), may hold values from -0.0017089844 to 0.0017089844
- second_projection: float32 [768, 4608], P('narrow'), may hold values from 1.12881086e-10 to 4.5152435e-10
- second_context: float32 [768, 768], P('narrow'), may hold values from 2.2576217e-11 to 9.030487e-11
- second_expand: float32 [768, 3072], P('narrow'), may hold values from 1.12881086e-10 to 4.5152435e-10
- second_reduce: float32 [3072, 768], P('narrow'), may hold values from 1.12881086e-10 to 4.5152435e-10
- second_vectors: float32 [15, 768], P(None, 'narrow'), may hold values from 1.1288108e-09 to 4.5152433e-09
Outputs:
- block_out: bfloat16 [64, 640, 768], P(('wide', 'narrow'))
- input_grad: bfloat16 [64, 640, 768], P(('wide', 'narrow'))
- grad_norm: float32 [], replicated
- new_projection: float32 [768, 4608], P('narrow')
- new_context: float32 [768, 768], P('narrow')
- new_expand: float32 [768, 3072], P('narrow')
- new_reduce: float32 [3072, 768], P('narrow')
- new_vectors: float32 [15, 768], P(None, 'narrow')
- next_first_projection: float32 [768, 4608], P('narrow')
- next_first_context: float32 [768, 768], P('narrow')
- next_first_expand: float32 [768, 3072], P('narrow')
- next_first_reduce: float32 [3072, 768], P('narrow')
- next_first_vectors: float32 [15, 768], P(None, 'narrow')
- next_second_projection: float32 [768, 4608], P('narrow')
- next_second_context: float32 [768, 768], P('narrow')
- next_second_expand: float32 [768, 3072], P('narrow')
- next_second_reduce: float32 [3072, 768], P('narrow')
- next_second_vectors: float32 [15, 768], P(None, 'narrow')
- copy_projection: bfloat16 [768, 4608], P('narrow')
- copy_context: bfloat16 [768, 768], P('narrow')
- copy_expand: bfloat16 [768, 3072], P('narrow')
- copy_reduce: bfloat16 [3072, 768], P('narrow')
- copy_vectors: bfloat16 [15, 768], P(None, 'narrow')
The draws below stay inside these ranges and needn't reach their ends.
Inputs may be any that keep to these rules, and one draw needn't show every extreme that they name: `segment_ids`: ids never fall along a sequence; each document holds 1 to 320 positions.
All inputs are finite; a program needn't handle non-finite values. No bound on the sum of `type_ids` on one device may be relied on, other than what follows from the above.
Results may differ from the reference program's by a relative error of at most 0.017.
Values may be sent and summed in bfloat16 or wider, within the bound.
A program may use at most 256 MiB of HBM per device.

```python
import math
import jax
import jax.numpy as jnp
import numpy as np
from jax import lax

D = 768
HEADS = 12
HEAD = 64
FF = 3072
LEN = 640
SEGS = 8
STEP = 10
SEQS = 64
VROWS = 15
NPARAM = 8858880


def draw_x_in(key, part):
    key = jax.random.fold_in(key, 11)
    column = jnp.arange(D, dtype=jnp.float32) / (D - 1)
    base = jax.random.normal(key, (SEQS, LEN, D), jnp.float32)
    rising = 0.6 * 3.0 ** column
    return (base * rising[None, None, :]).astype(jnp.bfloat16)


def draw_vector_params(key, part):
    key = jax.random.fold_in(key, 23)
    column = jnp.arange(D, dtype=jnp.float32) / (D - 1)
    noise = jax.random.normal(key, (VROWS, D), jnp.float32)
    rising = 0.6 * 3.0 ** column
    row_index = jnp.arange(VROWS)[:, None]
    gains = rising[None, :] * (1.0 + 0.1 * noise)
    is_gain = (row_index == 6) | (row_index == 9)
    return jnp.where(is_gain, gains, 0.3 * noise).astype(jnp.float32)


def plant(array, stream_key, smallest, high):
    extent = array.shape
    spot = [jax.random.randint(jax.random.fold_in(stream_key, axis), (), 0, extent[axis]) for axis in range(len(extent))]
    array = array.at[tuple(spot)].set(smallest)
    longest = extent.index(max(extent))
    spot[longest] = (spot[longest] + 1) % extent[longest]
    return array.at[tuple(spot)].set(high)


def shard_levels(rng, dims, cuts, smallest, high):
    gain, own = 1.0, jax.random.fold_in(rng, 6)
    for dim, blocks in cuts:
        heights = jnp.exp(jax.random.uniform(jax.random.fold_in(own, dim), (blocks,), jnp.float32, smallest / len(cuts), high / len(cuts)))
        gain = gain * jnp.repeat(heights, dims[dim] // blocks).reshape([-1 if axis == dim else 1 for axis in range(len(dims))])
    return gain


def profile(number_of, total, bound, slope):
    portions = [(1 << 20) // math.isqrt(grade ** slope) + 1 for grade in range(2, number_of + 1)]
    surplus, given = total - bound - (number_of - 1), [1] * (number_of - 1)
    while surplus > 0:
        candidates = [i for i in range(number_of - 1) if given[i] < bound]
        pool, budget = sum([portions[i] for i in candidates]), surplus
        for i in candidates:
            more = min(bound - given[i], max(1, budget * portions[i] // pool), surplus)
            given[i] = given[i] + more
            surplus = surplus - more
    return np.array([bound] + given)


def ragged_sizes(own_key, amount, total, reach, slope):
    if amount == 2:
        one = jax.random.randint(own_key, (), max(1, total - reach), min(reach, total - 1) + 1)
        return jnp.stack([one, total - one])
    lengths = jnp.asarray(profile(amount, total, reach, slope), jnp.int32)
    twos = (amount - 1) // 2
    giver, taker = lengths[1:1 + 2 * twos:2], lengths[2:2 + 2 * twos:2]
    slack = jnp.minimum(giver - 1, reach - taker)
    moved = jax.random.randint(jax.random.fold_in(own_key, 1), (twos,), 0, 1 << 20) % (slack + 1)
    lengths = lengths.at[1:1 + 2 * twos:2].set(giver - moved).at[2:2 + 2 * twos:2].set(taker + moved)
    return lengths[jax.random.permutation(jax.random.fold_in(own_key, 2), amount)]


def scatter_about(key, dims, deviation, limit, cuts=(), kind=jnp.bfloat16):
    loudness = shard_levels(key, dims, cuts, -0.22, 0.18) if cuts else 1.0
    array = jax.random.normal(key, dims, jnp.float32) * deviation * loudness
    return jnp.minimum(jnp.maximum(array, -limit), limit).astype(kind)


def setup_inputs(seed: int = 0) -> dict:
    streams_of = jax.random.split(jax.random.key(seed), 20)
    return {
        "x_in": draw_x_in(jax.random.fold_in(streams_of[19], 71), 0),
        "cotangent": scatter_about(streams_of[1], (SEQS, LEN, D), 1.0, 6.0, ((0, 32),)),
        "segment_ids": jax.vmap(lambda own: jnp.searchsorted(jnp.cumsum(ragged_sizes(own, SEGS, LEN, LEN // 2, 2)), jnp.arange(LEN), side="right"))(jax.random.split(streams_of[2], SEQS)).reshape((SEQS, LEN)).astype(jnp.int32),
        "type_ids": plant((jax.random.randint(streams_of[3], (SEQS, LEN), 0, 5) < 1).astype(jnp.int32), jax.random.fold_in(streams_of[3], 1), 0, 1),
        "projection": scatter_about(streams_of[4], (D, 6 * D), D ** -0.5, 0.21875, ((0, 8),), jnp.float32),
        "context_out": scatter_about(streams_of[5], (D, D), (max(1, D * SEGS // LEN)) ** -0.5, 2.0, ((0, 8),), jnp.float32),
        "expand_weight": scatter_about(streams_of[6], (D, FF), D ** -0.5, 0.21875, ((0, 8),), jnp.float32),
        "reduce_weight": scatter_about(streams_of[7], (FF, D), FF ** -0.5, 0.109375, ((0, 8),), jnp.float32),
        "vector_params": draw_vector_params(jax.random.fold_in(streams_of[19], 71), 0),
        "first_projection": scatter_about(streams_of[9], (D, 6 * D), (0.11 / NPARAM ** 0.5), 0.00048828125, ((0, 8),), jnp.float32),
        "first_context": scatter_about(streams_of[10], (D, D), (0.11 / NPARAM ** 0.5), 0.00048828125, ((0, 8),), jnp.float32),
        "first_expand": scatter_about(streams_of[11], (D, FF), (0.11 / NPARAM ** 0.5), 0.00048828125, ((0, 8),), jnp.float32),
        "first_reduce": scatter_about(streams_of[12], (FF, D), (0.11 / NPARAM ** 0.5), 0.00048828125, ((0, 8),), jnp.float32),
        "first_vectors": scatter_about(streams_of[13], (VROWS, D), (0.33 / NPARAM ** 0.5), 0.0017089844, ((1, 8),), jnp.float32),
        "second_projection": jnp.clip(jnp.exp(math.log(4.5152434569040167e-10) - 1.3862944 * jax.random.uniform(streams_of[14], (D, 6 * D), jnp.float32) ** shard_levels(streams_of[14], (D, 6 * D), ((0, 8),), -0.2, 0.2)), 1.1288108642260042e-10, 4.5152434569040167e-10),
        "second_context": jnp.clip(jnp.exp(math.log(9.030486775030155e-11) - 1.3862944 * jax.random.uniform(streams_of[15], (D, D), jnp.float32) ** shard_levels(streams_of[15], (D, D), ((0, 8),), -0.2, 0.2)), 2.257621693757539e-11, 9.030486775030155e-11),
        "second_expand": jnp.clip(jnp.exp(math.log(4.5152434569040167e-10) - 1.3862944 * jax.random.uniform(streams_of[16], (D, FF), jnp.float32) ** shard_levels(streams_of[16], (D, FF), ((0, 8),), -0.2, 0.2)), 1.1288108642260042e-10, 4.5152434569040167e-10),
        "second_reduce": jnp.clip(jnp.exp(math.log(4.5152434569040167e-10) - 1.3862944 * jax.random.uniform(streams_of[17], (FF, D), jnp.float32) ** shard_levels(streams_of[17], (FF, D), ((0, 8),), -0.2, 0.2)), 1.1288108642260042e-10, 4.5152434569040167e-10),
        "second_vectors": jnp.clip(jnp.exp(math.log(4.515243290370563e-09) - 1.3862944 * jax.random.uniform(streams_of[18], (VROWS, D), jnp.float32) ** shard_levels(streams_of[18], (VROWS, D), ((1, 8),), -0.2, 0.2)), 1.1288108225926408e-09, 4.515243290370563e-09),
    }


@jax.custom_vjp
def low(v):
    return lax.optimization_barrier(v.astype(jnp.bfloat16)).astype(jnp.float32)

@jax.custom_vjp
def low_back(v):
    return v

def low_keep(v):
    return (low(v), None)

def low_pass(kept, grad):
    return (grad,)

def back_keep(v):
    return (v, None)

def back_low(kept, grad):
    return (low(grad),)
low.defvjp(low_keep, low_pass)
low_back.defvjp(back_keep, back_low)
HIGHEST = lax.Precision.HIGHEST
beta_one = 0.9
beta_two = 0.999
adam_eps = 1e-08
norm_eps = 1e-05
clip_limit = 1.0
rate_table = (0.03, 0.3, 0.03, 0.015, 0.4)
decay_table = (0.01, 0.01, 0.01, 0.01, 0.0)

def rounded_both(values_in):
    return low(low_back(values_in))

def layer_norm(resid, gain_row, shift_row):
    center = resid - lax.optimization_barrier(jnp.mean(resid, axis=-1, keepdims=True))
    spread = lax.optimization_barrier(jnp.mean(center * center, axis=-1, keepdims=True))
    return center * lax.rsqrt(spread + norm_eps) * gain_row + shift_row

def per_head(array_in):
    return array_in.reshape(array_in.shape[0], HEADS, HEAD)

def forward(params, hidden_in, segment_row, type_row):
    proj_w, ctx_w, expand_w, reduce_w, vec_w = [low(weight_item) for weight_item in params]
    score_scale = HEAD ** (-0.5)
    word_rows = (type_row == 0)[:, None]
    projected = jnp.dot(low(hidden_in), proj_w, precision=HIGHEST)
    queries = projected[:, 0:4 * D] + vec_w[0:4].reshape(1, 4 * D)
    to_words = rounded_both(jnp.where(word_rows, queries[:, 0:D], queries[:, 2 * D:3 * D]))
    to_ents = rounded_both(jnp.where(word_rows, queries[:, D:2 * D], queries[:, 3 * D:4 * D]))
    keys_all = rounded_both(projected[:, 4 * D:5 * D])
    values_all = rounded_both(projected[:, 5 * D:6 * D] + vec_w[4])
    score_w = jnp.einsum('ihd,jhd->hij', per_head(to_words), per_head(keys_all), precision=HIGHEST) * score_scale
    score_e = jnp.einsum('ihd,jhd->hij', per_head(to_ents), per_head(keys_all), precision=HIGHEST) * score_scale
    scores = low_back(jnp.where((type_row == 0)[None, None, :], score_w, score_e))
    same_doc = segment_row[:, None] == segment_row[None, :]
    scores = jnp.where(same_doc[None], scores, -1e+30)
    prob_low = low(jax.nn.softmax(scores, axis=-1))
    context = jnp.einsum('hij,jhd->ihd', prob_low, per_head(values_all), precision=HIGHEST)
    context = rounded_both(context.reshape(hidden_in.shape[0], D))
    attn_out = low_back(jnp.dot(context, ctx_w, precision=HIGHEST) + vec_w[5])
    normed_one = layer_norm(hidden_in + attn_out, vec_w[6], vec_w[7])
    inner_bias = vec_w[11:].reshape(FF)
    pre_act = low_back(jnp.dot(low(normed_one), expand_w, precision=HIGHEST) + inner_bias)
    activated = low(jax.nn.gelu(pre_act, approximate=False))
    branch = low_back(jnp.dot(activated, reduce_w, precision=HIGHEST) + vec_w[8])
    return layer_norm(normed_one + branch, vec_w[9], vec_w[10])

def reference(x_in, cotangent, segment_ids, type_ids, projection, context_out, expand_weight, reduce_weight, vector_params, first_projection, first_context, first_expand, first_reduce, first_vectors, second_projection, second_context, second_expand, second_reduce, second_vectors):
    params = (projection, context_out, expand_weight, reduce_weight, vector_params)

    def per_sequence(totals, batch_item):
        hidden_seq, cot_seq, seg_seq, type_seq = batch_item

        def run_layer(weights, hidden):
            return forward(weights, hidden, seg_seq, type_seq)
        output, pullback = jax.vjp(run_layer, params, hidden_seq.astype(jnp.float32))
        grad_params, grad_hidden = pullback(cot_seq.astype(jnp.float32))
        totals = jax.tree.map(jnp.add, totals, tuple(grad_params))
        return (totals, (output.astype(jnp.bfloat16), grad_hidden.astype(jnp.bfloat16)))
    start = tuple((jnp.zeros_like(weight_item) for weight_item in params))
    grads, (block_out, input_grad) = lax.scan(per_sequence, start, (x_in, cotangent, segment_ids, type_ids))
    squares = sum((jnp.sum(grad_item * grad_item) for grad_item in grads))
    grad_norm = jnp.sqrt(squares)
    factor = jnp.minimum(1.0, clip_limit / (grad_norm + 1e-06))
    firsts = (first_projection, first_context, first_expand, first_reduce, first_vectors)
    seconds = (second_projection, second_context, second_expand, second_reduce, second_vectors)
    new_weights = []
    new_firsts = []
    new_seconds = []
    copies = []
    for index in range(5):
        clipped = grads[index] * factor
        new_first = beta_one * firsts[index] + (1.0 - beta_one) * clipped
        new_second = beta_two * seconds[index] + (1.0 - beta_two) * clipped * clipped
        direction = new_first / (1.0 - beta_one ** STEP) / (jnp.sqrt(new_second / (1.0 - beta_two ** STEP)) + adam_eps)
        new_weight = params[index] - rate_table[index] * (direction + decay_table[index] * params[index])
        new_weights.append(new_weight)
        new_firsts.append(new_first)
        new_seconds.append(new_second)
        copies.append(new_weight.astype(jnp.bfloat16))
    return (block_out, input_grad, grad_norm, new_weights[0], new_weights[1], new_weights[2], new_weights[3], new_weights[4], new_firsts[0], new_firsts[1], new_firsts[2], new_firsts[3], new_firsts[4], new_seconds[0], new_seconds[1], new_seconds[2], new_seconds[3], new_seconds[4], copies[0], copies[1], copies[2], copies[3], copies[4])
```

```python
import functools

import jax
import jax.numpy as jnp
from jax import lax
from jax.experimental import pallas as pl
from jax.experimental.pallas import tpu as pltpu
from jax.sharding import PartitionSpec as P

HEAD = 64
STEP = 10
LANES = 128
GROUP = 6 * HEAD
LOG2E = 1.4426950408889634
FAR = -1e30
VMEM_LIMIT = 60 * 1024 * 1024

beta_one = 0.9
beta_two = 0.999
adam_eps = 1e-08
norm_eps = 1e-05
clip_limit = 1.0
rate_table = (0.03, 0.3, 0.03, 0.015, 0.4)
decay_table = (0.01, 0.01, 0.01, 0.01, 0.0)

F32 = jnp.float32
BF16 = jnp.bfloat16


def mm(a, b):
    return lax.dot_general(a, b, (((1,), (0,)), ((), ())), preferred_element_type=F32)


def mm_nt(a, b):
    return lax.dot_general(a, b, (((1,), (1,)), ((), ())), preferred_element_type=F32)


def mm_tn(a, b):
    return lax.dot_general(a, b, (((0,), (0,)), ((), ())), preferred_element_type=F32)


def low_lanes(rows):
    return lax.broadcasted_iota(jnp.int32, (rows, LANES), 1) < HEAD


def swap_halves(tile):
    return pltpu.roll(tile, HEAD, 1)


def split_three(col):
    high = col.astype(BF16).astype(F32)
    rest = col - high
    mid = rest.astype(BF16).astype(F32)
    return high, mid, rest - mid


def qkv_tile(prod, bias, word):
    full = prod + bias
    query = jnp.where(word, full[:, 0:LANES], full[:, LANES : 2 * LANES])
    return (query.astype(BF16).astype(F32) * (HEAD**-0.5)).astype(BF16), full[
        :, 2 * LANES :
    ].astype(BF16)


def qkv_kernel(x_ref, w_ref, b_ref, word_ref, q_ref, kv_ref):
    word = word_ref[...] > 0
    for part in range(2):
        cols = slice(part * GROUP, (part + 1) * GROUP)
        query, keyval = qkv_tile(mm(x_ref[...], w_ref[:, cols]), b_ref[:, cols], word)
        out = slice(part * LANES, (part + 1) * LANES)
        q_ref[:, out] = query
        kv_ref[:, out] = keyval


def qkv_call(x, w, bias, word):
    rows, width = x.shape
    steps = w.shape[1] // (2 * GROUP)
    out = jax.ShapeDtypeStruct((rows, steps * 2 * LANES), BF16)
    return pl.pallas_call(
        qkv_kernel,
        grid=(steps,),
        in_specs=[
            pl.BlockSpec((rows, width), lambda i: (0, 0)),
            pl.BlockSpec((width, 2 * GROUP), lambda i: (0, i)),
            pl.BlockSpec((1, 2 * GROUP), lambda i: (0, i)),
            pl.BlockSpec((rows, LANES), lambda i: (0, 0)),
        ],
        out_specs=[pl.BlockSpec((rows, 2 * LANES), lambda i: (0, i))] * 2,
        out_shape=[out, out],
        compiler_params=pltpu.CompilerParams(vmem_limit_bytes=VMEM_LIMIT),
        name="qkv",
    )(x, w, bias, word)


def key_pair(keyval, kmask, low):
    wide = keyval.astype(F32)
    return (jnp.where(low, wide, swap_halves(wide)) * kmask.astype(F32)).astype(BF16)


def attend_kernel(q_ref, kv_ref, qa_ref, ka_ref, km_ref, ctx_ref, aug_ref):
    rows = q_ref.shape[0]
    low = low_lanes(rows)
    lane = lax.broadcasted_iota(jnp.int32, (rows, LANES), 1)
    outs = []
    for part in range(2):
        cols = slice(part * LANES, (part + 1) * LANES)
        keyval = kv_ref[:, cols]
        keys = jnp.concatenate([key_pair(keyval, km_ref[...], low), ka_ref[...]], axis=1)
        query = jnp.concatenate([q_ref[:, cols], qa_ref[...]], axis=1)
        scores = mm_nt(query, keys)
        top = jnp.max(scores, axis=1, keepdims=True)
        weight = jnp.exp2((scores - top) * LOG2E).astype(BF16)
        ones_val = jnp.where(low, 1.0, keyval.astype(F32)).astype(BF16)
        both = mm(weight, ones_val)
        total = swap_halves(both)
        outs.append(both / total)
        log_total = top + jnp.log(jnp.where(low, both, total))
        high, mid, rest = split_three(log_total)
        extra = jnp.where(lane == 8, -high, jnp.where(lane == 9, -mid, jnp.where(lane == 10, -rest, 0.0)))
        aug_ref[:, cols] = jnp.where(lane < 8, qa_ref[...].astype(F32), extra).astype(BF16)
    ctx_ref[...] = jnp.where(low, swap_halves(outs[0]), outs[1]).astype(BF16)


def attend_call(q, kv, qa, ka, km, length):
    rows, cols = q.shape
    seqs, steps = rows // length, cols // (2 * LANES)
    pair = pl.BlockSpec((length, 2 * LANES), lambda s, i: (s, i))
    one = pl.BlockSpec((length, LANES), lambda s, i: (s, 0))
    return pl.pallas_call(
        attend_kernel,
        grid=(seqs, steps),
        in_specs=[pair, pair, one, one, one],
        out_specs=[pl.BlockSpec((length, LANES), lambda s, i: (s, i)), pair],
        out_shape=[
            jax.ShapeDtypeStruct((rows, cols // 2), BF16),
            jax.ShapeDtypeStruct((rows, cols), BF16),
        ],
        compiler_params=pltpu.CompilerParams(vmem_limit_bytes=VMEM_LIMIT),
        name="attend",
    )(q, kv, qa, ka, km)


def attend_back_head(query, keyval, aug, gcon, con, kaug, kmask, word, odd, low, lane):
    keys = key_pair(keyval, kmask, low)
    scores_t = mm_nt(jnp.concatenate([keys, kaug], axis=1), jnp.concatenate([query, aug], axis=1))
    probs_t = jnp.exp2(scores_t * LOG2E)
    gwide = gcon.astype(F32)
    prod = gwide * con.astype(F32)
    mine = low != odd
    delta = jnp.sum(jnp.where(mine, prod, 0.0), axis=1, keepdims=True)
    high, mid, rest = split_three(delta)
    extra = jnp.where(lane == 0, -high, jnp.where(lane == 1, -mid, jnp.where(lane == 2, -rest, 0.0)))
    ghead = jnp.where(low, extra, jnp.where(odd, gwide, swap_halves(gwide))).astype(BF16)
    ones_val = jnp.where(low, jnp.where(lane < 3, 1.0, 0.0), keyval.astype(F32)).astype(BF16)
    gscores_t = (probs_t * mm_nt(ones_val, ghead)).astype(BF16)
    gval = mm(probs_t.astype(BF16), ghead)
    gkey = mm(gscores_t, query)
    gquery = (jnp.transpose(mm_tn(keys, gscores_t)) * (HEAD**-0.5)).astype(BF16)
    zero = jnp.zeros_like(gquery)
    gkey = jnp.where(kmask.astype(F32) > 0, gkey, 0.0)
    gkey = gkey + swap_halves(gkey)
    return (
        jnp.where(word, gquery, zero),
        jnp.where(word, zero, gquery),
        jnp.where(low, gkey, gval).astype(BF16),
    )


def attend_back_kernel(
    length, x_ref, q_ref, kv_ref, aug_ref, gc_ref, ctx_ref, ka_ref, km_ref, word_ref, gp_ref, gw_ref, sum_ref, xt
):
    step = pl.program_id(0)
    rows = x_ref.shape[0]

    @pl.when(step == 0)
    def _():
        xt[...] = jnp.transpose(x_ref[...])

    low = low_lanes(length)
    lane = lax.broadcasted_iota(jnp.int32, (length, LANES), 1)
    odd = lax.rem(step, 2) == 1
    for seq in range(rows // length):
        here = slice(seq * length, (seq + 1) * length)
        tiles = attend_back_head(
            q_ref[here], kv_ref[here], aug_ref[here], gc_ref[here], ctx_ref[here],
            ka_ref[here], km_ref[here], word_ref[here] > 0, odd, low, lane,
        )
        for index, tile in enumerate(tiles):
            gp_ref[here, index * LANES : (index + 1) * LANES] = tile
    grads = gp_ref[...]
    gw_ref[...] = mm(xt[...], grads).astype(BF16)
    sums = jnp.sum(grads.astype(F32).reshape(rows // 8, 8, GROUP), axis=0)
    sum_ref[...] = jnp.sum(sums, axis=0, keepdims=True)


def attend_back_call(x, q, kv, aug, gc, ctx, ka, km, word, length):
    rows, width = x.shape
    heads = q.shape[1] // LANES
    head = pl.BlockSpec((rows, LANES), lambda h: (0, h))
    pair = pl.BlockSpec((rows, LANES), lambda h: (0, h // 2))
    one = pl.BlockSpec((rows, LANES), lambda h: (0, 0))
    return pl.pallas_call(
        functools.partial(attend_back_kernel, length),
        grid=(heads,),
        in_specs=[pl.BlockSpec((rows, width), lambda h: (0, 0)), head, head, head, pair, pair, one, one, one],
        out_specs=[
            pl.BlockSpec((rows, GROUP), lambda h: (0, h)),
            pl.BlockSpec((width, GROUP), lambda h: (0, h)),
            pl.BlockSpec((1, GROUP), lambda h: (0, h)),
        ],
        out_shape=[
            jax.ShapeDtypeStruct((rows, heads * GROUP), BF16),
            jax.ShapeDtypeStruct((width, heads * GROUP), BF16),
            jax.ShapeDtypeStruct((1, heads * GROUP), F32),
        ],
        scratch_shapes=[pltpu.VMEM((width, rows), BF16)],
        compiler_params=pltpu.CompilerParams(vmem_limit_bytes=VMEM_LIMIT),
        name="attend_back",
    )(x, q, kv, aug, gc, ctx, ka, km, word)


def gelu_pair(pre):
    size = jnp.abs(pre) * (0.5**0.5)
    bell = jnp.exp2(pre * pre * (-0.5 * LOG2E))
    t = 1.0 / (1.0 + 0.3275911 * size)
    poly = t * (0.254829592 + t * (-0.284496736 + t * (1.421413741 + t * (-1.453152027 + t * 1.061405429))))
    tail = 0.5 * poly * bell
    share = jnp.where(pre >= 0, 1.0 - tail, tail)
    return pre * share, share + pre * bell * 0.3989422804014327


def fold(array_in):
    rows, cols = array_in.shape
    return jnp.sum(array_in.reshape(rows // 8, 8, cols), axis=0)


def middle_kernel(
    tiles, x_ref, ctx_ref, cot_ref, vec_ref, wo_hbm, w1_hbm, w2_hbm,
    out_ref, gr1_ref, gctx_ref, gw2_ref, gw1_ref, gwo_ref, gvec_ref,
    wo, w1, w2, h1_s, act_s, gb_s, gp_s, ga_s, ctx_s, dg_s, acc, sems,
):
    step = pl.program_id(0)
    size, width = x_ref.shape
    inner = w1.shape[1]
    chunks = inner // width

    def weight_copies():
        return (
            pltpu.make_async_copy(wo_hbm, wo, sems.at[0]),
            pltpu.make_async_copy(w1_hbm, w1, sems.at[1]),
            pltpu.make_async_copy(w2_hbm, w2, sems.at[2]),
        )

    @pl.when(step == 0)
    def _():
        for copy in weight_copies():
            copy.start()
        acc[...] = jnp.zeros_like(acc)

    def vec(row):
        return vec_ref[row : row + 1, :].astype(F32)

    @pl.when(step < tiles)
    def _():
        here = pl.ds(pl.multiple_of(step * size, size), size)

        @pl.when(step == 0)
        def _():
            weight_copies()[0].wait()

        ctx_s[here, :] = ctx_ref[...]
        resid = x_ref[...].astype(F32) + mm(ctx_ref[...], wo[...]) + vec(5)
        center = resid - jnp.mean(resid, axis=1, keepdims=True)
        inv1 = lax.rsqrt(jnp.mean(center * center, axis=1, keepdims=True) + norm_eps)
        n1 = center * inv1
        h1 = n1 * vec(6) + vec(7)
        h1b = h1.astype(BF16)
        h1_s[here, :] = h1b

        @pl.when(step == 0)
        def _():
            weight_copies()[1].wait()
            weight_copies()[2].wait()

        branch = h1 + vec(8)
        for c in range(chunks):
            cols = slice(c * width, (c + 1) * width)
            act, slope = gelu_pair(mm(h1b, w1[:, cols]) + vec(11 + c))
            act = act.astype(BF16)
            act_s[here, cols] = act
            dg_s[:, cols] = slope
            branch = branch + mm(act, w2[cols, :])
        center = branch - jnp.mean(branch, axis=1, keepdims=True)
        inv2 = lax.rsqrt(jnp.mean(center * center, axis=1, keepdims=True) + norm_eps)
        n2 = center * inv2
        out_ref[...] = (n2 * vec(9) + vec(10)).astype(BF16)
        grad = cot_ref[...].astype(F32)
        gn = grad * n2
        acc[9] += fold(gn)
        acc[10] += fold(grad)
        scaled = grad * vec(9)
        gr2 = inv2 * (
            scaled
            - jnp.mean(scaled, axis=1, keepdims=True)
            - n2 * jnp.mean(scaled * n2, axis=1, keepdims=True)
        )
        gb = gr2.astype(BF16)
        gb_s[here, :] = gb
        acc[8] += fold(gb.astype(F32))
        gh1 = gr2
        for c in range(chunks):
            cols = slice(c * width, (c + 1) * width)
            gpre = (mm_nt(gb, w2[cols, :]) * dg_s[:, cols]).astype(BF16)
            gp_s[here, cols] = gpre
            acc[11 + c] += fold(gpre.astype(F32))
            gh1 = gh1 + mm_nt(gpre, w1[:, cols])
        acc[6] += fold(gh1 * n1)
        acc[7] += fold(gh1)
        scaled = gh1 * vec(6)
        gr1 = inv1 * (
            scaled
            - jnp.mean(scaled, axis=1, keepdims=True)
            - n1 * jnp.mean(scaled * n1, axis=1, keepdims=True)
        )
        gr1_ref[...] = gr1
        ga = gr1.astype(BF16)
        ga_s[here, :] = ga
        acc[5] += fold(ga.astype(F32))
        gctx_ref[...] = mm_nt(ga, wo[...]).astype(BF16)

    for c in range(chunks):
        cols = slice(c * width, (c + 1) * width)

        @pl.when(step == tiles + c)
        def _():
            gw2_ref[...] = mm_tn(act_s[:, cols], gb_s[...]).astype(BF16)

        @pl.when(step == tiles + chunks + c)
        def _():
            gw1_ref[...] = mm_tn(h1_s[...], gp_s[:, cols]).astype(BF16)

    @pl.when(step == tiles + 2 * chunks)
    def _():
        gwo_ref[...] = mm_tn(ctx_s[...], ga_s[...]).astype(BF16)
        for row in range(acc.shape[0]):
            gvec_ref[row : row + 1, :] = jnp.sum(acc[row], axis=0, keepdims=True)


def middle_call(x, ctx, cot, vec, wo, w1, w2, size):
    rows, width = x.shape
    inner = w1.shape[1]
    tiles, chunks = rows // size, inner // width
    tile = pl.BlockSpec((size, width), lambda i: (jnp.minimum(i, tiles - 1), 0))
    hbm = pl.BlockSpec(memory_space=pl.ANY)

    def after(start):
        return lambda i: jnp.clip(i - start, 0, chunks - 1)

    shape = jax.ShapeDtypeStruct
    return pl.pallas_call(
        functools.partial(middle_kernel, tiles),
        grid=(tiles + 2 * chunks + 1,),
        in_specs=[tile, tile, tile, pl.BlockSpec(vec.shape, lambda i: (0, 0)), hbm, hbm, hbm],
        out_specs=[
            tile,
            tile,
            tile,
            pl.BlockSpec((width, width), lambda i: (after(tiles)(i), 0)),
            pl.BlockSpec((width, width), lambda i: (0, after(tiles + chunks)(i))),
            pl.BlockSpec((width, width), lambda i: (0, 0)),
            pl.BlockSpec(vec.shape, lambda i: (0, 0)),
        ],
        out_shape=[
            shape((rows, width), BF16),
            shape((rows, width), F32),
            shape((rows, width), BF16),
            shape((inner, width), BF16),
            shape((width, inner), BF16),
            shape((width, width), BF16),
            shape(vec.shape, F32),
        ],
        scratch_shapes=[
            pltpu.VMEM((width, width), BF16),
            pltpu.VMEM((width, inner), BF16),
            pltpu.VMEM((inner, width), BF16),
            pltpu.VMEM((rows, width), BF16),
            pltpu.VMEM((rows, inner), BF16),
            pltpu.VMEM((rows, width), BF16),
            pltpu.VMEM((rows, inner), BF16),
            pltpu.VMEM((rows, width), BF16),
            pltpu.VMEM((rows, width), BF16),
            pltpu.VMEM((size, inner), F32),
            pltpu.VMEM((vec.shape[0], 8, width), F32),
            pltpu.SemaphoreType.DMA((3,)),
        ],
        compiler_params=pltpu.CompilerParams(vmem_limit_bytes=VMEM_LIMIT),
        name="middle",
    )(x, ctx, cot, vec, wo, w1, w2)


def input_grad_kernel(gp_ref, w_ref, gr1_ref, out_ref):
    out_ref[...] = (gr1_ref[...] + mm_nt(gp_ref[...], w_ref[...])).astype(BF16)


def input_grad_call(gp, w, gr1, size):
    rows, cols = gp.shape
    width = w.shape[0]
    return pl.pallas_call(
        input_grad_kernel,
        grid=(rows // size,),
        in_specs=[
            pl.BlockSpec((size, cols), lambda i: (i, 0)),
            pl.BlockSpec((width, cols), lambda i: (0, 0)),
            pl.BlockSpec((size, width), lambda i: (i, 0)),
        ],
        out_specs=pl.BlockSpec((size, width), lambda i: (i, 0)),
        out_shape=jax.ShapeDtypeStruct((rows, width), BF16),
        compiler_params=pltpu.CompilerParams(vmem_limit_bytes=VMEM_LIMIT),
        name="input_grad",
    )(gp, w, gr1)


def adam_update(master, first_old, second_old, grad_shard, factor, index):
    clipped = grad_shard * factor
    new_first = beta_one * first_old + (1.0 - beta_one) * clipped
    new_second = beta_two * second_old + (1.0 - beta_two) * clipped * clipped
    direction = (
        new_first
        / (1.0 - beta_one**STEP)
        / (jnp.sqrt(new_second / (1.0 - beta_two**STEP)) + adam_eps)
    )
    new_weight = master - rate_table[index] * (direction + decay_table[index] * master)
    return (new_weight, new_first, new_second)


def by_head(array_in):
    rows, cols = array_in.shape
    heads = cols // GROUP
    return array_in.reshape(rows, 6, heads, HEAD).transpose(0, 2, 1, 3).reshape(rows, cols)


def by_block(array_in):
    rows, cols = array_in.shape
    heads = cols // GROUP
    return array_in.reshape(rows, heads, 6, HEAD).transpose(0, 2, 1, 3).reshape(rows, cols)


def body(
    x_in, cotangent, segment_ids, type_ids,
    projection, context_out, expand_weight, reduce_weight, vector_params,
    first_projection, first_context, first_expand, first_reduce, first_vectors,
    second_projection, second_context, second_expand, second_reduce, second_vectors,
):
    seq_count, seq_len, width = x_in.shape
    rows = seq_count * seq_len

    def gather(array_in, axis):
        return lax.all_gather(array_in.astype(BF16), "narrow", axis=axis, tiled=True)

    proj_w = gather(by_head(projection), 0)
    vec_half = gather(vector_params, 1)
    ctx_w, expand_w, reduce_w = gather(context_out, 0), gather(expand_weight, 0), gather(reduce_weight, 0)

    hidden = x_in.reshape(rows, width)
    cot = cotangent.reshape(rows, width)
    word_col = (type_ids == 0).reshape(rows, 1)
    lane = lax.broadcasted_iota(jnp.int32, (rows, LANES), 1)
    word = jnp.broadcast_to(word_col, (rows, LANES)).astype(BF16)
    kmask = ((lane < HEAD) == word_col).astype(BF16)
    same = segment_ids.reshape(rows, 1) == lane
    qaug = jnp.where(same & (lane < 8), 1.0, 0.0).astype(BF16)
    kaug = jnp.where(lane < 8, jnp.where(same, 0.0, FAR), jnp.where(lane < 11, 1.0, 0.0)).astype(BF16)

    zero_row = jnp.zeros((1, width), BF16)
    bias = by_head(jnp.concatenate([vec_half[0:4], zero_row, vec_half[4:5]]).reshape(1, -1)).astype(F32)

    query, keyval = qkv_call(hidden, proj_w, bias, word)
    context, aug = attend_call(query, keyval, qaug, kaug, kmask, seq_len)
    block_out, grad_r1, grad_context, grad_reduce, grad_expand, grad_ctx_w, grad_mid = middle_call(
        hidden, context, cot, vec_half, ctx_w, expand_w, reduce_w, 256
    )
    grad_proj, grad_proj_w, grad_sums = attend_back_call(
        hidden, query, keyval, aug, grad_context, context, kaug, kmask, word, seq_len
    )
    input_grad = input_grad_call(grad_proj, proj_w, grad_r1, 256)
    sum_rows = by_block(grad_sums).reshape(6, width)
    grad_vectors = jnp.concatenate([sum_rows[0:4], sum_rows[5:6], grad_mid[5:]], axis=0)

    def scatter(array_in, axis):
        return lax.psum_scatter(array_in, "narrow", scatter_dimension=axis, tiled=True)

    def over_wide(array_in):
        return lax.psum(array_in.astype(BF16), "wide").astype(F32)

    shards = (
        by_block(over_wide(scatter(grad_proj_w, 0))),
        over_wide(scatter(grad_ctx_w, 0)),
        over_wide(scatter(grad_expand, 0)),
        over_wide(scatter(grad_reduce, 0)),
        over_wide(scatter(grad_vectors, 1)),
    )
    masters = (projection, context_out, expand_weight, reduce_weight, vector_params)
    firsts = (first_projection, first_context, first_expand, first_reduce, first_vectors)
    seconds = (second_projection, second_context, second_expand, second_reduce, second_vectors)
    local_squares = sum((jnp.sum(shard_item * shard_item) for shard_item in shards))
    total_squares = lax.psum(local_squares, "narrow")
    grad_norm = jnp.sqrt(total_squares)
    factor = jnp.minimum(1.0, clip_limit / (grad_norm + 1e-06))
    results = [
        adam_update(masters[index], firsts[index], seconds[index], shards[index], factor, index)
        for index in range(5)
    ]
    out_shape = (seq_count, seq_len, width)
    return (
        block_out.reshape(out_shape),
        input_grad.reshape(out_shape),
        grad_norm,
        *(item[0] for item in results),
        *(item[1] for item in results),
        *(item[2] for item in results),
        *(item[0].astype(BF16) for item in results),
    )


def solution(mesh):
    shard, col = P("narrow", None), P(None, "narrow")
    seqs = P(("wide", "narrow"), None, None)
    group = (shard, shard, shard, shard, col)
    return jax.shard_map(
        body,
        mesh=mesh,
        in_specs=(seqs, seqs, P(("wide", "narrow"), None), P(("wide", "narrow"), None), *group, *group, *group),
        out_specs=(seqs, seqs, P(), *group, *group, *group, *group),
        check_vma=False,
    )
```

```python
import functools

import jax
import jax.numpy as jnp
from jax import lax
from jax.experimental import pallas as pl
from jax.experimental.pallas import tpu as pltpu
from jax.sharding import PartitionSpec as P

HEAD = 64
STEP = 10
LANES = 128
GROUP = 6 * HEAD
LOG2E = 1.4426950408889634
FAR = -1e30
VMEM_LIMIT = 60 * 1024 * 1024

beta_one = 0.9
beta_two = 0.999
adam_eps = 1e-08
norm_eps = 1e-05
clip_limit = 1.0
rate_table = (0.03, 0.3, 0.03, 0.015, 0.4)
decay_table = (0.01, 0.01, 0.01, 0.01, 0.0)

F32 = jnp.float32
BF16 = jnp.bfloat16


def mm(a, b):
    return lax.dot_general(a, b, (((1,), (0,)), ((), ())), preferred_element_type=F32)


def mm_nt(a, b):
    return lax.dot_general(a, b, (((1,), (1,)), ((), ())), preferred_element_type=F32)


def mm_tn(a, b):
    return lax.dot_general(a, b, (((0,), (0,)), ((), ())), preferred_element_type=F32)


def low_lanes(rows):
    return lax.broadcasted_iota(jnp.int32, (rows, LANES), 1) < HEAD


def swap_halves(tile):
    return pltpu.roll(tile, HEAD, 1)


def split_three(col):
    high = col.astype(BF16).astype(F32)
    rest = col - high
    mid = rest.astype(BF16).astype(F32)
    return high, mid, rest - mid


def qkv_tile(prod, bias, word):
    full = prod + bias
    query = jnp.where(word, full[:, 0:LANES], full[:, LANES : 2 * LANES])
    return (query.astype(BF16).astype(F32) * (HEAD**-0.5)).astype(BF16), full[
        :, 2 * LANES :
    ].astype(BF16)


def qkv_kernel(x_ref, w_ref, b_ref, word_ref, q_ref, kv_ref):
    word = word_ref[...] > 0
    for part in range(2):
        cols = slice(part * GROUP, (part + 1) * GROUP)
        query, keyval = qkv_tile(mm(x_ref[...], w_ref[:, cols]), b_ref[:, cols], word)
        out = slice(part * LANES, (part + 1) * LANES)
        q_ref[:, out] = query
        kv_ref[:, out] = keyval


def qkv_call(x, w, bias, word):
    rows, width = x.shape
    steps = w.shape[1] // (2 * GROUP)
    out = jax.ShapeDtypeStruct((rows, steps * 2 * LANES), BF16)
    return pl.pallas_call(
        qkv_kernel,
        grid=(steps,),
        in_specs=[
            pl.BlockSpec((rows, width), lambda i: (0, 0)),
            pl.BlockSpec((width, 2 * GROUP), lambda i: (0, i)),
            pl.BlockSpec((1, 2 * GROUP), lambda i: (0, i)),
            pl.BlockSpec((rows, LANES), lambda i: (0, 0)),
        ],
        out_specs=[pl.BlockSpec((rows, 2 * LANES), lambda i: (0, i))] * 2,
        out_shape=[out, out],
        compiler_params=pltpu.CompilerParams(vmem_limit_bytes=VMEM_LIMIT),
        name="qkv",
    )(x, w, bias, word)


class Links:
    def __init__(self, send, recv):
        self.send, self.recv = send, recv
        self.count = 0
        self.slots = {}
        self.open = []

    def slot(self, key):
        if key not in self.slots:
            self.slots[key] = len(self.slots)
        return self.slots[key]

    def copy(self, key, src, dst, device):
        index = self.slot(key)
        return pltpu.make_async_remote_copy(
            src_ref=src,
            dst_ref=dst,
            send_sem=self.send.at[index],
            recv_sem=self.recv.at[index],
            device_id=device,
            device_id_type=pl.DeviceIdType.MESH,
        )

    def start(self, key, src, dst, device):
        copy = self.copy(key, src, dst, device)
        copy.start()
        self.open.append(copy)

    def arrived(self, key, dst, device):
        self.copy(key, dst, dst, device).wait_recv()

    def finish(self):
        for copy in self.open:
            copy.wait_send()
        self.open = []


class Place:
    def __init__(self, narrow):
        self.wide, self.me = lax.axis_index("wide"), lax.axis_index("narrow")
        self.core = lax.rem(self.me, 2)
        self.z = self.me // 2
        self.depth = narrow // 2
        self.x_quarter = self.wide + 1 - 2 * lax.rem(self.wide, 2)
        self.y_quarter = lax.rem(self.wide + 2, 4)
        self.d_quarter = lax.rem(self.x_quarter + 2, 4)
        self.sib = self.me + 1 - 2 * self.core
        self.x_dev, self.y_dev = {"wide": self.x_quarter}, {"wide": self.y_quarter}
        self.sib_dev = {"narrow": self.sib}

    def ahead(self, k):
        return 2 * lax.rem(self.z + k, self.depth) + self.core

    def behind(self, k, other=False):
        core = 1 - self.core if other else self.core
        return 2 * lax.rem(self.z + self.depth - k, self.depth) + core

    def z_dev(self, k):
        return {"narrow": self.ahead(k)}

    def greet(self):
        barrier = pltpu.get_barrier_semaphore()
        partners = [self.x_dev, self.y_dev, self.sib_dev] + [self.z_dev(k) for k in range(1, self.depth)]
        for device in partners:
            pl.semaphore_signal(barrier, inc=1, device_id=device, device_id_type=pl.DeviceIdType.MESH)
        pl.semaphore_wait(barrier, len(partners))


def spot(start, size, unit):
    return pl.ds(pl.multiple_of(start, unit), size)


def gather_kernel(
    narrow, x_ref, proj_ref, wo_ref, w1_ref, w2_ref, vec_ref, word_ref,
    q_out, kv_out, a_out, e_out, w2_out, vec_out,
    a_full, e_own, w2_own, v_all, bias, q_s, kv_s, send, recv, local,
):
    rows, width = x_ref.shape
    share = proj_ref.shape[0]
    deep = w2_ref.shape[0]
    half, quarter, equarter, dquarter = share // 2, proj_ref.shape[1] // 4, e_own.shape[1] // 4, deep // 4
    heads = width // HEAD
    here = Place(narrow)
    links = Links(send, recv)
    me, steps = here.me, range(1, here.depth)

    def region(kind, owner, part, side=None):
        size, start = (share, 0) if side is None else (half, side * half)
        if kind == "a":
            return a_full.at[spot(owner * share + start, size, 16), spot(part * quarter, quarter, LANES)]
        if kind == "e":
            return e_out.at[spot(owner * share + start, size, 16), spot(part * equarter, equarter, LANES)]
        size, start = (dquarter, 0) if side is None else (dquarter // 2, side * (dquarter // 2))
        return w2_out.at[spot(owner * deep + part * dquarter + start, size, 16), :]

    def whole(kind, owner):
        if kind == "a":
            return a_full.at[spot(owner * share, share, 16), :]
        if kind == "e":
            return e_out.at[spot(owner * share, share, 16), :]
        if kind == "w":
            return w2_out.at[spot(owner * deep, deep, 16), :]
        return v_all.at[owner]

    def own(kind):
        return {"a": whole("a", me), "e": e_own, "w": w2_own, "v": v_all.at[me]}[kind]

    def own_quarter(kind):
        if kind == "a":
            return region("a", me, here.wide)
        if kind == "e":
            return e_own.at[:, spot(here.wide * equarter, equarter, LANES)]
        return w2_own.at[spot(here.wide * dquarter, dquarter, 16), :]

    def send_z(kind, k):
        links.start((kind, "z", k), own_quarter(kind), region(kind, me, here.wide), here.z_dev(k))

    def send_own(kind):
        links.start((kind, "o"), own(kind), whole(kind, me), here.sib_dev)

    def pass_z(kind, k):
        piece = region(kind, here.behind(k), here.wide)
        links.arrived((kind, "z", k), piece, here.z_dev(k))
        links.start((kind, "x", k), piece, piece, here.x_dev)
        links.start((kind, "y", k), piece, piece, here.y_dev)
        links.start((kind, "sz", k), piece, piece, here.sib_dev)

    def pass_xy(kind, k):
        owner = here.behind(k)
        piece = region(kind, owner, here.x_quarter)
        links.arrived((kind, "x", k), piece, here.x_dev)
        part = region(kind, owner, here.x_quarter, 0)
        links.start((kind, "dy", k), part, part, here.y_dev)
        links.start((kind, "sx", k), piece, piece, here.sib_dev)
        piece = region(kind, owner, here.y_quarter)
        links.arrived((kind, "y", k), piece, here.y_dev)
        part = region(kind, owner, here.y_quarter, 1)
        links.start((kind, "dx", k), part, part, here.x_dev)
        links.start((kind, "sy", k), piece, piece, here.sib_dev)

    def pass_d(kind, k):
        owner = here.behind(k)
        links.arrived((kind, "dy", k), region(kind, owner, here.d_quarter, 0), here.y_dev)
        links.arrived((kind, "dx", k), region(kind, owner, here.d_quarter, 1), here.x_dev)
        piece = region(kind, owner, here.d_quarter)
        links.start((kind, "sd", k), piece, piece, here.sib_dev)

    def from_sib(kind, way, part):
        for k in steps:
            links.arrived((kind, way, k), region(kind, here.behind(k, True), part), here.sib_dev)

    low = low_lanes(share)
    for pair in range(heads // 2):
        tiles = [proj_ref[:, slice(b * width + pair * LANES, b * width + (pair + 1) * LANES)] for b in range(6)]
        turned = [swap_halves(tile) for tile in tiles]
        for odd in range(2):
            for b in range(3):
                left, right = (turned[2 * b], tiles[2 * b + 1]) if odd else (tiles[2 * b], turned[2 * b + 1])
                at = (2 * pair + odd) * GROUP + b * LANES
                a_full[spot(me * share, share, 16), at : at + LANES] = jnp.where(low, left, right).astype(BF16)
    v_all[me] = jnp.zeros_like(v_all[me])
    v_all[me, 0 : vec_ref.shape[0], 0 : vec_ref.shape[1]] = vec_ref[...].astype(BF16)

    here.greet()
    for k in steps:
        send_z("a", k)
        links.start(("v", "z", k), v_all.at[me], v_all.at[me], here.z_dev(k))
    send_own("v")
    send_own("a")

    inner = w1_ref.shape[1]
    e_own[:, 0:inner] = w1_ref[...].astype(BF16)
    e_own[:, inner : inner + width] = wo_ref[...].astype(BF16)
    e_own[:, inner + width :] = jnp.zeros((share, e_own.shape[1] - inner - width), BF16)
    w2_own[...] = w2_ref[...].astype(BF16)
    copy_e = pltpu.make_async_copy(e_own, whole("e", me), local.at[0])
    copy_w = pltpu.make_async_copy(w2_own, whole("w", me), local.at[1])
    copy_e.start()
    copy_w.start()

    for k in steps:
        pass_z("a", k)
        send_z("e", k)
        owner = here.behind(k)
        links.arrived(("v", "z", k), v_all.at[owner], here.z_dev(k))
        links.start(("v", "sz", k), v_all.at[owner], v_all.at[owner], here.sib_dev)
    for k in steps:
        pass_xy("a", k)
    send_own("e")
    send_own("w")

    links.arrived(("v", "o"), v_all.at[here.sib], here.sib_dev)
    for k in steps:
        owner = here.behind(k, True)
        links.arrived(("v", "sz", k), v_all.at[owner], here.sib_dev)
    span = vec_ref.shape[1]
    vec_out[...] = jnp.concatenate([v_all[n].astype(F32)[:, 0:span] for n in range(narrow)], axis=1)
    low1 = low_lanes(1)
    for head in range(heads):
        cols = slice((head // 2) * LANES, (head // 2 + 1) * LANES)
        row = [vec_out[r : r + 1, cols] for r in range(4)] + [jnp.zeros((1, LANES), F32), vec_out[4:5, cols]]
        for b in range(3):
            left, right = row[2 * b], row[2 * b + 1]
            left, right = (swap_halves(left), right) if head % 2 else (left, swap_halves(right))
            at = head * GROUP + b * LANES
            bias[0:1, at : at + LANES] = jnp.where(low1, left, right)

    links.arrived(("a", "o"), whole("a", here.sib), here.sib_dev)
    outs = []

    def project(index, part):
        size = 256
        cols = spot(part * quarter, quarter, LANES)
        add = bias[0:1, cols]

        def tile(i, carry):
            at = spot(i * size, size, size)
            prod = mm(x_ref[at, :], a_full[:, cols])
            word = word_ref[at, :] > 0
            for head in range(quarter // GROUP):
                group = slice(head * GROUP, (head + 1) * GROUP)
                out = slice(head * LANES, (head + 1) * LANES)
                query, keyval = qkv_tile(prod[:, group], add[:, group], word)
                q_s[index, at, out] = query
                kv_s[index, at, out] = keyval
            return carry

        lax.fori_loop(0, rows // size, tile, 0)
        wide = q_s.shape[2]
        for number, (source, target) in enumerate(((q_s, q_out), (kv_s, kv_out))):
            copy = pltpu.make_async_copy(
                source.at[index], target.at[:, spot(part * wide, wide, LANES)], local.at[2 + 2 * index + number]
            )
            copy.start()
            outs.append(copy)

    from_sib("a", "sz", here.wide)
    project(0, here.wide)
    for k in steps:
        pass_z("e", k)
        send_z("w", k)
    for k in steps:
        pass_d("a", k)
    from_sib("a", "sx", here.x_quarter)
    project(1, here.x_quarter)
    for k in steps:
        pass_xy("e", k)
    from_sib("a", "sy", here.y_quarter)
    project(2, here.y_quarter)
    from_sib("a", "sd", here.d_quarter)
    project(3, here.d_quarter)
    copy_a = pltpu.make_async_copy(a_full, a_out, local.at[10])
    copy_a.start()
    for k in steps:
        pass_z("w", k)
    for k in steps:
        pass_d("e", k)
    for k in steps:
        pass_xy("w", k)
    for k in steps:
        pass_d("w", k)
    for kind in ("e", "w"):
        links.arrived((kind, "o"), whole(kind, here.sib), here.sib_dev)
        for way, part in (("sz", here.wide), ("sx", here.x_quarter), ("sy", here.y_quarter), ("sd", here.d_quarter)):
            from_sib(kind, way, part)
    links.finish()
    for copy in (copy_e, copy_w, copy_a, *outs):
        copy.wait()


def gather_call(narrow, x, proj, wo, w1, w2, vec, word):
    rows, width = x.shape
    share, deep, inner = proj.shape[0], w2.shape[0], w1.shape[1]
    ecols = inner + width + 2 * LANES
    heads = width // HEAD
    depth = narrow // 2
    count = 3 * (1 + 9 * (depth - 1)) + 1 + 2 * (depth - 1)
    vmem = pl.BlockSpec(memory_space=pltpu.VMEM)
    hbm = pl.BlockSpec(memory_space=pl.ANY)
    shape = jax.ShapeDtypeStruct
    part = heads // 4 * LANES
    return pl.pallas_call(
        functools.partial(gather_kernel, narrow),
        in_specs=[vmem] * 7,
        out_specs=[hbm] * 5 + [vmem],
        out_shape=[
            shape((rows, heads * LANES), BF16),
            shape((rows, heads * LANES), BF16),
            shape((width, proj.shape[1]), BF16),
            shape((width, ecols), BF16),
            shape((deep * narrow, width), BF16),
            shape((16, width), F32),
        ],
        scratch_shapes=[
            pltpu.VMEM((width, proj.shape[1]), BF16),
            pltpu.VMEM((share, ecols), BF16),
            pltpu.VMEM((deep, width), BF16),
            pltpu.VMEM((narrow, 16, LANES), BF16),
            pltpu.VMEM((8, proj.shape[1]), F32),
            pltpu.VMEM((4, rows, part), BF16),
            pltpu.VMEM((4, rows, part), BF16),
            pltpu.SemaphoreType.DMA((count,)),
            pltpu.SemaphoreType.DMA((count,)),
            pltpu.SemaphoreType.DMA((11,)),
        ],
        compiler_params=pltpu.CompilerParams(
            vmem_limit_bytes=VMEM_LIMIT, collective_id=0, has_side_effects=True
        ),
        name="gather",
    )(x, proj, wo, w1, w2, vec, word)


def key_pair(keyval, kmask, low):
    wide = keyval.astype(F32)
    return (jnp.where(low, wide, swap_halves(wide)) * kmask.astype(F32)).astype(BF16)


def attend_kernel(q_ref, kv_ref, qa_ref, ka_ref, km_ref, ctx_ref, aug_ref):
    rows = q_ref.shape[0]
    low = low_lanes(rows)
    lane = lax.broadcasted_iota(jnp.int32, (rows, LANES), 1)
    outs = []
    for part in range(2):
        cols = slice(part * LANES, (part + 1) * LANES)
        keyval = kv_ref[:, cols]
        keys = jnp.concatenate([key_pair(keyval, km_ref[...], low), ka_ref[...]], axis=1)
        query = jnp.concatenate([q_ref[:, cols], qa_ref[...]], axis=1)
        scores = mm_nt(query, keys)
        top = jnp.max(scores, axis=1, keepdims=True)
        weight = jnp.exp2((scores - top) * LOG2E).astype(BF16)
        ones_val = jnp.where(low, 1.0, keyval.astype(F32)).astype(BF16)
        both = mm(weight, ones_val)
        total = swap_halves(both)
        outs.append(both / total)
        log_total = top + jnp.log(jnp.where(low, both, total))
        high, mid, rest = split_three(log_total)
        extra = jnp.where(lane == 8, -high, jnp.where(lane == 9, -mid, jnp.where(lane == 10, -rest, 0.0)))
        aug_ref[:, cols] = jnp.where(lane < 8, qa_ref[...].astype(F32), extra).astype(BF16)
    ctx_ref[...] = jnp.where(low, swap_halves(outs[0]), outs[1]).astype(BF16)


def attend_call(q, kv, qa, ka, km, length):
    rows, cols = q.shape
    seqs, steps = rows // length, cols // (2 * LANES)
    pair = pl.BlockSpec((length, 2 * LANES), lambda s, i: (s, i))
    one = pl.BlockSpec((length, LANES), lambda s, i: (s, 0))
    return pl.pallas_call(
        attend_kernel,
        grid=(seqs, steps),
        in_specs=[pair, pair, one, one, one],
        out_specs=[pl.BlockSpec((length, LANES), lambda s, i: (s, i)), pair],
        out_shape=[
            jax.ShapeDtypeStruct((rows, cols // 2), BF16),
            jax.ShapeDtypeStruct((rows, cols), BF16),
        ],
        compiler_params=pltpu.CompilerParams(vmem_limit_bytes=VMEM_LIMIT),
        name="attend",
    )(q, kv, qa, ka, km)


def attend_back_head(query, keyval, aug, gcon, con, kaug, kmask, word, odd, low, lane):
    keys = key_pair(keyval, kmask, low)
    scores_t = mm_nt(jnp.concatenate([keys, kaug], axis=1), jnp.concatenate([query, aug], axis=1))
    probs_t = jnp.exp2(scores_t * LOG2E)
    gwide = gcon.astype(F32)
    prod = gwide * con.astype(F32)
    mine = low != odd
    delta = jnp.sum(jnp.where(mine, prod, 0.0), axis=1, keepdims=True)
    high, mid, rest = split_three(delta)
    extra = jnp.where(lane == 0, -high, jnp.where(lane == 1, -mid, jnp.where(lane == 2, -rest, 0.0)))
    ghead = jnp.where(low, extra, jnp.where(odd, gwide, swap_halves(gwide))).astype(BF16)
    ones_val = jnp.where(low, jnp.where(lane < 3, 1.0, 0.0), keyval.astype(F32)).astype(BF16)
    gscores_t = (probs_t * mm_nt(ones_val, ghead)).astype(BF16)
    gval = mm(probs_t.astype(BF16), ghead)
    gkey = mm(gscores_t, query)
    gquery = (jnp.transpose(mm_tn(keys, gscores_t)) * (HEAD**-0.5)).astype(BF16)
    zero = jnp.zeros_like(gquery)
    gkey = jnp.where(kmask.astype(F32) > 0, gkey, 0.0)
    gkey = gkey + swap_halves(gkey)
    return (
        jnp.where(word, gquery, zero),
        jnp.where(word, zero, gquery),
        jnp.where(low, gkey, gval).astype(BF16),
    )


def attend_back_kernel(
    length, x_ref, q_ref, kv_ref, aug_ref, gc_ref, ctx_ref, ka_ref, km_ref, word_ref, gp_ref, gw_ref, sum_ref, xt
):
    step = pl.program_id(0)
    rows = x_ref.shape[0]

    @pl.when(step == 0)
    def _():
        xt[...] = jnp.transpose(x_ref[...])

    low = low_lanes(length)
    lane = lax.broadcasted_iota(jnp.int32, (length, LANES), 1)
    odd = lax.rem(step, 2) == 1
    for seq in range(rows // length):
        here = slice(seq * length, (seq + 1) * length)
        tiles = attend_back_head(
            q_ref[here], kv_ref[here], aug_ref[here], gc_ref[here], ctx_ref[here],
            ka_ref[here], km_ref[here], word_ref[here] > 0, odd, low, lane,
        )
        for index, tile in enumerate(tiles):
            gp_ref[here, index * LANES : (index + 1) * LANES] = tile
    grads = gp_ref[...]
    gw_ref[...] = mm(xt[...], grads).astype(BF16)
    sums = jnp.sum(grads.astype(F32).reshape(rows // 8, 8, GROUP), axis=0)
    sum_ref[...] = jnp.sum(sums, axis=0, keepdims=True)


def attend_back_call(x, q, kv, aug, gc, ctx, ka, km, word, length):
    rows, width = x.shape
    heads = q.shape[1] // LANES
    head = pl.BlockSpec((rows, LANES), lambda h: (0, h))
    pair = pl.BlockSpec((rows, LANES), lambda h: (0, h // 2))
    one = pl.BlockSpec((rows, LANES), lambda h: (0, 0))
    return pl.pallas_call(
        functools.partial(attend_back_kernel, length),
        grid=(heads,),
        in_specs=[pl.BlockSpec((rows, width), lambda h: (0, 0)), head, head, head, pair, pair, one, one, one],
        out_specs=[
            pl.BlockSpec((rows, GROUP), lambda h: (0, h)),
            pl.BlockSpec((width, GROUP), lambda h: (0, h)),
            pl.BlockSpec((1, GROUP), lambda h: (0, h)),
        ],
        out_shape=[
            jax.ShapeDtypeStruct((rows, heads * GROUP), BF16),
            jax.ShapeDtypeStruct((width, heads * GROUP), BF16),
            jax.ShapeDtypeStruct((1, heads * GROUP), F32),
        ],
        scratch_shapes=[pltpu.VMEM((width, rows), BF16)],
        compiler_params=pltpu.CompilerParams(vmem_limit_bytes=VMEM_LIMIT),
        name="attend_back",
    )(x, q, kv, aug, gc, ctx, ka, km, word)


def gelu_pair(pre):
    size = jnp.abs(pre) * (0.5**0.5)
    bell = jnp.exp2(pre * pre * (-0.5 * LOG2E))
    t = 1.0 / (1.0 + 0.3275911 * size)
    poly = t * (0.254829592 + t * (-0.284496736 + t * (1.421413741 + t * (-1.453152027 + t * 1.061405429))))
    tail = 0.5 * poly * bell
    share = jnp.where(pre >= 0, 1.0 - tail, tail)
    return pre * share, share + pre * bell * 0.3989422804014327


def fold(array_in):
    rows, cols = array_in.shape
    return jnp.sum(array_in.reshape(rows // 8, 8, cols), axis=0)


def middle_kernel(
    tiles, x_ref, ctx_ref, cot_ref, vec_ref, e_hbm, w2_hbm,
    out_ref, gr1_ref, gctx_ref, gw2_ref, gw1_ref, gwo_ref, gvec_ref,
    wo, w1, w2, h1_s, act_s, gb_s, gp_s, ga_s, ctx_s, dg_s, acc, sems,
):
    step = pl.program_id(0)
    size, width = x_ref.shape
    inner = w1.shape[1]
    chunks = inner // width

    def weight_copies(index):
        source, target = (
            (e_hbm.at[:, inner : inner + width], wo),
            (e_hbm.at[:, 0:inner], w1),
            (w2_hbm, w2),
        )[index]
        return pltpu.make_async_copy(source, target, sems.at[index])

    @pl.when(step == 0)
    def _():
        for index in range(3):
            weight_copies(index).start()
        acc[...] = jnp.zeros_like(acc)

    def vec(row):
        return vec_ref[row : row + 1, :].astype(F32)

    @pl.when(step < tiles)
    def _():
        here = pl.ds(pl.multiple_of(step * size, size), size)

        @pl.when(step == 0)
        def _():
            weight_copies(0).wait()

        ctx_s[here, :] = ctx_ref[...]
        resid = x_ref[...].astype(F32) + mm(ctx_ref[...], wo[...]) + vec(5)
        center = resid - jnp.mean(resid, axis=1, keepdims=True)
        inv1 = lax.rsqrt(jnp.mean(center * center, axis=1, keepdims=True) + norm_eps)
        n1 = center * inv1
        h1 = n1 * vec(6) + vec(7)
        h1b = h1.astype(BF16)
        h1_s[here, :] = h1b

        @pl.when(step == 0)
        def _():
            weight_copies(1).wait()
            weight_copies(2).wait()

        branch = h1 + vec(8)
        for c in range(chunks):
            cols = slice(c * width, (c + 1) * width)
            act, slope = gelu_pair(mm(h1b, w1[:, cols]) + vec(11 + c))
            act = act.astype(BF16)
            act_s[here, cols] = act
            dg_s[:, cols] = slope
            branch = branch + mm(act, w2[cols, :])
        center = branch - jnp.mean(branch, axis=1, keepdims=True)
        inv2 = lax.rsqrt(jnp.mean(center * center, axis=1, keepdims=True) + norm_eps)
        n2 = center * inv2
        out_ref[...] = (n2 * vec(9) + vec(10)).astype(BF16)
        grad = cot_ref[...].astype(F32)
        gn = grad * n2
        acc[9] += fold(gn)
        acc[10] += fold(grad)
        scaled = grad * vec(9)
        gr2 = inv2 * (
            scaled
            - jnp.mean(scaled, axis=1, keepdims=True)
            - n2 * jnp.mean(scaled * n2, axis=1, keepdims=True)
        )
        gb = gr2.astype(BF16)
        gb_s[here, :] = gb
        acc[8] += fold(gb.astype(F32))
        gh1 = gr2
        for c in range(chunks):
            cols = slice(c * width, (c + 1) * width)
            gpre = (mm_nt(gb, w2[cols, :]) * dg_s[:, cols]).astype(BF16)
            gp_s[here, cols] = gpre
            acc[11 + c] += fold(gpre.astype(F32))
            gh1 = gh1 + mm_nt(gpre, w1[:, cols])
        acc[6] += fold(gh1 * n1)
        acc[7] += fold(gh1)
        scaled = gh1 * vec(6)
        gr1 = inv1 * (
            scaled
            - jnp.mean(scaled, axis=1, keepdims=True)
            - n1 * jnp.mean(scaled * n1, axis=1, keepdims=True)
        )
        gr1_ref[...] = gr1
        ga = gr1.astype(BF16)
        ga_s[here, :] = ga
        acc[5] += fold(ga.astype(F32))
        gctx_ref[...] = mm_nt(ga, wo[...]).astype(BF16)

    for c in range(chunks):
        cols = slice(c * width, (c + 1) * width)

        @pl.when(step == tiles + c)
        def _():
            gw2_ref[...] = mm_tn(act_s[:, cols], gb_s[...]).astype(BF16)

        @pl.when(step == tiles + chunks + c)
        def _():
            gw1_ref[...] = mm_tn(h1_s[...], gp_s[:, cols]).astype(BF16)

    @pl.when(step == tiles + 2 * chunks)
    def _():
        gwo_ref[...] = mm_tn(ctx_s[...], ga_s[...]).astype(BF16)
        for row in range(acc.shape[0]):
            gvec_ref[row : row + 1, :] = jnp.sum(acc[row], axis=0, keepdims=True)


def middle_call(x, ctx, cot, vec, e, w2, size):
    rows, width = x.shape
    inner = w2.shape[0]
    tiles, chunks = rows // size, inner // width
    tile = pl.BlockSpec((size, width), lambda i: (jnp.minimum(i, tiles - 1), 0))
    hbm = pl.BlockSpec(memory_space=pl.ANY)

    def after(start):
        return lambda i: jnp.clip(i - start, 0, chunks - 1)

    shape = jax.ShapeDtypeStruct
    return pl.pallas_call(
        functools.partial(middle_kernel, tiles),
        grid=(tiles + 2 * chunks + 1,),
        in_specs=[tile, tile, tile, pl.BlockSpec(vec.shape, lambda i: (0, 0)), hbm, hbm],
        out_specs=[
            tile,
            tile,
            tile,
            pl.BlockSpec((width, width), lambda i: (after(tiles)(i), 0)),
            pl.BlockSpec((width, width), lambda i: (0, after(tiles + chunks)(i))),
            pl.BlockSpec((width, width), lambda i: (0, 0)),
            pl.BlockSpec(vec.shape, lambda i: (0, 0)),
        ],
        out_shape=[
            shape((rows, width), BF16),
            shape((rows, width), F32),
            shape((rows, width), BF16),
            shape((inner, width), BF16),
            shape((width, inner), BF16),
            shape((width, width), BF16),
            shape(vec.shape, F32),
        ],
        scratch_shapes=[
            pltpu.VMEM((width, width), BF16),
            pltpu.VMEM((width, inner), BF16),
            pltpu.VMEM((inner, width), BF16),
            pltpu.VMEM((rows, width), BF16),
            pltpu.VMEM((rows, inner), BF16),
            pltpu.VMEM((rows, width), BF16),
            pltpu.VMEM((rows, inner), BF16),
            pltpu.VMEM((rows, width), BF16),
            pltpu.VMEM((rows, width), BF16),
            pltpu.VMEM((size, inner), F32),
            pltpu.VMEM((vec.shape[0], 8, width), F32),
            pltpu.SemaphoreType.DMA((3,)),
        ],
        compiler_params=pltpu.CompilerParams(vmem_limit_bytes=VMEM_LIMIT),
        name="middle",
    )(x, ctx, cot, vec, e, w2)


def input_grad_kernel(gp_ref, w_ref, gr1_ref, out_ref):
    out_ref[...] = (gr1_ref[...] + mm_nt(gp_ref[...], w_ref[...])).astype(BF16)


def input_grad_call(gp, w, gr1, size):
    rows, cols = gp.shape
    width = w.shape[0]
    return pl.pallas_call(
        input_grad_kernel,
        grid=(rows // size,),
        in_specs=[
            pl.BlockSpec((size, cols), lambda i: (i, 0)),
            pl.BlockSpec((width, cols), lambda i: (0, 0)),
            pl.BlockSpec((size, width), lambda i: (i, 0)),
        ],
        out_specs=pl.BlockSpec((size, width), lambda i: (i, 0)),
        out_shape=jax.ShapeDtypeStruct((rows, width), BF16),
        compiler_params=pltpu.CompilerParams(vmem_limit_bytes=VMEM_LIMIT),
        name="input_grad",
    )(gp, w, gr1)


def adam_update(master, first_old, second_old, grad_shard, factor, index):
    clipped = grad_shard * factor
    new_first = beta_one * first_old + (1.0 - beta_one) * clipped
    new_second = beta_two * second_old + (1.0 - beta_two) * clipped * clipped
    direction = (
        new_first
        / (1.0 - beta_one**STEP)
        / (jnp.sqrt(new_second / (1.0 - beta_two**STEP)) + adam_eps)
    )
    new_weight = master - rate_table[index] * (direction + decay_table[index] * master)
    return (new_weight, new_first, new_second)


def by_head(array_in):
    rows, cols = array_in.shape
    heads = cols // GROUP
    return array_in.reshape(rows, 6, heads, HEAD).transpose(0, 2, 1, 3).reshape(rows, cols)


def by_block(array_in):
    rows, cols = array_in.shape
    heads = cols // GROUP
    return array_in.reshape(rows, heads, 6, HEAD).transpose(0, 2, 1, 3).reshape(rows, cols)


def can_pass_pieces(wide, narrow, width, deep):
    share = width // narrow
    return wide == 4 and narrow % 2 == 0 and narrow > 2 and share % 32 == 0 and deep % 128 == 0


def body(
    x_in, cotangent, segment_ids, type_ids,
    projection, context_out, expand_weight, reduce_weight, vector_params,
    first_projection, first_context, first_expand, first_reduce, first_vectors,
    second_projection, second_context, second_expand, second_reduce, second_vectors,
):
    seq_count, seq_len, width = x_in.shape
    rows = seq_count * seq_len

    def gather(array_in, axis):
        return lax.all_gather(array_in.astype(BF16), "narrow", axis=axis, tiled=True)

    hidden = x_in.reshape(rows, width)
    cot = cotangent.reshape(rows, width)
    word_col = (type_ids == 0).reshape(rows, 1)
    lane = lax.broadcasted_iota(jnp.int32, (rows, LANES), 1)
    word = jnp.broadcast_to(word_col, (rows, LANES)).astype(BF16)
    kmask = ((lane < HEAD) == word_col).astype(BF16)
    same = segment_ids.reshape(rows, 1) == lane
    qaug = jnp.where(same & (lane < 8), 1.0, 0.0).astype(BF16)
    kaug = jnp.where(lane < 8, jnp.where(same, 0.0, FAR), jnp.where(lane < 11, 1.0, 0.0)).astype(BF16)

    narrow = lax.axis_size("narrow")
    if can_pass_pieces(lax.axis_size("wide"), narrow, width, reduce_weight.shape[0]):
        query, keyval, proj_w, mid_w, reduce_w, vec_rows = gather_call(
            narrow, hidden, projection, context_out, expand_weight, reduce_weight, vector_params, word
        )
    else:
        proj_w, vec_half = gather(by_head(projection), 0), gather(vector_params, 1)
        reduce_w = gather(reduce_weight, 0)
        mid_w = jnp.concatenate(
            [gather(expand_weight, 0), gather(context_out, 0), jnp.zeros((width, 2 * LANES), BF16)], axis=1
        )
        zero_row = jnp.zeros((1, width), BF16)
        bias = by_head(jnp.concatenate([vec_half[0:4], zero_row, vec_half[4:5]]).reshape(1, -1)).astype(F32)
        vec_rows = jnp.pad(vec_half.astype(F32), ((0, 1), (0, 0)))
        query, keyval = qkv_call(hidden, proj_w, bias, word)
    context, aug = attend_call(query, keyval, qaug, kaug, kmask, seq_len)
    block_out, grad_r1, grad_context, grad_reduce, grad_expand, grad_ctx_w, grad_mid = middle_call(
        hidden, context, cot, vec_rows, mid_w, reduce_w, 256
    )
    grad_proj, grad_proj_w, grad_sums = attend_back_call(
        hidden, query, keyval, aug, grad_context, context, kaug, kmask, word, seq_len
    )
    input_grad = input_grad_call(grad_proj, proj_w, grad_r1, 256)
    sum_rows = by_block(grad_sums).reshape(6, width)
    grad_vectors = jnp.concatenate([sum_rows[0:4], sum_rows[5:6], grad_mid[5:15]], axis=0)

    def scatter(array_in, axis):
        return lax.psum_scatter(array_in, "narrow", scatter_dimension=axis, tiled=True)

    def over_wide(array_in):
        return lax.psum(array_in.astype(BF16), "wide").astype(F32)

    shards = (
        by_block(over_wide(scatter(grad_proj_w, 0))),
        over_wide(scatter(grad_ctx_w, 0)),
        over_wide(scatter(grad_expand, 0)),
        over_wide(scatter(grad_reduce, 0)),
        over_wide(scatter(grad_vectors, 1)),
    )
    masters = (projection, context_out, expand_weight, reduce_weight, vector_params)
    firsts = (first_projection, first_context, first_expand, first_reduce, first_vectors)
    seconds = (second_projection, second_context, second_expand, second_reduce, second_vectors)
    local_squares = sum((jnp.sum(shard_item * shard_item) for shard_item in shards))
    total_squares = lax.psum(local_squares, "narrow")
    grad_norm = jnp.sqrt(total_squares)
    factor = jnp.minimum(1.0, clip_limit / (grad_norm + 1e-06))
    results = [
        adam_update(masters[index], firsts[index], seconds[index], shards[index], factor, index)
        for index in range(5)
    ]
    out_shape = (seq_count, seq_len, width)
    return (
        block_out.reshape(out_shape),
        input_grad.reshape(out_shape),
        grad_norm,
        *(item[0] for item in results),
        *(item[1] for item in results),
        *(item[2] for item in results),
        *(item[0].astype(BF16) for item in results),
    )


def solution(mesh):
    shard, col = P("narrow", None), P(None, "narrow")
    seqs = P(("wide", "narrow"), None, None)
    group = (shard, shard, shard, shard, col)
    return jax.shard_map(
        body,
        mesh=mesh,
        in_specs=(seqs, seqs, P(("wide", "narrow"), None), P(("wide", "narrow"), None), *group, *group, *group),
        out_specs=(seqs, seqs, P(), *group, *group, *group, *group),
        check_vma=False,
    )
```

```python
import functools

import jax
import jax.numpy as jnp
from jax import lax
from jax.experimental import pallas as pl
from jax.experimental.pallas import tpu as pltpu
from jax.sharding import PartitionSpec as P

HEAD = 64
STEP = 10
LANES = 128
GROUP = 6 * HEAD
LOG2E = 1.4426950408889634
FAR = -1e30
VMEM_LIMIT = 60 * 1024 * 1024

beta_one = 0.9
beta_two = 0.999
adam_eps = 1e-08
norm_eps = 1e-05
clip_limit = 1.0
rate_table = (0.03, 0.3, 0.03, 0.015, 0.4)
decay_table = (0.01, 0.01, 0.01, 0.01, 0.0)

F32 = jnp.float32
BF16 = jnp.bfloat16


def mm(a, b):
    return lax.dot_general(a, b, (((1,), (0,)), ((), ())), preferred_element_type=F32)


def mm_nt(a, b):
    return lax.dot_general(a, b, (((1,), (1,)), ((), ())), preferred_element_type=F32)


def mm_tn(a, b):
    return lax.dot_general(a, b, (((0,), (0,)), ((), ())), preferred_element_type=F32)


def low_lanes(rows):
    return lax.broadcasted_iota(jnp.int32, (rows, LANES), 1) < HEAD


def swap_halves(tile):
    return pltpu.roll(tile, HEAD, 1)


def split_three(col):
    high = col.astype(BF16).astype(F32)
    rest = col - high
    mid = rest.astype(BF16).astype(F32)
    return high, mid, rest - mid


def qkv_tile(prod, bias, word):
    full = prod + bias
    query = jnp.where(word, full[:, 0:LANES], full[:, LANES : 2 * LANES])
    return (query.astype(BF16).astype(F32) * (HEAD**-0.5)).astype(BF16), full[
        :, 2 * LANES :
    ].astype(BF16)


def qkv_kernel(x_ref, w_ref, b_ref, word_ref, q_ref, kv_ref):
    word = word_ref[...] > 0
    for part in range(2):
        cols = slice(part * GROUP, (part + 1) * GROUP)
        query, keyval = qkv_tile(mm(x_ref[...], w_ref[:, cols]), b_ref[:, cols], word)
        out = slice(part * LANES, (part + 1) * LANES)
        q_ref[:, out] = query
        kv_ref[:, out] = keyval


def qkv_call(x, w, bias, word):
    rows, width = x.shape
    steps = w.shape[1] // (2 * GROUP)
    out = jax.ShapeDtypeStruct((rows, steps * 2 * LANES), BF16)
    return pl.pallas_call(
        qkv_kernel,
        grid=(steps,),
        in_specs=[
            pl.BlockSpec((rows, width), lambda i: (0, 0)),
            pl.BlockSpec((width, 2 * GROUP), lambda i: (0, i)),
            pl.BlockSpec((1, 2 * GROUP), lambda i: (0, i)),
            pl.BlockSpec((rows, LANES), lambda i: (0, 0)),
        ],
        out_specs=[pl.BlockSpec((rows, 2 * LANES), lambda i: (0, i))] * 2,
        out_shape=[out, out],
        compiler_params=pltpu.CompilerParams(vmem_limit_bytes=VMEM_LIMIT),
        name="qkv",
    )(x, w, bias, word)


class Links:
    def __init__(self, send, recv):
        self.send, self.recv = send, recv
        self.count = 0
        self.slots = {}
        self.open = []

    def slot(self, key):
        if key not in self.slots:
            self.slots[key] = len(self.slots)
        return self.slots[key]

    def copy(self, key, src, dst, device):
        index = self.slot(key)
        return pltpu.make_async_remote_copy(
            src_ref=src,
            dst_ref=dst,
            send_sem=self.send.at[index],
            recv_sem=self.recv.at[index],
            device_id=device,
            device_id_type=pl.DeviceIdType.MESH,
        )

    def start(self, key, src, dst, device):
        copy = self.copy(key, src, dst, device)
        copy.start()
        self.open.append(copy)

    def arrived(self, key, dst, device):
        self.copy(key, dst, dst, device).wait_recv()

    def finish(self):
        for copy in self.open:
            copy.wait_send()
        self.open = []


class Place:
    def __init__(self, narrow):
        self.wide, self.me = lax.axis_index("wide"), lax.axis_index("narrow")
        self.core = lax.rem(self.me, 2)
        self.z = self.me // 2
        self.depth = narrow // 2
        self.x_quarter = self.wide + 1 - 2 * lax.rem(self.wide, 2)
        self.y_quarter = lax.rem(self.wide + 2, 4)
        self.d_quarter = lax.rem(self.x_quarter + 2, 4)
        self.sib = self.me + 1 - 2 * self.core
        self.x_dev, self.y_dev = {"wide": self.x_quarter}, {"wide": self.y_quarter}
        self.sib_dev = {"narrow": self.sib}

    def ahead(self, k):
        return 2 * lax.rem(self.z + k, self.depth) + self.core

    def behind(self, k, other=False):
        core = 1 - self.core if other else self.core
        return 2 * lax.rem(self.z + self.depth - k, self.depth) + core

    def z_dev(self, k):
        return {"narrow": self.ahead(k)}

    def greet(self):
        barrier = pltpu.get_barrier_semaphore()
        partners = [self.x_dev, self.y_dev, self.sib_dev] + [self.z_dev(k) for k in range(1, self.depth)]
        for device in partners:
            pl.semaphore_signal(barrier, inc=1, device_id=device, device_id_type=pl.DeviceIdType.MESH)
        pl.semaphore_wait(barrier, len(partners))


def spot(start, size, unit):
    return pl.ds(pl.multiple_of(start, unit), size)


def gather_kernel(
    narrow, x_ref, proj_ref, wo_ref, w1_ref, w2_ref, vec_ref, word_ref,
    q_out, kv_out, a_out, e_out, w2_out, vec_out,
    a_full, e_own, w2_own, v_all, bias, q_s, kv_s, send, recv, local,
):
    rows, width = x_ref.shape
    share = proj_ref.shape[0]
    deep = w2_ref.shape[0]
    half, quarter, equarter, dquarter = share // 2, proj_ref.shape[1] // 4, e_own.shape[1] // 4, deep // 4
    heads = width // HEAD
    here = Place(narrow)
    links = Links(send, recv)
    me, steps = here.me, range(1, here.depth)

    def region(kind, owner, part, side=None):
        size, start = (share, 0) if side is None else (half, side * half)
        if kind == "a":
            return a_full.at[spot(owner * share + start, size, 16), spot(part * quarter, quarter, LANES)]
        if kind == "e":
            return e_out.at[spot(owner * share + start, size, 16), spot(part * equarter, equarter, LANES)]
        size, start = (dquarter, 0) if side is None else (dquarter // 2, side * (dquarter // 2))
        return w2_out.at[spot(owner * deep + part * dquarter + start, size, 16), :]

    def whole(kind, owner):
        if kind == "a":
            return a_full.at[spot(owner * share, share, 16), :]
        if kind == "e":
            return e_out.at[spot(owner * share, share, 16), :]
        if kind == "w":
            return w2_out.at[spot(owner * deep, deep, 16), :]
        return v_all.at[owner]

    def own(kind):
        return {"a": whole("a", me), "e": e_own, "w": w2_own, "v": v_all.at[me]}[kind]

    def own_quarter(kind):
        if kind == "a":
            return region("a", me, here.wide)
        if kind == "e":
            return e_own.at[:, spot(here.wide * equarter, equarter, LANES)]
        return w2_own.at[spot(here.wide * dquarter, dquarter, 16), :]

    def send_z(kind, k):
        links.start((kind, "z", k), own_quarter(kind), region(kind, me, here.wide), here.z_dev(k))

    def send_own(kind):
        links.start((kind, "o"), own(kind), whole(kind, me), here.sib_dev)

    def pass_z(kind, k):
        piece = region(kind, here.behind(k), here.wide)
        links.arrived((kind, "z", k), piece, here.z_dev(k))
        links.start((kind, "x", k), piece, piece, here.x_dev)
        links.start((kind, "y", k), piece, piece, here.y_dev)
        links.start((kind, "sz", k), piece, piece, here.sib_dev)

    def pass_xy(kind, k):
        owner = here.behind(k)
        piece = region(kind, owner, here.x_quarter)
        links.arrived((kind, "x", k), piece, here.x_dev)
        part = region(kind, owner, here.x_quarter, 0)
        links.start((kind, "dy", k), part, part, here.y_dev)
        links.start((kind, "sx", k), piece, piece, here.sib_dev)
        piece = region(kind, owner, here.y_quarter)
        links.arrived((kind, "y", k), piece, here.y_dev)
        part = region(kind, owner, here.y_quarter, 1)
        links.start((kind, "dx", k), part, part, here.x_dev)
        links.start((kind, "sy", k), piece, piece, here.sib_dev)

    def pass_d(kind, k):
        owner = here.behind(k)
        links.arrived((kind, "dy", k), region(kind, owner, here.d_quarter, 0), here.y_dev)
        links.arrived((kind, "dx", k), region(kind, owner, here.d_quarter, 1), here.x_dev)
        piece = region(kind, owner, here.d_quarter)
        links.start((kind, "sd", k), piece, piece, here.sib_dev)

    def from_sib(kind, way, part):
        for k in steps:
            links.arrived((kind, way, k), region(kind, here.behind(k, True), part), here.sib_dev)

    low = low_lanes(share)
    for pair in range(heads // 2):
        tiles = [proj_ref[:, slice(b * width + pair * LANES, b * width + (pair + 1) * LANES)] for b in range(6)]
        turned = [swap_halves(tile) for tile in tiles]
        for odd in range(2):
            for b in range(3):
                left, right = (turned[2 * b], tiles[2 * b + 1]) if odd else (tiles[2 * b], turned[2 * b + 1])
                at = (2 * pair + odd) * GROUP + b * LANES
                a_full[spot(me * share, share, 16), at : at + LANES] = jnp.where(low, left, right).astype(BF16)
    v_all[me] = jnp.zeros_like(v_all[me])
    v_all[me, 0 : vec_ref.shape[0], 0 : vec_ref.shape[1]] = vec_ref[...].astype(BF16)

    here.greet()
    for k in steps:
        send_z("a", k)
        links.start(("v", "z", k), v_all.at[me], v_all.at[me], here.z_dev(k))
    send_own("v")
    send_own("a")

    inner = w1_ref.shape[1]
    e_own[:, 0:inner] = w1_ref[...].astype(BF16)
    e_own[:, inner : inner + width] = wo_ref[...].astype(BF16)
    e_own[:, inner + width :] = jnp.zeros((share, e_own.shape[1] - inner - width), BF16)
    w2_own[...] = w2_ref[...].astype(BF16)
    copy_e = pltpu.make_async_copy(e_own, whole("e", me), local.at[0])
    copy_w = pltpu.make_async_copy(w2_own, whole("w", me), local.at[1])
    copy_e.start()
    copy_w.start()

    for k in steps:
        pass_z("a", k)
        send_z("e", k)
        owner = here.behind(k)
        links.arrived(("v", "z", k), v_all.at[owner], here.z_dev(k))
        links.start(("v", "sz", k), v_all.at[owner], v_all.at[owner], here.sib_dev)
    for k in steps:
        pass_xy("a", k)
    send_own("e")
    send_own("w")

    links.arrived(("v", "o"), v_all.at[here.sib], here.sib_dev)
    for k in steps:
        owner = here.behind(k, True)
        links.arrived(("v", "sz", k), v_all.at[owner], here.sib_dev)
    span = vec_ref.shape[1]
    vec_out[...] = jnp.concatenate([v_all[n].astype(F32)[:, 0:span] for n in range(narrow)], axis=1)
    low1 = low_lanes(1)
    for head in range(heads):
        cols = slice((head // 2) * LANES, (head // 2 + 1) * LANES)
        row = [vec_out[r : r + 1, cols] for r in range(4)] + [jnp.zeros((1, LANES), F32), vec_out[4:5, cols]]
        for b in range(3):
            left, right = row[2 * b], row[2 * b + 1]
            left, right = (swap_halves(left), right) if head % 2 else (left, swap_halves(right))
            at = head * GROUP + b * LANES
            bias[0:1, at : at + LANES] = jnp.where(low1, left, right)

    links.arrived(("a", "o"), whole("a", here.sib), here.sib_dev)
    outs = []

    def project(index, part):
        size = 256
        cols = spot(part * quarter, quarter, LANES)
        add = bias[0:1, cols]

        def tile(i, carry):
            at = spot(i * size, size, size)
            prod = mm(x_ref[at, :], a_full[:, cols])
            word = word_ref[at, :] > 0
            for head in range(quarter // GROUP):
                group = slice(head * GROUP, (head + 1) * GROUP)
                out = slice(head * LANES, (head + 1) * LANES)
                query, keyval = qkv_tile(prod[:, group], add[:, group], word)
                q_s[index, at, out] = query
                kv_s[index, at, out] = keyval
            return carry

        lax.fori_loop(0, rows // size, tile, 0)
        wide = q_s.shape[2]
        for number, (source, target) in enumerate(((q_s, q_out), (kv_s, kv_out))):
            copy = pltpu.make_async_copy(
                source.at[index], target.at[:, spot(part * wide, wide, LANES)], local.at[2 + 2 * index + number]
            )
            copy.start()
            outs.append(copy)

    from_sib("a", "sz", here.wide)
    project(0, here.wide)
    for k in steps:
        pass_z("e", k)
        send_z("w", k)
    for k in steps:
        pass_d("a", k)
    from_sib("a", "sx", here.x_quarter)
    project(1, here.x_quarter)
    for k in steps:
        pass_xy("e", k)
    from_sib("a", "sy", here.y_quarter)
    project(2, here.y_quarter)
    from_sib("a", "sd", here.d_quarter)
    project(3, here.d_quarter)
    copy_a = pltpu.make_async_copy(a_full, a_out, local.at[10])
    copy_a.start()
    for k in steps:
        pass_z("w", k)
    for k in steps:
        pass_d("e", k)
    for k in steps:
        pass_xy("w", k)
    for k in steps:
        pass_d("w", k)
    for kind in ("e", "w"):
        links.arrived((kind, "o"), whole(kind, here.sib), here.sib_dev)
        for way, part in (("sz", here.wide), ("sx", here.x_quarter), ("sy", here.y_quarter), ("sd", here.d_quarter)):
            from_sib(kind, way, part)
    links.finish()
    for copy in (copy_e, copy_w, copy_a, *outs):
        copy.wait()


def gather_call(narrow, x, proj, wo, w1, w2, vec, word):
    rows, width = x.shape
    share, deep, inner = proj.shape[0], w2.shape[0], w1.shape[1]
    ecols = inner + width + 2 * LANES
    heads = width // HEAD
    depth = narrow // 2
    count = 3 * (1 + 9 * (depth - 1)) + 1 + 2 * (depth - 1)
    vmem = pl.BlockSpec(memory_space=pltpu.VMEM)
    hbm = pl.BlockSpec(memory_space=pl.ANY)
    shape = jax.ShapeDtypeStruct
    part = heads // 4 * LANES
    return pl.pallas_call(
        functools.partial(gather_kernel, narrow),
        in_specs=[vmem] * 7,
        out_specs=[hbm] * 5 + [vmem],
        out_shape=[
            shape((rows, heads * LANES), BF16),
            shape((rows, heads * LANES), BF16),
            shape((width, proj.shape[1]), BF16),
            shape((width, ecols), BF16),
            shape((deep * narrow, width), BF16),
            shape((16, width), F32),
        ],
        scratch_shapes=[
            pltpu.VMEM((width, proj.shape[1]), BF16),
            pltpu.VMEM((share, ecols), BF16),
            pltpu.VMEM((deep, width), BF16),
            pltpu.VMEM((narrow, 16, LANES), BF16),
            pltpu.VMEM((8, proj.shape[1]), F32),
            pltpu.VMEM((4, rows, part), BF16),
            pltpu.VMEM((4, rows, part), BF16),
            pltpu.SemaphoreType.DMA((count,)),
            pltpu.SemaphoreType.DMA((count,)),
            pltpu.SemaphoreType.DMA((11,)),
        ],
        compiler_params=pltpu.CompilerParams(
            vmem_limit_bytes=VMEM_LIMIT, collective_id=0, has_side_effects=True
        ),
        name="gather",
    )(x, proj, wo, w1, w2, vec, word)


def key_pair(keyval, kmask, low):
    wide = keyval.astype(F32)
    return (jnp.where(low, wide, swap_halves(wide)) * kmask.astype(F32)).astype(BF16)


def attend_kernel(q_ref, kv_ref, qa_ref, ka_ref, km_ref, ctx_ref, aug_ref):
    rows = q_ref.shape[0]
    low = low_lanes(rows)
    lane = lax.broadcasted_iota(jnp.int32, (rows, LANES), 1)
    outs = []
    for part in range(2):
        cols = slice(part * LANES, (part + 1) * LANES)
        keyval = kv_ref[:, cols]
        keys = jnp.concatenate([key_pair(keyval, km_ref[...], low), ka_ref[...]], axis=1)
        query = jnp.concatenate([q_ref[:, cols], qa_ref[...]], axis=1)
        scores = mm_nt(query, keys)
        top = jnp.max(scores, axis=1, keepdims=True)
        weight = jnp.exp2((scores - top) * LOG2E).astype(BF16)
        ones_val = jnp.where(low, 1.0, keyval.astype(F32)).astype(BF16)
        both = mm(weight, ones_val)
        total = swap_halves(both)
        outs.append(both / total)
        log_total = top + jnp.log(jnp.where(low, both, total))
        high, mid, rest = split_three(log_total)
        extra = jnp.where(lane == 8, -high, jnp.where(lane == 9, -mid, jnp.where(lane == 10, -rest, 0.0)))
        aug_ref[:, cols] = jnp.where(lane < 8, qa_ref[...].astype(F32), extra).astype(BF16)
    ctx_ref[...] = jnp.where(low, swap_halves(outs[0]), outs[1]).astype(BF16)


def attend_call(q, kv, qa, ka, km, length):
    rows, cols = q.shape
    seqs, steps = rows // length, cols // (2 * LANES)
    pair = pl.BlockSpec((length, 2 * LANES), lambda s, i: (s, i))
    one = pl.BlockSpec((length, LANES), lambda s, i: (s, 0))
    return pl.pallas_call(
        attend_kernel,
        grid=(seqs, steps),
        in_specs=[pair, pair, one, one, one],
        out_specs=[pl.BlockSpec((length, LANES), lambda s, i: (s, i)), pair],
        out_shape=[
            jax.ShapeDtypeStruct((rows, cols // 2), BF16),
            jax.ShapeDtypeStruct((rows, cols), BF16),
        ],
        compiler_params=pltpu.CompilerParams(vmem_limit_bytes=VMEM_LIMIT),
        name="attend",
    )(q, kv, qa, ka, km)


def attend_back_head(query, keyval, aug, gcon, con, kaug, kmask, word, odd, low, lane):
    keys = key_pair(keyval, kmask, low)
    scores_t = mm_nt(jnp.concatenate([keys, kaug], axis=1), jnp.concatenate([query, aug], axis=1))
    probs_t = jnp.exp2(scores_t * LOG2E)
    gwide = gcon.astype(F32)
    prod = gwide * con.astype(F32)
    mine = low != odd
    delta = jnp.sum(jnp.where(mine, prod, 0.0), axis=1, keepdims=True)
    high, mid, rest = split_three(delta)
    extra = jnp.where(lane == 0, -high, jnp.where(lane == 1, -mid, jnp.where(lane == 2, -rest, 0.0)))
    ghead = jnp.where(low, extra, jnp.where(odd, gwide, swap_halves(gwide))).astype(BF16)
    ones_val = jnp.where(low, jnp.where(lane < 3, 1.0, 0.0), keyval.astype(F32)).astype(BF16)
    gscores_t = (probs_t * mm_nt(ones_val, ghead)).astype(BF16)
    gval = mm(probs_t.astype(BF16), ghead)
    gkey = mm(gscores_t, query)
    gquery = (jnp.transpose(mm_tn(keys, gscores_t)) * (HEAD**-0.5)).astype(BF16)
    zero = jnp.zeros_like(gquery)
    gkey = jnp.where(kmask.astype(F32) > 0, gkey, 0.0)
    gkey = gkey + swap_halves(gkey)
    return (
        jnp.where(word, gquery, zero),
        jnp.where(word, zero, gquery),
        jnp.where(low, gkey, gval).astype(BF16),
    )


def attend_back_kernel(
    length, x_ref, q_ref, kv_ref, aug_ref, gc_ref, ctx_ref, ka_ref, km_ref, word_ref, gp_ref, gw_ref, sum_ref, xt
):
    step = pl.program_id(0)
    rows = x_ref.shape[0]

    @pl.when(step == 0)
    def _():
        xt[...] = jnp.transpose(x_ref[...])

    low = low_lanes(length)
    lane = lax.broadcasted_iota(jnp.int32, (length, LANES), 1)
    odd = lax.rem(step, 2) == 1
    for seq in range(rows // length):
        here = slice(seq * length, (seq + 1) * length)
        tiles = attend_back_head(
            q_ref[here], kv_ref[here], aug_ref[here], gc_ref[here], ctx_ref[here],
            ka_ref[here], km_ref[here], word_ref[here] > 0, odd, low, lane,
        )
        for index, tile in enumerate(tiles):
            gp_ref[here, index * LANES : (index + 1) * LANES] = tile
    grads = gp_ref[...]
    gw_ref[...] = mm(xt[...], grads).astype(BF16)
    sums = jnp.sum(grads.astype(F32).reshape(rows // 8, 8, GROUP), axis=0)
    sum_ref[...] = jnp.sum(sums, axis=0, keepdims=True)


def attend_back_call(x, q, kv, aug, gc, ctx, ka, km, word, length):
    rows, width = x.shape
    heads = q.shape[1] // LANES
    head = pl.BlockSpec((rows, LANES), lambda h: (0, h))
    pair = pl.BlockSpec((rows, LANES), lambda h: (0, h // 2))
    one = pl.BlockSpec((rows, LANES), lambda h: (0, 0))
    return pl.pallas_call(
        functools.partial(attend_back_kernel, length),
        grid=(heads,),
        in_specs=[pl.BlockSpec((rows, width), lambda h: (0, 0)), head, head, head, pair, pair, one, one, one],
        out_specs=[
            pl.BlockSpec((rows, GROUP), lambda h: (0, h)),
            pl.BlockSpec((width, GROUP), lambda h: (0, h)),
            pl.BlockSpec((1, GROUP), lambda h: (0, h)),
        ],
        out_shape=[
            jax.ShapeDtypeStruct((rows, heads * GROUP), BF16),
            jax.ShapeDtypeStruct((width, heads * GROUP), BF16),
            jax.ShapeDtypeStruct((1, heads * GROUP), F32),
        ],
        scratch_shapes=[pltpu.VMEM((width, rows), BF16)],
        compiler_params=pltpu.CompilerParams(vmem_limit_bytes=VMEM_LIMIT),
        name="attend_back",
    )(x, q, kv, aug, gc, ctx, ka, km, word)


class Chunk:
    def __init__(self, name, refs, by_rows):
        self.name = name
        self.total, self.r1a, self.r1b, self.r2a, self.r2b, self.rz, self.final = refs
        self.by_rows = by_rows
        _, self.rows, self.cols = self.total.shape

    def cut(self, part, side=None):
        if self.by_rows:
            size = self.rows // 4
            if side is None:
                return spot(part * size, size, 16), slice(None)
            return spot(part * size + side * (size // 2), size // 2, 16), slice(None)
        size, half = self.cols // 4, self.rows // 2
        rows = slice(0, self.rows) if side is None else slice(side * half, (side + 1) * half)
        return rows, spot(part * size, size, LANES)


def chunk_scratch(depth, rows, cols, by_rows):
    if by_rows:
        piece, half = (rows // 4, cols), (rows // 8, cols)
    else:
        piece, half = (rows, cols // 4), (rows // 2, cols // 4)
    return [
        pltpu.VMEM((depth, rows, cols), BF16),
        pltpu.VMEM((2, depth, *half), BF16),
        pltpu.VMEM((2, depth, *half), BF16),
        pltpu.VMEM((depth, *half), BF16),
        pltpu.VMEM((depth, *half), BF16),
        pltpu.VMEM((depth - 1, *piece), BF16),
        pltpu.VMEM((rows, cols), BF16),
    ]


class Reducer:
    def __init__(self, here, send, recv):
        self.here = here
        self.links = Links(send, recv)
        self.sent = []

    def send(self, key, build):
        copy = self.links.copy(key, *build())
        copy.start()
        self.sent.append((key, build))

    def arrived(self, key, dst, device):
        self.links.arrived(key, dst, device)

    def finish(self):
        for key, build in self.sent:
            self.links.copy(key, *build()).wait_send()

    def pair_send(self, chunk, sources):
        here = self.here
        for z in range(here.depth):
            for part, (_, cols) in enumerate(sources(0)):

                def build(z=z, part=part, cols=cols):
                    owner = 2 * z + 1 - here.core
                    return sources(owner)[part][0], chunk.total.at[z, :, cols], here.sib_dev

                self.send((chunk.name, "s", z, part), build)

    def pair_wait(self, chunk, sources):
        for z in range(self.here.depth):
            for part, (_, cols) in enumerate(sources(0)):
                self.arrived((chunk.name, "s", z, part), chunk.total.at[z, :, cols], self.here.sib_dev)

    def plane_send(self, chunk):
        here = self.here
        for index, (a, b) in enumerate(((here.x_quarter, here.y_quarter), (here.d_quarter, here.d_quarter))):

            def first(index=index, part=a):
                rows, cols = chunk.cut(part, 0)
                return chunk.total.at[:, rows, cols], chunk.r1a.at[index], here.x_dev

            def second(index=index, part=b):
                rows, cols = chunk.cut(part, 1)
                return chunk.total.at[:, rows, cols], chunk.r1b.at[index], here.y_dev

            self.send((chunk.name, "1a", index), first)
            self.send((chunk.name, "1b", index), second)

    def add(self, chunk, part, side, value):
        rows, cols = chunk.cut(part, side)
        chunk.total[:, rows, cols] = chunk.total[:, rows, cols] + value

    def plane_turn(self, chunk):
        here = self.here
        for index in range(2):
            self.arrived((chunk.name, "1a", index), chunk.r1a.at[index], here.x_dev)
            self.arrived((chunk.name, "1b", index), chunk.r1b.at[index], here.y_dev)
        self.add(chunk, here.y_quarter, 0, chunk.r1a[1])
        self.add(chunk, here.x_quarter, 1, chunk.r1b[1])

        def first():
            rows, cols = chunk.cut(here.y_quarter, 0)
            return chunk.total.at[:, rows, cols], chunk.r2a, here.y_dev

        def second():
            rows, cols = chunk.cut(here.x_quarter, 1)
            return chunk.total.at[:, rows, cols], chunk.r2b, here.x_dev

        self.send((chunk.name, "2a"), first)
        self.send((chunk.name, "2b"), second)
        self.add(chunk, here.wide, 0, chunk.r1a[0])
        self.add(chunk, here.wide, 1, chunk.r1b[0])

    def depth_send(self, chunk):
        here = self.here
        self.arrived((chunk.name, "2a"), chunk.r2a, here.y_dev)
        self.arrived((chunk.name, "2b"), chunk.r2b, here.x_dev)
        self.add(chunk, here.wide, 0, chunk.r2a[...])
        self.add(chunk, here.wide, 1, chunk.r2b[...])
        for k in range(1, here.depth):

            def build(k=k):
                rows, cols = chunk.cut(here.wide)
                return chunk.total.at[lax.rem(here.z + k, here.depth), rows, cols], chunk.rz.at[k - 1], here.z_dev(k)

            self.send((chunk.name, "z", k), build)

    def share_send(self, chunk):
        here = self.here
        for k in range(1, here.depth):
            self.arrived((chunk.name, "z", k), chunk.rz.at[k - 1], here.z_dev(k))
        rows, cols = chunk.cut(here.wide)
        done = chunk.total[here.z, rows, cols].astype(F32)
        for k in range(1, here.depth):
            done = done + chunk.rz[k - 1].astype(F32)
        chunk.final[rows, cols] = done.astype(BF16)

        def build(device):
            rows, cols = chunk.cut(here.wide)
            return chunk.final.at[rows, cols], chunk.final.at[rows, cols], device

        self.send((chunk.name, "fx"), lambda: build(here.x_dev))
        self.send((chunk.name, "fy"), lambda: build(here.y_dev))

    def share_pass(self, chunk):
        here = self.here

        def part(quarter, side, device):
            rows, cols = chunk.cut(quarter, side)
            return chunk.final.at[rows, cols], chunk.final.at[rows, cols], device

        self.arrived((chunk.name, "fx"), *part(here.x_quarter, None, here.x_dev)[1:])
        self.send((chunk.name, "fdy"), lambda: part(here.x_quarter, 0, here.y_dev))
        self.arrived((chunk.name, "fy"), *part(here.y_quarter, None, here.y_dev)[1:])
        self.send((chunk.name, "fdx"), lambda: part(here.y_quarter, 1, here.x_dev))

    def share_wait(self, chunk):
        here = self.here
        for key, side, device in (("fdy", 0, here.y_dev), ("fdx", 1, here.x_dev)):
            rows, cols = chunk.cut(here.d_quarter, side)
            self.arrived((chunk.name, key), chunk.final.at[rows, cols], device)


CHUNK_HEADS = 4


def squares(ref, cols):
    total = jnp.zeros((8, LANES), F32)
    rows = ref.shape[0]
    for start in range(0, cols, LANES):
        tile = ref[:, start : start + LANES].astype(F32)
        total = total + jnp.sum((tile * tile).reshape(rows // 8, 8, LANES), axis=0)
    return total


def reduce_kernel(
    narrow, length, groups,
    x_ref, q_ref, kv_ref, aug_ref, gc_ref, ctx_ref, ka_ref, km_ref, word_ref, gvec_ref, gw1_ref, gwo_ref, gw2_ref,
    gp_ref, fw_ref, fe_ref, fa_ref, v_ref, n_ref,
    xt, gw, *scratch,
):
    step = pl.program_id(0)
    rows, width = x_ref.shape
    heads = groups * CHUNK_HEADS
    inner = gw1_ref.shape[1]
    here = Place(narrow)
    scratch = list(scratch)
    chunk_w = Chunk("w", scratch[0:7], True)
    chunk_e = Chunk("e", scratch[7:14], False)
    chunk_a = [Chunk(("a", j), scratch[14 + 7 * j : 21 + 7 * j], False) for j in range(groups)]
    own_w, own_e, v0, v1, v2, vs, vx, vy, vz, n0, ns, nz, send, recv, local = scratch[14 + 7 * groups :]
    red = Reducer(here, send, recv)
    share, deep = chunk_e.rows, chunk_w.rows

    def sources_w(owner):
        return [(gw2_ref.at[spot(owner * deep, deep, 16), :], slice(0, width))]

    def sources_e(owner):
        at = spot(owner * share, share, 16)
        return [(gw1_ref.at[at, :], slice(0, inner)), (gwo_ref.at[at, :], slice(inner, inner + width))]

    def sources_a(j):
        return lambda owner: [(gw.at[j, spot(owner * share, share, 16), :], slice(0, CHUNK_HEADS * GROUP))]

    def own_copies():
        copies = []
        for own, sources in ((own_w, sources_w), (own_e, sources_e)):
            for z in range(here.depth):
                for source, cols in sources(2 * z + here.core):
                    copies.append(pltpu.make_async_copy(source, own.at[z, :, cols], local.at[len(copies)]))
        return copies

    def out_copies():
        copies = [(chunk_w.final, fw_ref), (chunk_e.final, fe_ref)]
        wide = CHUNK_HEADS * GROUP
        copies += [(chunk.final, fa_ref.at[:, j * wide : (j + 1) * wide]) for j, chunk in enumerate(chunk_a)]
        base = 3 * here.depth
        return [pltpu.make_async_copy(a, b, local.at[base + i]) for i, (a, b) in enumerate(copies)]

    def merge(chunk, own):
        def one(z, carry):
            chunk.total[z] = chunk.total[z] + own(z)
            return carry

        lax.fori_loop(0, here.depth, one, 0)

    def own_a(j):
        return lambda z: gw[j, spot((2 * z + here.core) * share, share, 16), :]

    @pl.when(step == 0)
    def _():
        for copy in own_copies():
            copy.start()
        here.greet()
        red.pair_send(chunk_w, sources_w)
        red.pair_send(chunk_e, sources_e)
        pad = chunk_e.cols - inner - width
        chunk_e.total[:, :, inner + width :] = jnp.zeros((here.depth, share, pad), BF16)
        own_e[:, :, inner + width :] = jnp.zeros((here.depth, share, pad), BF16)
        xt[...] = jnp.transpose(x_ref[...])
        v0[...] = gvec_ref[...]

    def advance(at, action):
        pl.when(step == at)(action)

    def act_w1():
        for copy in own_copies():
            copy.wait()
        red.pair_wait(chunk_w, sources_w)
        merge(chunk_w, lambda z: own_w[z])
        red.plane_send(chunk_w)

    def act_e1():
        red.pair_wait(chunk_e, sources_e)
        merge(chunk_e, lambda z: own_e[z])
        red.plane_send(chunk_e)

    def act_a1(j):
        red.pair_wait(chunk_a[j], sources_a(j))
        merge(chunk_a[j], own_a(j))
        red.plane_send(chunk_a[j])

    advance(1, act_w1)
    advance(2, act_e1)
    advance(4, lambda: red.plane_turn(chunk_w))
    advance(5, lambda: act_a1(0))
    advance(6, lambda: red.depth_send(chunk_w))
    advance(8, lambda: red.plane_turn(chunk_e))
    advance(9, lambda: act_a1(1))
    advance(10, lambda: red.depth_send(chunk_e))
    advance(11, lambda: red.share_send(chunk_w))

    low = low_lanes(length)
    lane = lax.broadcasted_iota(jnp.int32, (length, LANES), 1)
    odd = lax.rem(step, 2) == 1
    for seq in range(rows // length):
        at = slice(seq * length, (seq + 1) * length)
        tiles = attend_back_head(
            q_ref[at], kv_ref[at], aug_ref[at], gc_ref[at], ctx_ref[at],
            ka_ref[at], km_ref[at], word_ref[at] > 0, odd, low, lane,
        )
        for index, tile in enumerate(tiles):
            gp_ref[at, index * LANES : (index + 1) * LANES] = tile
    grads = gp_ref[...]
    group, inside = step // CHUNK_HEADS, lax.rem(step, CHUNK_HEADS)
    gw[group, :, spot(inside * GROUP, GROUP, LANES)] = mm(xt[...], grads).astype(BF16)
    sums = jnp.sum(jnp.sum(grads.astype(F32).reshape(rows // 8, 8, GROUP), axis=0), axis=0, keepdims=True)

    low1 = low_lanes(1)
    pair = spot(step // 2 * LANES, LANES, LANES)
    mine = low1 != odd
    for b in range(3):
        tile = sums[:, b * LANES : (b + 1) * LANES]
        turned = swap_halves(tile)
        first = jnp.where(odd, turned, tile)
        second = jnp.where(odd, tile, turned)
        if b < 2:
            v0[2 * b : 2 * b + 1, pair] = jnp.where(mine, first, v0[2 * b : 2 * b + 1, pair])
            v0[2 * b + 1 : 2 * b + 2, pair] = jnp.where(mine, second, v0[2 * b + 1 : 2 * b + 2, pair])
        else:
            v0[4:5, pair] = jnp.where(mine, second, v0[4:5, pair])

    for j in range(groups):
        advance((j + 1) * CHUNK_HEADS - 1, lambda j=j: red.pair_send(chunk_a[j], sources_a(j)))

    @pl.when(step == heads - 1)
    def _():
        last = chunk_a[-1]
        red.send(("v", "s"), lambda: (v0, vs, here.sib_dev))
        red.plane_turn(chunk_a[0])
        red.share_send(chunk_e)
        red.share_pass(chunk_w)
        act_a1(groups - 1)
        red.arrived(("v", "s"), vs, here.sib_dev)
        v1[...] = v0[...] + vs[...]
        red.send(("v", "x"), lambda: (v1, vx, here.x_dev))
        red.depth_send(chunk_a[0])
        for chunk in chunk_a[1:-1]:
            red.plane_turn(chunk)
        red.share_pass(chunk_e)
        for chunk in chunk_a[1:-1]:
            red.depth_send(chunk)
        red.plane_turn(last)
        red.arrived(("v", "x"), vx, here.x_dev)
        v2[...] = v1[...] + vx[...]
        red.send(("v", "y"), lambda: (v2, vy, here.y_dev))
        for chunk in chunk_a[:-1]:
            red.share_send(chunk)
        red.depth_send(last)
        red.arrived(("v", "y"), vy, here.y_dev)
        vz[here.z] = v2[...] + vy[...]
        for k in range(1, here.depth):
            red.send(("v", "z", k), lambda k=k: (vz.at[here.z], vz.at[here.z], here.z_dev(k)))
        red.share_wait(chunk_w)
        red.share_wait(chunk_e)
        for chunk in chunk_a[:-1]:
            red.share_pass(chunk)
        norm = squares(chunk_w.final, width) + squares(chunk_e.final, inner + width)
        for chunk in chunk_a[:-1]:
            red.share_wait(chunk)
            norm = norm + squares(chunk.final, chunk.cols)
        red.share_send(last)
        for k in range(1, here.depth):
            source = here.behind(k) // 2
            red.arrived(("v", "z", k), vz.at[source], here.z_dev(k))
        vec = vz[0]
        for z in range(1, here.depth):
            vec = vec + vz[z]
        v_ref[...] = vec
        red.share_pass(last)
        red.share_wait(last)
        for copy in out_copies():
            copy.start()
        n0[...] = norm + squares(last.final, last.cols)
        red.send(("n", "s"), lambda: (n0, ns, here.sib_dev))
        red.arrived(("n", "s"), ns, here.sib_dev)
        nz[here.z] = n0[...] + ns[...]
        for k in range(1, here.depth):
            red.send(("n", "z", k), lambda k=k: (nz.at[here.z], nz.at[here.z], here.z_dev(k)))
        for k in range(1, here.depth):
            source = here.behind(k) // 2
            red.arrived(("n", "z", k), nz.at[source], here.z_dev(k))
        total = nz[0]
        for z in range(1, here.depth):
            total = total + nz[z]
        every = jnp.sum(jnp.sum(total, axis=0, keepdims=True), axis=1, keepdims=True)
        square = jnp.sum(jnp.sum(vec * vec, axis=0, keepdims=True), axis=1, keepdims=True)
        n_ref[...] = jnp.broadcast_to(every + square, n_ref.shape)
        red.finish()
        for copy in out_copies():
            copy.wait()


def reduce_call(narrow, x, q, kv, aug, gc, ctx, ka, km, word, gvec, gw1, gwo, gw2, length):
    rows, width = x.shape
    inner = gw2.shape[0]
    heads = q.shape[1] // LANES
    groups = heads // CHUNK_HEADS
    depth = narrow // 2
    share, deep, ecols, acols = width // narrow, inner // narrow, inner + width + 2 * LANES, CHUNK_HEADS * GROUP
    head = pl.BlockSpec((rows, LANES), lambda h: (0, h))
    pair = pl.BlockSpec((rows, LANES), lambda h: (0, h // 2))
    one = pl.BlockSpec((rows, LANES), lambda h: (0, 0), pipeline_mode=pl.Buffered(1))
    hbm = pl.BlockSpec(memory_space=pl.ANY)
    shape = jax.ShapeDtypeStruct
    vec = pltpu.VMEM((16, width), F32)
    tile = pltpu.VMEM((8, LANES), F32)
    scratch = [pltpu.VMEM((width, rows), BF16), pltpu.VMEM((groups, width, acols), BF16)]
    scratch += chunk_scratch(depth, deep, width, True)
    scratch += chunk_scratch(depth, share, ecols, False)
    for _ in range(groups):
        scratch += chunk_scratch(depth, share, acols, False)
    scratch += [pltpu.VMEM((depth, deep, width), BF16), pltpu.VMEM((depth, share, ecols), BF16)]
    scratch += [vec] * 6 + [pltpu.VMEM((depth, 16, width), F32), tile, tile, pltpu.VMEM((depth, 8, LANES), F32)]
    count = (2 + groups) * (depth + 10 + depth - 1) + depth + 2 * (3 + depth)
    scratch += [pltpu.SemaphoreType.DMA((count,))] * 2 + [pltpu.SemaphoreType.DMA((3 * depth + 2 + groups,))]
    return pl.pallas_call(
        functools.partial(reduce_kernel, narrow, length, groups),
        grid=(heads,),
        in_specs=[
            pl.BlockSpec((rows, width), lambda h: (0, 0), pipeline_mode=pl.Buffered(1)),
            head, head, head, pair, pair, one, one, one,
            pl.BlockSpec((16, width), lambda h: (0, 0), pipeline_mode=pl.Buffered(1)),
            hbm, hbm, hbm,
        ],
        out_specs=[
            pl.BlockSpec((rows, GROUP), lambda h: (0, h)),
            hbm, hbm, hbm,
            pl.BlockSpec((16, width), lambda h: (0, 0)),
            pl.BlockSpec((8, LANES), lambda h: (0, 0)),
        ],
        out_shape=[
            shape((rows, heads * GROUP), BF16),
            shape((deep, width), BF16),
            shape((share, ecols), BF16),
            shape((share, heads * GROUP), BF16),
            shape((16, width), F32),
            shape((8, LANES), F32),
        ],
        scratch_shapes=scratch,
        compiler_params=pltpu.CompilerParams(
            vmem_limit_bytes=VMEM_LIMIT, collective_id=1, has_side_effects=True
        ),
        name="reduce",
    )(x, q, kv, aug, gc, ctx, ka, km, word, gvec, gw1, gwo, gw2)


def gelu_pair(pre):
    size = jnp.abs(pre) * (0.5**0.5)
    bell = jnp.exp2(pre * pre * (-0.5 * LOG2E))
    t = 1.0 / (1.0 + 0.3275911 * size)
    poly = t * (0.254829592 + t * (-0.284496736 + t * (1.421413741 + t * (-1.453152027 + t * 1.061405429))))
    tail = 0.5 * poly * bell
    share = jnp.where(pre >= 0, 1.0 - tail, tail)
    return pre * share, share + pre * bell * 0.3989422804014327


def fold(array_in):
    rows, cols = array_in.shape
    return jnp.sum(array_in.reshape(rows // 8, 8, cols), axis=0)


def middle_kernel(
    tiles, x_ref, ctx_ref, cot_ref, vec_ref, e_hbm, w2_hbm,
    out_ref, gr1_ref, gctx_ref, gw2_ref, gw1_ref, gwo_ref, gvec_ref,
    wo, w1, w2, h1_s, act_s, gb_s, gp_s, ga_s, ctx_s, dg_s, acc, sems,
):
    step = pl.program_id(0)
    size, width = x_ref.shape
    inner = w1.shape[1]
    chunks = inner // width

    def weight_copies(index):
        source, target = (
            (e_hbm.at[:, inner : inner + width], wo),
            (e_hbm.at[:, 0:inner], w1),
            (w2_hbm, w2),
        )[index]
        return pltpu.make_async_copy(source, target, sems.at[index])

    @pl.when(step == 0)
    def _():
        for index in range(3):
            weight_copies(index).start()
        acc[...] = jnp.zeros_like(acc)

    def vec(row):
        return vec_ref[row : row + 1, :].astype(F32)

    @pl.when(step < tiles)
    def _():
        here = pl.ds(pl.multiple_of(step * size, size), size)

        @pl.when(step == 0)
        def _():
            weight_copies(0).wait()

        ctx_s[here, :] = ctx_ref[...]
        resid = x_ref[...].astype(F32) + mm(ctx_ref[...], wo[...]) + vec(5)
        center = resid - jnp.mean(resid, axis=1, keepdims=True)
        inv1 = lax.rsqrt(jnp.mean(center * center, axis=1, keepdims=True) + norm_eps)
        n1 = center * inv1
        h1 = n1 * vec(6) + vec(7)
        h1b = h1.astype(BF16)
        h1_s[here, :] = h1b

        @pl.when(step == 0)
        def _():
            weight_copies(1).wait()
            weight_copies(2).wait()

        branch = h1 + vec(8)
        for c in range(chunks):
            cols = slice(c * width, (c + 1) * width)
            act, slope = gelu_pair(mm(h1b, w1[:, cols]) + vec(11 + c))
            act = act.astype(BF16)
            act_s[here, cols] = act
            dg_s[:, cols] = slope
            branch = branch + mm(act, w2[cols, :])
        center = branch - jnp.mean(branch, axis=1, keepdims=True)
        inv2 = lax.rsqrt(jnp.mean(center * center, axis=1, keepdims=True) + norm_eps)
        n2 = center * inv2
        out_ref[...] = (n2 * vec(9) + vec(10)).astype(BF16)
        grad = cot_ref[...].astype(F32)
        gn = grad * n2
        acc[9] += fold(gn)
        acc[10] += fold(grad)
        scaled = grad * vec(9)
        gr2 = inv2 * (
            scaled
            - jnp.mean(scaled, axis=1, keepdims=True)
            - n2 * jnp.mean(scaled * n2, axis=1, keepdims=True)
        )
        gb = gr2.astype(BF16)
        gb_s[here, :] = gb
        acc[8] += fold(gb.astype(F32))
        gh1 = gr2
        for c in range(chunks):
            cols = slice(c * width, (c + 1) * width)
            gpre = (mm_nt(gb, w2[cols, :]) * dg_s[:, cols]).astype(BF16)
            gp_s[here, cols] = gpre
            acc[11 + c] += fold(gpre.astype(F32))
            gh1 = gh1 + mm_nt(gpre, w1[:, cols])
        acc[6] += fold(gh1 * n1)
        acc[7] += fold(gh1)
        scaled = gh1 * vec(6)
        gr1 = inv1 * (
            scaled
            - jnp.mean(scaled, axis=1, keepdims=True)
            - n1 * jnp.mean(scaled * n1, axis=1, keepdims=True)
        )
        gr1_ref[...] = gr1
        ga = gr1.astype(BF16)
        ga_s[here, :] = ga
        acc[5] += fold(ga.astype(F32))
        gctx_ref[...] = mm_nt(ga, wo[...]).astype(BF16)

    for c in range(chunks):
        cols = slice(c * width, (c + 1) * width)

        @pl.when(step == tiles + c)
        def _():
            gw2_ref[...] = mm_tn(act_s[:, cols], gb_s[...]).astype(BF16)

        @pl.when(step == tiles + chunks + c)
        def _():
            gw1_ref[...] = mm_tn(h1_s[...], gp_s[:, cols]).astype(BF16)

    @pl.when(step == tiles + 2 * chunks)
    def _():
        gwo_ref[...] = mm_tn(ctx_s[...], ga_s[...]).astype(BF16)
        for row in range(acc.shape[0]):
            gvec_ref[row : row + 1, :] = jnp.sum(acc[row], axis=0, keepdims=True)


def middle_call(x, ctx, cot, vec, e, w2, size):
    rows, width = x.shape
    inner = w2.shape[0]
    tiles, chunks = rows // size, inner // width
    tile = pl.BlockSpec((size, width), lambda i: (jnp.minimum(i, tiles - 1), 0))
    hbm = pl.BlockSpec(memory_space=pl.ANY)

    def after(start):
        return lambda i: jnp.clip(i - start, 0, chunks - 1)

    shape = jax.ShapeDtypeStruct
    return pl.pallas_call(
        functools.partial(middle_kernel, tiles),
        grid=(tiles + 2 * chunks + 1,),
        in_specs=[tile, tile, tile, pl.BlockSpec(vec.shape, lambda i: (0, 0)), hbm, hbm],
        out_specs=[
            tile,
            tile,
            tile,
            pl.BlockSpec((width, width), lambda i: (after(tiles)(i), 0)),
            pl.BlockSpec((width, width), lambda i: (0, after(tiles + chunks)(i))),
            pl.BlockSpec((width, width), lambda i: (0, 0)),
            pl.BlockSpec(vec.shape, lambda i: (0, 0)),
        ],
        out_shape=[
            shape((rows, width), BF16),
            shape((rows, width), F32),
            shape((rows, width), BF16),
            shape((inner, width), BF16),
            shape((width, inner), BF16),
            shape((width, width), BF16),
            shape(vec.shape, F32),
        ],
        scratch_shapes=[
            pltpu.VMEM((width, width), BF16),
            pltpu.VMEM((width, inner), BF16),
            pltpu.VMEM((inner, width), BF16),
            pltpu.VMEM((rows, width), BF16),
            pltpu.VMEM((rows, inner), BF16),
            pltpu.VMEM((rows, width), BF16),
            pltpu.VMEM((rows, inner), BF16),
            pltpu.VMEM((rows, width), BF16),
            pltpu.VMEM((rows, width), BF16),
            pltpu.VMEM((size, inner), F32),
            pltpu.VMEM((vec.shape[0], 8, width), F32),
            pltpu.SemaphoreType.DMA((3,)),
        ],
        compiler_params=pltpu.CompilerParams(vmem_limit_bytes=VMEM_LIMIT),
        name="middle",
    )(x, ctx, cot, vec, e, w2)


def input_grad_kernel(gp_ref, w_ref, gr1_ref, out_ref):
    out_ref[...] = (gr1_ref[...] + mm_nt(gp_ref[...], w_ref[...])).astype(BF16)


def input_grad_call(gp, w, gr1, size):
    rows, cols = gp.shape
    width = w.shape[0]
    return pl.pallas_call(
        input_grad_kernel,
        grid=(rows // size,),
        in_specs=[
            pl.BlockSpec((size, cols), lambda i: (i, 0)),
            pl.BlockSpec((width, cols), lambda i: (0, 0)),
            pl.BlockSpec((size, width), lambda i: (i, 0)),
        ],
        out_specs=pl.BlockSpec((size, width), lambda i: (i, 0)),
        out_shape=jax.ShapeDtypeStruct((rows, width), BF16),
        compiler_params=pltpu.CompilerParams(vmem_limit_bytes=VMEM_LIMIT),
        name="input_grad",
    )(gp, w, gr1)


def adam_update(master, first_old, second_old, grad_shard, factor, index):
    clipped = grad_shard * factor
    new_first = beta_one * first_old + (1.0 - beta_one) * clipped
    new_second = beta_two * second_old + (1.0 - beta_two) * clipped * clipped
    direction = (
        new_first
        / (1.0 - beta_one**STEP)
        / (jnp.sqrt(new_second / (1.0 - beta_two**STEP)) + adam_eps)
    )
    new_weight = master - rate_table[index] * (direction + decay_table[index] * master)
    return (new_weight, new_first, new_second)


def update_tile(master, first, second, grad, factor, index):
    weight, first, second = adam_update(master, first, second, grad.astype(F32), factor, index)
    return weight, first, second, weight.astype(BF16)


def update_kernel(narrow, n_ref, fa_ref, fe_ref, fw_ref, v_ref, *refs):
    ins, outs = refs[0:15], refs[15:35]
    heads = fa_ref.shape[1] // GROUP
    width = heads * HEAD
    norm = jnp.sqrt(n_ref[0:1, 0:1])
    factor = jnp.minimum(1.0, clip_limit / (norm + 1e-06))

    def store(index, rows, cols, grad):
        news = update_tile(*(ins[5 * t + index][rows, cols] for t in range(3)), grad, factor, index)
        for t, new in enumerate(news):
            outs[5 * t + index][rows, cols] = new

    every = slice(None)
    low = low_lanes(fa_ref.shape[0])
    for pair in range(heads // 2):
        at = 2 * pair * GROUP
        for b in range(3):
            even = fa_ref[:, at + b * LANES : at + (b + 1) * LANES].astype(F32)
            odd = fa_ref[:, at + GROUP + b * LANES : at + GROUP + (b + 1) * LANES].astype(F32)
            for second in range(2):
                if second:
                    grad = jnp.where(low, swap_halves(even), odd)
                else:
                    grad = jnp.where(low, even, swap_halves(odd))
                start = (2 * b + second) * width + pair * LANES
                store(0, every, slice(start, start + LANES), grad)
    inner = ins[2].shape[1]
    store(1, every, every, fe_ref[:, inner : inner + width])
    store(2, every, every, fe_ref[:, 0:inner])
    store(3, every, every, fw_ref[...])

    @pl.when(pl.program_id(0) == 0)
    def _():
        count, span = ins[4].shape
        me = lax.axis_index("narrow")
        turned = pltpu.roll(v_ref[...], lax.rem(width - me * span, width), 1)
        store(4, every, every, turned[0:count, 0:span])


def update_call(narrow, norm, fa, fe, fw, vec, masters, firsts, seconds):
    share = fa.shape[0]
    steps = share // 16

    def rows_of(array_in):
        return pl.BlockSpec((array_in.shape[0] // steps, array_in.shape[1]), lambda i: (i, 0))

    def fixed(array_in):
        return pl.BlockSpec(array_in.shape, lambda i: (0, 0))

    def group(arrays):
        return [rows_of(a) for a in arrays[:4]] + [fixed(arrays[4])]

    def shapes(arrays, dtype):
        return [jax.ShapeDtypeStruct(a.shape, dtype) for a in arrays]

    return pl.pallas_call(
        functools.partial(update_kernel, narrow),
        grid=(steps,),
        in_specs=[fixed(norm), rows_of(fa), rows_of(fe), rows_of(fw), fixed(vec)] + group(masters) * 3,
        out_specs=group(masters) * 4,
        out_shape=shapes(masters, F32) * 3 + shapes(masters, BF16),
        compiler_params=pltpu.CompilerParams(vmem_limit_bytes=VMEM_LIMIT),
        name="update",
    )(norm, fa, fe, fw, vec, *masters, *firsts, *seconds)


def by_head(array_in):
    rows, cols = array_in.shape
    heads = cols // GROUP
    return array_in.reshape(rows, 6, heads, HEAD).transpose(0, 2, 1, 3).reshape(rows, cols)


def by_block(array_in):
    rows, cols = array_in.shape
    heads = cols // GROUP
    return array_in.reshape(rows, heads, 6, HEAD).transpose(0, 2, 1, 3).reshape(rows, cols)


def can_pass_pieces(wide, narrow, width, deep):
    share = width // narrow
    return wide == 4 and narrow % 2 == 0 and narrow > 2 and share % 32 == 0 and deep % 128 == 0


def body(
    x_in, cotangent, segment_ids, type_ids,
    projection, context_out, expand_weight, reduce_weight, vector_params,
    first_projection, first_context, first_expand, first_reduce, first_vectors,
    second_projection, second_context, second_expand, second_reduce, second_vectors,
):
    seq_count, seq_len, width = x_in.shape
    rows = seq_count * seq_len

    def gather(array_in, axis):
        return lax.all_gather(array_in.astype(BF16), "narrow", axis=axis, tiled=True)

    hidden = x_in.reshape(rows, width)
    cot = cotangent.reshape(rows, width)
    word_col = (type_ids == 0).reshape(rows, 1)
    lane = lax.broadcasted_iota(jnp.int32, (rows, LANES), 1)
    word = jnp.broadcast_to(word_col, (rows, LANES)).astype(BF16)
    kmask = ((lane < HEAD) == word_col).astype(BF16)
    same = segment_ids.reshape(rows, 1) == lane
    qaug = jnp.where(same & (lane < 8), 1.0, 0.0).astype(BF16)
    kaug = jnp.where(lane < 8, jnp.where(same, 0.0, FAR), jnp.where(lane < 11, 1.0, 0.0)).astype(BF16)

    narrow = lax.axis_size("narrow")
    pieces = can_pass_pieces(lax.axis_size("wide"), narrow, width, reduce_weight.shape[0])
    if pieces:
        query, keyval, proj_w, mid_w, reduce_w, vec_rows = gather_call(
            narrow, hidden, projection, context_out, expand_weight, reduce_weight, vector_params, word
        )
    else:
        proj_w, vec_half = gather(by_head(projection), 0), gather(vector_params, 1)
        reduce_w = gather(reduce_weight, 0)
        mid_w = jnp.concatenate(
            [gather(expand_weight, 0), gather(context_out, 0), jnp.zeros((width, 2 * LANES), BF16)], axis=1
        )
        zero_row = jnp.zeros((1, width), BF16)
        bias = by_head(jnp.concatenate([vec_half[0:4], zero_row, vec_half[4:5]]).reshape(1, -1)).astype(F32)
        vec_rows = jnp.pad(vec_half.astype(F32), ((0, 1), (0, 0)))
        query, keyval = qkv_call(hidden, proj_w, bias, word)
    context, aug = attend_call(query, keyval, qaug, kaug, kmask, seq_len)
    block_out, grad_r1, grad_context, grad_reduce, grad_expand, grad_ctx_w, grad_mid = middle_call(
        hidden, context, cot, vec_rows, mid_w, reduce_w, 256
    )
    masters = (projection, context_out, expand_weight, reduce_weight, vector_params)
    firsts = (first_projection, first_context, first_expand, first_reduce, first_vectors)
    seconds = (second_projection, second_context, second_expand, second_reduce, second_vectors)
    out_shape = (seq_count, seq_len, width)
    if pieces:
        grad_proj, shard_w, shard_e, shard_a, grad_vectors, norm = reduce_call(
            narrow, hidden, query, keyval, aug, grad_context, context, kaug, kmask, word, grad_mid,
            grad_expand, grad_ctx_w, grad_reduce, seq_len,
        )
        input_grad = input_grad_call(grad_proj, proj_w, grad_r1, 256)
        updated = update_call(narrow, norm, shard_a, shard_e, shard_w, grad_vectors, masters, firsts, seconds)
        return (
            block_out.reshape(out_shape),
            input_grad.reshape(out_shape),
            jnp.sqrt(norm[0, 0]),
            *updated,
        )
    grad_proj, grad_proj_w, grad_sums = attend_back_call(
        hidden, query, keyval, aug, grad_context, context, kaug, kmask, word, seq_len
    )
    input_grad = input_grad_call(grad_proj, proj_w, grad_r1, 256)
    sum_rows = by_block(grad_sums).reshape(6, width)
    grad_vectors = jnp.concatenate([sum_rows[0:4], sum_rows[5:6], grad_mid[5:15]], axis=0)

    def scatter(array_in, axis):
        return lax.psum_scatter(array_in, "narrow", scatter_dimension=axis, tiled=True)

    def over_wide(array_in):
        return lax.psum(array_in.astype(BF16), "wide").astype(F32)

    shards = (
        by_block(over_wide(scatter(grad_proj_w, 0))),
        over_wide(scatter(grad_ctx_w, 0)),
        over_wide(scatter(grad_expand, 0)),
        over_wide(scatter(grad_reduce, 0)),
        over_wide(scatter(grad_vectors, 1)),
    )
    local_squares = sum((jnp.sum(shard_item * shard_item) for shard_item in shards))
    total_squares = lax.psum(local_squares, "narrow")
    grad_norm = jnp.sqrt(total_squares)
    factor = jnp.minimum(1.0, clip_limit / (grad_norm + 1e-06))
    results = [
        adam_update(masters[index], firsts[index], seconds[index], shards[index], factor, index)
        for index in range(5)
    ]
    return (
        block_out.reshape(out_shape),
        input_grad.reshape(out_shape),
        grad_norm,
        *(item[0] for item in results),
        *(item[1] for item in results),
        *(item[2] for item in results),
        *(item[0].astype(BF16) for item in results),
    )


def solution(mesh):
    shard, col = P("narrow", None), P(None, "narrow")
    seqs = P(("wide", "narrow"), None, None)
    group = (shard, shard, shard, shard, col)
    return jax.shard_map(
        body,
        mesh=mesh,
        in_specs=(seqs, seqs, P(("wide", "narrow"), None), P(("wide", "narrow"), None), *group, *group, *group),
        out_specs=(seqs, seqs, P(), *group, *group, *group, *group),
        check_vma=False,
    )
```

```python
import functools

import jax
import jax.numpy as jnp
from jax import lax
from jax.experimental import pallas as pl
from jax.experimental.pallas import tpu as pltpu
from jax.sharding import PartitionSpec as P

HEAD = 64
STEP = 10
LANES = 128
GROUP = 6 * HEAD
LOG2E = 1.4426950408889634
FAR = -1e30
VMEM_LIMIT = 60 * 1024 * 1024

beta_one = 0.9
beta_two = 0.999
adam_eps = 1e-08
norm_eps = 1e-05
clip_limit = 1.0
rate_table = (0.03, 0.3, 0.03, 0.015, 0.4)
decay_table = (0.01, 0.01, 0.01, 0.01, 0.0)

F32 = jnp.float32
BF16 = jnp.bfloat16


def mm(a, b):
    return lax.dot_general(a, b, (((1,), (0,)), ((), ())), preferred_element_type=F32)


def mm_nt(a, b):
    return lax.dot_general(a, b, (((1,), (1,)), ((), ())), preferred_element_type=F32)


def mm_tn(a, b):
    return lax.dot_general(a, b, (((0,), (0,)), ((), ())), preferred_element_type=F32)


def low_lanes(rows):
    return lax.broadcasted_iota(jnp.int32, (rows, LANES), 1) < HEAD


def swap_halves(tile):
    return pltpu.roll(tile, HEAD, 1)


def split_three(col):
    high = col.astype(BF16).astype(F32)
    rest = col - high
    mid = rest.astype(BF16).astype(F32)
    return high, mid, rest - mid


def qkv_tile(prod, bias, word):
    full = prod + bias
    query = jnp.where(word, full[:, 0:LANES], full[:, LANES : 2 * LANES])
    return (query.astype(BF16).astype(F32) * (HEAD**-0.5)).astype(BF16), full[
        :, 2 * LANES :
    ].astype(BF16)


def qkv_kernel(x_ref, w_ref, b_ref, word_ref, q_ref, kv_ref):
    word = word_ref[...] > 0
    for part in range(2):
        cols = slice(part * GROUP, (part + 1) * GROUP)
        query, keyval = qkv_tile(mm(x_ref[...], w_ref[:, cols]), b_ref[:, cols], word)
        out = slice(part * LANES, (part + 1) * LANES)
        q_ref[:, out] = query
        kv_ref[:, out] = keyval


def qkv_call(x, w, bias, word):
    rows, width = x.shape
    steps = w.shape[1] // (2 * GROUP)
    out = jax.ShapeDtypeStruct((rows, steps * 2 * LANES), BF16)
    return pl.pallas_call(
        qkv_kernel,
        grid=(steps,),
        in_specs=[
            pl.BlockSpec((rows, width), lambda i: (0, 0)),
            pl.BlockSpec((width, 2 * GROUP), lambda i: (0, i)),
            pl.BlockSpec((1, 2 * GROUP), lambda i: (0, i)),
            pl.BlockSpec((rows, LANES), lambda i: (0, 0)),
        ],
        out_specs=[pl.BlockSpec((rows, 2 * LANES), lambda i: (0, i))] * 2,
        out_shape=[out, out],
        compiler_params=pltpu.CompilerParams(vmem_limit_bytes=VMEM_LIMIT),
        name="qkv",
    )(x, w, bias, word)


class Links:
    def __init__(self, send, recv):
        self.send, self.recv = send, recv
        self.count = 0
        self.slots = {}
        self.open = []

    def slot(self, key):
        if key not in self.slots:
            self.slots[key] = len(self.slots)
        return self.slots[key]

    def copy(self, key, src, dst, device):
        index = self.slot(key)
        return pltpu.make_async_remote_copy(
            src_ref=src,
            dst_ref=dst,
            send_sem=self.send.at[index],
            recv_sem=self.recv.at[index],
            device_id=device,
            device_id_type=pl.DeviceIdType.MESH,
        )

    def start(self, key, src, dst, device):
        copy = self.copy(key, src, dst, device)
        copy.start()
        self.open.append(copy)

    def arrived(self, key, dst, device):
        self.copy(key, dst, dst, device).wait_recv()

    def finish(self):
        for copy in self.open:
            copy.wait_send()
        self.open = []


class Place:
    def __init__(self, narrow):
        self.wide, self.me = lax.axis_index("wide"), lax.axis_index("narrow")
        self.core = lax.rem(self.me, 2)
        self.z = self.me // 2
        self.depth = narrow // 2
        self.x_quarter = self.wide + 1 - 2 * lax.rem(self.wide, 2)
        self.y_quarter = lax.rem(self.wide + 2, 4)
        self.d_quarter = lax.rem(self.x_quarter + 2, 4)
        self.sib = self.me + 1 - 2 * self.core
        self.x_dev, self.y_dev = {"wide": self.x_quarter}, {"wide": self.y_quarter}
        self.sib_dev = {"narrow": self.sib}

    def ahead(self, k):
        return 2 * lax.rem(self.z + k, self.depth) + self.core

    def behind(self, k, other=False):
        core = 1 - self.core if other else self.core
        return 2 * lax.rem(self.z + self.depth - k, self.depth) + core

    def z_dev(self, k):
        return {"narrow": self.ahead(k)}

    def greet(self):
        barrier = pltpu.get_barrier_semaphore()
        partners = [self.x_dev, self.y_dev, self.sib_dev] + [self.z_dev(k) for k in range(1, self.depth)]
        for device in partners:
            pl.semaphore_signal(barrier, inc=1, device_id=device, device_id_type=pl.DeviceIdType.MESH)
        pl.semaphore_wait(barrier, len(partners))


def spot(start, size, unit):
    return pl.ds(pl.multiple_of(start, unit), size)


def gather_kernel(
    narrow, x_ref, proj_ref, wo_ref, w1_ref, w2_ref, vec_ref, seg_ref, type_ref,
    q_out, kv_out, ctx_out, aug_out, a_out, e_out, w2_out, vec_out, word_ref, km_ref, ka_ref,
    a_full, e_own, w2_own, v_all, bias, q_s, kv_s, ctx_s, aug_s, qa_ref, send, recv, local,
):
    rows, width = x_ref.shape
    share = proj_ref.shape[0]
    deep = w2_ref.shape[0]
    half, quarter, equarter, dquarter = share // 2, proj_ref.shape[1] // 4, e_own.shape[1] // 4, deep // 4
    heads = width // HEAD
    here = Place(narrow)
    links = Links(send, recv)
    me, steps = here.me, range(1, here.depth)

    def region(kind, owner, part, side=None):
        size, start = (share, 0) if side is None else (half, side * half)
        if kind == "a":
            return a_full.at[spot(owner * share + start, size, 16), spot(part * quarter, quarter, LANES)]
        if kind == "e":
            return e_out.at[spot(owner * share + start, size, 16), spot(part * equarter, equarter, LANES)]
        size, start = (dquarter, 0) if side is None else (dquarter // 2, side * (dquarter // 2))
        return w2_out.at[spot(owner * deep + part * dquarter + start, size, 16), :]

    def whole(kind, owner):
        if kind == "a":
            return a_full.at[spot(owner * share, share, 16), :]
        if kind == "e":
            return e_out.at[spot(owner * share, share, 16), :]
        if kind == "w":
            return w2_out.at[spot(owner * deep, deep, 16), :]
        return v_all.at[owner]

    def own(kind):
        return {"a": whole("a", me), "e": e_own, "w": w2_own, "v": v_all.at[me]}[kind]

    def own_quarter(kind):
        if kind == "a":
            return region("a", me, here.wide)
        if kind == "e":
            return e_own.at[:, spot(here.wide * equarter, equarter, LANES)]
        return w2_own.at[spot(here.wide * dquarter, dquarter, 16), :]

    def send_z(kind, k):
        links.start((kind, "z", k), own_quarter(kind), region(kind, me, here.wide), here.z_dev(k))

    def send_own(kind):
        links.start((kind, "o"), own(kind), whole(kind, me), here.sib_dev)

    def pass_z(kind, k):
        piece = region(kind, here.behind(k), here.wide)
        links.arrived((kind, "z", k), piece, here.z_dev(k))
        links.start((kind, "x", k), piece, piece, here.x_dev)
        links.start((kind, "y", k), piece, piece, here.y_dev)
        links.start((kind, "sz", k), piece, piece, here.sib_dev)

    def pass_xy(kind, k):
        owner = here.behind(k)
        piece = region(kind, owner, here.x_quarter)
        links.arrived((kind, "x", k), piece, here.x_dev)
        part = region(kind, owner, here.x_quarter, 0)
        links.start((kind, "dy", k), part, part, here.y_dev)
        links.start((kind, "sx", k), piece, piece, here.sib_dev)
        piece = region(kind, owner, here.y_quarter)
        links.arrived((kind, "y", k), piece, here.y_dev)
        part = region(kind, owner, here.y_quarter, 1)
        links.start((kind, "dx", k), part, part, here.x_dev)
        links.start((kind, "sy", k), piece, piece, here.sib_dev)

    def pass_d(kind, k):
        owner = here.behind(k)
        links.arrived((kind, "dy", k), region(kind, owner, here.d_quarter, 0), here.y_dev)
        links.arrived((kind, "dx", k), region(kind, owner, here.d_quarter, 1), here.x_dev)
        piece = region(kind, owner, here.d_quarter)
        links.start((kind, "sd", k), piece, piece, here.sib_dev)

    def from_sib(kind, way, part):
        for k in steps:
            links.arrived((kind, way, k), region(kind, here.behind(k, True), part), here.sib_dev)

    low = low_lanes(share)
    for pair in range(heads // 2):
        tiles = [proj_ref[:, slice(b * width + pair * LANES, b * width + (pair + 1) * LANES)] for b in range(6)]
        turned = [swap_halves(tile) for tile in tiles]
        for odd in range(2):
            for b in range(3):
                left, right = (turned[2 * b], tiles[2 * b + 1]) if odd else (tiles[2 * b], turned[2 * b + 1])
                at = (2 * pair + odd) * GROUP + b * LANES
                a_full[spot(me * share, share, 16), at : at + LANES] = jnp.where(low, left, right).astype(BF16)
    v_all[me] = jnp.zeros_like(v_all[me])
    v_all[me, 0 : vec_ref.shape[0], 0 : vec_ref.shape[1]] = vec_ref[...].astype(BF16)

    here.greet()
    for k in steps:
        send_z("a", k)
        links.start(("v", "z", k), v_all.at[me], v_all.at[me], here.z_dev(k))
    send_own("v")
    send_own("a")

    inner = w1_ref.shape[1]
    e_own[:, 0:inner] = w1_ref[...].astype(BF16)
    e_own[:, inner : inner + width] = wo_ref[...].astype(BF16)
    e_own[:, inner + width :] = jnp.zeros((share, e_own.shape[1] - inner - width), BF16)
    w2_own[...] = w2_ref[...].astype(BF16)
    copy_e = pltpu.make_async_copy(e_own, whole("e", me), local.at[0])
    copy_w = pltpu.make_async_copy(w2_own, whole("w", me), local.at[1])
    copy_e.start()
    copy_w.start()

    length = seg_ref.shape[1]
    lane = lax.broadcasted_iota(jnp.int32, (length, LANES), 1)
    for seq in range(seg_ref.shape[0]):
        at = slice(seq * length, (seq + 1) * length)
        segment, kind = (
            jnp.transpose(jnp.broadcast_to(ref[seq : seq + 1, :].astype(F32), (LANES, length)))
            for ref in (seg_ref, type_ref)
        )
        same = segment == lane.astype(F32)
        word = jnp.where(kind == 0.0, 1.0, 0.0)
        word_ref[at] = word.astype(BF16)
        km_ref[at] = jnp.where(lane < HEAD, word, 1.0 - word).astype(BF16)
        qa_ref[at] = jnp.where(same & (lane < 8), 1.0, 0.0).astype(BF16)
        ka_ref[at] = jnp.where(
            lane < 8, jnp.where(same, 0.0, FAR), jnp.where(lane < 11, 1.0, 0.0)
        ).astype(BF16)

    for k in steps:
        pass_z("a", k)
        send_z("e", k)
        owner = here.behind(k)
        links.arrived(("v", "z", k), v_all.at[owner], here.z_dev(k))
        links.start(("v", "sz", k), v_all.at[owner], v_all.at[owner], here.sib_dev)
    for k in steps:
        pass_xy("a", k)
    send_own("e")
    send_own("w")

    links.arrived(("v", "o"), v_all.at[here.sib], here.sib_dev)
    for k in steps:
        owner = here.behind(k, True)
        links.arrived(("v", "sz", k), v_all.at[owner], here.sib_dev)
    span = vec_ref.shape[1]
    vec_out[...] = jnp.concatenate([v_all[n].astype(F32)[:, 0:span] for n in range(narrow)], axis=1)
    low1 = low_lanes(1)
    for head in range(heads):
        cols = slice((head // 2) * LANES, (head // 2 + 1) * LANES)
        row = [vec_out[r : r + 1, cols] for r in range(4)] + [jnp.zeros((1, LANES), F32), vec_out[4:5, cols]]
        for b in range(3):
            left, right = row[2 * b], row[2 * b + 1]
            left, right = (swap_halves(left), right) if head % 2 else (left, swap_halves(right))
            at = head * GROUP + b * LANES
            bias[0:1, at : at + LANES] = jnp.where(low1, left, right)

    links.arrived(("a", "o"), whole("a", here.sib), here.sib_dev)
    outs = []

    def project(index, part):
        size = 256
        cols = spot(part * quarter, quarter, LANES)
        add = bias[0:1, cols]

        def tile(i, carry):
            at = spot(i * size, size, size)
            prod = mm(x_ref[at, :], a_full[:, cols])
            word = word_ref[at, :] > 0
            for head in range(quarter // GROUP):
                group = slice(head * GROUP, (head + 1) * GROUP)
                out = slice(head * LANES, (head + 1) * LANES)
                query, keyval = qkv_tile(prod[:, group], add[:, group], word)
                q_s[part, at, out] = query
                kv_s[part, at, out] = keyval
            return carry

        lax.fori_loop(0, rows // size, tile, 0)
        wide = q_s.shape[2]
        for number, (source, target) in enumerate(((q_s, q_out), (kv_s, kv_out))):
            copy = pltpu.make_async_copy(
                source.at[part], target.at[:, spot(part * wide, wide, LANES)], local.at[2 + 2 * index + number]
            )
            copy.start()
            outs.append(copy)

    from_sib("a", "sz", here.wide)
    project(0, here.wide)
    for k in steps:
        pass_z("e", k)
        send_z("w", k)
    for k in steps:
        pass_d("a", k)
    from_sib("a", "sx", here.x_quarter)
    project(1, here.x_quarter)
    for k in steps:
        pass_xy("e", k)
    from_sib("a", "sy", here.y_quarter)
    project(2, here.y_quarter)
    from_sib("a", "sd", here.d_quarter)
    project(3, here.d_quarter)
    copy_a = pltpu.make_async_copy(a_full, a_out, local.at[10])
    copy_a.start()
    low_seq = low_lanes(length)
    per = quarter // GROUP

    def attend(pair):
        for seq in range(seg_ref.shape[0]):
            at = slice(seq * length, (seq + 1) * length)
            contexts = []
            for head in (2 * pair, 2 * pair + 1):
                cols = slice(head % per * LANES, (head % per + 1) * LANES)
                context, extra = attend_head(
                    q_s[head // per, at, cols], kv_s[head // per, at, cols], qa_ref[at], ka_ref[at], km_ref[at]
                )
                aug_s[at, head * LANES : (head + 1) * LANES] = extra
                contexts.append(context)
            both = jnp.where(low_seq, swap_halves(contexts[0]), contexts[1])
            ctx_s[at, pair * LANES : (pair + 1) * LANES] = both.astype(BF16)
        for number, (source, target, wide) in enumerate(((ctx_s, ctx_out, LANES), (aug_s, aug_out, 2 * LANES))):
            cols = slice(pair * wide, (pair + 1) * wide)
            copy = pltpu.make_async_copy(source.at[:, cols], target.at[:, cols], local.at[11 + 2 * pair + number])
            copy.start()
            outs.append(copy)

    between = [
        lambda: [pass_z("w", k) for k in steps],
        lambda: [pass_d("e", k) for k in steps],
        lambda: [pass_xy("w", k) for k in steps],
        lambda: [pass_d("w", k) for k in steps],
    ]
    for pair in range(heads // 2):
        attend(pair)
        if pair < len(between):
            between[pair]()
    for later in between[heads // 2 :]:
        later()
    for kind in ("e", "w"):
        links.arrived((kind, "o"), whole(kind, here.sib), here.sib_dev)
        for way, part in (("sz", here.wide), ("sx", here.x_quarter), ("sy", here.y_quarter), ("sd", here.d_quarter)):
            from_sib(kind, way, part)
    links.finish()
    for copy in (copy_e, copy_w, copy_a, *outs):
        copy.wait()


def gather_call(narrow, x, proj, wo, w1, w2, vec, segments, types):
    rows, width = x.shape
    share, deep, inner = proj.shape[0], w2.shape[0], w1.shape[1]
    ecols = inner + width + 2 * LANES
    heads = width // HEAD
    depth = narrow // 2
    count = 3 * (1 + 9 * (depth - 1)) + 1 + 2 * (depth - 1)
    vmem = pl.BlockSpec(memory_space=pltpu.VMEM)
    hbm = pl.BlockSpec(memory_space=pl.ANY)
    shape = jax.ShapeDtypeStruct
    part = heads // 4 * LANES
    return pl.pallas_call(
        functools.partial(gather_kernel, narrow),
        in_specs=[vmem] * 8,
        out_specs=[hbm] * 7 + [vmem] * 4,
        out_shape=[
            shape((rows, heads * LANES), BF16),
            shape((rows, heads * LANES), BF16),
            shape((rows, width), BF16),
            shape((rows, heads * LANES), BF16),
            shape((width, proj.shape[1]), BF16),
            shape((width, ecols), BF16),
            shape((deep * narrow, width), BF16),
            shape((16, width), F32),
            shape((rows, LANES), BF16),
            shape((rows, LANES), BF16),
            shape((rows, LANES), BF16),
        ],
        scratch_shapes=[
            pltpu.VMEM((width, proj.shape[1]), BF16),
            pltpu.VMEM((share, ecols), BF16),
            pltpu.VMEM((deep, width), BF16),
            pltpu.VMEM((narrow, 16, LANES), BF16),
            pltpu.VMEM((8, proj.shape[1]), F32),
            pltpu.VMEM((4, rows, part), BF16),
            pltpu.VMEM((4, rows, part), BF16),
            pltpu.VMEM((rows, width), BF16),
            pltpu.VMEM((rows, heads * LANES), BF16),
            pltpu.VMEM((rows, LANES), BF16),
            pltpu.SemaphoreType.DMA((count,)),
            pltpu.SemaphoreType.DMA((count,)),
            pltpu.SemaphoreType.DMA((11 + heads,)),
        ],
        compiler_params=pltpu.CompilerParams(
            vmem_limit_bytes=VMEM_LIMIT, collective_id=0, has_side_effects=True
        ),
        name="gather",
    )(x, proj, wo, w1, w2, vec, segments, types)


def key_pair(keyval, kmask, low):
    wide = keyval.astype(F32)
    return (jnp.where(low, wide, swap_halves(wide)) * kmask.astype(F32)).astype(BF16)


def attend_head(query, keyval, qaug, kaug, kmask):
    rows = query.shape[0]
    low = low_lanes(rows)
    lane = lax.broadcasted_iota(jnp.int32, (rows, LANES), 1)
    keys = jnp.concatenate([key_pair(keyval, kmask, low), kaug], axis=1)
    scores = mm_nt(jnp.concatenate([query, qaug], axis=1), keys)
    top = jnp.max(scores, axis=1, keepdims=True)
    weight = jnp.exp2((scores - top) * LOG2E).astype(BF16)
    ones_val = jnp.where(low, 1.0, keyval.astype(F32)).astype(BF16)
    both = mm(weight, ones_val)
    total = swap_halves(both)
    log_total = top + jnp.log(jnp.where(low, both, total))
    high, mid, rest = split_three(log_total)
    extra = jnp.where(lane == 8, -high, jnp.where(lane == 9, -mid, jnp.where(lane == 10, -rest, 0.0)))
    return both / total, jnp.where(lane < 8, qaug.astype(F32), extra).astype(BF16)


def attend_kernel(q_ref, kv_ref, qa_ref, ka_ref, km_ref, ctx_ref, aug_ref):
    outs = []
    for part in range(2):
        cols = slice(part * LANES, (part + 1) * LANES)
        out, aug_ref[:, cols] = attend_head(q_ref[:, cols], kv_ref[:, cols], qa_ref[...], ka_ref[...], km_ref[...])
        outs.append(out)
    ctx_ref[...] = jnp.where(low_lanes(q_ref.shape[0]), swap_halves(outs[0]), outs[1]).astype(BF16)


def attend_call(q, kv, qa, ka, km, length):
    rows, cols = q.shape
    seqs, steps = rows // length, cols // (2 * LANES)
    pair = pl.BlockSpec((length, 2 * LANES), lambda s, i: (s, i))
    one = pl.BlockSpec((length, LANES), lambda s, i: (s, 0))
    return pl.pallas_call(
        attend_kernel,
        grid=(seqs, steps),
        in_specs=[pair, pair, one, one, one],
        out_specs=[pl.BlockSpec((length, LANES), lambda s, i: (s, i)), pair],
        out_shape=[
            jax.ShapeDtypeStruct((rows, cols // 2), BF16),
            jax.ShapeDtypeStruct((rows, cols), BF16),
        ],
        compiler_params=pltpu.CompilerParams(vmem_limit_bytes=VMEM_LIMIT),
        name="attend",
    )(q, kv, qa, ka, km)


def attend_back_head(query, keyval, aug, gcon, con, kaug, kmask, word, odd, low, lane):
    keys = key_pair(keyval, kmask, low)
    scores_t = mm_nt(jnp.concatenate([keys, kaug], axis=1), jnp.concatenate([query, aug], axis=1))
    probs_t = jnp.exp2(scores_t * LOG2E)
    gwide = gcon.astype(F32)
    prod = gwide * con.astype(F32)
    mine = low != odd
    delta = jnp.sum(jnp.where(mine, prod, 0.0), axis=1, keepdims=True)
    high, mid, rest = split_three(delta)
    extra = jnp.where(lane == 0, -high, jnp.where(lane == 1, -mid, jnp.where(lane == 2, -rest, 0.0)))
    ghead = jnp.where(low, extra, jnp.where(odd, gwide, swap_halves(gwide))).astype(BF16)
    ones_val = jnp.where(low, jnp.where(lane < 3, 1.0, 0.0), keyval.astype(F32)).astype(BF16)
    gscores_t = (probs_t * mm_nt(ones_val, ghead)).astype(BF16)
    gval = mm(probs_t.astype(BF16), ghead)
    gkey = mm(gscores_t, query)
    gquery = (jnp.transpose(mm_tn(keys, gscores_t)) * (HEAD**-0.5)).astype(BF16)
    zero = jnp.zeros_like(gquery)
    gkey = jnp.where(kmask.astype(F32) > 0, gkey, 0.0)
    gkey = gkey + swap_halves(gkey)
    return (
        jnp.where(word, gquery, zero),
        jnp.where(word, zero, gquery),
        jnp.where(low, gkey, gval).astype(BF16),
    )


def attend_back_kernel(
    length, x_ref, q_ref, kv_ref, aug_ref, gc_ref, ctx_ref, ka_ref, km_ref, word_ref, gp_ref, gw_ref, sum_ref, xt
):
    step = pl.program_id(0)
    rows = x_ref.shape[0]

    @pl.when(step == 0)
    def _():
        xt[...] = jnp.transpose(x_ref[...])

    low = low_lanes(length)
    lane = lax.broadcasted_iota(jnp.int32, (length, LANES), 1)
    odd = lax.rem(step, 2) == 1
    for seq in range(rows // length):
        here = slice(seq * length, (seq + 1) * length)
        tiles = attend_back_head(
            q_ref[here], kv_ref[here], aug_ref[here], gc_ref[here], ctx_ref[here],
            ka_ref[here], km_ref[here], word_ref[here] > 0, odd, low, lane,
        )
        for index, tile in enumerate(tiles):
            gp_ref[here, index * LANES : (index + 1) * LANES] = tile
    grads = gp_ref[...]
    gw_ref[...] = mm(xt[...], grads).astype(BF16)
    sums = jnp.sum(grads.astype(F32).reshape(rows // 8, 8, GROUP), axis=0)
    sum_ref[...] = jnp.sum(sums, axis=0, keepdims=True)


def attend_back_call(x, q, kv, aug, gc, ctx, ka, km, word, length):
    rows, width = x.shape
    heads = q.shape[1] // LANES
    head = pl.BlockSpec((rows, LANES), lambda h: (0, h))
    pair = pl.BlockSpec((rows, LANES), lambda h: (0, h // 2))
    one = pl.BlockSpec((rows, LANES), lambda h: (0, 0))
    return pl.pallas_call(
        functools.partial(attend_back_kernel, length),
        grid=(heads,),
        in_specs=[pl.BlockSpec((rows, width), lambda h: (0, 0)), head, head, head, pair, pair, one, one, one],
        out_specs=[
            pl.BlockSpec((rows, GROUP), lambda h: (0, h)),
            pl.BlockSpec((width, GROUP), lambda h: (0, h)),
            pl.BlockSpec((1, GROUP), lambda h: (0, h)),
        ],
        out_shape=[
            jax.ShapeDtypeStruct((rows, heads * GROUP), BF16),
            jax.ShapeDtypeStruct((width, heads * GROUP), BF16),
            jax.ShapeDtypeStruct((1, heads * GROUP), F32),
        ],
        scratch_shapes=[pltpu.VMEM((width, rows), BF16)],
        compiler_params=pltpu.CompilerParams(vmem_limit_bytes=VMEM_LIMIT),
        name="attend_back",
    )(x, q, kv, aug, gc, ctx, ka, km, word)


class Chunk:
    def __init__(self, name, refs, by_rows):
        self.name = name
        self.total, self.r1a, self.r1b, self.r2a, self.r2b, self.rz, self.final = refs
        self.by_rows = by_rows
        _, self.rows, self.cols = self.total.shape

    def cut(self, part, side=None):
        if self.by_rows:
            size = self.rows // 4
            if side is None:
                return spot(part * size, size, 16), slice(None)
            return spot(part * size + side * (size // 2), size // 2, 16), slice(None)
        size, half = self.cols // 4, self.rows // 2
        rows = slice(0, self.rows) if side is None else slice(side * half, (side + 1) * half)
        return rows, spot(part * size, size, LANES)


def chunk_scratch(depth, rows, cols, by_rows):
    if by_rows:
        piece, half = (rows // 4, cols), (rows // 8, cols)
    else:
        piece, half = (rows, cols // 4), (rows // 2, cols // 4)
    return [
        pltpu.VMEM((depth, rows, cols), BF16),
        pltpu.VMEM((2, depth, *half), BF16),
        pltpu.VMEM((2, depth, *half), BF16),
        pltpu.VMEM((depth, *half), BF16),
        pltpu.VMEM((depth, *half), BF16),
        pltpu.VMEM((depth - 1, *piece), BF16),
        pltpu.VMEM((rows, cols), BF16),
    ]


class Reducer:
    def __init__(self, here, send, recv):
        self.here = here
        self.links = Links(send, recv)
        self.sent = []

    def send(self, key, build):
        copy = self.links.copy(key, *build())
        copy.start()
        self.sent.append((key, build))

    def arrived(self, key, dst, device):
        self.links.arrived(key, dst, device)

    def finish(self):
        for key, build in self.sent:
            self.links.copy(key, *build()).wait_send()

    def pair_send(self, chunk, sources):
        here = self.here
        for z in range(here.depth):
            for part, (_, cols) in enumerate(sources(0)):

                def build(z=z, part=part, cols=cols):
                    owner = 2 * z + 1 - here.core
                    return sources(owner)[part][0], chunk.total.at[z, :, cols], here.sib_dev

                self.send((chunk.name, "s", z, part), build)

    def pair_wait(self, chunk, sources):
        for z in range(self.here.depth):
            for part, (_, cols) in enumerate(sources(0)):
                self.arrived((chunk.name, "s", z, part), chunk.total.at[z, :, cols], self.here.sib_dev)

    def plane_send(self, chunk):
        here = self.here
        for index, (a, b) in enumerate(((here.x_quarter, here.y_quarter), (here.d_quarter, here.d_quarter))):

            def first(index=index, part=a):
                rows, cols = chunk.cut(part, 0)
                return chunk.total.at[:, rows, cols], chunk.r1a.at[index], here.x_dev

            def second(index=index, part=b):
                rows, cols = chunk.cut(part, 1)
                return chunk.total.at[:, rows, cols], chunk.r1b.at[index], here.y_dev

            self.send((chunk.name, "1a", index), first)
            self.send((chunk.name, "1b", index), second)

    def add(self, chunk, part, side, value):
        rows, cols = chunk.cut(part, side)
        chunk.total[:, rows, cols] = chunk.total[:, rows, cols] + value

    def plane_turn(self, chunk):
        here = self.here
        for index in range(2):
            self.arrived((chunk.name, "1a", index), chunk.r1a.at[index], here.x_dev)
            self.arrived((chunk.name, "1b", index), chunk.r1b.at[index], here.y_dev)
        self.add(chunk, here.y_quarter, 0, chunk.r1a[1])
        self.add(chunk, here.x_quarter, 1, chunk.r1b[1])

        def first():
            rows, cols = chunk.cut(here.y_quarter, 0)
            return chunk.total.at[:, rows, cols], chunk.r2a, here.y_dev

        def second():
            rows, cols = chunk.cut(here.x_quarter, 1)
            return chunk.total.at[:, rows, cols], chunk.r2b, here.x_dev

        self.send((chunk.name, "2a"), first)
        self.send((chunk.name, "2b"), second)
        self.add(chunk, here.wide, 0, chunk.r1a[0])
        self.add(chunk, here.wide, 1, chunk.r1b[0])

    def depth_send(self, chunk):
        here = self.here
        self.arrived((chunk.name, "2a"), chunk.r2a, here.y_dev)
        self.arrived((chunk.name, "2b"), chunk.r2b, here.x_dev)
        self.add(chunk, here.wide, 0, chunk.r2a[...])
        self.add(chunk, here.wide, 1, chunk.r2b[...])
        for k in range(1, here.depth):

            def build(k=k):
                rows, cols = chunk.cut(here.wide)
                return chunk.total.at[lax.rem(here.z + k, here.depth), rows, cols], chunk.rz.at[k - 1], here.z_dev(k)

            self.send((chunk.name, "z", k), build)

    def share_send(self, chunk):
        here = self.here
        for k in range(1, here.depth):
            self.arrived((chunk.name, "z", k), chunk.rz.at[k - 1], here.z_dev(k))
        rows, cols = chunk.cut(here.wide)
        done = chunk.total[here.z, rows, cols].astype(F32)
        for k in range(1, here.depth):
            done = done + chunk.rz[k - 1].astype(F32)
        chunk.final[rows, cols] = done.astype(BF16)

        def build(device):
            rows, cols = chunk.cut(here.wide)
            return chunk.final.at[rows, cols], chunk.final.at[rows, cols], device

        self.send((chunk.name, "fx"), lambda: build(here.x_dev))
        self.send((chunk.name, "fy"), lambda: build(here.y_dev))

    def share_pass(self, chunk):
        here = self.here

        def part(quarter, side, device):
            rows, cols = chunk.cut(quarter, side)
            return chunk.final.at[rows, cols], chunk.final.at[rows, cols], device

        self.arrived((chunk.name, "fx"), *part(here.x_quarter, None, here.x_dev)[1:])
        self.send((chunk.name, "fdy"), lambda: part(here.x_quarter, 0, here.y_dev))
        self.arrived((chunk.name, "fy"), *part(here.y_quarter, None, here.y_dev)[1:])
        self.send((chunk.name, "fdx"), lambda: part(here.y_quarter, 1, here.x_dev))

    def share_wait(self, chunk):
        here = self.here
        for key, side, device in (("fdy", 0, here.y_dev), ("fdx", 1, here.x_dev)):
            rows, cols = chunk.cut(here.d_quarter, side)
            self.arrived((chunk.name, key), chunk.final.at[rows, cols], device)


CHUNK_HEADS = 4


def squares(ref, cols):
    total = jnp.zeros((8, LANES), F32)
    rows = ref.shape[0]
    for start in range(0, cols, LANES):
        tile = ref[:, start : start + LANES].astype(F32)
        total = total + jnp.sum((tile * tile).reshape(rows // 8, 8, LANES), axis=0)
    return total


def reduce_kernel(
    narrow, length, groups,
    x_ref, q_ref, kv_ref, aug_ref, gc_ref, ctx_ref, wp_ref, ka_ref, km_ref, word_ref, gvec_ref,
    gr1_ref, gw1_ref, gwo_ref, gw2_ref,
    ig_ref, fw_ref, fe_ref, fa_ref, v_ref, n_ref,
    xt, gw, gp_ref, ig, *scratch,
):
    step = pl.program_id(0)
    rows, width = x_ref.shape
    heads = groups * CHUNK_HEADS
    inner = gw1_ref.shape[1]
    here = Place(narrow)
    scratch = list(scratch)
    chunk_w = Chunk("w", scratch[0:7], True)
    chunk_e = Chunk("e", scratch[7:14], False)
    chunk_a = [Chunk(("a", j), scratch[14 + 7 * j : 21 + 7 * j], False) for j in range(groups)]
    own_w, own_e, v0, v1, v2, vs, vx, vy, vz, n0, ns, nz, send, recv, local = scratch[14 + 7 * groups :]
    red = Reducer(here, send, recv)
    share, deep = chunk_e.rows, chunk_w.rows

    def sources_w(owner):
        return [(gw2_ref.at[spot(owner * deep, deep, 16), :], slice(0, width))]

    def sources_e(owner):
        at = spot(owner * share, share, 16)
        return [(gw1_ref.at[at, :], slice(0, inner)), (gwo_ref.at[at, :], slice(inner, inner + width))]

    def sources_a(j):
        return lambda owner: [(gw.at[j, spot(owner * share, share, 16), :], slice(0, CHUNK_HEADS * GROUP))]

    def own_copies():
        copies = []
        for own, sources in ((own_w, sources_w), (own_e, sources_e)):
            for z in range(here.depth):
                for source, cols in sources(2 * z + here.core):
                    copies.append(pltpu.make_async_copy(source, own.at[z, :, cols], local.at[len(copies)]))
        return copies

    def out_copies():
        copies = [(chunk_w.final, fw_ref), (chunk_e.final, fe_ref)]
        wide = CHUNK_HEADS * GROUP
        copies += [(chunk.final, fa_ref.at[:, j * wide : (j + 1) * wide]) for j, chunk in enumerate(chunk_a)]
        base = 3 * here.depth
        return [pltpu.make_async_copy(a, b, local.at[base + i]) for i, (a, b) in enumerate(copies)]

    def copy_ig():
        return pltpu.make_async_copy(gr1_ref, ig, local.at[3 * here.depth + 2 + groups])

    def merge(chunk, own):
        def one(z, carry):
            chunk.total[z] = chunk.total[z] + own(z)
            return carry

        lax.fori_loop(0, here.depth, one, 0)

    def own_a(j):
        return lambda z: gw[j, spot((2 * z + here.core) * share, share, 16), :]

    @pl.when(step == 0)
    def _():
        for copy in own_copies():
            copy.start()
        copy_ig().start()
        here.greet()
        red.pair_send(chunk_w, sources_w)
        red.pair_send(chunk_e, sources_e)
        pad = chunk_e.cols - inner - width
        chunk_e.total[:, :, inner + width :] = jnp.zeros((here.depth, share, pad), BF16)
        own_e[:, :, inner + width :] = jnp.zeros((here.depth, share, pad), BF16)
        xt[...] = jnp.transpose(x_ref[...])
        v0[...] = gvec_ref[...]

    def advance(at, action):
        pl.when(step == at)(action)

    def act_w1():
        for copy in own_copies():
            copy.wait()
        red.pair_wait(chunk_w, sources_w)
        merge(chunk_w, lambda z: own_w[z])
        red.plane_send(chunk_w)

    def act_e1():
        red.pair_wait(chunk_e, sources_e)
        merge(chunk_e, lambda z: own_e[z])
        red.plane_send(chunk_e)

    def act_a1(j):
        red.pair_wait(chunk_a[j], sources_a(j))
        merge(chunk_a[j], own_a(j))
        red.plane_send(chunk_a[j])

    advance(1, act_w1)
    advance(2, act_e1)
    advance(4, lambda: red.plane_turn(chunk_w))
    advance(5, lambda: act_a1(0))
    advance(6, lambda: red.depth_send(chunk_w))
    advance(8, lambda: red.plane_turn(chunk_e))
    advance(9, lambda: act_a1(1))
    advance(10, lambda: red.depth_send(chunk_e))
    advance(11, lambda: red.share_send(chunk_w))

    low = low_lanes(length)
    lane = lax.broadcasted_iota(jnp.int32, (length, LANES), 1)
    odd = lax.rem(step, 2) == 1
    for seq in range(rows // length):
        at = slice(seq * length, (seq + 1) * length)
        tiles = attend_back_head(
            q_ref[at], kv_ref[at], aug_ref[at], gc_ref[at], ctx_ref[at],
            ka_ref[at], km_ref[at], word_ref[at] > 0, odd, low, lane,
        )
        for index, tile in enumerate(tiles):
            gp_ref[at, index * LANES : (index + 1) * LANES] = tile
    grads = gp_ref[...]
    group, inside = step // CHUNK_HEADS, lax.rem(step, CHUNK_HEADS)
    gw[group, :, spot(inside * GROUP, GROUP, LANES)] = mm(xt[...], grads).astype(BF16)
    sums = jnp.sum(jnp.sum(grads.astype(F32).reshape(rows // 8, 8, GROUP), axis=0), axis=0, keepdims=True)

    @pl.when(step == 0)
    def _():
        copy_ig().wait()

    ig[...] += mm_nt(grads, wp_ref[...])

    low1 = low_lanes(1)
    pair = spot(step // 2 * LANES, LANES, LANES)
    mine = low1 != odd
    for b in range(3):
        tile = sums[:, b * LANES : (b + 1) * LANES]
        turned = swap_halves(tile)
        first = jnp.where(odd, turned, tile)
        second = jnp.where(odd, tile, turned)
        if b < 2:
            v0[2 * b : 2 * b + 1, pair] = jnp.where(mine, first, v0[2 * b : 2 * b + 1, pair])
            v0[2 * b + 1 : 2 * b + 2, pair] = jnp.where(mine, second, v0[2 * b + 1 : 2 * b + 2, pair])
        else:
            v0[4:5, pair] = jnp.where(mine, second, v0[4:5, pair])

    for j in range(groups):
        advance((j + 1) * CHUNK_HEADS - 1, lambda j=j: red.pair_send(chunk_a[j], sources_a(j)))

    @pl.when(step == heads - 1)
    def _():
        ig_ref[...] = ig[...].astype(BF16)
        last = chunk_a[-1]
        red.send(("v", "s"), lambda: (v0, vs, here.sib_dev))
        red.plane_turn(chunk_a[0])
        red.share_send(chunk_e)
        red.share_pass(chunk_w)
        act_a1(groups - 1)
        red.arrived(("v", "s"), vs, here.sib_dev)
        v1[...] = v0[...] + vs[...]
        red.send(("v", "x"), lambda: (v1, vx, here.x_dev))
        red.depth_send(chunk_a[0])
        for chunk in chunk_a[1:-1]:
            red.plane_turn(chunk)
        red.share_pass(chunk_e)
        for chunk in chunk_a[1:-1]:
            red.depth_send(chunk)
        red.plane_turn(last)
        red.arrived(("v", "x"), vx, here.x_dev)
        v2[...] = v1[...] + vx[...]
        red.send(("v", "y"), lambda: (v2, vy, here.y_dev))
        for chunk in chunk_a[:-1]:
            red.share_send(chunk)
        red.depth_send(last)
        red.arrived(("v", "y"), vy, here.y_dev)
        vz[here.z] = v2[...] + vy[...]
        for k in range(1, here.depth):
            red.send(("v", "z", k), lambda k=k: (vz.at[here.z], vz.at[here.z], here.z_dev(k)))
        red.share_wait(chunk_w)
        red.share_wait(chunk_e)
        for chunk in chunk_a[:-1]:
            red.share_pass(chunk)
        norm = squares(chunk_w.final, width) + squares(chunk_e.final, inner + width)
        for chunk in chunk_a[:-1]:
            red.share_wait(chunk)
            norm = norm + squares(chunk.final, chunk.cols)
        red.share_send(last)
        for k in range(1, here.depth):
            source = here.behind(k) // 2
            red.arrived(("v", "z", k), vz.at[source], here.z_dev(k))
        vec = vz[0]
        for z in range(1, here.depth):
            vec = vec + vz[z]
        v_ref[...] = vec
        red.share_pass(last)
        red.share_wait(last)
        for copy in out_copies():
            copy.start()
        n0[...] = norm + squares(last.final, last.cols)
        red.send(("n", "s"), lambda: (n0, ns, here.sib_dev))
        red.arrived(("n", "s"), ns, here.sib_dev)
        nz[here.z] = n0[...] + ns[...]
        for k in range(1, here.depth):
            red.send(("n", "z", k), lambda k=k: (nz.at[here.z], nz.at[here.z], here.z_dev(k)))
        for k in range(1, here.depth):
            source = here.behind(k) // 2
            red.arrived(("n", "z", k), nz.at[source], here.z_dev(k))
        total = nz[0]
        for z in range(1, here.depth):
            total = total + nz[z]
        every = jnp.sum(jnp.sum(total, axis=0, keepdims=True), axis=1, keepdims=True)
        square = jnp.sum(jnp.sum(vec * vec, axis=0, keepdims=True), axis=1, keepdims=True)
        n_ref[...] = jnp.broadcast_to(every + square, n_ref.shape)
        red.finish()
        for copy in out_copies():
            copy.wait()


def reduce_call(narrow, x, q, kv, aug, gc, ctx, wp, ka, km, word, gvec, gr1, gw1, gwo, gw2, length):
    rows, width = x.shape
    inner = gw2.shape[0]
    heads = q.shape[1] // LANES
    groups = heads // CHUNK_HEADS
    depth = narrow // 2
    share, deep, ecols, acols = width // narrow, inner // narrow, inner + width + 2 * LANES, CHUNK_HEADS * GROUP
    head = pl.BlockSpec((rows, LANES), lambda h: (0, h))
    pair = pl.BlockSpec((rows, LANES), lambda h: (0, h // 2))
    one = pl.BlockSpec((rows, LANES), lambda h: (0, 0), pipeline_mode=pl.Buffered(1))
    hbm = pl.BlockSpec(memory_space=pl.ANY)
    shape = jax.ShapeDtypeStruct
    vec = pltpu.VMEM((16, width), F32)
    tile = pltpu.VMEM((8, LANES), F32)
    scratch = [pltpu.VMEM((width, rows), BF16), pltpu.VMEM((groups, width, acols), BF16)]
    scratch += [pltpu.VMEM((rows, GROUP), BF16), pltpu.VMEM((rows, width), F32)]
    scratch += chunk_scratch(depth, deep, width, True)
    scratch += chunk_scratch(depth, share, ecols, False)
    for _ in range(groups):
        scratch += chunk_scratch(depth, share, acols, False)
    scratch += [pltpu.VMEM((depth, deep, width), BF16), pltpu.VMEM((depth, share, ecols), BF16)]
    scratch += [vec] * 6 + [pltpu.VMEM((depth, 16, width), F32), tile, tile, pltpu.VMEM((depth, 8, LANES), F32)]
    count = (2 + groups) * (depth + 10 + depth - 1) + depth + 2 * (3 + depth)
    scratch += [pltpu.SemaphoreType.DMA((count,))] * 2 + [pltpu.SemaphoreType.DMA((3 * depth + 3 + groups,))]
    return pl.pallas_call(
        functools.partial(reduce_kernel, narrow, length, groups),
        grid=(heads,),
        in_specs=[
            pl.BlockSpec((rows, width), lambda h: (0, 0), pipeline_mode=pl.Buffered(1)),
            head, head, head, pair, pair, pl.BlockSpec((width, GROUP), lambda h: (0, h)), one, one, one,
            pl.BlockSpec((16, width), lambda h: (0, 0), pipeline_mode=pl.Buffered(1)),
            hbm, hbm, hbm, hbm,
        ],
        out_specs=[
            pl.BlockSpec((rows, width), lambda h: (0, 0), pipeline_mode=pl.Buffered(1)),
            hbm, hbm, hbm,
            pl.BlockSpec((16, width), lambda h: (0, 0)),
            pl.BlockSpec((8, LANES), lambda h: (0, 0)),
        ],
        out_shape=[
            shape((rows, width), BF16),
            shape((deep, width), BF16),
            shape((share, ecols), BF16),
            shape((share, heads * GROUP), BF16),
            shape((16, width), F32),
            shape((8, LANES), F32),
        ],
        scratch_shapes=scratch,
        compiler_params=pltpu.CompilerParams(
            vmem_limit_bytes=VMEM_LIMIT, collective_id=1, has_side_effects=True
        ),
        name="reduce",
    )(x, q, kv, aug, gc, ctx, wp, ka, km, word, gvec, gr1, gw1, gwo, gw2)


def gelu_pair(pre):
    size = jnp.abs(pre) * (0.5**0.5)
    bell = jnp.exp2(pre * pre * (-0.5 * LOG2E))
    t = 1.0 / (1.0 + 0.3275911 * size)
    poly = t * (0.254829592 + t * (-0.284496736 + t * (1.421413741 + t * (-1.453152027 + t * 1.061405429))))
    tail = 0.5 * poly * bell
    share = jnp.where(pre >= 0, 1.0 - tail, tail)
    return pre * share, share + pre * bell * 0.3989422804014327


def fold(array_in):
    rows, cols = array_in.shape
    return jnp.sum(array_in.reshape(rows // 8, 8, cols), axis=0)


def middle_kernel(
    tiles, x_ref, ctx_ref, cot_ref, vec_ref, e_hbm, w2_hbm,
    out_ref, gr1_ref, gctx_ref, gw2_ref, gw1_ref, gwo_ref, gvec_ref,
    wo, w1, w2, h1_s, act_s, gb_s, gp_s, ga_s, ctx_s, dg_s, acc, sems,
):
    step = pl.program_id(0)
    size, width = x_ref.shape
    inner = w1.shape[1]
    chunks = inner // width

    def weight_copies(index):
        source, target = (
            (e_hbm.at[:, inner : inner + width], wo),
            (e_hbm.at[:, 0:inner], w1),
            (w2_hbm, w2),
        )[index]
        return pltpu.make_async_copy(source, target, sems.at[index])

    @pl.when(step == 0)
    def _():
        for index in range(3):
            weight_copies(index).start()
        acc[...] = jnp.zeros_like(acc)

    def vec(row):
        return vec_ref[row : row + 1, :].astype(F32)

    @pl.when(step < tiles)
    def _():
        here = pl.ds(pl.multiple_of(step * size, size), size)

        @pl.when(step == 0)
        def _():
            weight_copies(0).wait()

        ctx_s[here, :] = ctx_ref[...]
        resid = x_ref[...].astype(F32) + mm(ctx_ref[...], wo[...]) + vec(5)
        center = resid - jnp.mean(resid, axis=1, keepdims=True)
        inv1 = lax.rsqrt(jnp.mean(center * center, axis=1, keepdims=True) + norm_eps)
        n1 = center * inv1
        h1 = n1 * vec(6) + vec(7)
        h1b = h1.astype(BF16)
        h1_s[here, :] = h1b

        @pl.when(step == 0)
        def _():
            weight_copies(1).wait()
            weight_copies(2).wait()

        branch = h1 + vec(8)
        for c in range(chunks):
            cols = slice(c * width, (c + 1) * width)
            act, slope = gelu_pair(mm(h1b, w1[:, cols]) + vec(11 + c))
            act = act.astype(BF16)
            act_s[here, cols] = act
            dg_s[:, cols] = slope
            branch = branch + mm(act, w2[cols, :])
        center = branch - jnp.mean(branch, axis=1, keepdims=True)
        inv2 = lax.rsqrt(jnp.mean(center * center, axis=1, keepdims=True) + norm_eps)
        n2 = center * inv2
        out_ref[...] = (n2 * vec(9) + vec(10)).astype(BF16)
        grad = cot_ref[...].astype(F32)
        gn = grad * n2
        acc[9] += fold(gn)
        acc[10] += fold(grad)
        scaled = grad * vec(9)
        gr2 = inv2 * (
            scaled
            - jnp.mean(scaled, axis=1, keepdims=True)
            - n2 * jnp.mean(scaled * n2, axis=1, keepdims=True)
        )
        gb = gr2.astype(BF16)
        gb_s[here, :] = gb
        acc[8] += fold(gb.astype(F32))
        gh1 = gr2
        for c in range(chunks):
            cols = slice(c * width, (c + 1) * width)
            gpre = (mm_nt(gb, w2[cols, :]) * dg_s[:, cols]).astype(BF16)
            gp_s[here, cols] = gpre
            acc[11 + c] += fold(gpre.astype(F32))
            gh1 = gh1 + mm_nt(gpre, w1[:, cols])
        acc[6] += fold(gh1 * n1)
        acc[7] += fold(gh1)
        scaled = gh1 * vec(6)
        gr1 = inv1 * (
            scaled
            - jnp.mean(scaled, axis=1, keepdims=True)
            - n1 * jnp.mean(scaled * n1, axis=1, keepdims=True)
        )
        gr1_ref[...] = gr1
        ga = gr1.astype(BF16)
        ga_s[here, :] = ga
        acc[5] += fold(ga.astype(F32))
        gctx_ref[...] = mm_nt(ga, wo[...]).astype(BF16)

    for c in range(chunks):
        cols = slice(c * width, (c + 1) * width)

        @pl.when(step == tiles + c)
        def _():
            gw2_ref[...] = mm_tn(act_s[:, cols], gb_s[...]).astype(BF16)

        @pl.when(step == tiles + chunks + c)
        def _():
            gw1_ref[...] = mm_tn(h1_s[...], gp_s[:, cols]).astype(BF16)

    @pl.when(step == tiles + 2 * chunks)
    def _():
        gwo_ref[...] = mm_tn(ctx_s[...], ga_s[...]).astype(BF16)
        for row in range(acc.shape[0]):
            gvec_ref[row : row + 1, :] = jnp.sum(acc[row], axis=0, keepdims=True)


def middle_call(x, ctx, cot, vec, e, w2, size):
    rows, width = x.shape
    inner = w2.shape[0]
    tiles, chunks = rows // size, inner // width
    tile = pl.BlockSpec((size, width), lambda i: (jnp.minimum(i, tiles - 1), 0))
    hbm = pl.BlockSpec(memory_space=pl.ANY)

    def after(start):
        return lambda i: jnp.clip(i - start, 0, chunks - 1)

    shape = jax.ShapeDtypeStruct
    return pl.pallas_call(
        functools.partial(middle_kernel, tiles),
        grid=(tiles + 2 * chunks + 1,),
        in_specs=[tile, tile, tile, pl.BlockSpec(vec.shape, lambda i: (0, 0)), hbm, hbm],
        out_specs=[
            tile,
            tile,
            tile,
            pl.BlockSpec((width, width), lambda i: (after(tiles)(i), 0)),
            pl.BlockSpec((width, width), lambda i: (0, after(tiles + chunks)(i))),
            pl.BlockSpec((width, width), lambda i: (0, 0)),
            pl.BlockSpec(vec.shape, lambda i: (0, 0)),
        ],
        out_shape=[
            shape((rows, width), BF16),
            shape((rows, width), F32),
            shape((rows, width), BF16),
            shape((inner, width), BF16),
            shape((width, inner), BF16),
            shape((width, width), BF16),
            shape(vec.shape, F32),
        ],
        scratch_shapes=[
            pltpu.VMEM((width, width), BF16),
            pltpu.VMEM((width, inner), BF16),
            pltpu.VMEM((inner, width), BF16),
            pltpu.VMEM((rows, width), BF16),
            pltpu.VMEM((rows, inner), BF16),
            pltpu.VMEM((rows, width), BF16),
            pltpu.VMEM((rows, inner), BF16),
            pltpu.VMEM((rows, width), BF16),
            pltpu.VMEM((rows, width), BF16),
            pltpu.VMEM((size, inner), F32),
            pltpu.VMEM((vec.shape[0], 8, width), F32),
            pltpu.SemaphoreType.DMA((3,)),
        ],
        compiler_params=pltpu.CompilerParams(vmem_limit_bytes=VMEM_LIMIT),
        name="middle",
    )(x, ctx, cot, vec, e, w2)


def input_grad_kernel(gp_ref, w_ref, gr1_ref, out_ref):
    out_ref[...] = (gr1_ref[...] + mm_nt(gp_ref[...], w_ref[...])).astype(BF16)


def input_grad_call(gp, w, gr1, size):
    rows, cols = gp.shape
    width = w.shape[0]
    return pl.pallas_call(
        input_grad_kernel,
        grid=(rows // size,),
        in_specs=[
            pl.BlockSpec((size, cols), lambda i: (i, 0)),
            pl.BlockSpec((width, cols), lambda i: (0, 0)),
            pl.BlockSpec((size, width), lambda i: (i, 0)),
        ],
        out_specs=pl.BlockSpec((size, width), lambda i: (i, 0)),
        out_shape=jax.ShapeDtypeStruct((rows, width), BF16),
        compiler_params=pltpu.CompilerParams(vmem_limit_bytes=VMEM_LIMIT),
        name="input_grad",
    )(gp, w, gr1)


def adam_update(master, first_old, second_old, grad_shard, factor, index):
    clipped = grad_shard * factor
    new_first = beta_one * first_old + (1.0 - beta_one) * clipped
    new_second = beta_two * second_old + (1.0 - beta_two) * clipped * clipped
    direction = (
        new_first
        / (1.0 - beta_one**STEP)
        / (jnp.sqrt(new_second / (1.0 - beta_two**STEP)) + adam_eps)
    )
    new_weight = master - rate_table[index] * (direction + decay_table[index] * master)
    return (new_weight, new_first, new_second)


def update_tile(master, first, second, grad, factor, index):
    weight, first, second = adam_update(master, first, second, grad.astype(F32), factor, index)
    return weight, first, second, weight.astype(BF16)


def update_kernel(narrow, n_ref, fa_ref, fe_ref, fw_ref, v_ref, *refs):
    ins, outs = refs[0:15], refs[15:35]
    heads = fa_ref.shape[1] // GROUP
    width = heads * HEAD
    norm = jnp.sqrt(n_ref[0:1, 0:1])
    factor = jnp.minimum(1.0, clip_limit / (norm + 1e-06))

    def store(index, rows, cols, grad):
        news = update_tile(*(ins[5 * t + index][rows, cols] for t in range(3)), grad, factor, index)
        for t, new in enumerate(news):
            outs[5 * t + index][rows, cols] = new

    every = slice(None)
    low = low_lanes(fa_ref.shape[0])
    for pair in range(heads // 2):
        at = 2 * pair * GROUP
        for b in range(3):
            even = fa_ref[:, at + b * LANES : at + (b + 1) * LANES].astype(F32)
            odd = fa_ref[:, at + GROUP + b * LANES : at + GROUP + (b + 1) * LANES].astype(F32)
            for second in range(2):
                if second:
                    grad = jnp.where(low, swap_halves(even), odd)
                else:
                    grad = jnp.where(low, even, swap_halves(odd))
                start = (2 * b + second) * width + pair * LANES
                store(0, every, slice(start, start + LANES), grad)
    inner = ins[2].shape[1]
    store(1, every, every, fe_ref[:, inner : inner + width])
    store(2, every, every, fe_ref[:, 0:inner])
    store(3, every, every, fw_ref[...])

    @pl.when(pl.program_id(0) == 0)
    def _():
        count, span = ins[4].shape
        me = lax.axis_index("narrow")
        turned = pltpu.roll(v_ref[...], lax.rem(width - me * span, width), 1)
        store(4, every, every, turned[0:count, 0:span])


def update_call(narrow, norm, fa, fe, fw, vec, masters, firsts, seconds):
    share = fa.shape[0]
    steps = share // 16

    def rows_of(array_in):
        return pl.BlockSpec((array_in.shape[0] // steps, array_in.shape[1]), lambda i: (i, 0))

    def fixed(array_in):
        return pl.BlockSpec(array_in.shape, lambda i: (0, 0))

    def group(arrays):
        return [rows_of(a) for a in arrays[:4]] + [fixed(arrays[4])]

    def shapes(arrays, dtype):
        return [jax.ShapeDtypeStruct(a.shape, dtype) for a in arrays]

    return pl.pallas_call(
        functools.partial(update_kernel, narrow),
        grid=(steps,),
        in_specs=[fixed(norm), rows_of(fa), rows_of(fe), rows_of(fw), fixed(vec)] + group(masters) * 3,
        out_specs=group(masters) * 4,
        out_shape=shapes(masters, F32) * 3 + shapes(masters, BF16),
        compiler_params=pltpu.CompilerParams(vmem_limit_bytes=VMEM_LIMIT),
        name="update",
    )(norm, fa, fe, fw, vec, *masters, *firsts, *seconds)


def by_head(array_in):
    rows, cols = array_in.shape
    heads = cols // GROUP
    return array_in.reshape(rows, 6, heads, HEAD).transpose(0, 2, 1, 3).reshape(rows, cols)


def by_block(array_in):
    rows, cols = array_in.shape
    heads = cols // GROUP
    return array_in.reshape(rows, heads, 6, HEAD).transpose(0, 2, 1, 3).reshape(rows, cols)


def can_pass_pieces(wide, narrow, width, deep):
    share = width // narrow
    return wide == 4 and narrow % 2 == 0 and narrow > 2 and share % 32 == 0 and deep % 128 == 0


def body(
    x_in, cotangent, segment_ids, type_ids,
    projection, context_out, expand_weight, reduce_weight, vector_params,
    first_projection, first_context, first_expand, first_reduce, first_vectors,
    second_projection, second_context, second_expand, second_reduce, second_vectors,
):
    seq_count, seq_len, width = x_in.shape
    rows = seq_count * seq_len

    def gather(array_in, axis):
        return lax.all_gather(array_in.astype(BF16), "narrow", axis=axis, tiled=True)

    hidden = x_in.reshape(rows, width)
    cot = cotangent.reshape(rows, width)
    narrow = lax.axis_size("narrow")
    pieces = can_pass_pieces(lax.axis_size("wide"), narrow, width, reduce_weight.shape[0])
    if pieces:
        query, keyval, context, aug, proj_w, mid_w, reduce_w, vec_rows, word, kmask, kaug = gather_call(
            narrow, hidden, projection, context_out, expand_weight, reduce_weight, vector_params,
            segment_ids, type_ids,
        )
    else:
        word_col = (type_ids == 0).reshape(rows, 1)
        lane = lax.broadcasted_iota(jnp.int32, (rows, LANES), 1)
        word = jnp.broadcast_to(word_col, (rows, LANES)).astype(BF16)
        kmask = ((lane < HEAD) == word_col).astype(BF16)
        same = segment_ids.reshape(rows, 1) == lane
        qaug = jnp.where(same & (lane < 8), 1.0, 0.0).astype(BF16)
        kaug = jnp.where(lane < 8, jnp.where(same, 0.0, FAR), jnp.where(lane < 11, 1.0, 0.0)).astype(BF16)
        proj_w, vec_half = gather(by_head(projection), 0), gather(vector_params, 1)
        reduce_w = gather(reduce_weight, 0)
        mid_w = jnp.concatenate(
            [gather(expand_weight, 0), gather(context_out, 0), jnp.zeros((width, 2 * LANES), BF16)], axis=1
        )
        zero_row = jnp.zeros((1, width), BF16)
        bias = by_head(jnp.concatenate([vec_half[0:4], zero_row, vec_half[4:5]]).reshape(1, -1)).astype(F32)
        vec_rows = jnp.pad(vec_half.astype(F32), ((0, 1), (0, 0)))
        query, keyval = qkv_call(hidden, proj_w, bias, word)
        context, aug = attend_call(query, keyval, qaug, kaug, kmask, seq_len)
    block_out, grad_r1, grad_context, grad_reduce, grad_expand, grad_ctx_w, grad_mid = middle_call(
        hidden, context, cot, vec_rows, mid_w, reduce_w, 256
    )
    masters = (projection, context_out, expand_weight, reduce_weight, vector_params)
    firsts = (first_projection, first_context, first_expand, first_reduce, first_vectors)
    seconds = (second_projection, second_context, second_expand, second_reduce, second_vectors)
    out_shape = (seq_count, seq_len, width)
    if pieces:
        input_grad, shard_w, shard_e, shard_a, grad_vectors, norm = reduce_call(
            narrow, hidden, query, keyval, aug, grad_context, context, proj_w, kaug, kmask, word, grad_mid,
            grad_r1, grad_expand, grad_ctx_w, grad_reduce, seq_len,
        )
        updated = update_call(narrow, norm, shard_a, shard_e, shard_w, grad_vectors, masters, firsts, seconds)
        return (
            block_out.reshape(out_shape),
            input_grad.reshape(out_shape),
            jnp.sqrt(norm[0, 0]),
            *updated,
        )
    grad_proj, grad_proj_w, grad_sums = attend_back_call(
        hidden, query, keyval, aug, grad_context, context, kaug, kmask, word, seq_len
    )
    input_grad = input_grad_call(grad_proj, proj_w, grad_r1, 256)
    sum_rows = by_block(grad_sums).reshape(6, width)
    grad_vectors = jnp.concatenate([sum_rows[0:4], sum_rows[5:6], grad_mid[5:15]], axis=0)

    def scatter(array_in, axis):
        return lax.psum_scatter(array_in, "narrow", scatter_dimension=axis, tiled=True)

    def over_wide(array_in):
        return lax.psum(array_in.astype(BF16), "wide").astype(F32)

    shards = (
        by_block(over_wide(scatter(grad_proj_w, 0))),
        over_wide(scatter(grad_ctx_w, 0)),
        over_wide(scatter(grad_expand, 0)),
        over_wide(scatter(grad_reduce, 0)),
        over_wide(scatter(grad_vectors, 1)),
    )
    local_squares = sum((jnp.sum(shard_item * shard_item) for shard_item in shards))
    total_squares = lax.psum(local_squares, "narrow")
    grad_norm = jnp.sqrt(total_squares)
    factor = jnp.minimum(1.0, clip_limit / (grad_norm + 1e-06))
    results = [
        adam_update(masters[index], firsts[index], seconds[index], shards[index], factor, index)
        for index in range(5)
    ]
    return (
        block_out.reshape(out_shape),
        input_grad.reshape(out_shape),
        grad_norm,
        *(item[0] for item in results),
        *(item[1] for item in results),
        *(item[2] for item in results),
        *(item[0].astype(BF16) for item in results),
    )


def solution(mesh):
    shard, col = P("narrow", None), P(None, "narrow")
    seqs = P(("wide", "narrow"), None, None)
    group = (shard, shard, shard, shard, col)
    return jax.shard_map(
        body,
        mesh=mesh,
        in_specs=(seqs, seqs, P(("wide", "narrow"), None), P(("wide", "narrow"), None), *group, *group, *group),
        out_specs=(seqs, seqs, P(), *group, *group, *group, *group),
        check_vma=False,
    )
```

```python
import functools

import jax
import jax.numpy as jnp
from jax import lax
from jax.experimental import pallas as pl
from jax.experimental.pallas import tpu as pltpu
from jax.sharding import PartitionSpec as P

HEAD = 64
STEP = 10
LANES = 128
GROUP = 6 * HEAD
LOG2E = 1.4426950408889634
FAR = -1e30
VMEM_LIMIT = 60 * 1024 * 1024

beta_one = 0.9
beta_two = 0.999
adam_eps = 1e-08
norm_eps = 1e-05
clip_limit = 1.0
rate_table = (0.03, 0.3, 0.03, 0.015, 0.4)
decay_table = (0.01, 0.01, 0.01, 0.01, 0.0)

F32 = jnp.float32
BF16 = jnp.bfloat16


def mm(a, b):
    return lax.dot_general(a, b, (((1,), (0,)), ((), ())), preferred_element_type=F32)


def mm_nt(a, b):
    return lax.dot_general(a, b, (((1,), (1,)), ((), ())), preferred_element_type=F32)


def mm_tn(a, b):
    return lax.dot_general(a, b, (((0,), (0,)), ((), ())), preferred_element_type=F32)


def low_lanes(rows):
    return lax.broadcasted_iota(jnp.int32, (rows, LANES), 1) < HEAD


def swap_halves(tile):
    return pltpu.roll(tile, HEAD, 1)


def split_three(col):
    high = col.astype(BF16).astype(F32)
    rest = col - high
    mid = rest.astype(BF16).astype(F32)
    return high, mid, rest - mid


def qkv_tile(prod, bias, word):
    full = prod + bias
    query = jnp.where(word, full[:, 0:LANES], full[:, LANES : 2 * LANES])
    return (query.astype(BF16).astype(F32) * (HEAD**-0.5)).astype(BF16), full[
        :, 2 * LANES :
    ].astype(BF16)


def qkv_kernel(x_ref, w_ref, b_ref, word_ref, q_ref, kv_ref):
    word = word_ref[...] > 0
    for part in range(2):
        cols = slice(part * GROUP, (part + 1) * GROUP)
        query, keyval = qkv_tile(mm(x_ref[...], w_ref[:, cols]), b_ref[:, cols], word)
        out = slice(part * LANES, (part + 1) * LANES)
        q_ref[:, out] = query
        kv_ref[:, out] = keyval


def qkv_call(x, w, bias, word):
    rows, width = x.shape
    steps = w.shape[1] // (2 * GROUP)
    out = jax.ShapeDtypeStruct((rows, steps * 2 * LANES), BF16)
    return pl.pallas_call(
        qkv_kernel,
        grid=(steps,),
        in_specs=[
            pl.BlockSpec((rows, width), lambda i: (0, 0)),
            pl.BlockSpec((width, 2 * GROUP), lambda i: (0, i)),
            pl.BlockSpec((1, 2 * GROUP), lambda i: (0, i)),
            pl.BlockSpec((rows, LANES), lambda i: (0, 0)),
        ],
        out_specs=[pl.BlockSpec((rows, 2 * LANES), lambda i: (0, i))] * 2,
        out_shape=[out, out],
        compiler_params=pltpu.CompilerParams(vmem_limit_bytes=VMEM_LIMIT),
        name="qkv",
    )(x, w, bias, word)


class Links:
    def __init__(self, send, recv):
        self.send_sem, self.recv_sem = send, recv
        self.slots = {}
        self.sent = []

    def copy(self, key, src, dst, device):
        index = self.slots.setdefault(key, len(self.slots))
        return pltpu.make_async_remote_copy(
            src_ref=src,
            dst_ref=dst,
            send_sem=self.send_sem.at[index],
            recv_sem=self.recv_sem.at[index],
            device_id=device,
            device_id_type=pl.DeviceIdType.MESH,
        )

    def send(self, key, build, *guards):
        def start():
            self.copy(key, *build()).start()

        guarded(start, guards)
        self.sent.append((key, build, guards))

    def arrived(self, key, dst, device):
        self.copy(key, dst, dst, device).wait_recv()

    def finish(self):
        for key, build, guards in self.sent:

            def wait(key=key, build=build):
                self.copy(key, *build()).wait_send()

            guarded(wait, guards)


def guarded(action, guards):
    if not guards:
        action()
        return
    holds = guards[0]()
    for guard in guards[1:]:
        holds = jnp.logical_and(holds, guard())
    pl.when(holds)(action)


class Place:
    def __init__(self, narrow):
        self.wide, self.me = lax.axis_index("wide"), lax.axis_index("narrow")
        self.core = lax.rem(self.me, 2)
        self.z = self.me // 2
        self.depth = narrow // 2
        self.x_quarter = self.wide + 1 - 2 * lax.rem(self.wide, 2)
        self.y_quarter = lax.rem(self.wide + 2, 4)
        self.d_quarter = lax.rem(self.x_quarter + 2, 4)
        self.sib = self.me + 1 - 2 * self.core
        self.x_dev, self.y_dev = {"wide": self.x_quarter}, {"wide": self.y_quarter}
        self.sib_dev = {"narrow": self.sib}

    def ahead(self, k):
        return 2 * lax.rem(self.z + k, self.depth) + self.core

    def behind(self, k, other=False):
        core = 1 - self.core if other else self.core
        return 2 * lax.rem(self.z + self.depth - k, self.depth) + core

    def z_dev(self, k):
        return {"narrow": self.ahead(k)}

    def has_next(self, way):
        return lambda: self.z + 1 < self.depth if way == 0 else self.z > 0

    def comes(self, way, hop):
        return lambda: self.z >= hop if way == 0 else self.z + hop < self.depth

    def origin(self, way, hop, other=False):
        core = 1 - self.core if other else self.core
        return 2 * (self.z - hop if way == 0 else self.z + hop) + core

    def next_dev(self, way):
        return {"narrow": self.me + 2 if way == 0 else self.me - 2}

    def greet_near(self):
        barrier = pltpu.get_barrier_semaphore()

        def greet(device):
            pl.semaphore_signal(barrier, inc=1, device_id=device, device_id_type=pl.DeviceIdType.MESH)

        for device in (self.x_dev, self.y_dev, self.sib_dev):
            greet(device)
        for way in range(2):
            guarded(lambda way=way: greet(self.next_dev(way)), (self.has_next(way),))
        pl.semaphore_wait(barrier, 3 + jnp.minimum(self.z, 1) + jnp.minimum(self.depth - 1 - self.z, 1))

    def greet(self):
        barrier = pltpu.get_barrier_semaphore()
        partners = [self.x_dev, self.y_dev, self.sib_dev] + [self.z_dev(k) for k in range(1, self.depth)]
        for device in partners:
            pl.semaphore_signal(barrier, inc=1, device_id=device, device_id_type=pl.DeviceIdType.MESH)
        pl.semaphore_wait(barrier, len(partners))


def spot(start, size, unit):
    return pl.ds(pl.multiple_of(start, unit), size)


def gather_kernel(
    narrow, x_ref, proj_ref, wo_ref, w1_ref, w2_ref, vec_ref, seg_ref, type_ref,
    q_out, kv_out, ctx_out, aug_out, a_out, e_out, w2_out, vec_out, word_ref, km_ref, ka_ref,
    a_full, e_own, w2_own, v_all, bias, q_s, kv_s, ctx_s, aug_s, qa_ref, send, recv, local,
):
    rows, width = x_ref.shape
    share = proj_ref.shape[0]
    deep = w2_ref.shape[0]
    half, quarter, equarter, dquarter = share // 2, proj_ref.shape[1] // 4, e_own.shape[1] // 4, deep // 4
    heads = width // HEAD
    here = Place(narrow)
    links = Links(send, recv)
    me, hops = here.me, range(1, here.depth)
    routes = [(way, hop) for hop in hops for way in range(2)]

    def region(kind, owner, part, side=None):
        size, start = (share, 0) if side is None else (half, side * half)
        if kind == "a":
            return a_full.at[spot(owner * share + start, size, 16), spot(part * quarter, quarter, LANES)]
        if kind == "e":
            return e_out.at[spot(owner * share + start, size, 16), spot(part * equarter, equarter, LANES)]
        size, start = (dquarter, 0) if side is None else (dquarter // 2, side * (dquarter // 2))
        return w2_out.at[spot(owner * deep + part * dquarter + start, size, 16), :]

    def whole(kind, owner):
        if kind == "a":
            return a_full.at[spot(owner * share, share, 16), :]
        if kind == "e":
            return e_out.at[spot(owner * share, share, 16), :]
        if kind == "w":
            return w2_out.at[spot(owner * deep, deep, 16), :]
        return v_all.at[owner]

    def own(kind):
        return {"a": whole("a", me), "e": e_own, "w": w2_own, "v": v_all.at[me]}[kind]

    def own_part(kind, part, side=None):
        if kind == "a":
            return region("a", me, part, side)
        if kind == "e":
            rows = slice(0, share) if side is None else slice(side * half, (side + 1) * half)
            return e_own.at[rows, spot(part * equarter, equarter, LANES)]
        size, start = (dquarter, 0) if side is None else (dquarter // 2, side * (dquarter // 2))
        return w2_own.at[spot(part * dquarter + start, size, 16), :]

    def send_own(kind):
        links.send((kind, "o"), lambda: (own(kind), whole(kind, me), here.sib_dev))

    def send_z(kind):
        for way in range(2):
            ahead = here.has_next(way)
            if kind == "v":
                links.send(("v", "z", way, 1), lambda way=way: (own("v"), own("v"), here.next_dev(way)), ahead)
                continue
            links.send(
                (kind, "z", way, 1),
                lambda way=way: (own_part(kind, here.wide), region(kind, me, here.wide), here.next_dev(way)),
                ahead,
            )
            links.send(
                (kind, "h", way, 1),
                lambda way=way: (
                    own_part(kind, here.d_quarter, 0), region(kind, me, here.d_quarter, 0), here.next_dev(way)
                ),
                ahead,
            )

    def relay(key, target, device, *guards):
        links.send(key, lambda: (target(), target(), device()), *guards)

    def receive(key, target, guard):
        guarded(lambda: links.arrived(key, target(), here.sib_dev), (guard,))

    def pass_z(kind, hop):
        for way in range(2):
            comes, ahead = here.comes(way, hop), here.has_next(way)
            onward = lambda way=way: here.next_dev(way)
            if kind == "v":
                piece = lambda way=way: whole("v", here.origin(way, hop))
            else:
                piece = lambda way=way: region(kind, here.origin(way, hop), here.wide)
            receive((kind, "z", way, hop), piece, comes)
            if hop + 1 < here.depth:
                relay((kind, "z", way, hop + 1), piece, onward, comes, ahead)
            if kind != "v":
                relay((kind, "x", way, hop), piece, lambda: here.x_dev, comes)
                relay((kind, "y", way, hop), piece, lambda: here.y_dev, comes)
            relay((kind, "sz", way, hop), piece, lambda: here.sib_dev, comes)
            if kind != "v":
                other = lambda way=way: region(kind, here.origin(way, hop), here.d_quarter, 0)
                receive((kind, "h", way, hop), other, comes)
                if hop + 1 < here.depth:
                    relay((kind, "h", way, hop + 1), other, onward, comes, ahead)
                relay((kind, "sh", way, hop), other, lambda: here.sib_dev, comes)

    def by_x(kind, hop):
        return kind == "a" or (kind == "w" and hop % 2 == 1)

    def pass_xy(kind, hop):
        for way in range(2):
            comes = here.comes(way, hop)
            for name, part, back in (("x", here.x_quarter, "y"), ("y", here.y_quarter, "x")):
                piece = lambda way=way, part=part: region(kind, here.origin(way, hop), part)
                receive((kind, name, way, hop), piece, comes)
                if by_x(kind, hop) == (back == "x"):
                    device = here.x_dev if back == "x" else here.y_dev
                    rest = lambda way=way, part=part: region(kind, here.origin(way, hop), part, 1)
                    relay((kind, "d", way, hop), rest, lambda device=device: device, comes)
                relay((kind, "s" + name, way, hop), piece, lambda: here.sib_dev, comes)

    def pass_d(kind):
        for way, hop in routes:
            comes = here.comes(way, hop)
            rest = lambda way=way, hop=hop: region(kind, here.origin(way, hop), here.d_quarter, 1)
            receive((kind, "d", way, hop), rest, comes)
            relay((kind, "sd", way, hop), rest, lambda: here.sib_dev, comes)

    def from_sib(kind, name, part, side=None):
        for way, hop in routes:
            piece = lambda way=way, hop=hop: region(kind, here.origin(way, hop, True), part, side)
            receive((kind, name, way, hop), piece, here.comes(way, hop))

    low = low_lanes(share)
    for pair in range(heads // 2):
        tiles = [proj_ref[:, slice(b * width + pair * LANES, b * width + (pair + 1) * LANES)] for b in range(6)]
        turned = [swap_halves(tile) for tile in tiles]
        for odd in range(2):
            for b in range(3):
                left, right = (turned[2 * b], tiles[2 * b + 1]) if odd else (tiles[2 * b], turned[2 * b + 1])
                at = (2 * pair + odd) * GROUP + b * LANES
                a_full[spot(me * share, share, 16), at : at + LANES] = jnp.where(low, left, right).astype(BF16)
    v_all[me] = jnp.zeros_like(v_all[me])
    v_all[me, 0 : vec_ref.shape[0], 0 : vec_ref.shape[1]] = vec_ref[...].astype(BF16)

    here.greet_near()
    send_z("a")
    send_z("v")
    send_own("v")
    send_own("a")

    inner = w1_ref.shape[1]
    e_own[:, 0:inner] = w1_ref[...].astype(BF16)
    e_own[:, inner : inner + width] = wo_ref[...].astype(BF16)
    e_own[:, inner + width :] = jnp.zeros((share, e_own.shape[1] - inner - width), BF16)
    w2_own[...] = w2_ref[...].astype(BF16)
    copy_e = pltpu.make_async_copy(e_own, whole("e", me), local.at[0])
    copy_w = pltpu.make_async_copy(w2_own, whole("w", me), local.at[1])
    copy_e.start()
    copy_w.start()

    length = seg_ref.shape[1]
    lane = lax.broadcasted_iota(jnp.int32, (length, LANES), 1)
    for seq in range(seg_ref.shape[0]):
        at = slice(seq * length, (seq + 1) * length)
        segment, kind = (
            jnp.transpose(jnp.broadcast_to(ref[seq : seq + 1, :].astype(F32), (LANES, length)))
            for ref in (seg_ref, type_ref)
        )
        same = segment == lane.astype(F32)
        word = jnp.where(kind == 0.0, 1.0, 0.0)
        word_ref[at] = word.astype(BF16)
        km_ref[at] = jnp.where(lane < HEAD, word, 1.0 - word).astype(BF16)
        qa_ref[at] = jnp.where(same & (lane < 8), 1.0, 0.0).astype(BF16)
        ka_ref[at] = jnp.where(
            lane < 8, jnp.where(same, 0.0, FAR), jnp.where(lane < 11, 1.0, 0.0)
        ).astype(BF16)

    def hop(kind, number):
        if number < here.depth:
            pass_z(kind, number)
            if kind == "a":
                pass_z("v", number)

    def turn(kind, number):
        if number < here.depth:
            pass_xy(kind, number)

    hop("a", 1)
    hop("a", 2)
    send_z("e")
    send_own("e")
    turn("a", 1)
    hop("a", 3)
    turn("a", 2)
    hop("e", 1)
    turn("a", 3)
    for number in range(4, here.depth):
        hop("a", number)
        turn("a", number)
    hop("e", 2)
    send_z("w")
    send_own("w")
    hop("e", 3)
    for number in range(4, here.depth):
        hop("e", number)

    links.arrived(("v", "o"), v_all.at[here.sib], here.sib_dev)
    for way, number in routes:
        receive(
            ("v", "sz", way, number),
            lambda way=way, number=number: v_all.at[here.origin(way, number, True)],
            here.comes(way, number),
        )
    span = vec_ref.shape[1]
    vec_out[...] = jnp.concatenate([v_all[n].astype(F32)[:, 0:span] for n in range(narrow)], axis=1)
    low1 = low_lanes(1)
    for head in range(heads):
        cols = slice((head // 2) * LANES, (head // 2 + 1) * LANES)
        row = [vec_out[r : r + 1, cols] for r in range(4)] + [jnp.zeros((1, LANES), F32), vec_out[4:5, cols]]
        for b in range(3):
            left, right = row[2 * b], row[2 * b + 1]
            left, right = (swap_halves(left), right) if head % 2 else (left, swap_halves(right))
            at = head * GROUP + b * LANES
            bias[0:1, at : at + LANES] = jnp.where(low1, left, right)

    links.arrived(("a", "o"), whole("a", here.sib), here.sib_dev)
    outs = []

    def project(index, part):
        size = 256
        cols = spot(part * quarter, quarter, LANES)
        add = bias[0:1, cols]

        def tile(i, carry):
            at = spot(i * size, size, size)
            prod = mm(x_ref[at, :], a_full[:, cols])
            word = word_ref[at, :] > 0
            for head in range(quarter // GROUP):
                group = slice(head * GROUP, (head + 1) * GROUP)
                out = slice(head * LANES, (head + 1) * LANES)
                query, keyval = qkv_tile(prod[:, group], add[:, group], word)
                q_s[part, at, out] = query
                kv_s[part, at, out] = keyval
            return carry

        lax.fori_loop(0, rows // size, tile, 0)
        wide = q_s.shape[2]
        for number, (source, target) in enumerate(((q_s, q_out), (kv_s, kv_out))):
            copy = pltpu.make_async_copy(
                source.at[part], target.at[:, spot(part * wide, wide, LANES)], local.at[2 + 2 * index + number]
            )
            copy.start()
            outs.append(copy)

    from_sib("a", "sz", here.wide)
    project(0, here.wide)
    turn("e", 1)
    pass_d("a")
    from_sib("a", "sx", here.x_quarter)
    project(1, here.x_quarter)
    hop("w", 1)
    turn("e", 2)
    hop("w", 2)
    from_sib("a", "sy", here.y_quarter)
    project(2, here.y_quarter)
    turn("e", 3)
    hop("w", 3)
    for number in range(4, here.depth):
        turn("e", number)
        hop("w", number)
    from_sib("a", "sh", here.d_quarter, 0)
    from_sib("a", "sd", here.d_quarter, 1)
    project(3, here.d_quarter)
    copy_a = pltpu.make_async_copy(a_full, a_out, local.at[10])
    copy_a.start()
    low_seq = low_lanes(length)
    per = quarter // GROUP

    def attend(pair):
        for seq in range(seg_ref.shape[0]):
            at = slice(seq * length, (seq + 1) * length)
            contexts = []
            for head in (2 * pair, 2 * pair + 1):
                cols = slice(head % per * LANES, (head % per + 1) * LANES)
                context, extra = attend_head(
                    q_s[head // per, at, cols], kv_s[head // per, at, cols], qa_ref[at], ka_ref[at], km_ref[at]
                )
                aug_s[at, head * LANES : (head + 1) * LANES] = extra
                contexts.append(context)
            both = jnp.where(low_seq, swap_halves(contexts[0]), contexts[1])
            ctx_s[at, pair * LANES : (pair + 1) * LANES] = both.astype(BF16)
        for number, (source, target, wide) in enumerate(((ctx_s, ctx_out, LANES), (aug_s, aug_out, 2 * LANES))):
            cols = slice(pair * wide, (pair + 1) * wide)
            copy = pltpu.make_async_copy(source.at[:, cols], target.at[:, cols], local.at[11 + 2 * pair + number])
            copy.start()
            outs.append(copy)

    between = [
        lambda: [pass_d("e"), turn("w", 1)],
        lambda: turn("w", 2),
        lambda: [turn("w", number) for number in range(3, here.depth)],
        lambda: pass_d("w"),
    ]
    for pair in range(heads // 2):
        attend(pair)
        if pair < len(between):
            between[pair]()
    for later in between[heads // 2 :]:
        later()
    for kind in ("e", "w"):
        links.arrived((kind, "o"), whole(kind, here.sib), here.sib_dev)
        for name, part in (("sz", here.wide), ("sx", here.x_quarter), ("sy", here.y_quarter)):
            from_sib(kind, name, part)
        from_sib(kind, "sh", here.d_quarter, 0)
        from_sib(kind, "sd", here.d_quarter, 1)
    links.finish()
    for copy in (copy_e, copy_w, copy_a, *outs):
        copy.wait()


def gather_call(narrow, x, proj, wo, w1, w2, vec, segments, types):
    rows, width = x.shape
    share, deep, inner = proj.shape[0], w2.shape[0], w1.shape[1]
    ecols = inner + width + 2 * LANES
    heads = width // HEAD
    depth = narrow // 2
    count = 3 * (1 + 20 * (depth - 1)) + 1 + 4 * (depth - 1)
    vmem = pl.BlockSpec(memory_space=pltpu.VMEM)
    hbm = pl.BlockSpec(memory_space=pl.ANY)
    shape = jax.ShapeDtypeStruct
    part = heads // 4 * LANES
    return pl.pallas_call(
        functools.partial(gather_kernel, narrow),
        in_specs=[vmem] * 8,
        out_specs=[hbm] * 7 + [vmem] * 4,
        out_shape=[
            shape((rows, heads * LANES), BF16),
            shape((rows, heads * LANES), BF16),
            shape((rows, width), BF16),
            shape((rows, heads * LANES), BF16),
            shape((width, proj.shape[1]), BF16),
            shape((width, ecols), BF16),
            shape((deep * narrow, width), BF16),
            shape((16, width), F32),
            shape((rows, LANES), BF16),
            shape((rows, LANES), BF16),
            shape((rows, LANES), BF16),
        ],
        scratch_shapes=[
            pltpu.VMEM((width, proj.shape[1]), BF16),
            pltpu.VMEM((share, ecols), BF16),
            pltpu.VMEM((deep, width), BF16),
            pltpu.VMEM((narrow, 16, LANES), BF16),
            pltpu.VMEM((8, proj.shape[1]), F32),
            pltpu.VMEM((4, rows, part), BF16),
            pltpu.VMEM((4, rows, part), BF16),
            pltpu.VMEM((rows, width), BF16),
            pltpu.VMEM((rows, heads * LANES), BF16),
            pltpu.VMEM((rows, LANES), BF16),
            pltpu.SemaphoreType.DMA((count,)),
            pltpu.SemaphoreType.DMA((count,)),
            pltpu.SemaphoreType.DMA((11 + heads,)),
        ],
        compiler_params=pltpu.CompilerParams(
            vmem_limit_bytes=VMEM_LIMIT, collective_id=0, has_side_effects=True
        ),
        name="gather",
    )(x, proj, wo, w1, w2, vec, segments, types)


def key_pair(keyval, kmask, low):
    wide = keyval.astype(F32)
    return (jnp.where(low, wide, swap_halves(wide)) * kmask.astype(F32)).astype(BF16)


def attend_head(query, keyval, qaug, kaug, kmask):
    rows = query.shape[0]
    low = low_lanes(rows)
    lane = lax.broadcasted_iota(jnp.int32, (rows, LANES), 1)
    keys = jnp.concatenate([key_pair(keyval, kmask, low), kaug], axis=1)
    scores = mm_nt(jnp.concatenate([query, qaug], axis=1), keys)
    top = jnp.max(scores, axis=1, keepdims=True)
    weight = jnp.exp2((scores - top) * LOG2E).astype(BF16)
    ones_val = jnp.where(low, 1.0, keyval.astype(F32)).astype(BF16)
    both = mm(weight, ones_val)
    total = swap_halves(both)
    log_total = top + jnp.log(jnp.where(low, both, total))
    high, mid, rest = split_three(log_total)
    extra = jnp.where(lane == 8, -high, jnp.where(lane == 9, -mid, jnp.where(lane == 10, -rest, 0.0)))
    return both / total, jnp.where(lane < 8, qaug.astype(F32), extra).astype(BF16)


def attend_kernel(q_ref, kv_ref, qa_ref, ka_ref, km_ref, ctx_ref, aug_ref):
    outs = []
    for part in range(2):
        cols = slice(part * LANES, (part + 1) * LANES)
        out, aug_ref[:, cols] = attend_head(q_ref[:, cols], kv_ref[:, cols], qa_ref[...], ka_ref[...], km_ref[...])
        outs.append(out)
    ctx_ref[...] = jnp.where(low_lanes(q_ref.shape[0]), swap_halves(outs[0]), outs[1]).astype(BF16)


def attend_call(q, kv, qa, ka, km, length):
    rows, cols = q.shape
    seqs, steps = rows // length, cols // (2 * LANES)
    pair = pl.BlockSpec((length, 2 * LANES), lambda s, i: (s, i))
    one = pl.BlockSpec((length, LANES), lambda s, i: (s, 0))
    return pl.pallas_call(
        attend_kernel,
        grid=(seqs, steps),
        in_specs=[pair, pair, one, one, one],
        out_specs=[pl.BlockSpec((length, LANES), lambda s, i: (s, i)), pair],
        out_shape=[
            jax.ShapeDtypeStruct((rows, cols // 2), BF16),
            jax.ShapeDtypeStruct((rows, cols), BF16),
        ],
        compiler_params=pltpu.CompilerParams(vmem_limit_bytes=VMEM_LIMIT),
        name="attend",
    )(q, kv, qa, ka, km)


def attend_back_head(query, keyval, aug, gcon, con, kaug, kmask, word, odd, low, lane):
    keys = key_pair(keyval, kmask, low)
    scores_t = mm_nt(jnp.concatenate([keys, kaug], axis=1), jnp.concatenate([query, aug], axis=1))
    probs_t = jnp.exp2(scores_t * LOG2E)
    gwide = gcon.astype(F32)
    prod = gwide * con.astype(F32)
    mine = low != odd
    delta = jnp.sum(jnp.where(mine, prod, 0.0), axis=1, keepdims=True)
    high, mid, rest = split_three(delta)
    extra = jnp.where(lane == 0, -high, jnp.where(lane == 1, -mid, jnp.where(lane == 2, -rest, 0.0)))
    ghead = jnp.where(low, extra, jnp.where(odd, gwide, swap_halves(gwide))).astype(BF16)
    ones_val = jnp.where(low, jnp.where(lane < 3, 1.0, 0.0), keyval.astype(F32)).astype(BF16)
    gscores_t = (probs_t * mm_nt(ones_val, ghead)).astype(BF16)
    gval = mm(probs_t.astype(BF16), ghead)
    gkey = mm(gscores_t, query)
    gquery = (jnp.transpose(mm_tn(keys, gscores_t)) * (HEAD**-0.5)).astype(BF16)
    zero = jnp.zeros_like(gquery)
    gkey = jnp.where(kmask.astype(F32) > 0, gkey, 0.0)
    gkey = gkey + swap_halves(gkey)
    return (
        jnp.where(word, gquery, zero),
        jnp.where(word, zero, gquery),
        jnp.where(low, gkey, gval).astype(BF16),
    )


def attend_back_kernel(
    length, x_ref, q_ref, kv_ref, aug_ref, gc_ref, ctx_ref, ka_ref, km_ref, word_ref, gp_ref, gw_ref, sum_ref, xt
):
    step = pl.program_id(0)
    rows = x_ref.shape[0]

    @pl.when(step == 0)
    def _():
        xt[...] = jnp.transpose(x_ref[...])

    low = low_lanes(length)
    lane = lax.broadcasted_iota(jnp.int32, (length, LANES), 1)
    odd = lax.rem(step, 2) == 1
    for seq in range(rows // length):
        here = slice(seq * length, (seq + 1) * length)
        tiles = attend_back_head(
            q_ref[here], kv_ref[here], aug_ref[here], gc_ref[here], ctx_ref[here],
            ka_ref[here], km_ref[here], word_ref[here] > 0, odd, low, lane,
        )
        for index, tile in enumerate(tiles):
            gp_ref[here, index * LANES : (index + 1) * LANES] = tile
    grads = gp_ref[...]
    gw_ref[...] = mm(xt[...], grads).astype(BF16)
    sums = jnp.sum(grads.astype(F32).reshape(rows // 8, 8, GROUP), axis=0)
    sum_ref[...] = jnp.sum(sums, axis=0, keepdims=True)


def attend_back_call(x, q, kv, aug, gc, ctx, ka, km, word, length):
    rows, width = x.shape
    heads = q.shape[1] // LANES
    head = pl.BlockSpec((rows, LANES), lambda h: (0, h))
    pair = pl.BlockSpec((rows, LANES), lambda h: (0, h // 2))
    one = pl.BlockSpec((rows, LANES), lambda h: (0, 0))
    return pl.pallas_call(
        functools.partial(attend_back_kernel, length),
        grid=(heads,),
        in_specs=[pl.BlockSpec((rows, width), lambda h: (0, 0)), head, head, head, pair, pair, one, one, one],
        out_specs=[
            pl.BlockSpec((rows, GROUP), lambda h: (0, h)),
            pl.BlockSpec((width, GROUP), lambda h: (0, h)),
            pl.BlockSpec((1, GROUP), lambda h: (0, h)),
        ],
        out_shape=[
            jax.ShapeDtypeStruct((rows, heads * GROUP), BF16),
            jax.ShapeDtypeStruct((width, heads * GROUP), BF16),
            jax.ShapeDtypeStruct((1, heads * GROUP), F32),
        ],
        scratch_shapes=[pltpu.VMEM((width, rows), BF16)],
        compiler_params=pltpu.CompilerParams(vmem_limit_bytes=VMEM_LIMIT),
        name="attend_back",
    )(x, q, kv, aug, gc, ctx, ka, km, word)


class Chunk:
    def __init__(self, name, by_rows, shape, total, plane=None, end=None):
        self.name, self.by_rows = name, by_rows
        self.rows, self.cols = shape
        self.total = total
        if plane is not None:
            self.r1a, self.r1b, self.r2a, self.r2b = plane
        if end is not None:
            self.rz, self.final = end

    def mine(self, z, wide):
        if self.total.shape[1:] != (self.rows, self.cols):
            return self.total.at[z]
        rows, cols = self.cut(wide)
        return self.total.at[z, rows, cols]

    def cut(self, part, side=None):
        if self.by_rows:
            size = self.rows // 4
            if side is None:
                return spot(part * size, size, 16), slice(None)
            return spot(part * size + side * (size // 2), size // 2, 16), slice(None)
        size, half = self.cols // 4, self.rows // 2
        rows = slice(0, self.rows) if side is None else slice(side * half, (side + 1) * half)
        return rows, spot(part * size, size, LANES)


def piece_shapes(rows, cols, by_rows):
    if by_rows:
        return (rows // 4, cols), (rows // 8, cols)
    return (rows, cols // 4), (rows // 2, cols // 4)


def plane_scratch(depth, rows, cols, by_rows):
    _, half = piece_shapes(rows, cols, by_rows)
    return [
        pltpu.VMEM((2, depth, *half), BF16),
        pltpu.VMEM((2, depth, *half), BF16),
        pltpu.VMEM((depth, *half), BF16),
        pltpu.VMEM((depth, *half), BF16),
    ]


def end_scratch(depth, rows, cols, by_rows):
    piece, _ = piece_shapes(rows, cols, by_rows)
    return [pltpu.VMEM((depth - 1, *piece), BF16), pltpu.VMEM((rows, cols), BF16)]


class Reducer:
    def __init__(self, here, send, recv):
        self.here = here
        self.links = Links(send, recv)
        self.send, self.arrived, self.finish = self.links.send, self.links.arrived, self.links.finish

    def pair_send(self, chunk, sources, only=None):
        here = self.here
        for z in range(here.depth) if only is None else (only,):
            for part, (_, cols) in enumerate(sources(0)):

                def build(z=z, part=part, cols=cols):
                    owner = 2 * z + 1 - here.core
                    return sources(owner)[part][0], chunk.total.at[z, :, cols], here.sib_dev

                self.send((chunk.name, "s", z, part), build)

    def pair_wait(self, chunk, sources):
        for z in range(self.here.depth):
            for part, (_, cols) in enumerate(sources(0)):
                self.arrived((chunk.name, "s", z, part), chunk.total.at[z, :, cols], self.here.sib_dev)

    def plane_send(self, chunk):
        here = self.here
        for index, (a, b) in enumerate(((here.x_quarter, here.y_quarter), (here.d_quarter, here.d_quarter))):

            def first(index=index, part=a):
                rows, cols = chunk.cut(part, 0)
                return chunk.total.at[:, rows, cols], chunk.r1a.at[index], here.x_dev

            def second(index=index, part=b):
                rows, cols = chunk.cut(part, 1)
                return chunk.total.at[:, rows, cols], chunk.r1b.at[index], here.y_dev

            self.send((chunk.name, "1a", index), first)
            self.send((chunk.name, "1b", index), second)

    def add(self, chunk, part, side, value):
        rows, cols = chunk.cut(part, side)
        chunk.total[:, rows, cols] = chunk.total[:, rows, cols] + value

    def plane_turn(self, chunk):
        here = self.here
        for index in range(2):
            self.arrived((chunk.name, "1a", index), chunk.r1a.at[index], here.x_dev)
            self.arrived((chunk.name, "1b", index), chunk.r1b.at[index], here.y_dev)
        self.add(chunk, here.y_quarter, 0, chunk.r1a[1])
        self.add(chunk, here.x_quarter, 1, chunk.r1b[1])

        def first():
            rows, cols = chunk.cut(here.y_quarter, 0)
            return chunk.total.at[:, rows, cols], chunk.r2a, here.y_dev

        def second():
            rows, cols = chunk.cut(here.x_quarter, 1)
            return chunk.total.at[:, rows, cols], chunk.r2b, here.x_dev

        self.send((chunk.name, "2a"), first)
        self.send((chunk.name, "2b"), second)
        self.add(chunk, here.wide, 0, chunk.r1a[0])
        self.add(chunk, here.wide, 1, chunk.r1b[0])

    def plane_done(self, chunk):
        here = self.here
        self.arrived((chunk.name, "2a"), chunk.r2a, here.y_dev)
        self.arrived((chunk.name, "2b"), chunk.r2b, here.x_dev)
        self.add(chunk, here.wide, 0, chunk.r2a[...])
        self.add(chunk, here.wide, 1, chunk.r2b[...])

    def depth_send(self, chunk):
        here = self.here
        for k in range(1, here.depth):

            def build(k=k):
                piece = chunk.mine(lax.rem(here.z + k, here.depth), here.wide)
                return piece, chunk.rz.at[k - 1], here.z_dev(k)

            self.send((chunk.name, "z", k), build)

    def share_send(self, chunk):
        here = self.here
        for k in range(1, here.depth):
            self.arrived((chunk.name, "z", k), chunk.rz.at[k - 1], here.z_dev(k))
        rows, cols = chunk.cut(here.wide)
        done = chunk.mine(here.z, here.wide)[...].astype(F32)
        for k in range(1, here.depth):
            done = done + chunk.rz[k - 1].astype(F32)
        chunk.final[rows, cols] = done.astype(BF16)

        def build(device):
            rows, cols = chunk.cut(here.wide)
            return chunk.final.at[rows, cols], chunk.final.at[rows, cols], device

        self.send((chunk.name, "fx"), lambda: build(here.x_dev))
        self.send((chunk.name, "fy"), lambda: build(here.y_dev))

    def share_pass(self, chunk):
        here = self.here

        def part(quarter, side, device):
            rows, cols = chunk.cut(quarter, side)
            return chunk.final.at[rows, cols], chunk.final.at[rows, cols], device

        self.arrived((chunk.name, "fx"), *part(here.x_quarter, None, here.x_dev)[1:])
        self.send((chunk.name, "fdy"), lambda: part(here.x_quarter, 0, here.y_dev))
        self.arrived((chunk.name, "fy"), *part(here.y_quarter, None, here.y_dev)[1:])
        self.send((chunk.name, "fdx"), lambda: part(here.y_quarter, 1, here.x_dev))

    def share_wait(self, chunk):
        here = self.here
        for key, side, device in (("fdy", 0, here.y_dev), ("fdx", 1, here.x_dev)):
            rows, cols = chunk.cut(here.d_quarter, side)
            self.arrived((chunk.name, key), chunk.final.at[rows, cols], device)


CHUNK_HEADS = 4


def squares(ref, cols):
    total = jnp.zeros((8, LANES), F32)
    rows = ref.shape[0]
    for start in range(0, cols, LANES):
        tile = ref[:, start : start + LANES].astype(F32)
        total = total + jnp.sum((tile * tile).reshape(rows // 8, 8, LANES), axis=0)
    return total


def reduce_kernel(
    narrow, length, groups, deep,
    x_ref, q_ref, kv_ref, aug_ref, gc_ref, ctx_ref, wp_ref, ka_ref, km_ref, word_ref, gvec_ref,
    gr1_ref, t1_ref, tw_ref, gwo_ref,
    ig_ref, f1_ref, fo_ref, fw_ref, fa_ref, v_ref, n_ref,
    xt, gp, ig, *scratch,
):
    step = pl.program_id(0)
    rows, width = x_ref.shape
    heads = groups * CHUNK_HEADS
    share, inner = t1_ref.shape[1:]
    here = Place(narrow)
    scratch = list(scratch)
    red = Reducer(here, scratch[-3], scratch[-2])
    local = scratch[-1]

    def take(count):
        taken, scratch[:count] = scratch[:count], []
        return taken

    chunk_w = Chunk("w", True, (deep, width), take(1)[0], None, take(2))
    chunk_1 = Chunk("1", False, (share, inner), take(1)[0], take(4), take(2))
    gw, chunk_a = [], []
    for j in range(groups):
        gw += take(1)
        chunk_a.append(Chunk(("a", j), False, (share, gw[j].shape[1]), take(1)[0], take(4), take(2)))
    v0, v1, v2, vs, vx, vy, vz, n0, ns, nz = take(10)
    wide = CHUNK_HEADS * GROUP

    def sources_a(j):
        return lambda owner: [(gw[j].at[spot(owner * share, share, 16), :], slice(0, gw[j].shape[1]))]

    def load(index):
        source, target = (
            (t1_ref, chunk_1.total),
            (tw_ref, chunk_w.total),
            (gwo_ref, gw[0].at[:, wide : wide + width]),
            (gr1_ref, ig),
        )[index]
        return pltpu.make_async_copy(source, target, local.at[index])

    def stores():
        copies = [(chunk_w.final, fw_ref), (chunk_1.final, f1_ref)]
        copies += [(chunk_a[0].final.at[:, wide : wide + width], fo_ref)]
        copies += [
            (chunk.final.at[:, 0:wide], fa_ref.at[:, j * wide : (j + 1) * wide]) for j, chunk in enumerate(chunk_a)
        ]
        return [pltpu.make_async_copy(a, b, local.at[4 + i]) for i, (a, b) in enumerate(copies)]

    def merge(j):
        def one(z, carry):
            mine = spot((2 * z + here.core) * share, share, 16)
            chunk_a[j].total[z] = chunk_a[j].total[z] + gw[j][mine, :]
            return carry

        red.pair_wait(chunk_a[j], sources_a(j))
        lax.fori_loop(0, here.depth, one, 0)
        red.plane_send(chunk_a[j])

    def turn_z(chunk):
        red.plane_done(chunk)
        red.depth_send(chunk)

    @pl.when(step == 0)
    def _():
        for index in range(4):
            load(index).start()
        here.greet()
        load(0).wait()
        red.plane_send(chunk_1)
        load(1).wait()
        red.depth_send(chunk_w)
        v0[...] = gvec_ref[...]
        pad = gw[0].shape[1] - wide - width
        gw[0][:, wide + width :] = jnp.zeros((width, pad), BF16)
        xt[...] = jnp.transpose(x_ref[...])

    def at(when):
        def run(action):
            def body():
                action()

            pl.when(step == when)(body)

        return run

    at(2)(lambda: load(2).wait())
    at(3)(lambda: red.plane_turn(chunk_1))
    at(4)(lambda: red.share_send(chunk_w))
    at(5)(lambda: merge(0))
    at(6)(lambda: [turn_z(chunk_1), red.share_pass(chunk_w)])
    at(8)(lambda: [red.plane_turn(chunk_a[0]), red.share_wait(chunk_w)])
    at(9)(lambda: [merge(1), red.share_send(chunk_1)])
    at(10)(lambda: turn_z(chunk_a[0]))
    at(11)(lambda: [red.plane_turn(chunk_a[1]), red.share_pass(chunk_1)])

    @pl.when(step < heads)
    def _():
        low = low_lanes(length)
        lane = lax.broadcasted_iota(jnp.int32, (length, LANES), 1)
        odd = lax.rem(step, 2) == 1
        for seq in range(rows // length):
            here_rows = slice(seq * length, (seq + 1) * length)
            tiles = attend_back_head(
                q_ref[here_rows], kv_ref[here_rows], aug_ref[here_rows], gc_ref[here_rows], ctx_ref[here_rows],
                ka_ref[here_rows], km_ref[here_rows], word_ref[here_rows] > 0, odd, low, lane,
            )
            for index, tile in enumerate(tiles):
                gp[step, here_rows, index * LANES : (index + 1) * LANES] = tile
        grads = gp[step]
        product = mm(xt[...], grads).astype(BF16)
        inside = spot(lax.rem(step, CHUNK_HEADS) * GROUP, GROUP, LANES)
        for j in range(groups):

            @pl.when(step // CHUNK_HEADS == j)
            def _():
                gw[j][:, inside] = product

        sums = jnp.sum(jnp.sum(grads.astype(F32).reshape(rows // 8, 8, GROUP), axis=0), axis=0, keepdims=True)

        low1 = low_lanes(1)
        pair = spot(step // 2 * LANES, LANES, LANES)
        mine = low1 != odd
        for b in range(3):
            tile = sums[:, b * LANES : (b + 1) * LANES]
            turned = swap_halves(tile)
            first = jnp.where(odd, turned, tile)
            second = jnp.where(odd, tile, turned)
            if b < 2:
                v0[2 * b : 2 * b + 1, pair] = jnp.where(mine, first, v0[2 * b : 2 * b + 1, pair])
                v0[2 * b + 1 : 2 * b + 2, pair] = jnp.where(mine, second, v0[2 * b + 1 : 2 * b + 2, pair])
            else:
                v0[4:5, pair] = jnp.where(mine, second, v0[4:5, pair])

    for j in range(groups):
        at((j + 1) * CHUNK_HEADS - 1)(lambda j=j: red.pair_send(chunk_a[j], sources_a(j)))

    last = chunk_a[-1]

    def vec_pair():
        red.arrived(("v", "s"), vs, here.sib_dev)
        v1[...] = v0[...] + vs[...]
        red.send(("v", "x"), lambda: (v1, vx, here.x_dev))

    def vec_plane():
        red.arrived(("v", "x"), vx, here.x_dev)
        v2[...] = v1[...] + vx[...]
        red.send(("v", "y"), lambda: (v2, vy, here.y_dev))

    def vec_depth():
        red.arrived(("v", "y"), vy, here.y_dev)
        vz[here.z] = v2[...] + vy[...]
        for k in range(1, here.depth):
            red.send(("v", "z", k), lambda k=k: (vz.at[here.z], vz.at[here.z], here.z_dev(k)))

    def vec_done():
        for k in range(1, here.depth):
            red.arrived(("v", "z", k), vz.at[here.behind(k) // 2], here.z_dev(k))
        vec = vz[0]
        for z in range(1, here.depth):
            vec = vec + vz[z]
        v_ref[...] = vec

    at(heads - 1)(lambda: red.send(("v", "s"), lambda: (v0, vs, here.sib_dev)))
    at(heads)(lambda: load(3).wait())

    @pl.when(step >= heads)
    def _():
        ig[...] += mm_nt(gp[step - heads], wp_ref[...])

    at(heads + 1)(lambda: [merge(groups - 1), vec_pair()])
    at(heads + 2)(lambda: [red.share_send(chunk_a[0]), red.share_wait(chunk_1)])
    at(heads + 3)(lambda: turn_z(chunk_a[1]))
    at(heads + 4)(lambda: [red.share_pass(chunk_a[0]), vec_plane()])
    at(heads + 6)(lambda: [red.plane_turn(last), red.share_wait(chunk_a[0])])
    at(heads + 8)(lambda: [red.share_send(chunk_a[1]), vec_depth()])
    at(heads + 9)(lambda: turn_z(last))
    at(heads + 10)(lambda: [red.share_pass(chunk_a[1]), vec_done()])

    @pl.when(step == 2 * heads - 1)
    def _():
        ig_ref[...] = ig[...].astype(BF16)
        red.share_wait(chunk_a[1])
        norm = squares(chunk_w.final, width) + squares(chunk_1.final, inner)
        norm = norm + squares(chunk_a[0].final, wide + width)
        for chunk in chunk_a[1:-1]:
            norm = norm + squares(chunk.final, wide)
        red.share_send(last)
        vec = v_ref[...]
        square = jnp.sum(jnp.sum(vec * vec, axis=0, keepdims=True), axis=1, keepdims=True)
        red.share_pass(last)
        red.share_wait(last)
        for copy in stores():
            copy.start()
        n0[...] = norm + squares(last.final, wide)
        red.send(("n", "s"), lambda: (n0, ns, here.sib_dev))
        red.arrived(("n", "s"), ns, here.sib_dev)
        nz[here.z] = n0[...] + ns[...]
        for k in range(1, here.depth):
            red.send(("n", "z", k), lambda k=k: (nz.at[here.z], nz.at[here.z], here.z_dev(k)))
        for k in range(1, here.depth):
            red.arrived(("n", "z", k), nz.at[here.behind(k) // 2], here.z_dev(k))
        total = nz[0]
        for z in range(1, here.depth):
            total = total + nz[z]
        every = jnp.sum(jnp.sum(total, axis=0, keepdims=True), axis=1, keepdims=True)
        n_ref[...] = jnp.broadcast_to(every + square, n_ref.shape)
        red.finish()
        for copy in stores():
            copy.wait()


def reduce_call(narrow, x, q, kv, aug, gc, ctx, wp, ka, km, word, gvec, gr1, t1, tw, gwo, deep, length):
    rows, width = x.shape
    heads = q.shape[1] // LANES
    groups = heads // CHUNK_HEADS
    depth, share, inner = t1.shape
    acols = CHUNK_HEADS * GROUP

    def now(h):
        return jnp.minimum(h, heads - 1)

    def fixed(shape):
        return pl.BlockSpec(shape, lambda h: (0, 0), pipeline_mode=pl.Buffered(1))

    head = pl.BlockSpec((rows, LANES), lambda h: (0, now(h)))
    pair = pl.BlockSpec((rows, LANES), lambda h: (0, now(h) // 2))
    later = pl.BlockSpec((width, GROUP), lambda h: (0, jnp.maximum(h - heads, 0)))
    one = fixed((rows, LANES))
    hbm = pl.BlockSpec(memory_space=pl.ANY)
    shape = jax.ShapeDtypeStruct
    vec = pltpu.VMEM((16, width), F32)
    tile = pltpu.VMEM((8, LANES), F32)
    scratch = [pltpu.VMEM((width, rows), BF16), pltpu.VMEM((heads, rows, GROUP), BF16), pltpu.VMEM((rows, width), F32)]
    scratch += [pltpu.VMEM(tw.shape, BF16), *end_scratch(depth, deep, width, True)]
    scratch += [
        pltpu.VMEM(t1.shape, BF16),
        *plane_scratch(depth, share, inner, False),
        *end_scratch(depth, share, inner, False),
    ]
    for j in range(groups):
        cols = acols + (width + 2 * LANES if j == 0 else 0)
        scratch += [
            pltpu.VMEM((width, cols), BF16),
            pltpu.VMEM((depth, share, cols), BF16),
            *plane_scratch(depth, share, cols, False),
            *end_scratch(depth, share, cols, False),
        ]
    scratch += [vec] * 6 + [pltpu.VMEM((depth, 16, width), F32), tile, tile, pltpu.VMEM((depth, 8, LANES), F32)]
    count = (2 + groups) * (depth + 10 + depth - 1) + 2 * (3 + depth)
    scratch += [pltpu.SemaphoreType.DMA((count,))] * 2 + [pltpu.SemaphoreType.DMA((7 + groups,))]
    return pl.pallas_call(
        functools.partial(reduce_kernel, narrow, length, groups, deep),
        grid=(2 * heads,),
        in_specs=[
            fixed((rows, width)), head, head, head, pair, pair, later, one, one, one, fixed((16, width)),
            hbm, hbm, hbm, hbm,
        ],
        out_specs=[fixed((rows, width)), hbm, hbm, hbm, hbm, fixed((16, width)), fixed((8, LANES))],
        out_shape=[
            shape((rows, width), BF16),
            shape((share, inner), BF16),
            shape((share, width), BF16),
            shape((deep, width), BF16),
            shape((share, heads * GROUP), BF16),
            shape((16, width), F32),
            shape((8, LANES), F32),
        ],
        scratch_shapes=scratch,
        compiler_params=pltpu.CompilerParams(
            vmem_limit_bytes=VMEM_LIMIT, collective_id=1, has_side_effects=True
        ),
        name="reduce",
    )(x, q, kv, aug, gc, ctx, wp, ka, km, word, gvec, gr1, t1, tw, gwo)


def gelu_pair(pre):
    bell = jnp.exp2(pre * pre * (-0.5 * LOG2E))
    share = 0.5 + 0.5 * lax.erf(pre * (0.5**0.5))
    return pre * share, share + pre * bell * 0.3989422804014327


def fold(array_in):
    rows, cols = array_in.shape
    return jnp.sum(array_in.reshape(rows // 8, 8, cols), axis=0)


def middle_kernel(
    narrow, x_hbm, ctx_hbm, cot_hbm, vec_ref, e_hbm, w2_hbm,
    out_hbm, gr1_hbm, gctx_hbm, gw1_hbm, gwo_hbm, gw2_hbm, gvec_ref,
    wo, w1, w2, io, ctx, h1_s, n1_s, inv_s, act_s, slope_s, gb_s, sum_s, gw2_s, gwo_s, acc, sems, *scratch,
):
    rows, width = io.shape
    inner = w1.shape[1]
    blocks, size, block = inner // width, 256, 256
    red = None

    def load(index):
        source, target = (
            (x_hbm, io),
            (ctx_hbm, ctx),
            (e_hbm.at[:, inner : inner + width], wo),
            (e_hbm.at[:, 0:inner], w1),
            (w2_hbm, w2),
            (cot_hbm, io),
        )[index]
        return pltpu.make_async_copy(source, target, sems.at[index])

    def store(index):
        source, target = (
            (io, out_hbm),
            (sum_s, gr1_hbm),
            (io, gctx_hbm),
            (gwo_s, gwo_hbm),
            (gw2_s, gw2_hbm) if red is None else (chunk.total.at[:, chunk.cut(here.wide)[0], :], gw2_hbm),
            (act_s.at[0:width, :] if red is None else chunk_1.total, gw1_hbm),
        )[index]
        return pltpu.make_async_copy(source, target, sems.at[6 + index])

    def vec(row):
        return vec_ref[row : row + 1, :].astype(F32)

    def over_rows(step):
        def one(i, carry):
            step(spot(i * size, size, size))
            return carry

        lax.fori_loop(0, rows // size, one, 0)

    def over_cols(first, last, step):
        def one(i, carry):
            step(spot(i * block, block, block), i)
            return carry

        lax.fori_loop(first, last, one, 0)

    for index in (1, 2, 0, 3, 4):
        load(index).start()
    acc[...] = jnp.zeros_like(acc)
    if narrow is not None:
        here = Place(narrow)
        red = Reducer(here, scratch[0], scratch[1])
        deep, share = scratch[2].shape[1], scratch[7].shape[1]
        chunk = Chunk("w", True, (deep, width), scratch[2], scratch[3:7])
        chunk_1 = Chunk("1", False, (share, inner), scratch[7])
        here.greet()

        def sources(owner):
            return [(gw2_s.at[spot(owner * deep, deep, 16), :], slice(0, width))]

        def sources_1(owner):
            return [(act_s.at[spot(owner * share, share, 16), :], slice(0, inner))]

    for index in (1, 2, 0):
        load(index).wait()

    def norm_one(at):
        resid = io[at, :].astype(F32) + mm(ctx[at, :], wo[...]) + vec(5)
        center = resid - jnp.mean(resid, axis=1, keepdims=True)
        inverse = lax.rsqrt(jnp.mean(center * center, axis=1, keepdims=True) + norm_eps)
        unit = center * inverse
        hidden = unit * vec(6) + vec(7)
        n1_s[at, :] = unit.astype(BF16)
        inv_s[at, :] = jnp.broadcast_to(inverse, (size, LANES))
        h1_s[at, :] = hidden.astype(BF16)
        sum_s[at, :] = hidden + vec(8)

    over_rows(norm_one)
    load(5).start()
    load(3).wait()
    per = width // block

    def expand(at, i):
        bias = vec_ref[11 + i // per, spot(lax.rem(i, per) * block, block, LANES)].astype(F32).reshape(1, block)
        act, slope = gelu_pair(mm(h1_s[...], w1[:, at]) + bias)
        act_s[:, at] = act.astype(BF16)
        slope_s[:, at] = slope.astype(BF16)

    over_cols(0, inner // block, expand)
    load(4).wait()

    def reduce(at, i):
        sum_s[:, at] += mm(act_s[...], w2[:, at])

    over_cols(0, per, reduce)
    load(5).wait()

    def norm_two(at):
        resid = sum_s[at, :]
        center = resid - jnp.mean(resid, axis=1, keepdims=True)
        inverse = lax.rsqrt(jnp.mean(center * center, axis=1, keepdims=True) + norm_eps)
        unit = center * inverse
        grad = io[at, :].astype(F32)
        io[at, :] = (unit * vec(9) + vec(10)).astype(BF16)
        acc[9] += fold(grad * unit)
        acc[10] += fold(grad)
        scaled = grad * vec(9)
        back = inverse * (
            scaled
            - jnp.mean(scaled, axis=1, keepdims=True)
            - unit * jnp.mean(scaled * unit, axis=1, keepdims=True)
        )
        sum_s[at, :] = back
        half = back.astype(BF16)
        gb_s[at, :] = half
        acc[8] += fold(half.astype(F32))

    over_rows(norm_two)
    store(0).start()
    for z in range(blocks):
        cols = slice(z * width, (z + 1) * width)
        gw2_s[cols, :] = mm_tn(act_s[:, cols], gb_s[...]).astype(BF16)
        if red is not None:
            red.pair_send(chunk, sources, z)

    def expand_back(at, i):
        grad = (mm_nt(gb_s[...], w2[at, :]) * slope_s[:, at].astype(F32)).astype(BF16)
        slope_s[:, at] = grad
        row = 11 + i // per
        cols = spot(lax.rem(i, per) * block, block, LANES)
        acc[row, :, cols] = acc[row, :, cols] + fold(grad.astype(F32))

    def hidden_back(at, i):
        sum_s[:, at] += mm_nt(slope_s[...], w1[at, :])

    def norm_one_back(at):
        grad, unit = sum_s[at, :], n1_s[at, :].astype(F32)
        acc[6] += fold(grad * unit)
        acc[7] += fold(grad)
        scaled = grad * vec(6)
        back = inv_s[at, 0:1] * (
            scaled
            - jnp.mean(scaled, axis=1, keepdims=True)
            - unit * jnp.mean(scaled * unit, axis=1, keepdims=True)
        )
        sum_s[at, :] = back
        half = back.astype(BF16)
        gb_s[at, :] = half
        acc[5] += fold(half.astype(F32))

    def merge(target, source, size):
        def one(z, carry):
            mine = spot((2 * z + here.core) * size, size, 16)
            target[z] = target[z] + source[mine, :]
            return carry

        lax.fori_loop(0, here.depth, one, 0)

    count = inner // block
    over_cols(0, count // 3, expand_back)
    if red is not None:
        red.pair_wait(chunk, sources)
        merge(chunk.total, gw2_s, deep)
        red.plane_send(chunk)
    over_cols(count // 3, count, expand_back)
    for c in range(blocks):
        cols = slice(c * width, (c + 1) * width)
        act_s[0:width, cols] = mm_tn(h1_s[...], slope_s[:, cols]).astype(BF16)
    if red is not None:
        red.pair_send(chunk_1, sources_1)
    over_cols(0, per, hidden_back)
    if red is not None:
        red.plane_turn(chunk)
        red.pair_wait(chunk_1, sources_1)
        merge(chunk_1.total, act_s, share)
    store(5).start()
    over_rows(norm_one_back)
    store(1).start()
    store(0).wait()
    io[...] = mm_nt(gb_s[...], wo[...]).astype(BF16)
    store(2).start()
    gwo_s[...] = mm_tn(ctx[...], gb_s[...]).astype(BF16)
    store(3).start()
    for row in range(acc.shape[0]):
        gvec_ref[row : row + 1, :] = jnp.sum(acc[row], axis=0, keepdims=True)
    if red is not None:
        red.plane_done(chunk)
    store(4).start()
    if red is not None:
        red.finish()
    for index in range(1, 6):
        store(index).wait()


def middle_call(narrow, x, ctx, cot, vec, e, w2):
    rows, width = x.shape
    inner = w2.shape[0]
    hbm, vmem = pl.BlockSpec(memory_space=pl.ANY), pl.BlockSpec(memory_space=pltpu.VMEM)
    shape = jax.ShapeDtypeStruct
    scratch, params = [], {}
    shape_w, shape_1 = (inner, width), (width, inner)
    if narrow is not None:
        depth, deep, share = narrow // 2, inner // narrow, width // narrow
        shape_w, shape_1 = (depth, deep // 4, width), (depth, share, inner)
        scratch = [pltpu.SemaphoreType.DMA((2 * depth + 6,))] * 2
        scratch += [pltpu.VMEM((depth, deep, width), BF16), *plane_scratch(depth, deep, width, True)]
        scratch += [pltpu.VMEM((depth, share, inner), BF16)]
        params = dict(collective_id=2, has_side_effects=True)
    return pl.pallas_call(
        functools.partial(middle_kernel, narrow),
        in_specs=[hbm, hbm, hbm, vmem, hbm, hbm],
        out_specs=[hbm] * 6 + [vmem],
        out_shape=[
            shape((rows, width), BF16),
            shape((rows, width), F32),
            shape((rows, width), BF16),
            shape(shape_1, BF16),
            shape((width, width), BF16),
            shape(shape_w, BF16),
            shape(vec.shape, F32),
        ],
        scratch_shapes=[
            pltpu.VMEM((width, width), BF16),
            pltpu.VMEM((width, inner), BF16),
            pltpu.VMEM((inner, width), BF16),
            pltpu.VMEM((rows, width), BF16),
            pltpu.VMEM((rows, width), BF16),
            pltpu.VMEM((rows, width), BF16),
            pltpu.VMEM((rows, width), BF16),
            pltpu.VMEM((rows, LANES), F32),
            pltpu.VMEM((rows, inner), BF16),
            pltpu.VMEM((rows, inner), BF16),
            pltpu.VMEM((rows, width), BF16),
            pltpu.VMEM((rows, width), F32),
            pltpu.VMEM((inner, width), BF16),
            pltpu.VMEM((width, width), BF16),
            pltpu.VMEM((vec.shape[0], 8, width), F32),
            pltpu.SemaphoreType.DMA((12,)),
            *scratch,
        ],
        compiler_params=pltpu.CompilerParams(vmem_limit_bytes=VMEM_LIMIT, **params),
        name="middle",
    )(x, ctx, cot, vec, e, w2)


def input_grad_kernel(gp_ref, w_ref, gr1_ref, out_ref):
    out_ref[...] = (gr1_ref[...] + mm_nt(gp_ref[...], w_ref[...])).astype(BF16)


def input_grad_call(gp, w, gr1, size):
    rows, cols = gp.shape
    width = w.shape[0]
    return pl.pallas_call(
        input_grad_kernel,
        grid=(rows // size,),
        in_specs=[
            pl.BlockSpec((size, cols), lambda i: (i, 0)),
            pl.BlockSpec((width, cols), lambda i: (0, 0)),
            pl.BlockSpec((size, width), lambda i: (i, 0)),
        ],
        out_specs=pl.BlockSpec((size, width), lambda i: (i, 0)),
        out_shape=jax.ShapeDtypeStruct((rows, width), BF16),
        compiler_params=pltpu.CompilerParams(vmem_limit_bytes=VMEM_LIMIT),
        name="input_grad",
    )(gp, w, gr1)


def adam_update(master, first_old, second_old, grad_shard, factor, index):
    clipped = grad_shard * factor
    new_first = beta_one * first_old + (1.0 - beta_one) * clipped
    new_second = beta_two * second_old + (1.0 - beta_two) * clipped * clipped
    direction = (
        new_first
        / (1.0 - beta_one**STEP)
        / (jnp.sqrt(new_second / (1.0 - beta_two**STEP)) + adam_eps)
    )
    new_weight = master - rate_table[index] * (direction + decay_table[index] * master)
    return (new_weight, new_first, new_second)


def update_tile(master, first, second, grad, factor, index):
    weight, first, second = adam_update(master, first, second, grad.astype(F32), factor, index)
    return weight, first, second, weight.astype(BF16)


def update_kernel(narrow, n_ref, fa_ref, fo_ref, f1_ref, fw_ref, v_ref, *refs):
    ins, outs = refs[0:15], refs[15:35]
    heads = fa_ref.shape[1] // GROUP
    width = heads * HEAD
    norm = jnp.sqrt(n_ref[0:1, 0:1])
    factor = jnp.minimum(1.0, clip_limit / (norm + 1e-06))

    def store(index, rows, cols, grad):
        news = update_tile(*(ins[5 * t + index][rows, cols] for t in range(3)), grad, factor, index)
        for t, new in enumerate(news):
            outs[5 * t + index][rows, cols] = new

    every = slice(None)
    low = low_lanes(fa_ref.shape[0])
    for pair in range(heads // 2):
        at = 2 * pair * GROUP
        for b in range(3):
            even = fa_ref[:, at + b * LANES : at + (b + 1) * LANES].astype(F32)
            odd = fa_ref[:, at + GROUP + b * LANES : at + GROUP + (b + 1) * LANES].astype(F32)
            for second in range(2):
                if second:
                    grad = jnp.where(low, swap_halves(even), odd)
                else:
                    grad = jnp.where(low, even, swap_halves(odd))
                start = (2 * b + second) * width + pair * LANES
                store(0, every, slice(start, start + LANES), grad)
    store(1, every, every, fo_ref[...])
    store(2, every, every, f1_ref[...])
    store(3, every, every, fw_ref[...])

    @pl.when(pl.program_id(0) == 0)
    def _():
        count, span = ins[4].shape
        me = lax.axis_index("narrow")
        turned = pltpu.roll(v_ref[...], lax.rem(width - me * span, width), 1)
        store(4, every, every, turned[0:count, 0:span])


def update_call(narrow, norm, shards, vec, masters, firsts, seconds):
    share = shards[0].shape[0]
    steps = share // 16

    def rows_of(array_in):
        return pl.BlockSpec((array_in.shape[0] // steps, array_in.shape[1]), lambda i: (i, 0))

    def fixed(array_in):
        return pl.BlockSpec(array_in.shape, lambda i: (0, 0))

    def group(arrays):
        return [rows_of(a) for a in arrays[:4]] + [fixed(arrays[4])]

    def shapes(arrays, dtype):
        return [jax.ShapeDtypeStruct(a.shape, dtype) for a in arrays]

    return pl.pallas_call(
        functools.partial(update_kernel, narrow),
        grid=(steps,),
        in_specs=[fixed(norm), *(rows_of(a) for a in shards), fixed(vec)] + group(masters) * 3,
        out_specs=group(masters) * 4,
        out_shape=shapes(masters, F32) * 3 + shapes(masters, BF16),
        compiler_params=pltpu.CompilerParams(vmem_limit_bytes=VMEM_LIMIT),
        name="update",
    )(norm, *shards, vec, *masters, *firsts, *seconds)


def by_head(array_in):
    rows, cols = array_in.shape
    heads = cols // GROUP
    return array_in.reshape(rows, 6, heads, HEAD).transpose(0, 2, 1, 3).reshape(rows, cols)


def by_block(array_in):
    rows, cols = array_in.shape
    heads = cols // GROUP
    return array_in.reshape(rows, heads, 6, HEAD).transpose(0, 2, 1, 3).reshape(rows, cols)


def can_pass_pieces(wide, narrow, width, deep):
    share = width // narrow
    return wide == 4 and narrow % 2 == 0 and narrow > 2 and share % 32 == 0 and deep % 128 == 0 and 2 * deep == width


def body(
    x_in, cotangent, segment_ids, type_ids,
    projection, context_out, expand_weight, reduce_weight, vector_params,
    first_projection, first_context, first_expand, first_reduce, first_vectors,
    second_projection, second_context, second_expand, second_reduce, second_vectors,
):
    seq_count, seq_len, width = x_in.shape
    rows = seq_count * seq_len

    def gather(array_in, axis):
        return lax.all_gather(array_in.astype(BF16), "narrow", axis=axis, tiled=True)

    hidden = x_in.reshape(rows, width)
    cot = cotangent.reshape(rows, width)
    narrow = lax.axis_size("narrow")
    pieces = can_pass_pieces(lax.axis_size("wide"), narrow, width, reduce_weight.shape[0])
    if pieces:
        query, keyval, context, aug, proj_w, mid_w, reduce_w, vec_rows, word, kmask, kaug = gather_call(
            narrow, hidden, projection, context_out, expand_weight, reduce_weight, vector_params,
            segment_ids, type_ids,
        )
    else:
        word_col = (type_ids == 0).reshape(rows, 1)
        lane = lax.broadcasted_iota(jnp.int32, (rows, LANES), 1)
        word = jnp.broadcast_to(word_col, (rows, LANES)).astype(BF16)
        kmask = ((lane < HEAD) == word_col).astype(BF16)
        same = segment_ids.reshape(rows, 1) == lane
        qaug = jnp.where(same & (lane < 8), 1.0, 0.0).astype(BF16)
        kaug = jnp.where(lane < 8, jnp.where(same, 0.0, FAR), jnp.where(lane < 11, 1.0, 0.0)).astype(BF16)
        proj_w, vec_half = gather(by_head(projection), 0), gather(vector_params, 1)
        reduce_w = gather(reduce_weight, 0)
        mid_w = jnp.concatenate(
            [gather(expand_weight, 0), gather(context_out, 0), jnp.zeros((width, 2 * LANES), BF16)], axis=1
        )
        zero_row = jnp.zeros((1, width), BF16)
        bias = by_head(jnp.concatenate([vec_half[0:4], zero_row, vec_half[4:5]]).reshape(1, -1)).astype(F32)
        vec_rows = jnp.pad(vec_half.astype(F32), ((0, 1), (0, 0)))
        query, keyval = qkv_call(hidden, proj_w, bias, word)
        context, aug = attend_call(query, keyval, qaug, kaug, kmask, seq_len)
    block_out, grad_r1, grad_context, grad_expand, grad_ctx_w, grad_reduce, grad_mid = middle_call(
        narrow if pieces else None, hidden, context, cot, vec_rows, mid_w, reduce_w
    )
    masters = (projection, context_out, expand_weight, reduce_weight, vector_params)
    firsts = (first_projection, first_context, first_expand, first_reduce, first_vectors)
    seconds = (second_projection, second_context, second_expand, second_reduce, second_vectors)
    out_shape = (seq_count, seq_len, width)
    if pieces:
        input_grad, shard_1, shard_o, shard_w, shard_a, grad_vectors, norm = reduce_call(
            narrow, hidden, query, keyval, aug, grad_context, context, proj_w, kaug, kmask, word, grad_mid,
            grad_r1, grad_expand, grad_reduce, grad_ctx_w, reduce_weight.shape[0], seq_len,
        )
        shards = (shard_a, shard_o, shard_1, shard_w)
        updated = update_call(narrow, norm, shards, grad_vectors, masters, firsts, seconds)
        return (
            block_out.reshape(out_shape),
            input_grad.reshape(out_shape),
            jnp.sqrt(norm[0, 0]),
            *updated,
        )
    grad_proj, grad_proj_w, grad_sums = attend_back_call(
        hidden, query, keyval, aug, grad_context, context, kaug, kmask, word, seq_len
    )
    input_grad = input_grad_call(grad_proj, proj_w, grad_r1, 256)
    sum_rows = by_block(grad_sums).reshape(6, width)
    grad_vectors = jnp.concatenate([sum_rows[0:4], sum_rows[5:6], grad_mid[5:15]], axis=0)

    def scatter(array_in, axis):
        return lax.psum_scatter(array_in, "narrow", scatter_dimension=axis, tiled=True)

    def over_wide(array_in):
        return lax.psum(array_in.astype(BF16), "wide").astype(F32)

    shards = (
        by_block(over_wide(scatter(grad_proj_w, 0))),
        over_wide(scatter(grad_ctx_w, 0)),
        over_wide(scatter(grad_expand, 0)),
        over_wide(scatter(grad_reduce, 0)),
        over_wide(scatter(grad_vectors, 1)),
    )
    local_squares = sum((jnp.sum(shard_item * shard_item) for shard_item in shards))
    total_squares = lax.psum(local_squares, "narrow")
    grad_norm = jnp.sqrt(total_squares)
    factor = jnp.minimum(1.0, clip_limit / (grad_norm + 1e-06))
    results = [
        adam_update(masters[index], firsts[index], seconds[index], shards[index], factor, index)
        for index in range(5)
    ]
    return (
        block_out.reshape(out_shape),
        input_grad.reshape(out_shape),
        grad_norm,
        *(item[0] for item in results),
        *(item[1] for item in results),
        *(item[2] for item in results),
        *(item[0].astype(BF16) for item in results),
    )


def solution(mesh):
    shard, col = P("narrow", None), P(None, "narrow")
    seqs = P(("wide", "narrow"), None, None)
    group = (shard, shard, shard, shard, col)
    return jax.shard_map(
        body,
        mesh=mesh,
        in_specs=(seqs, seqs, P(("wide", "narrow"), None), P(("wide", "narrow"), None), *group, *group, *group),
        out_specs=(seqs, seqs, P(), *group, *group, *group, *group),
        check_vma=False,
    )
```

```python
import functools

import jax
import jax.numpy as jnp
from jax import lax
from jax.experimental import pallas as pl
from jax.experimental.pallas import tpu as pltpu
from jax.sharding import PartitionSpec as P

HEAD = 64
STEP = 10
LANES = 128
GROUP = 6 * HEAD
LOG2E = 1.4426950408889634
FAR = -1e30
VMEM_LIMIT = 60 * 1024 * 1024

beta_one = 0.9
beta_two = 0.999
adam_eps = 1e-08
norm_eps = 1e-05
clip_limit = 1.0
rate_table = (0.03, 0.3, 0.03, 0.015, 0.4)
decay_table = (0.01, 0.01, 0.01, 0.01, 0.0)

F32 = jnp.float32
BF16 = jnp.bfloat16


def mm(a, b):
    return lax.dot_general(a, b, (((1,), (0,)), ((), ())), preferred_element_type=F32)


def mm_nt(a, b):
    return lax.dot_general(a, b, (((1,), (1,)), ((), ())), preferred_element_type=F32)


def mm_tn(a, b):
    return lax.dot_general(a, b, (((0,), (0,)), ((), ())), preferred_element_type=F32)


def low_lanes(rows):
    return lax.broadcasted_iota(jnp.int32, (rows, LANES), 1) < HEAD


def swap_halves(tile):
    return pltpu.roll(tile, HEAD, 1)


def split_three(col):
    high = col.astype(BF16).astype(F32)
    rest = col - high
    mid = rest.astype(BF16).astype(F32)
    return high, mid, rest - mid


def qkv_tile(prod, bias, word):
    full = prod + bias
    query = jnp.where(word, full[:, 0:LANES], full[:, LANES : 2 * LANES])
    return (query.astype(BF16).astype(F32) * (HEAD**-0.5)).astype(BF16), full[
        :, 2 * LANES :
    ].astype(BF16)


def qkv_kernel(x_ref, w_ref, b_ref, word_ref, q_ref, kv_ref):
    word = word_ref[...] > 0
    for part in range(2):
        cols = slice(part * GROUP, (part + 1) * GROUP)
        query, keyval = qkv_tile(mm(x_ref[...], w_ref[:, cols]), b_ref[:, cols], word)
        out = slice(part * LANES, (part + 1) * LANES)
        q_ref[:, out] = query
        kv_ref[:, out] = keyval


def qkv_call(x, w, bias, word):
    rows, width = x.shape
    steps = w.shape[1] // (2 * GROUP)
    out = jax.ShapeDtypeStruct((rows, steps * 2 * LANES), BF16)
    return pl.pallas_call(
        qkv_kernel,
        grid=(steps,),
        in_specs=[
            pl.BlockSpec((rows, width), lambda i: (0, 0)),
            pl.BlockSpec((width, 2 * GROUP), lambda i: (0, i)),
            pl.BlockSpec((1, 2 * GROUP), lambda i: (0, i)),
            pl.BlockSpec((rows, LANES), lambda i: (0, 0)),
        ],
        out_specs=[pl.BlockSpec((rows, 2 * LANES), lambda i: (0, i))] * 2,
        out_shape=[out, out],
        compiler_params=pltpu.CompilerParams(vmem_limit_bytes=VMEM_LIMIT),
        name="qkv",
    )(x, w, bias, word)


class Links:
    def __init__(self, send, recv):
        self.send_sem, self.recv_sem = send, recv
        self.slots = {}
        self.sent = []

    def copy(self, key, src, dst, device):
        index = self.slots.setdefault(key, len(self.slots))
        return pltpu.make_async_remote_copy(
            src_ref=src,
            dst_ref=dst,
            send_sem=self.send_sem.at[index],
            recv_sem=self.recv_sem.at[index],
            device_id=device,
            device_id_type=pl.DeviceIdType.MESH,
        )

    def send(self, key, build, *guards):
        def start():
            self.copy(key, *build()).start()

        guarded(start, guards)
        self.sent.append((key, build, guards))

    def arrived(self, key, dst, device):
        self.copy(key, dst, dst, device).wait_recv()

    def finish(self):
        for key, build, guards in self.sent:

            def wait(key=key, build=build):
                self.copy(key, *build()).wait_send()

            guarded(wait, guards)


def guarded(action, guards):
    if not guards:
        action()
        return
    holds = guards[0]()
    for guard in guards[1:]:
        holds = jnp.logical_and(holds, guard())
    pl.when(holds)(action)


class Place:
    def __init__(self, narrow):
        self.wide, self.me = lax.axis_index("wide"), lax.axis_index("narrow")
        self.core = lax.rem(self.me, 2)
        self.z = self.me // 2
        self.depth = narrow // 2
        self.x_quarter = self.wide + 1 - 2 * lax.rem(self.wide, 2)
        self.y_quarter = lax.rem(self.wide + 2, 4)
        self.d_quarter = lax.rem(self.x_quarter + 2, 4)
        self.sib = self.me + 1 - 2 * self.core
        self.x_dev, self.y_dev = {"wide": self.x_quarter}, {"wide": self.y_quarter}
        self.d_dev = {"wide": self.d_quarter}
        self.sib_dev = {"narrow": self.sib}

    def ahead(self, k):
        return 2 * lax.rem(self.z + k, self.depth) + self.core

    def behind(self, k, other=False):
        core = 1 - self.core if other else self.core
        return 2 * lax.rem(self.z + self.depth - k, self.depth) + core

    def z_dev(self, k):
        return {"narrow": self.ahead(k)}

    def has_next(self, way):
        return lambda: self.z + 1 < self.depth if way == 0 else self.z > 0

    def comes(self, way, hop):
        return lambda: self.z >= hop if way == 0 else self.z + hop < self.depth

    def origin(self, way, hop, other=False):
        core = 1 - self.core if other else self.core
        return 2 * (self.z - hop if way == 0 else self.z + hop) + core

    def next_dev(self, way):
        return {"narrow": self.me + 2 if way == 0 else self.me - 2}

    def greet_near(self):
        barrier = pltpu.get_barrier_semaphore()

        def greet(device):
            pl.semaphore_signal(barrier, inc=1, device_id=device, device_id_type=pl.DeviceIdType.MESH)

        for device in (self.x_dev, self.y_dev, self.sib_dev):
            greet(device)
        for way in range(2):
            guarded(lambda way=way: greet(self.next_dev(way)), (self.has_next(way),))
        pl.semaphore_wait(barrier, 3 + jnp.minimum(self.z, 1) + jnp.minimum(self.depth - 1 - self.z, 1))

    def greet(self):
        barrier = pltpu.get_barrier_semaphore()
        partners = [self.x_dev, self.y_dev, self.d_dev, self.sib_dev] + [self.z_dev(k) for k in range(1, self.depth)]
        for device in partners:
            pl.semaphore_signal(barrier, inc=1, device_id=device, device_id_type=pl.DeviceIdType.MESH)
        pl.semaphore_wait(barrier, len(partners))


def spot(start, size, unit):
    return pl.ds(pl.multiple_of(start, unit), size)


def gather_kernel(
    narrow, x_ref, proj_ref, wo_ref, w1_ref, w2_ref, vec_ref, seg_ref, type_ref,
    q_out, kv_out, ctx_out, aug_out, a_out, e_out, w2_out, vec_out, word_ref, km_ref, ka_ref,
    a_full, e_own, w2_own, v_all, bias, q_s, kv_s, ctx_s, aug_s, qa_ref, send, recv, local,
):
    rows, width = x_ref.shape
    share = proj_ref.shape[0]
    deep = w2_ref.shape[0]
    half, quarter, equarter, dquarter = share // 2, proj_ref.shape[1] // 4, e_own.shape[1] // 4, deep // 4
    heads = width // HEAD
    here = Place(narrow)
    links = Links(send, recv)
    me, hops = here.me, range(1, here.depth)
    routes = [(way, hop) for hop in hops for way in range(2)]

    def region(kind, owner, part, side=None):
        size, start = (share, 0) if side is None else (half, side * half)
        if kind == "a":
            return a_full.at[spot(owner * share + start, size, 16), spot(part * quarter, quarter, LANES)]
        if kind == "e":
            return e_out.at[spot(owner * share + start, size, 16), spot(part * equarter, equarter, LANES)]
        size, start = (dquarter, 0) if side is None else (dquarter // 2, side * (dquarter // 2))
        return w2_out.at[spot(owner * deep + part * dquarter + start, size, 16), :]

    def whole(kind, owner):
        if kind == "a":
            return a_full.at[spot(owner * share, share, 16), :]
        if kind == "e":
            return e_out.at[spot(owner * share, share, 16), :]
        if kind == "w":
            return w2_out.at[spot(owner * deep, deep, 16), :]
        return v_all.at[owner]

    def own(kind):
        return {"a": whole("a", me), "e": e_own, "w": w2_own, "v": v_all.at[me]}[kind]

    def own_part(kind, part, side=None):
        if kind == "a":
            return region("a", me, part, side)
        if kind == "e":
            rows = slice(0, share) if side is None else slice(side * half, (side + 1) * half)
            return e_own.at[rows, spot(part * equarter, equarter, LANES)]
        size, start = (dquarter, 0) if side is None else (dquarter // 2, side * (dquarter // 2))
        return w2_own.at[spot(part * dquarter + start, size, 16), :]

    def send_own(kind):
        links.send((kind, "o"), lambda: (own(kind), whole(kind, me), here.sib_dev))

    def send_z(kind):
        for way in range(2):
            ahead = here.has_next(way)
            if kind == "v":
                links.send(("v", "z", way, 1), lambda way=way: (own("v"), own("v"), here.next_dev(way)), ahead)
                continue
            links.send(
                (kind, "z", way, 1),
                lambda way=way: (own_part(kind, here.wide), region(kind, me, here.wide), here.next_dev(way)),
                ahead,
            )
            if kind == "a":
                continue
            links.send(
                (kind, "h", way, 1),
                lambda way=way: (
                    own_part(kind, here.d_quarter, 0), region(kind, me, here.d_quarter, 0), here.next_dev(way)
                ),
                ahead,
            )

    def relay(key, target, device, *guards):
        links.send(key, lambda: (target(), target(), device()), *guards)

    def receive(key, target, guard):
        guarded(lambda: links.arrived(key, target(), here.sib_dev), (guard,))

    def pass_z(kind, hop):
        for way in range(2):
            comes, ahead = here.comes(way, hop), here.has_next(way)
            onward = lambda way=way: here.next_dev(way)
            if kind == "v":
                piece = lambda way=way: whole("v", here.origin(way, hop))
            else:
                piece = lambda way=way: region(kind, here.origin(way, hop), here.wide)
            receive((kind, "z", way, hop), piece, comes)
            if hop + 1 < here.depth:
                relay((kind, "z", way, hop + 1), piece, onward, comes, ahead)
            if kind != "v":
                relay((kind, "x", way, hop), piece, lambda: here.x_dev, comes)
                relay((kind, "y", way, hop), piece, lambda: here.y_dev, comes)
            relay((kind, "sz", way, hop), piece, lambda: here.sib_dev, comes)
            if kind not in "va":
                other = lambda way=way: region(kind, here.origin(way, hop), here.d_quarter, 0)
                receive((kind, "h", way, hop), other, comes)
                if hop + 1 < here.depth:
                    relay((kind, "h", way, hop + 1), other, onward, comes, ahead)
                relay((kind, "sh", way, hop), other, lambda: here.sib_dev, comes)

    def diagonal(kind, hop):
        by_y, by_x = ("x", 0 if kind == "a" else 1, here.y_dev), ("y", 1, here.x_dev)
        if kind == "a":
            return [by_y, by_x]
        return [by_x if (kind == "e") == (hop % 2 == 1) else by_y]

    def pass_xy(kind, hop):
        for way in range(2):
            comes = here.comes(way, hop)
            for name, part in (("x", here.x_quarter), ("y", here.y_quarter)):
                piece = lambda way=way, part=part: region(kind, here.origin(way, hop), part)
                receive((kind, name, way, hop), piece, comes)
                for back, side, device in diagonal(kind, hop):
                    if back == name:
                        rest = lambda way=way, part=part, side=side: region(kind, here.origin(way, hop), part, side)
                        relay((kind, "d", side, way, hop), rest, lambda device=device: device, comes)
                relay((kind, "s" + name, way, hop), piece, lambda: here.sib_dev, comes)

    def pass_d(kind, number):
        for way in range(2):
            comes = here.comes(way, number)
            for _, side, _ in diagonal(kind, number):
                rest = lambda way=way, side=side: region(kind, here.origin(way, number), here.d_quarter, side)
                receive((kind, "d", side, way, number), rest, comes)
                relay((kind, "sd", side, way, number), rest, lambda: here.sib_dev, comes)

    def from_sib(kind, name, part, side=None):
        if name == "sd":
            for side in range(2):
                if kind == "a" or side == 1:
                    from_sib(kind, ("sd", side), part, side)
                else:
                    from_sib(kind, "sh", part, side)
            return
        name = name if isinstance(name, tuple) else (name,)
        for way, hop in routes:
            piece = lambda way=way, hop=hop: region(kind, here.origin(way, hop, True), part, side)
            receive((kind, *name, way, hop), piece, here.comes(way, hop))

    low = low_lanes(share)
    for pair in range(heads // 2):
        tiles = [proj_ref[:, slice(b * width + pair * LANES, b * width + (pair + 1) * LANES)] for b in range(6)]
        turned = [swap_halves(tile) for tile in tiles]
        for odd in range(2):
            for b in range(3):
                left, right = (turned[2 * b], tiles[2 * b + 1]) if odd else (tiles[2 * b], turned[2 * b + 1])
                at = (2 * pair + odd) * GROUP + b * LANES
                a_full[spot(me * share, share, 16), at : at + LANES] = jnp.where(low, left, right).astype(BF16)
    v_all[me] = jnp.zeros_like(v_all[me])
    v_all[me, 0 : vec_ref.shape[0], 0 : vec_ref.shape[1]] = vec_ref[...].astype(BF16)

    here.greet_near()
    send_z("a")
    send_z("v")
    send_own("v")
    send_own("a")

    inner = w1_ref.shape[1]
    e_own[:, 0:inner] = w1_ref[...].astype(BF16)
    e_own[:, inner : inner + width] = wo_ref[...].astype(BF16)
    e_own[:, inner + width :] = jnp.zeros((share, e_own.shape[1] - inner - width), BF16)
    w2_own[...] = w2_ref[...].astype(BF16)
    copy_e = pltpu.make_async_copy(e_own, whole("e", me), local.at[0])
    copy_w = pltpu.make_async_copy(w2_own, whole("w", me), local.at[1])
    copy_e.start()
    copy_w.start()

    length = seg_ref.shape[1]
    lane = lax.broadcasted_iota(jnp.int32, (length, LANES), 1)
    for seq in range(seg_ref.shape[0]):
        at = slice(seq * length, (seq + 1) * length)
        segment, kind = (
            jnp.transpose(jnp.broadcast_to(ref[seq : seq + 1, :].astype(F32), (LANES, length)))
            for ref in (seg_ref, type_ref)
        )
        same = segment == lane.astype(F32)
        word = jnp.where(kind == 0.0, 1.0, 0.0)
        word_ref[at] = word.astype(BF16)
        km_ref[at] = jnp.where(lane < HEAD, word, 1.0 - word).astype(BF16)
        qa_ref[at] = jnp.where(same & (lane < 8), 1.0, 0.0).astype(BF16)
        ka_ref[at] = jnp.where(
            lane < 8, jnp.where(same, 0.0, FAR), jnp.where(lane < 11, 1.0, 0.0)
        ).astype(BF16)

    def hop(kind, number):
        if number < here.depth:
            pass_z(kind, number)
            if kind == "a":
                pass_z("v", number)

    def turn(kind, number):
        if number < here.depth:
            pass_xy(kind, number)

    deeper = range(4, here.depth)
    hop("a", 1)
    hop("a", 2)
    send_z("e")
    send_own("e")
    turn("a", 1)
    hop("a", 3)
    turn("a", 2)
    for number in deeper:
        hop("a", number)
        turn("a", number - 1)

    links.arrived(("v", "o"), v_all.at[here.sib], here.sib_dev)
    for way, number in routes:
        receive(
            ("v", "sz", way, number),
            lambda way=way, number=number: v_all.at[here.origin(way, number, True)],
            here.comes(way, number),
        )
    span = vec_ref.shape[1]
    vec_out[...] = jnp.concatenate([v_all[n].astype(F32)[:, 0:span] for n in range(narrow)], axis=1)
    low1 = low_lanes(1)
    for head in range(heads):
        cols = slice((head // 2) * LANES, (head // 2 + 1) * LANES)
        row = [vec_out[r : r + 1, cols] for r in range(4)] + [jnp.zeros((1, LANES), F32), vec_out[4:5, cols]]
        for b in range(3):
            left, right = row[2 * b], row[2 * b + 1]
            left, right = (swap_halves(left), right) if head % 2 else (left, swap_halves(right))
            at = head * GROUP + b * LANES
            bias[0:1, at : at + LANES] = jnp.where(low1, left, right)

    links.arrived(("a", "o"), whole("a", here.sib), here.sib_dev)
    outs = []

    def project(index, part):
        size = 256
        cols = spot(part * quarter, quarter, LANES)
        add = bias[0:1, cols]

        def tile(i, carry):
            at = spot(i * size, size, size)
            prod = mm(x_ref[at, :], a_full[:, cols])
            word = word_ref[at, :] > 0
            for head in range(quarter // GROUP):
                group = slice(head * GROUP, (head + 1) * GROUP)
                out = slice(head * LANES, (head + 1) * LANES)
                query, keyval = qkv_tile(prod[:, group], add[:, group], word)
                q_s[part, at, out] = query
                kv_s[part, at, out] = keyval
            return carry

        lax.fori_loop(0, rows // size, tile, 0)
        wide = q_s.shape[2]
        for number, (source, target) in enumerate(((q_s, q_out), (kv_s, kv_out))):
            copy = pltpu.make_async_copy(
                source.at[part], target.at[:, spot(part * wide, wide, LANES)], local.at[2 + 2 * index + number]
            )
            copy.start()
            outs.append(copy)

    from_sib("a", "sz", here.wide)
    project(0, here.wide)
    hop("e", 1)
    turn("a", here.depth - 1)
    from_sib("a", "sx", here.x_quarter)
    project(1, here.x_quarter)
    for number in hops:
        pass_d("a", number)
    hop("e", 2)
    send_z("w")
    send_own("w")
    turn("e", 1)
    from_sib("a", "sy", here.y_quarter)
    project(2, here.y_quarter)
    hop("e", 3)
    from_sib("a", "sd", here.d_quarter)
    project(3, here.d_quarter)
    copy_a = pltpu.make_async_copy(a_full, a_out, local.at[10])
    copy_a.start()
    low_seq = low_lanes(length)
    per = quarter // GROUP

    def attend(pair, seq):
        at = slice(seq * length, (seq + 1) * length)
        contexts = []
        for head in (2 * pair, 2 * pair + 1):
            cols = slice(head % per * LANES, (head % per + 1) * LANES)
            context, extra = attend_head(
                q_s[head // per, at, cols], kv_s[head // per, at, cols], qa_ref[at], ka_ref[at], km_ref[at]
            )
            aug_s[at, head * LANES : (head + 1) * LANES] = extra
            contexts.append(context)
        both = jnp.where(low_seq, swap_halves(contexts[0]), contexts[1])
        ctx_s[at, pair * LANES : (pair + 1) * LANES] = both.astype(BF16)

    def attended(pair):
        for number, (source, target, wide) in enumerate(((ctx_s, ctx_out, LANES), (aug_s, aug_out, 2 * LANES))):
            cols = slice(pair * wide, (pair + 1) * wide)
            copy = pltpu.make_async_copy(source.at[:, cols], target.at[:, cols], local.at[11 + 2 * pair + number])
            copy.start()
            outs.append(copy)

    def later(kind, first, last):
        for number in range(first, last):
            turn(kind, number)

    between = [
        lambda: [turn("e", 2), pass_d("e", 1)],
        lambda: hop("w", 1),
        lambda: [turn("e", 3), pass_d("e", 2)],
        lambda: [hop("w", 2), [hop("e", number) for number in deeper], later("e", 4, here.depth)],
        lambda: [turn("w", 1), [pass_d("e", number) for number in range(3, here.depth)]],
        lambda: hop("w", 3),
        lambda: [turn("w", 2), pass_d("w", 1)],
        lambda: [hop("w", number) for number in deeper],
        lambda: [later("w", 3, here.depth), pass_d("w", 2)],
        lambda: [pass_d("w", number) for number in range(3, here.depth)],
    ]
    units = [(pair, seq) for pair in range(heads // 2) for seq in range(seg_ref.shape[0])]
    for index, (pair, seq) in enumerate(units):
        attend(pair, seq)
        if seq == seg_ref.shape[0] - 1:
            attended(pair)
        if index < len(between):
            between[index]()
    for action in between[len(units) :]:
        action()
    for kind in ("e", "w"):
        links.arrived((kind, "o"), whole(kind, here.sib), here.sib_dev)
        for name, part in (("sz", here.wide), ("sx", here.x_quarter), ("sy", here.y_quarter)):
            from_sib(kind, name, part)
        from_sib(kind, "sd", here.d_quarter)
    links.finish()
    for copy in (copy_e, copy_w, copy_a, *outs):
        copy.wait()


def gather_call(narrow, x, proj, wo, w1, w2, vec, segments, types):
    rows, width = x.shape
    share, deep, inner = proj.shape[0], w2.shape[0], w1.shape[1]
    ecols = inner + width + 2 * LANES
    heads = width // HEAD
    depth = narrow // 2
    count = 3 * (1 + 20 * (depth - 1)) + 1 + 4 * (depth - 1)
    vmem = pl.BlockSpec(memory_space=pltpu.VMEM)
    hbm = pl.BlockSpec(memory_space=pl.ANY)
    shape = jax.ShapeDtypeStruct
    part = heads // 4 * LANES
    return pl.pallas_call(
        functools.partial(gather_kernel, narrow),
        in_specs=[vmem] * 8,
        out_specs=[hbm] * 7 + [vmem] * 4,
        out_shape=[
            shape((rows, heads * LANES), BF16),
            shape((rows, heads * LANES), BF16),
            shape((rows, width), BF16),
            shape((rows, heads * LANES), BF16),
            shape((width, proj.shape[1]), BF16),
            shape((width, ecols), BF16),
            shape((deep * narrow, width), BF16),
            shape((16, width), F32),
            shape((rows, LANES), BF16),
            shape((rows, LANES), BF16),
            shape((rows, LANES), BF16),
        ],
        scratch_shapes=[
            pltpu.VMEM((width, proj.shape[1]), BF16),
            pltpu.VMEM((share, ecols), BF16),
            pltpu.VMEM((deep, width), BF16),
            pltpu.VMEM((narrow, 16, LANES), BF16),
            pltpu.VMEM((8, proj.shape[1]), F32),
            pltpu.VMEM((4, rows, part), BF16),
            pltpu.VMEM((4, rows, part), BF16),
            pltpu.VMEM((rows, width), BF16),
            pltpu.VMEM((rows, heads * LANES), BF16),
            pltpu.VMEM((rows, LANES), BF16),
            pltpu.SemaphoreType.DMA((count,)),
            pltpu.SemaphoreType.DMA((count,)),
            pltpu.SemaphoreType.DMA((11 + heads,)),
        ],
        compiler_params=pltpu.CompilerParams(
            vmem_limit_bytes=VMEM_LIMIT, collective_id=0, has_side_effects=True
        ),
        name="gather",
    )(x, proj, wo, w1, w2, vec, segments, types)


def key_pair(keyval, kmask, low):
    wide = keyval.astype(F32)
    return (jnp.where(low, wide, swap_halves(wide)) * kmask.astype(F32)).astype(BF16)


def attend_head(query, keyval, qaug, kaug, kmask):
    rows = query.shape[0]
    low = low_lanes(rows)
    lane = lax.broadcasted_iota(jnp.int32, (rows, LANES), 1)
    keys = jnp.concatenate([key_pair(keyval, kmask, low), kaug], axis=1)
    scores = mm_nt(jnp.concatenate([query, qaug], axis=1), keys)
    top = jnp.max(scores, axis=1, keepdims=True)
    weight = jnp.exp2((scores - top) * LOG2E).astype(BF16)
    ones_val = jnp.where(low, 1.0, keyval.astype(F32)).astype(BF16)
    both = mm(weight, ones_val)
    total = swap_halves(both)
    log_total = top + jnp.log(jnp.where(low, both, total))
    high, mid, rest = split_three(log_total)
    extra = jnp.where(lane == 8, -high, jnp.where(lane == 9, -mid, jnp.where(lane == 10, -rest, 0.0)))
    return both / total, jnp.where(lane < 8, qaug.astype(F32), extra).astype(BF16)


def attend_kernel(q_ref, kv_ref, qa_ref, ka_ref, km_ref, ctx_ref, aug_ref):
    outs = []
    for part in range(2):
        cols = slice(part * LANES, (part + 1) * LANES)
        out, aug_ref[:, cols] = attend_head(q_ref[:, cols], kv_ref[:, cols], qa_ref[...], ka_ref[...], km_ref[...])
        outs.append(out)
    ctx_ref[...] = jnp.where(low_lanes(q_ref.shape[0]), swap_halves(outs[0]), outs[1]).astype(BF16)


def attend_call(q, kv, qa, ka, km, length):
    rows, cols = q.shape
    seqs, steps = rows // length, cols // (2 * LANES)
    pair = pl.BlockSpec((length, 2 * LANES), lambda s, i: (s, i))
    one = pl.BlockSpec((length, LANES), lambda s, i: (s, 0))
    return pl.pallas_call(
        attend_kernel,
        grid=(seqs, steps),
        in_specs=[pair, pair, one, one, one],
        out_specs=[pl.BlockSpec((length, LANES), lambda s, i: (s, i)), pair],
        out_shape=[
            jax.ShapeDtypeStruct((rows, cols // 2), BF16),
            jax.ShapeDtypeStruct((rows, cols), BF16),
        ],
        compiler_params=pltpu.CompilerParams(vmem_limit_bytes=VMEM_LIMIT),
        name="attend",
    )(q, kv, qa, ka, km)


def attend_back_head(query, keyval, aug, gcon, con, kaug, kmask, word, odd, low, lane):
    keys = key_pair(keyval, kmask, low)
    scores_t = mm_nt(jnp.concatenate([keys, kaug], axis=1), jnp.concatenate([query, aug], axis=1))
    probs_t = jnp.exp2(scores_t * LOG2E)
    gwide = gcon.astype(F32)
    prod = gwide * con.astype(F32)
    mine = low != odd
    delta = jnp.sum(jnp.where(mine, prod, 0.0), axis=1, keepdims=True)
    high, mid, rest = split_three(delta)
    extra = jnp.where(lane == 0, -high, jnp.where(lane == 1, -mid, jnp.where(lane == 2, -rest, 0.0)))
    ghead = jnp.where(low, extra, jnp.where(odd, gwide, swap_halves(gwide))).astype(BF16)
    ones_val = jnp.where(low, jnp.where(lane < 3, 1.0, 0.0), keyval.astype(F32)).astype(BF16)
    gscores_t = (probs_t * mm_nt(ones_val, ghead)).astype(BF16)
    gval = mm(probs_t.astype(BF16), ghead)
    gkey = mm(gscores_t, query)
    gquery = (jnp.transpose(mm_tn(keys, gscores_t)) * (HEAD**-0.5)).astype(BF16)
    zero = jnp.zeros_like(gquery)
    gkey = jnp.where(kmask.astype(F32) > 0, gkey, 0.0)
    gkey = gkey + swap_halves(gkey)
    return (
        jnp.where(word, gquery, zero),
        jnp.where(word, zero, gquery),
        jnp.where(low, gkey, gval).astype(BF16),
    )


def attend_back_kernel(
    length, x_ref, q_ref, kv_ref, aug_ref, gc_ref, ctx_ref, ka_ref, km_ref, word_ref, gp_ref, gw_ref, sum_ref, xt
):
    step = pl.program_id(0)
    rows = x_ref.shape[0]

    @pl.when(step == 0)
    def _():
        xt[...] = jnp.transpose(x_ref[...])

    low = low_lanes(length)
    lane = lax.broadcasted_iota(jnp.int32, (length, LANES), 1)
    odd = lax.rem(step, 2) == 1
    for seq in range(rows // length):
        here = slice(seq * length, (seq + 1) * length)
        tiles = attend_back_head(
            q_ref[here], kv_ref[here], aug_ref[here], gc_ref[here], ctx_ref[here],
            ka_ref[here], km_ref[here], word_ref[here] > 0, odd, low, lane,
        )
        for index, tile in enumerate(tiles):
            gp_ref[here, index * LANES : (index + 1) * LANES] = tile
    grads = gp_ref[...]
    gw_ref[...] = mm(xt[...], grads).astype(BF16)
    sums = jnp.sum(grads.astype(F32).reshape(rows // 8, 8, GROUP), axis=0)
    sum_ref[...] = jnp.sum(sums, axis=0, keepdims=True)


def attend_back_call(x, q, kv, aug, gc, ctx, ka, km, word, length):
    rows, width = x.shape
    heads = q.shape[1] // LANES
    head = pl.BlockSpec((rows, LANES), lambda h: (0, h))
    pair = pl.BlockSpec((rows, LANES), lambda h: (0, h // 2))
    one = pl.BlockSpec((rows, LANES), lambda h: (0, 0))
    return pl.pallas_call(
        functools.partial(attend_back_kernel, length),
        grid=(heads,),
        in_specs=[pl.BlockSpec((rows, width), lambda h: (0, 0)), head, head, head, pair, pair, one, one, one],
        out_specs=[
            pl.BlockSpec((rows, GROUP), lambda h: (0, h)),
            pl.BlockSpec((width, GROUP), lambda h: (0, h)),
            pl.BlockSpec((1, GROUP), lambda h: (0, h)),
        ],
        out_shape=[
            jax.ShapeDtypeStruct((rows, heads * GROUP), BF16),
            jax.ShapeDtypeStruct((width, heads * GROUP), BF16),
            jax.ShapeDtypeStruct((1, heads * GROUP), F32),
        ],
        scratch_shapes=[pltpu.VMEM((width, rows), BF16)],
        compiler_params=pltpu.CompilerParams(vmem_limit_bytes=VMEM_LIMIT),
        name="attend_back",
    )(x, q, kv, aug, gc, ctx, ka, km, word)


class Chunk:
    def __init__(self, name, shape, total, plane=None, end=None):
        self.name = name
        self.rows, self.cols = shape
        self.total = total
        if plane is not None:
            self.r1a, self.r1b, self.r2a, self.r2b = plane
        if end is not None:
            self.rz, self.final = end

    def row_half(self, wide):
        return spot(wide // 2 * (self.rows // 2), self.rows // 2, 16)

    def col_half(self, wide):
        return spot(lax.rem(wide, 2) * (self.cols // 2), self.cols // 2, LANES)

    def quarter(self, wide):
        return self.row_half(wide), self.col_half(wide)

    def mine(self, z, wide):
        if self.total.shape[1:] != (self.rows, self.cols):
            return self.total.at[z]
        return self.total.at[(z, *self.quarter(wide))]


def plane_scratch(depth, rows, cols):
    half = depth // 2
    return [
        pltpu.VMEM((half, rows, cols // 2), BF16),
        pltpu.VMEM((half, rows // 2, cols), BF16),
        pltpu.VMEM((half, rows // 2, cols // 2), BF16),
        pltpu.VMEM((half, rows // 2, cols // 2), BF16),
    ]


def end_scratch(depth, rows, cols):
    return [pltpu.VMEM((depth - 1, rows // 2, cols // 2), BF16), pltpu.VMEM((rows, cols), BF16)]


class Reducer:
    def __init__(self, here, send, recv):
        self.here = here
        self.links = Links(send, recv)
        self.send, self.arrived, self.finish = self.links.send, self.links.arrived, self.links.finish

    def pair_send(self, chunk, sources, only=None):
        here = self.here
        for z in range(here.depth) if only is None else (only,):
            for part, (_, cols) in enumerate(sources(0)):

                def build(z=z, part=part, cols=cols):
                    owner = 2 * z + 1 - here.core
                    return sources(owner)[part][0], chunk.total.at[z, :, cols], here.sib_dev

                self.send((chunk.name, "s", z, part), build)

    def pair_wait(self, chunk, sources):
        for z in range(self.here.depth):
            for part, (_, cols) in enumerate(sources(0)):
                self.arrived((chunk.name, "s", z, part), chunk.total.at[z, :, cols], self.here.sib_dev)

    def lower(self):
        return slice(0, self.here.depth // 2)

    def upper(self):
        return slice(self.here.depth // 2, self.here.depth)

    def plane_send(self, chunk):
        here = self.here
        cols, rows = (lambda: chunk.col_half(here.x_quarter)), (lambda: chunk.row_half(here.y_quarter))
        self.send((chunk.name, "1a"), lambda: (chunk.total.at[self.lower(), :, cols()], chunk.r1a, here.x_dev))
        self.send((chunk.name, "1b"), lambda: (chunk.total.at[self.upper(), rows(), :], chunk.r1b, here.y_dev))

    def plane_turn(self, chunk):
        here = self.here
        total = chunk.total
        self.arrived((chunk.name, "1a"), chunk.r1a, here.x_dev)
        self.arrived((chunk.name, "1b"), chunk.r1b, here.y_dev)
        rows, cols = chunk.quarter(here.wide)
        total[self.lower(), :, cols] = total[self.lower(), :, cols] + chunk.r1a[...]
        total[self.upper(), rows, :] = total[self.upper(), rows, :] + chunk.r1b[...]

        def first():
            return total.at[(self.lower(), *chunk.quarter(here.y_quarter))], chunk.r2a, here.y_dev

        def second():
            return total.at[(self.upper(), *chunk.quarter(here.x_quarter))], chunk.r2b, here.x_dev

        self.send((chunk.name, "2a"), first)
        self.send((chunk.name, "2b"), second)

    def plane_done(self, chunk):
        here = self.here
        self.arrived((chunk.name, "2a"), chunk.r2a, here.y_dev)
        self.arrived((chunk.name, "2b"), chunk.r2b, here.x_dev)
        rows, cols = chunk.quarter(here.wide)
        for part, value in ((self.lower(), chunk.r2a), (self.upper(), chunk.r2b)):
            chunk.total[part, rows, cols] = chunk.total[part, rows, cols] + value[...]

    def depth_send(self, chunk):
        here = self.here
        for k in range(1, here.depth):

            def build(k=k):
                piece = chunk.mine(lax.rem(here.z + k, here.depth), here.wide)
                return piece, chunk.rz.at[k - 1], here.z_dev(k)

            self.send((chunk.name, "z", k), build)

    def share_send(self, chunk):
        here = self.here
        for k in range(1, here.depth):
            self.arrived((chunk.name, "z", k), chunk.rz.at[k - 1], here.z_dev(k))
        done = chunk.mine(here.z, here.wide)[...].astype(F32)
        for k in range(1, here.depth):
            done = done + chunk.rz[k - 1].astype(F32)
        done = done.astype(BF16)
        rows, cols = chunk.quarter(here.wide)
        chunk.final[rows, cols] = done

        def build(device):
            piece = chunk.final.at[chunk.quarter(here.wide)]
            return piece, piece, device

        for name, device in (("fx", here.x_dev), ("fy", here.y_dev), ("fd", here.d_dev)):
            self.send((chunk.name, name), lambda device=device: build(device))
        return squares(done)

    def share_wait(self, chunk):
        here = self.here
        ways = (("fx", here.x_quarter, here.x_dev), ("fy", here.y_quarter, here.y_dev), ("fd", here.d_quarter, here.d_dev))
        for name, quarter, device in ways:
            self.arrived((chunk.name, name), chunk.final.at[chunk.quarter(quarter)], device)


def squares(value):
    total = jnp.zeros((8, LANES), F32)
    rows, cols = value.shape
    for start in range(0, cols, LANES):
        tile = value[:, start : start + LANES].astype(F32)
        total = total + jnp.sum((tile * tile).reshape(rows // 8, 8, LANES), axis=0)
    return total


def head_groups(heads):
    return (heads // 3, heads // 3, heads // 6, heads // 6)


def reduce_kernel(
    narrow, length, groups, deep,
    x_ref, q_ref, kv_ref, aug_ref, gc_ref, ctx_ref, wp_ref, ka_ref, km_ref, word_ref, gvec_ref,
    gr1_ref, t1_ref, tw_ref, gwo_ref,
    ig_ref, f1_ref, fo_ref, fw_ref, fa_ref, v_ref, n_ref,
    xt, gp, ig, *scratch,
):
    step = pl.program_id(0)
    rows, width = x_ref.shape
    heads = sum(groups)
    share, inner = t1_ref.shape[1:]
    here = Place(narrow)
    scratch = list(scratch)
    red = Reducer(here, scratch[-3], scratch[-2])
    local = scratch[-1]

    def take(count):
        taken, scratch[:count] = scratch[:count], []
        return taken

    chunk_w = Chunk("w", (deep, width), take(1)[0], None, take(2))
    chunk_1 = Chunk("1", (share, inner), take(1)[0], take(4), take(2))
    gw, chunk_a = [], []
    for j in range(len(groups)):
        gw += take(1)
        chunk_a.append(Chunk(("a", j), (share, gw[j].shape[1]), take(1)[0], take(4), take(2)))
    v0, v1, v2, vs, vx, vy, vz, n0, np, n1, ns, nz = take(12)
    begin = [sum(groups[:j]) for j in range(len(groups) + 1)]
    wide = groups[0] * GROUP

    def sources_a(j):
        return lambda owner: [(gw[j].at[spot(owner * share, share, 16), :], slice(0, gw[j].shape[1]))]

    def load(index):
        source, target = (
            (t1_ref, chunk_1.total),
            (tw_ref, chunk_w.total),
            (gwo_ref, gw[0].at[:, wide : wide + width]),
            (gr1_ref, ig),
        )[index]
        return pltpu.make_async_copy(source, target, local.at[index])

    def stores():
        copies = [(chunk_w.final, fw_ref), (chunk_1.final, f1_ref)]
        copies += [(chunk_a[0].final.at[:, wide : wide + width], fo_ref)]
        for j, chunk in enumerate(chunk_a):
            cols = slice(begin[j] * GROUP, begin[j + 1] * GROUP)
            copies.append((chunk.final.at[:, 0 : groups[j] * GROUP], fa_ref.at[:, cols]))
        return [pltpu.make_async_copy(a, b, local.at[4 + i]) for i, (a, b) in enumerate(copies)]

    def merge(j):
        def one(z, carry):
            mine = spot((2 * z + here.core) * share, share, 16)
            chunk_a[j].total[z] = chunk_a[j].total[z] + gw[j][mine, :]
            return carry

        red.pair_wait(chunk_a[j], sources_a(j))
        lax.fori_loop(0, here.depth, one, 0)
        red.plane_send(chunk_a[j])

    def turn_z(chunk):
        red.plane_done(chunk)
        red.depth_send(chunk)

    @pl.when(step == 0)
    def _():
        for index in range(4):
            load(index).start()
        here.greet()
        load(0).wait()
        red.plane_send(chunk_1)
        load(1).wait()
        red.depth_send(chunk_w)
        v0[...] = gvec_ref[...]
        n0[...] = jnp.zeros_like(n0)
        xt[...] = jnp.transpose(x_ref[...])

    def at(when):
        def run(action):
            def body():
                action()

            pl.when(step == when)(body)

        return run

    def finish(chunk):
        n0[...] += red.share_send(chunk)

    def vec_pair():
        red.arrived(("v", "s"), vs, here.sib_dev)
        v1[...] = v0[...] + vs[...]
        red.send(("v", "x"), lambda: (v1, vx, here.x_dev))

    def vec_plane():
        red.arrived(("v", "x"), vx, here.x_dev)
        v2[...] = v1[...] + vx[...]
        red.send(("v", "y"), lambda: (v2, vy, here.y_dev))

    def vec_depth():
        red.arrived(("v", "y"), vy, here.y_dev)
        vz[here.z] = v2[...] + vy[...]
        for k in range(1, here.depth):
            red.send(("v", "z", k), lambda k=k: (vz.at[here.z], vz.at[here.z], here.z_dev(k)))

    def vec_done():
        for k in range(1, here.depth):
            red.arrived(("v", "z", k), vz.at[here.behind(k) // 2], here.z_dev(k))
        vec = vz[0]
        for z in range(1, here.depth):
            vec = vec + vz[z]
        v_ref[...] = vec

    a = chunk_a
    last = len(groups) - 1
    plan = {
        2: [lambda: load(2).wait()],
        3: [lambda: red.plane_turn(chunk_1)],
        4: [lambda: finish(chunk_w)],
        5: [lambda: merge(0)],
        6: [lambda: turn_z(chunk_1)],
        8: [lambda: red.plane_turn(a[0])],
        9: [lambda: merge(1), lambda: finish(chunk_1)],
        10: [lambda: turn_z(a[0])],
        11: [lambda: red.plane_turn(a[1]), lambda: merge(2)],
        12: [lambda: turn_z(a[1])],
        13: [lambda: merge(3), lambda: vec_pair(), lambda: red.plane_turn(a[2])],
        15: [lambda: turn_z(a[2]), lambda: finish(a[0])],
        17: [lambda: red.plane_turn(a[3]), lambda: vec_plane()],
        19: [lambda: turn_z(a[3]), lambda: finish(a[1]), lambda: vec_depth()],
        21: [lambda: finish(a[2]), lambda: vec_done()],
        22: [lambda: red.share_wait(chunk_w), lambda: red.share_wait(chunk_1), lambda: red.share_wait(a[0])],
    }
    for when, actions in plan.items():
        for action in actions:
            at(when)(action)

    @pl.when(step < heads)
    def _():
        low = low_lanes(length)
        lane = lax.broadcasted_iota(jnp.int32, (length, LANES), 1)
        odd = lax.rem(step, 2) == 1
        for seq in range(rows // length):
            here_rows = slice(seq * length, (seq + 1) * length)
            tiles = attend_back_head(
                q_ref[here_rows], kv_ref[here_rows], aug_ref[here_rows], gc_ref[here_rows], ctx_ref[here_rows],
                ka_ref[here_rows], km_ref[here_rows], word_ref[here_rows] > 0, odd, low, lane,
            )
            for index, tile in enumerate(tiles):
                gp[step, here_rows, index * LANES : (index + 1) * LANES] = tile
        grads = gp[step]
        product = mm(xt[...], grads).astype(BF16)
        for j in range(len(groups)):

            @pl.when((step >= begin[j]) & (step < begin[j + 1]))
            def _():
                gw[j][:, spot((step - begin[j]) * GROUP, GROUP, LANES)] = product

        sums = jnp.sum(jnp.sum(grads.astype(F32).reshape(rows // 8, 8, GROUP), axis=0), axis=0, keepdims=True)

        low1 = low_lanes(1)
        pair = spot(step // 2 * LANES, LANES, LANES)
        mine = low1 != odd
        for b in range(3):
            tile = sums[:, b * LANES : (b + 1) * LANES]
            turned = swap_halves(tile)
            first = jnp.where(odd, turned, tile)
            second = jnp.where(odd, tile, turned)
            if b < 2:
                v0[2 * b : 2 * b + 1, pair] = jnp.where(mine, first, v0[2 * b : 2 * b + 1, pair])
                v0[2 * b + 1 : 2 * b + 2, pair] = jnp.where(mine, second, v0[2 * b + 1 : 2 * b + 2, pair])
            else:
                v0[4:5, pair] = jnp.where(mine, second, v0[4:5, pair])

    for j in range(len(groups)):
        at(begin[j + 1] - 1)(lambda j=j: red.pair_send(chunk_a[j], sources_a(j)))

    at(heads - 1)(lambda: red.send(("v", "s"), lambda: (v0, vs, here.sib_dev)))
    at(heads)(lambda: load(3).wait())

    @pl.when(step >= heads)
    def _():
        ig[...] += mm_nt(gp[step - heads], wp_ref[...])

    @pl.when(step == 2 * heads - 1)
    def _():
        finish(a[last])
        np[here.wide] = n0[...]
        for name, device in (("nx", here.x_dev), ("ny", here.y_dev), ("nd", here.d_dev)):
            red.send((name,), lambda device=device: (np.at[here.wide], np.at[here.wide], device))
        vec = v_ref[...]
        square = jnp.sum(jnp.sum(vec * vec, axis=0, keepdims=True), axis=1, keepdims=True)
        ig_ref[...] = ig[...].astype(BF16)
        ways = (("nx", here.x_quarter, here.x_dev), ("ny", here.y_quarter, here.y_dev), ("nd", here.d_quarter, here.d_dev))
        for name, quarter, device in ways:
            red.arrived((name,), np.at[quarter], device)
        n1[...] = (np[0] + np[1]) + (np[2] + np[3])
        red.send(("n", "s"), lambda: (n1, ns, here.sib_dev))
        for chunk in a[1:]:
            red.share_wait(chunk)
        for copy in stores():
            copy.start()
        red.arrived(("n", "s"), ns, here.sib_dev)
        nz[here.z] = n1[...] + ns[...]
        for k in range(1, here.depth):
            red.send(("n", "z", k), lambda k=k: (nz.at[here.z], nz.at[here.z], here.z_dev(k)))
        for k in range(1, here.depth):
            red.arrived(("n", "z", k), nz.at[here.behind(k) // 2], here.z_dev(k))
        total = nz[0]
        for z in range(1, here.depth):
            total = total + nz[z]
        every = jnp.sum(jnp.sum(total, axis=0, keepdims=True), axis=1, keepdims=True)
        n_ref[...] = jnp.broadcast_to(every + square, n_ref.shape)
        red.finish()
        for copy in stores():
            copy.wait()


def reduce_call(narrow, x, q, kv, aug, gc, ctx, wp, ka, km, word, gvec, gr1, t1, tw, gwo, deep, length):
    rows, width = x.shape
    heads = q.shape[1] // LANES
    groups = head_groups(heads)
    depth, share, inner = t1.shape

    def now(h):
        return jnp.minimum(h, heads - 1)

    def fixed(shape):
        return pl.BlockSpec(shape, lambda h: (0, 0), pipeline_mode=pl.Buffered(1))

    head = pl.BlockSpec((rows, LANES), lambda h: (0, now(h)))
    pair = pl.BlockSpec((rows, LANES), lambda h: (0, now(h) // 2))
    later = pl.BlockSpec((width, GROUP), lambda h: (0, jnp.maximum(h - heads, 0)))
    one = fixed((rows, LANES))
    hbm = pl.BlockSpec(memory_space=pl.ANY)
    shape = jax.ShapeDtypeStruct
    vec = pltpu.VMEM((16, width), F32)
    tile = pltpu.VMEM((8, LANES), F32)
    scratch = [pltpu.VMEM((width, rows), BF16), pltpu.VMEM((heads, rows, GROUP), BF16), pltpu.VMEM((rows, width), F32)]
    scratch += [pltpu.VMEM(tw.shape, BF16), *end_scratch(depth, deep, width)]
    scratch += [
        pltpu.VMEM(t1.shape, BF16),
        *plane_scratch(depth, share, inner),
        *end_scratch(depth, share, inner),
    ]
    for j, size in enumerate(groups):
        cols = size * GROUP + (width if j == 0 else 0)
        scratch += [
            pltpu.VMEM((width, cols), BF16),
            pltpu.VMEM((depth, share, cols), BF16),
            *plane_scratch(depth, share, cols),
            *end_scratch(depth, share, cols),
        ]
    several = pltpu.VMEM((depth, 8, LANES), F32)
    scratch += [vec] * 6 + [pltpu.VMEM((depth, 16, width), F32), tile, pltpu.VMEM((4, 8, LANES), F32), tile, tile, several]
    count = (2 + len(groups)) * (2 * depth + 6) + 2 * (4 + depth)
    scratch += [pltpu.SemaphoreType.DMA((count,))] * 2 + [pltpu.SemaphoreType.DMA((7 + len(groups),))]
    return pl.pallas_call(
        functools.partial(reduce_kernel, narrow, length, groups, deep),
        grid=(2 * heads,),
        in_specs=[
            fixed((rows, width)), head, head, head, pair, pair, later, one, one, one, fixed((16, width)),
            hbm, hbm, hbm, hbm,
        ],
        out_specs=[fixed((rows, width)), hbm, hbm, hbm, hbm, fixed((16, width)), fixed((8, LANES))],
        out_shape=[
            shape((rows, width), BF16),
            shape((share, inner), BF16),
            shape((share, width), BF16),
            shape((deep, width), BF16),
            shape((share, heads * GROUP), BF16),
            shape((16, width), F32),
            shape((8, LANES), F32),
        ],
        scratch_shapes=scratch,
        compiler_params=pltpu.CompilerParams(
            vmem_limit_bytes=VMEM_LIMIT, collective_id=1, has_side_effects=True
        ),
        name="reduce",
    )(x, q, kv, aug, gc, ctx, wp, ka, km, word, gvec, gr1, t1, tw, gwo)


def gelu_pair(pre):
    bell = jnp.exp2(pre * pre * (-0.5 * LOG2E))
    share = 0.5 + 0.5 * lax.erf(pre * (0.5**0.5))
    return pre * share, share + pre * bell * 0.3989422804014327


def fold(array_in):
    rows, cols = array_in.shape
    return jnp.sum(array_in.reshape(rows // 8, 8, cols), axis=0)


def middle_kernel(
    narrow, x_hbm, ctx_hbm, cot_hbm, vec_ref, e_hbm, w2_hbm,
    out_hbm, gr1_hbm, gctx_hbm, gw1_hbm, gwo_hbm, gw2_hbm, gvec_ref,
    wo, w1, w2, io, ctx, h1_s, n1_s, inv_s, act_s, slope_s, gb_s, sum_s, gw2_s, gwo_s, acc, sems, *scratch,
):
    rows, width = io.shape
    inner = w1.shape[1]
    blocks, size, block = inner // width, 256, 256
    red = None

    def load(index):
        source, target = (
            (x_hbm, io),
            (ctx_hbm, ctx),
            (e_hbm.at[:, inner : inner + width], wo),
            (e_hbm.at[:, 0:inner], w1),
            (w2_hbm, w2),
            (cot_hbm, io),
        )[index]
        return pltpu.make_async_copy(source, target, sems.at[index])

    def store(index):
        source, target = (
            (io, out_hbm),
            (sum_s, gr1_hbm),
            (io, gctx_hbm),
            (gwo_s, gwo_hbm),
            (gw2_s, gw2_hbm) if red is None else (chunk.total.at[(slice(None), *chunk.quarter(here.wide))], gw2_hbm),
            (act_s.at[0:width, :] if red is None else chunk_1.total, gw1_hbm),
        )[index]
        return pltpu.make_async_copy(source, target, sems.at[6 + index])

    def vec(row):
        return vec_ref[row : row + 1, :].astype(F32)

    def over_rows(step):
        def one(i, carry):
            step(spot(i * size, size, size))
            return carry

        lax.fori_loop(0, rows // size, one, 0)

    def over_cols(first, last, step):
        def one(i, carry):
            step(spot(i * block, block, block), i)
            return carry

        lax.fori_loop(first, last, one, 0)

    for index in (1, 2, 0, 3, 4):
        load(index).start()
    acc[...] = jnp.zeros_like(acc)
    if narrow is not None:
        here = Place(narrow)
        red = Reducer(here, scratch[0], scratch[1])
        deep, share = scratch[2].shape[1], scratch[7].shape[1]
        chunk = Chunk("w", (deep, width), scratch[2], scratch[3:7])
        chunk_1 = Chunk("1", (share, inner), scratch[7])
        here.greet()

        def sources(owner):
            return [(gw2_s.at[spot(owner * deep, deep, 16), :], slice(0, width))]

        def sources_1(owner):
            return [(act_s.at[spot(owner * share, share, 16), :], slice(0, inner))]

    for index in (1, 2, 0):
        load(index).wait()

    def norm_one(at):
        resid = io[at, :].astype(F32) + mm(ctx[at, :], wo[...]) + vec(5)
        center = resid - jnp.mean(resid, axis=1, keepdims=True)
        inverse = lax.rsqrt(jnp.mean(center * center, axis=1, keepdims=True) + norm_eps)
        unit = center * inverse
        hidden = unit * vec(6) + vec(7)
        n1_s[at, :] = unit.astype(BF16)
        inv_s[at, :] = jnp.broadcast_to(inverse, (size, LANES))
        h1_s[at, :] = hidden.astype(BF16)
        sum_s[at, :] = hidden + vec(8)

    over_rows(norm_one)
    load(5).start()
    load(3).wait()
    per = width // block

    def expand(at, i):
        bias = vec_ref[11 + i // per, spot(lax.rem(i, per) * block, block, LANES)].astype(F32).reshape(1, block)
        act, slope = gelu_pair(mm(h1_s[...], w1[:, at]) + bias)
        act_s[:, at] = act.astype(BF16)
        slope_s[:, at] = slope.astype(BF16)

    over_cols(0, inner // block, expand)
    load(4).wait()

    def reduce(at, i):
        sum_s[:, at] += mm(act_s[...], w2[:, at])

    over_cols(0, per, reduce)
    load(5).wait()

    def norm_two(at):
        resid = sum_s[at, :]
        center = resid - jnp.mean(resid, axis=1, keepdims=True)
        inverse = lax.rsqrt(jnp.mean(center * center, axis=1, keepdims=True) + norm_eps)
        unit = center * inverse
        grad = io[at, :].astype(F32)
        io[at, :] = (unit * vec(9) + vec(10)).astype(BF16)
        acc[9] += fold(grad * unit)
        acc[10] += fold(grad)
        scaled = grad * vec(9)
        back = inverse * (
            scaled
            - jnp.mean(scaled, axis=1, keepdims=True)
            - unit * jnp.mean(scaled * unit, axis=1, keepdims=True)
        )
        sum_s[at, :] = back
        half = back.astype(BF16)
        gb_s[at, :] = half
        acc[8] += fold(half.astype(F32))

    over_rows(norm_two)
    store(0).start()
    for z in range(blocks):
        cols = slice(z * width, (z + 1) * width)
        gw2_s[cols, :] = mm_tn(act_s[:, cols], gb_s[...]).astype(BF16)
        if red is not None:
            red.pair_send(chunk, sources, z)

    def expand_back(at, i):
        grad = (mm_nt(gb_s[...], w2[at, :]) * slope_s[:, at].astype(F32)).astype(BF16)
        slope_s[:, at] = grad
        row = 11 + i // per
        cols = spot(lax.rem(i, per) * block, block, LANES)
        acc[row, :, cols] = acc[row, :, cols] + fold(grad.astype(F32))

    def hidden_back(at, i):
        sum_s[:, at] += mm_nt(slope_s[...], w1[at, :])

    def norm_one_back(at):
        grad, unit = sum_s[at, :], n1_s[at, :].astype(F32)
        acc[6] += fold(grad * unit)
        acc[7] += fold(grad)
        scaled = grad * vec(6)
        back = inv_s[at, 0:1] * (
            scaled
            - jnp.mean(scaled, axis=1, keepdims=True)
            - unit * jnp.mean(scaled * unit, axis=1, keepdims=True)
        )
        sum_s[at, :] = back
        half = back.astype(BF16)
        gb_s[at, :] = half
        acc[5] += fold(half.astype(F32))

    def merge(target, source, size):
        def one(z, carry):
            mine = spot((2 * z + here.core) * size, size, 16)
            target[z] = target[z] + source[mine, :]
            return carry

        lax.fori_loop(0, here.depth, one, 0)

    count = inner // block
    over_cols(0, count // 3, expand_back)
    if red is not None:
        red.pair_wait(chunk, sources)
        merge(chunk.total, gw2_s, deep)
        red.plane_send(chunk)
    over_cols(count // 3, count, expand_back)
    for c in range(blocks):
        cols = slice(c * width, (c + 1) * width)
        act_s[0:width, cols] = mm_tn(h1_s[...], slope_s[:, cols]).astype(BF16)
    if red is not None:
        red.pair_send(chunk_1, sources_1)
    over_cols(0, per, hidden_back)
    if red is not None:
        red.plane_turn(chunk)
        red.pair_wait(chunk_1, sources_1)
        merge(chunk_1.total, act_s, share)
    store(5).start()
    over_rows(norm_one_back)
    store(1).start()
    store(0).wait()
    io[...] = mm_nt(gb_s[...], wo[...]).astype(BF16)
    store(2).start()
    gwo_s[...] = mm_tn(ctx[...], gb_s[...]).astype(BF16)
    store(3).start()
    for row in range(acc.shape[0]):
        gvec_ref[row : row + 1, :] = jnp.sum(acc[row], axis=0, keepdims=True)
    if red is not None:
        red.plane_done(chunk)
    store(4).start()
    if red is not None:
        red.finish()
    for index in range(1, 6):
        store(index).wait()


def middle_call(narrow, x, ctx, cot, vec, e, w2):
    rows, width = x.shape
    inner = w2.shape[0]
    hbm, vmem = pl.BlockSpec(memory_space=pl.ANY), pl.BlockSpec(memory_space=pltpu.VMEM)
    shape = jax.ShapeDtypeStruct
    scratch, params = [], {}
    shape_w, shape_1 = (inner, width), (width, inner)
    if narrow is not None:
        depth, deep, share = narrow // 2, inner // narrow, width // narrow
        shape_w, shape_1 = (depth, deep // 2, width // 2), (depth, share, inner)
        scratch = [pltpu.SemaphoreType.DMA((2 * depth + 6,))] * 2
        scratch += [pltpu.VMEM((depth, deep, width), BF16), *plane_scratch(depth, deep, width)]
        scratch += [pltpu.VMEM((depth, share, inner), BF16)]
        params = dict(collective_id=2, has_side_effects=True)
    return pl.pallas_call(
        functools.partial(middle_kernel, narrow),
        in_specs=[hbm, hbm, hbm, vmem, hbm, hbm],
        out_specs=[hbm] * 6 + [vmem],
        out_shape=[
            shape((rows, width), BF16),
            shape((rows, width), F32),
            shape((rows, width), BF16),
            shape(shape_1, BF16),
            shape((width, width), BF16),
            shape(shape_w, BF16),
            shape(vec.shape, F32),
        ],
        scratch_shapes=[
            pltpu.VMEM((width, width), BF16),
            pltpu.VMEM((width, inner), BF16),
            pltpu.VMEM((inner, width), BF16),
            pltpu.VMEM((rows, width), BF16),
            pltpu.VMEM((rows, width), BF16),
            pltpu.VMEM((rows, width), BF16),
            pltpu.VMEM((rows, width), BF16),
            pltpu.VMEM((rows, LANES), F32),
            pltpu.VMEM((rows, inner), BF16),
            pltpu.VMEM((rows, inner), BF16),
            pltpu.VMEM((rows, width), BF16),
            pltpu.VMEM((rows, width), F32),
            pltpu.VMEM((inner, width), BF16),
            pltpu.VMEM((width, width), BF16),
            pltpu.VMEM((vec.shape[0], 8, width), F32),
            pltpu.SemaphoreType.DMA((12,)),
            *scratch,
        ],
        compiler_params=pltpu.CompilerParams(vmem_limit_bytes=VMEM_LIMIT, **params),
        name="middle",
    )(x, ctx, cot, vec, e, w2)


def input_grad_kernel(gp_ref, w_ref, gr1_ref, out_ref):
    out_ref[...] = (gr1_ref[...] + mm_nt(gp_ref[...], w_ref[...])).astype(BF16)


def input_grad_call(gp, w, gr1, size):
    rows, cols = gp.shape
    width = w.shape[0]
    return pl.pallas_call(
        input_grad_kernel,
        grid=(rows // size,),
        in_specs=[
            pl.BlockSpec((size, cols), lambda i: (i, 0)),
            pl.BlockSpec((width, cols), lambda i: (0, 0)),
            pl.BlockSpec((size, width), lambda i: (i, 0)),
        ],
        out_specs=pl.BlockSpec((size, width), lambda i: (i, 0)),
        out_shape=jax.ShapeDtypeStruct((rows, width), BF16),
        compiler_params=pltpu.CompilerParams(vmem_limit_bytes=VMEM_LIMIT),
        name="input_grad",
    )(gp, w, gr1)


def adam_update(master, first_old, second_old, grad_shard, factor, index):
    clipped = grad_shard * factor
    new_first = beta_one * first_old + (1.0 - beta_one) * clipped
    new_second = beta_two * second_old + (1.0 - beta_two) * clipped * clipped
    direction = (
        new_first
        / (1.0 - beta_one**STEP)
        / (jnp.sqrt(new_second / (1.0 - beta_two**STEP)) + adam_eps)
    )
    new_weight = master - rate_table[index] * (direction + decay_table[index] * master)
    return (new_weight, new_first, new_second)


def update_tile(master, first, second, grad, factor, index):
    weight, first, second = adam_update(master, first, second, grad.astype(F32), factor, index)
    return weight, first, second, weight.astype(BF16)


def update_kernel(narrow, n_ref, fa_ref, fo_ref, f1_ref, fw_ref, v_ref, *refs):
    ins, outs = refs[0:15], refs[15:35]
    heads = fa_ref.shape[1] // GROUP
    width = heads * HEAD
    norm = jnp.sqrt(n_ref[0:1, 0:1])
    factor = jnp.minimum(1.0, clip_limit / (norm + 1e-06))

    def store(index, rows, cols, grad):
        news = update_tile(*(ins[5 * t + index][rows, cols] for t in range(3)), grad, factor, index)
        for t, new in enumerate(news):
            outs[5 * t + index][rows, cols] = new

    every = slice(None)
    low = low_lanes(fa_ref.shape[0])
    for pair in range(heads // 2):
        at = 2 * pair * GROUP
        for b in range(3):
            even = fa_ref[:, at + b * LANES : at + (b + 1) * LANES].astype(F32)
            odd = fa_ref[:, at + GROUP + b * LANES : at + GROUP + (b + 1) * LANES].astype(F32)
            for second in range(2):
                if second:
                    grad = jnp.where(low, swap_halves(even), odd)
                else:
                    grad = jnp.where(low, even, swap_halves(odd))
                start = (2 * b + second) * width + pair * LANES
                store(0, every, slice(start, start + LANES), grad)
    store(1, every, every, fo_ref[...])
    store(2, every, every, f1_ref[...])
    store(3, every, every, fw_ref[...])

    @pl.when(pl.program_id(0) == 0)
    def _():
        count, span = ins[4].shape
        me = lax.axis_index("narrow")
        turned = pltpu.roll(v_ref[...], lax.rem(width - me * span, width), 1)
        store(4, every, every, turned[0:count, 0:span])


def update_call(narrow, norm, shards, vec, masters, firsts, seconds):
    share = shards[0].shape[0]
    steps = share // 16

    def rows_of(array_in):
        return pl.BlockSpec((array_in.shape[0] // steps, array_in.shape[1]), lambda i: (i, 0))

    def fixed(array_in):
        return pl.BlockSpec(array_in.shape, lambda i: (0, 0))

    def group(arrays):
        return [rows_of(a) for a in arrays[:4]] + [fixed(arrays[4])]

    def shapes(arrays, dtype):
        return [jax.ShapeDtypeStruct(a.shape, dtype) for a in arrays]

    return pl.pallas_call(
        functools.partial(update_kernel, narrow),
        grid=(steps,),
        in_specs=[fixed(norm), *(rows_of(a) for a in shards), fixed(vec)] + group(masters) * 3,
        out_specs=group(masters) * 4,
        out_shape=shapes(masters, F32) * 3 + shapes(masters, BF16),
        compiler_params=pltpu.CompilerParams(vmem_limit_bytes=VMEM_LIMIT),
        name="update",
    )(norm, *shards, vec, *masters, *firsts, *seconds)


def by_head(array_in):
    rows, cols = array_in.shape
    heads = cols // GROUP
    return array_in.reshape(rows, 6, heads, HEAD).transpose(0, 2, 1, 3).reshape(rows, cols)


def by_block(array_in):
    rows, cols = array_in.shape
    heads = cols // GROUP
    return array_in.reshape(rows, heads, 6, HEAD).transpose(0, 2, 1, 3).reshape(rows, cols)


def can_pass_pieces(wide, narrow, width, deep):
    share = width // narrow
    return wide == 4 and narrow % 2 == 0 and narrow > 2 and share % 32 == 0 and deep % 128 == 0 and 2 * deep == width


def body(
    x_in, cotangent, segment_ids, type_ids,
    projection, context_out, expand_weight, reduce_weight, vector_params,
    first_projection, first_context, first_expand, first_reduce, first_vectors,
    second_projection, second_context, second_expand, second_reduce, second_vectors,
):
    seq_count, seq_len, width = x_in.shape
    rows = seq_count * seq_len

    def gather(array_in, axis):
        return lax.all_gather(array_in.astype(BF16), "narrow", axis=axis, tiled=True)

    hidden = x_in.reshape(rows, width)
    cot = cotangent.reshape(rows, width)
    narrow = lax.axis_size("narrow")
    pieces = can_pass_pieces(lax.axis_size("wide"), narrow, width, reduce_weight.shape[0])
    if pieces:
        query, keyval, context, aug, proj_w, mid_w, reduce_w, vec_rows, word, kmask, kaug = gather_call(
            narrow, hidden, projection, context_out, expand_weight, reduce_weight, vector_params,
            segment_ids, type_ids,
        )
    else:
        word_col = (type_ids == 0).reshape(rows, 1)
        lane = lax.broadcasted_iota(jnp.int32, (rows, LANES), 1)
        word = jnp.broadcast_to(word_col, (rows, LANES)).astype(BF16)
        kmask = ((lane < HEAD) == word_col).astype(BF16)
        same = segment_ids.reshape(rows, 1) == lane
        qaug = jnp.where(same & (lane < 8), 1.0, 0.0).astype(BF16)
        kaug = jnp.where(lane < 8, jnp.where(same, 0.0, FAR), jnp.where(lane < 11, 1.0, 0.0)).astype(BF16)
        proj_w, vec_half = gather(by_head(projection), 0), gather(vector_params, 1)
        reduce_w = gather(reduce_weight, 0)
        mid_w = jnp.concatenate(
            [gather(expand_weight, 0), gather(context_out, 0), jnp.zeros((width, 2 * LANES), BF16)], axis=1
        )
        zero_row = jnp.zeros((1, width), BF16)
        bias = by_head(jnp.concatenate([vec_half[0:4], zero_row, vec_half[4:5]]).reshape(1, -1)).astype(F32)
        vec_rows = jnp.pad(vec_half.astype(F32), ((0, 1), (0, 0)))
        query, keyval = qkv_call(hidden, proj_w, bias, word)
        context, aug = attend_call(query, keyval, qaug, kaug, kmask, seq_len)
    block_out, grad_r1, grad_context, grad_expand, grad_ctx_w, grad_reduce, grad_mid = middle_call(
        narrow if pieces else None, hidden, context, cot, vec_rows, mid_w, reduce_w
    )
    masters = (projection, context_out, expand_weight, reduce_weight, vector_params)
    firsts = (first_projection, first_context, first_expand, first_reduce, first_vectors)
    seconds = (second_projection, second_context, second_expand, second_reduce, second_vectors)
    out_shape = (seq_count, seq_len, width)
    if pieces:
        input_grad, shard_1, shard_o, shard_w, shard_a, grad_vectors, norm = reduce_call(
            narrow, hidden, query, keyval, aug, grad_context, context, proj_w, kaug, kmask, word, grad_mid,
            grad_r1, grad_expand, grad_reduce, grad_ctx_w, reduce_weight.shape[0], seq_len,
        )
        shards = (shard_a, shard_o, shard_1, shard_w)
        updated = update_call(narrow, norm, shards, grad_vectors, masters, firsts, seconds)
        return (
            block_out.reshape(out_shape),
            input_grad.reshape(out_shape),
            jnp.sqrt(norm[0, 0]),
            *updated,
        )
    grad_proj, grad_proj_w, grad_sums = attend_back_call(
        hidden, query, keyval, aug, grad_context, context, kaug, kmask, word, seq_len
    )
    input_grad = input_grad_call(grad_proj, proj_w, grad_r1, 256)
    sum_rows = by_block(grad_sums).reshape(6, width)
    grad_vectors = jnp.concatenate([sum_rows[0:4], sum_rows[5:6], grad_mid[5:15]], axis=0)

    def scatter(array_in, axis):
        return lax.psum_scatter(array_in, "narrow", scatter_dimension=axis, tiled=True)

    def over_wide(array_in):
        return lax.psum(array_in.astype(BF16), "wide").astype(F32)

    shards = (
        by_block(over_wide(scatter(grad_proj_w, 0))),
        over_wide(scatter(grad_ctx_w, 0)),
        over_wide(scatter(grad_expand, 0)),
        over_wide(scatter(grad_reduce, 0)),
        over_wide(scatter(grad_vectors, 1)),
    )
    local_squares = sum((jnp.sum(shard_item * shard_item) for shard_item in shards))
    total_squares = lax.psum(local_squares, "narrow")
    grad_norm = jnp.sqrt(total_squares)
    factor = jnp.minimum(1.0, clip_limit / (grad_norm + 1e-06))
    results = [
        adam_update(masters[index], firsts[index], seconds[index], shards[index], factor, index)
        for index in range(5)
    ]
    return (
        block_out.reshape(out_shape),
        input_grad.reshape(out_shape),
        grad_norm,
        *(item[0] for item in results),
        *(item[1] for item in results),
        *(item[2] for item in results),
        *(item[0].astype(BF16) for item in results),
    )


def solution(mesh):
    shard, col = P("narrow", None), P(None, "narrow")
    seqs = P(("wide", "narrow"), None, None)
    group = (shard, shard, shard, shard, col)
    return jax.shard_map(
        body,
        mesh=mesh,
        in_specs=(seqs, seqs, P(("wide", "narrow"), None), P(("wide", "narrow"), None), *group, *group, *group),
        out_specs=(seqs, seqs, P(), *group, *group, *group, *group),
        check_vma=False,
    )
```

```python
import functools

import jax
import jax.numpy as jnp
from jax import lax
from jax.experimental import pallas as pl
from jax.experimental.pallas import tpu as pltpu
from jax.sharding import PartitionSpec as P

HEAD = 64
STEP = 10
LANES = 128
GROUP = 6 * HEAD
LOG2E = 1.4426950408889634
FAR = -1e30
VMEM_LIMIT = 60 * 1024 * 1024

beta_one = 0.9
beta_two = 0.999
adam_eps = 1e-08
norm_eps = 1e-05
clip_limit = 1.0
rate_table = (0.03, 0.3, 0.03, 0.015, 0.4)
decay_table = (0.01, 0.01, 0.01, 0.01, 0.0)

F32 = jnp.float32
BF16 = jnp.bfloat16


def mm(a, b):
    return lax.dot_general(a, b, (((1,), (0,)), ((), ())), preferred_element_type=F32)


def mm_nt(a, b):
    return lax.dot_general(a, b, (((1,), (1,)), ((), ())), preferred_element_type=F32)


def mm_tn(a, b):
    return lax.dot_general(a, b, (((0,), (0,)), ((), ())), preferred_element_type=F32)


def low_lanes(rows):
    return lax.broadcasted_iota(jnp.int32, (rows, LANES), 1) < HEAD


def swap_halves(tile):
    return pltpu.roll(tile, HEAD, 1)


def split_three(col):
    high = col.astype(BF16).astype(F32)
    rest = col - high
    mid = rest.astype(BF16).astype(F32)
    return high, mid, rest - mid


def qkv_tile(prod, bias, word):
    full = prod + bias
    query = jnp.where(word, full[:, 0:LANES], full[:, LANES : 2 * LANES])
    return (query.astype(BF16).astype(F32) * (HEAD**-0.5)).astype(BF16), full[
        :, 2 * LANES :
    ].astype(BF16)


def qkv_kernel(x_ref, w_ref, b_ref, word_ref, q_ref, kv_ref):
    word = word_ref[...] > 0
    for part in range(2):
        cols = slice(part * GROUP, (part + 1) * GROUP)
        query, keyval = qkv_tile(mm(x_ref[...], w_ref[:, cols]), b_ref[:, cols], word)
        out = slice(part * LANES, (part + 1) * LANES)
        q_ref[:, out] = query
        kv_ref[:, out] = keyval


def qkv_call(x, w, bias, word):
    rows, width = x.shape
    steps = w.shape[1] // (2 * GROUP)
    out = jax.ShapeDtypeStruct((rows, steps * 2 * LANES), BF16)
    return pl.pallas_call(
        qkv_kernel,
        grid=(steps,),
        in_specs=[
            pl.BlockSpec((rows, width), lambda i: (0, 0)),
            pl.BlockSpec((width, 2 * GROUP), lambda i: (0, i)),
            pl.BlockSpec((1, 2 * GROUP), lambda i: (0, i)),
            pl.BlockSpec((rows, LANES), lambda i: (0, 0)),
        ],
        out_specs=[pl.BlockSpec((rows, 2 * LANES), lambda i: (0, i))] * 2,
        out_shape=[out, out],
        compiler_params=pltpu.CompilerParams(vmem_limit_bytes=VMEM_LIMIT),
        name="qkv",
    )(x, w, bias, word)


class Links:
    def __init__(self, send, recv):
        self.send_sem, self.recv_sem = send, recv
        self.slots = {}
        self.sent = []

    def copy(self, key, src, dst, device):
        index = self.slots.setdefault(key, len(self.slots))
        return pltpu.make_async_remote_copy(
            src_ref=src,
            dst_ref=dst,
            send_sem=self.send_sem.at[index],
            recv_sem=self.recv_sem.at[index],
            device_id=device,
            device_id_type=pl.DeviceIdType.MESH,
        )

    def send(self, key, build, *guards):
        def start():
            self.copy(key, *build()).start()

        guarded(start, guards)
        self.sent.append((key, build, guards))

    def arrived(self, key, dst, device):
        self.copy(key, dst, dst, device).wait_recv()

    def finish(self):
        for key, build, guards in self.sent:

            def wait(key=key, build=build):
                self.copy(key, *build()).wait_send()

            guarded(wait, guards)


def guarded(action, guards):
    if not guards:
        action()
        return
    holds = guards[0]()
    for guard in guards[1:]:
        holds = jnp.logical_and(holds, guard())
    pl.when(holds)(action)


class Place:
    def __init__(self, narrow):
        self.wide, self.me = lax.axis_index("wide"), lax.axis_index("narrow")
        self.core = lax.rem(self.me, 2)
        self.z = self.me // 2
        self.depth = narrow // 2
        self.x_quarter = self.wide + 1 - 2 * lax.rem(self.wide, 2)
        self.y_quarter = lax.rem(self.wide + 2, 4)
        self.d_quarter = lax.rem(self.x_quarter + 2, 4)
        self.sib = self.me + 1 - 2 * self.core
        self.x_dev, self.y_dev = {"wide": self.x_quarter}, {"wide": self.y_quarter}
        self.d_dev = {"wide": self.d_quarter}
        self.sib_dev = {"narrow": self.sib}

    def ahead(self, k):
        return 2 * lax.rem(self.z + k, self.depth) + self.core

    def behind(self, k, other=False):
        core = 1 - self.core if other else self.core
        return 2 * lax.rem(self.z + self.depth - k, self.depth) + core

    def z_dev(self, k):
        return {"narrow": self.ahead(k)}

    def has_next(self, way):
        return lambda: self.z + 1 < self.depth if way == 0 else self.z > 0

    def comes(self, way, hop):
        return lambda: self.z >= hop if way == 0 else self.z + hop < self.depth

    def origin(self, way, hop, other=False):
        core = 1 - self.core if other else self.core
        return 2 * (self.z - hop if way == 0 else self.z + hop) + core

    def next_dev(self, way):
        return {"narrow": self.me + 2 if way == 0 else self.me - 2}

    def greet_near(self):
        barrier = pltpu.get_barrier_semaphore()

        def greet(device):
            pl.semaphore_signal(barrier, inc=1, device_id=device, device_id_type=pl.DeviceIdType.MESH)

        for device in (self.x_dev, self.y_dev, self.sib_dev):
            greet(device)
        for way in range(2):
            guarded(lambda way=way: greet(self.next_dev(way)), (self.has_next(way),))
        pl.semaphore_wait(barrier, 3 + jnp.minimum(self.z, 1) + jnp.minimum(self.depth - 1 - self.z, 1))

    def greet(self):
        barrier = pltpu.get_barrier_semaphore()
        partners = [self.x_dev, self.y_dev, self.d_dev, self.sib_dev] + [self.z_dev(k) for k in range(1, self.depth)]
        for device in partners:
            pl.semaphore_signal(barrier, inc=1, device_id=device, device_id_type=pl.DeviceIdType.MESH)
        pl.semaphore_wait(barrier, len(partners))


def spot(start, size, unit):
    return pl.ds(pl.multiple_of(start, unit), size)


def gather_kernel(
    narrow, x_ref, proj_ref, wo_ref, w1_ref, w2_ref, vec_ref, seg_ref, type_ref,
    q_out, kv_out, ctx_out, aug_out, a_out, e_out, w2_out, vec_out, word_ref, km_ref, ka_ref, xt_ref,
    a_full, e_own, w2_own, v_all, bias, q_s, kv_s, ctx_s, aug_s, qa_ref, send, recv, local,
):
    rows, width = x_ref.shape
    share = proj_ref.shape[0]
    deep = w2_ref.shape[0]
    half, quarter, equarter, dquarter = share // 2, proj_ref.shape[1] // 4, e_own.shape[1] // 4, deep // 4
    heads = width // HEAD
    here = Place(narrow)
    links = Links(send, recv)
    me, hops = here.me, range(1, here.depth)
    routes = [(way, hop) for hop in hops for way in range(2)]

    def region(kind, owner, part, side=None):
        size, start = (share, 0) if side is None else (half, side * half)
        if kind == "a":
            return a_full.at[spot(owner * share + start, size, 16), spot(part * quarter, quarter, LANES)]
        if kind == "e":
            return e_out.at[spot(owner * share + start, size, 16), spot(part * equarter, equarter, LANES)]
        size, start = (dquarter, 0) if side is None else (dquarter // 2, side * (dquarter // 2))
        return w2_out.at[spot(owner * deep + part * dquarter + start, size, 16), :]

    def whole(kind, owner):
        if kind == "a":
            return a_full.at[spot(owner * share, share, 16), :]
        if kind == "e":
            return e_out.at[spot(owner * share, share, 16), :]
        if kind == "w":
            return w2_out.at[spot(owner * deep, deep, 16), :]
        return v_all.at[owner]

    def own(kind):
        return {"a": whole("a", me), "e": e_own, "w": w2_own, "v": v_all.at[me]}[kind]

    def own_part(kind, part, side=None):
        if kind == "a":
            return region("a", me, part, side)
        if kind == "e":
            rows = slice(0, share) if side is None else slice(side * half, (side + 1) * half)
            return e_own.at[rows, spot(part * equarter, equarter, LANES)]
        size, start = (dquarter, 0) if side is None else (dquarter // 2, side * (dquarter // 2))
        return w2_own.at[spot(part * dquarter + start, size, 16), :]

    def send_own(kind):
        links.send((kind, "o"), lambda: (own(kind), whole(kind, me), here.sib_dev))

    def send_z(kind):
        for way in range(2):
            ahead = here.has_next(way)
            if kind == "v":
                links.send(("v", "z", way, 1), lambda way=way: (own("v"), own("v"), here.next_dev(way)), ahead)
                continue
            links.send(
                (kind, "z", way, 1),
                lambda way=way: (own_part(kind, here.wide), region(kind, me, here.wide), here.next_dev(way)),
                ahead,
            )
            if kind == "a":
                continue
            links.send(
                (kind, "h", way, 1),
                lambda way=way: (
                    own_part(kind, here.d_quarter, 0), region(kind, me, here.d_quarter, 0), here.next_dev(way)
                ),
                ahead,
            )

    def relay(key, target, device, *guards):
        links.send(key, lambda: (target(), target(), device()), *guards)

    def receive(key, target, guard):
        guarded(lambda: links.arrived(key, target(), here.sib_dev), (guard,))

    def pass_z(kind, hop):
        for way in range(2):
            comes, ahead = here.comes(way, hop), here.has_next(way)
            onward = lambda way=way: here.next_dev(way)
            if kind == "v":
                piece = lambda way=way: whole("v", here.origin(way, hop))
            else:
                piece = lambda way=way: region(kind, here.origin(way, hop), here.wide)
            receive((kind, "z", way, hop), piece, comes)
            if hop + 1 < here.depth:
                relay((kind, "z", way, hop + 1), piece, onward, comes, ahead)
            if kind != "v":
                relay((kind, "x", way, hop), piece, lambda: here.x_dev, comes)
                relay((kind, "y", way, hop), piece, lambda: here.y_dev, comes)
            relay((kind, "sz", way, hop), piece, lambda: here.sib_dev, comes)
            if kind not in "va":
                other = lambda way=way: region(kind, here.origin(way, hop), here.d_quarter, 0)
                receive((kind, "h", way, hop), other, comes)
                if hop + 1 < here.depth:
                    relay((kind, "h", way, hop + 1), other, onward, comes, ahead)
                relay((kind, "sh", way, hop), other, lambda: here.sib_dev, comes)

    def diagonal(kind, hop):
        by_y, by_x = ("x", 0 if kind == "a" else 1, here.y_dev), ("y", 1, here.x_dev)
        if kind == "a":
            return [by_y, by_x]
        return [by_x if (kind == "e") == (hop % 2 == 1) else by_y]

    def pass_xy(kind, hop):
        for way in range(2):
            comes = here.comes(way, hop)
            for name, part in (("x", here.x_quarter), ("y", here.y_quarter)):
                piece = lambda way=way, part=part: region(kind, here.origin(way, hop), part)
                receive((kind, name, way, hop), piece, comes)
                for back, side, device in diagonal(kind, hop):
                    if back == name:
                        rest = lambda way=way, part=part, side=side: region(kind, here.origin(way, hop), part, side)
                        relay((kind, "d", side, way, hop), rest, lambda device=device: device, comes)
                relay((kind, "s" + name, way, hop), piece, lambda: here.sib_dev, comes)

    def pass_d(kind, number):
        for way in range(2):
            comes = here.comes(way, number)
            for _, side, _ in diagonal(kind, number):
                rest = lambda way=way, side=side: region(kind, here.origin(way, number), here.d_quarter, side)
                receive((kind, "d", side, way, number), rest, comes)
                relay((kind, "sd", side, way, number), rest, lambda: here.sib_dev, comes)

    def from_sib(kind, name, part, side=None):
        if name == "sd":
            for side in range(2):
                if kind == "a" or side == 1:
                    from_sib(kind, ("sd", side), part, side)
                else:
                    from_sib(kind, "sh", part, side)
            return
        name = name if isinstance(name, tuple) else (name,)
        for way, hop in routes:
            piece = lambda way=way, hop=hop: region(kind, here.origin(way, hop, True), part, side)
            receive((kind, *name, way, hop), piece, here.comes(way, hop))

    low = low_lanes(share)
    for pair in range(heads // 2):
        tiles = [proj_ref[:, slice(b * width + pair * LANES, b * width + (pair + 1) * LANES)] for b in range(6)]
        turned = [swap_halves(tile) for tile in tiles]
        for odd in range(2):
            for b in range(3):
                left, right = (turned[2 * b], tiles[2 * b + 1]) if odd else (tiles[2 * b], turned[2 * b + 1])
                at = (2 * pair + odd) * GROUP + b * LANES
                a_full[spot(me * share, share, 16), at : at + LANES] = jnp.where(low, left, right).astype(BF16)
    v_all[me] = jnp.zeros_like(v_all[me])
    v_all[me, 0 : vec_ref.shape[0], 0 : vec_ref.shape[1]] = vec_ref[...].astype(BF16)

    here.greet_near()
    send_z("a")
    send_z("v")
    send_own("v")
    send_own("a")

    inner = w1_ref.shape[1]
    e_own[:, 0:inner] = w1_ref[...].astype(BF16)
    e_own[:, inner : inner + width] = wo_ref[...].astype(BF16)
    e_own[:, inner + width :] = jnp.zeros((share, e_own.shape[1] - inner - width), BF16)
    w2_own[...] = w2_ref[...].astype(BF16)
    copy_e = pltpu.make_async_copy(e_own, whole("e", me), local.at[0])
    copy_w = pltpu.make_async_copy(w2_own, whole("w", me), local.at[1])
    copy_e.start()
    copy_w.start()

    xt_ref[...] = jnp.transpose(x_ref[...])

    length = seg_ref.shape[1]
    lane = lax.broadcasted_iota(jnp.int32, (length, LANES), 1)
    for seq in range(seg_ref.shape[0]):
        at = slice(seq * length, (seq + 1) * length)
        segment, kind = (
            jnp.transpose(jnp.broadcast_to(ref[seq : seq + 1, :].astype(F32), (LANES, length)))
            for ref in (seg_ref, type_ref)
        )
        same = segment == lane.astype(F32)
        word = jnp.where(kind == 0.0, 1.0, 0.0)
        word_ref[at] = word.astype(BF16)
        km_ref[at] = jnp.where(lane < HEAD, word, 1.0 - word).astype(BF16)
        qa_ref[at] = jnp.where(same & (lane < 8), 1.0, 0.0).astype(BF16)
        ka_ref[at] = jnp.where(
            lane < 8, jnp.where(same, 0.0, FAR), jnp.where(lane < 11, 1.0, 0.0)
        ).astype(BF16)

    def hop(kind, number):
        if number < here.depth:
            pass_z(kind, number)
            if kind == "a":
                pass_z("v", number)

    def turn(kind, number):
        if number < here.depth:
            pass_xy(kind, number)

    deeper = range(4, here.depth)
    hop("a", 1)
    hop("a", 2)
    send_z("e")
    send_own("e")
    turn("a", 1)
    hop("a", 3)
    turn("a", 2)
    for number in deeper:
        hop("a", number)
        turn("a", number - 1)

    links.arrived(("v", "o"), v_all.at[here.sib], here.sib_dev)
    for way, number in routes:
        receive(
            ("v", "sz", way, number),
            lambda way=way, number=number: v_all.at[here.origin(way, number, True)],
            here.comes(way, number),
        )
    span = vec_ref.shape[1]
    vec_out[...] = jnp.concatenate([v_all[n].astype(F32)[:, 0:span] for n in range(narrow)], axis=1)
    low1 = low_lanes(1)
    for head in range(heads):
        cols = slice((head // 2) * LANES, (head // 2 + 1) * LANES)
        row = [vec_out[r : r + 1, cols] for r in range(4)] + [jnp.zeros((1, LANES), F32), vec_out[4:5, cols]]
        for b in range(3):
            left, right = row[2 * b], row[2 * b + 1]
            left, right = (swap_halves(left), right) if head % 2 else (left, swap_halves(right))
            at = head * GROUP + b * LANES
            bias[0:1, at : at + LANES] = jnp.where(low1, left, right)

    links.arrived(("a", "o"), whole("a", here.sib), here.sib_dev)
    outs = []

    def project(index, part):
        size = 256
        cols = spot(part * quarter, quarter, LANES)
        add = bias[0:1, cols]

        def tile(i, carry):
            at = spot(i * size, size, size)
            prod = mm(x_ref[at, :], a_full[:, cols])
            word = word_ref[at, :] > 0
            for head in range(quarter // GROUP):
                group = slice(head * GROUP, (head + 1) * GROUP)
                out = slice(head * LANES, (head + 1) * LANES)
                query, keyval = qkv_tile(prod[:, group], add[:, group], word)
                q_s[part, at, out] = query
                kv_s[part, at, out] = keyval
            return carry

        lax.fori_loop(0, rows // size, tile, 0)
        wide = q_s.shape[2]
        for number, (source, target) in enumerate(((q_s, q_out), (kv_s, kv_out))):
            copy = pltpu.make_async_copy(
                source.at[part], target.at[:, spot(part * wide, wide, LANES)], local.at[2 + 2 * index + number]
            )
            copy.start()
            outs.append(copy)

    from_sib("a", "sz", here.wide)
    project(0, here.wide)
    hop("e", 1)
    turn("a", here.depth - 1)
    from_sib("a", "sx", here.x_quarter)
    project(1, here.x_quarter)
    for number in hops:
        pass_d("a", number)
    hop("e", 2)
    send_z("w")
    send_own("w")
    turn("e", 1)
    from_sib("a", "sy", here.y_quarter)
    project(2, here.y_quarter)
    hop("e", 3)
    from_sib("a", "sd", here.d_quarter)
    project(3, here.d_quarter)
    copy_a = pltpu.make_async_copy(a_full, a_out, local.at[10])
    copy_a.start()
    low_seq = low_lanes(length)
    per = quarter // GROUP

    def attend(pair, seq):
        at = slice(seq * length, (seq + 1) * length)
        contexts = []
        for head in (2 * pair, 2 * pair + 1):
            cols = slice(head % per * LANES, (head % per + 1) * LANES)
            context, extra = attend_head(
                q_s[head // per, at, cols], kv_s[head // per, at, cols], qa_ref[at], ka_ref[at], km_ref[at]
            )
            aug_s[at, head * LANES : (head + 1) * LANES] = extra
            contexts.append(context)
        both = jnp.where(low_seq, swap_halves(contexts[0]), contexts[1])
        ctx_s[at, pair * LANES : (pair + 1) * LANES] = both.astype(BF16)

    def attended(pair):
        for number, (source, target, wide) in enumerate(((ctx_s, ctx_out, LANES), (aug_s, aug_out, 2 * LANES))):
            cols = slice(pair * wide, (pair + 1) * wide)
            copy = pltpu.make_async_copy(source.at[:, cols], target.at[:, cols], local.at[11 + 2 * pair + number])
            copy.start()
            outs.append(copy)

    def later(kind, first, last):
        for number in range(first, last):
            turn(kind, number)

    between = [
        lambda: [turn("e", 2), pass_d("e", 1)],
        lambda: hop("w", 1),
        lambda: [turn("e", 3), pass_d("e", 2)],
        lambda: [hop("w", 2), [hop("e", number) for number in deeper], later("e", 4, here.depth)],
        lambda: [turn("w", 1), [pass_d("e", number) for number in range(3, here.depth)]],
        lambda: hop("w", 3),
        lambda: [turn("w", 2), pass_d("w", 1)],
        lambda: [hop("w", number) for number in deeper],
        lambda: [later("w", 3, here.depth), pass_d("w", 2)],
        lambda: [pass_d("w", number) for number in range(3, here.depth)],
    ]
    units = [(pair, seq) for pair in range(heads // 2) for seq in range(seg_ref.shape[0])]
    for index, (pair, seq) in enumerate(units):
        attend(pair, seq)
        if seq == seg_ref.shape[0] - 1:
            attended(pair)
        if index < len(between):
            between[index]()
    for action in between[len(units) :]:
        action()
    for kind in ("e", "w"):
        links.arrived((kind, "o"), whole(kind, here.sib), here.sib_dev)
        for name, part in (("sz", here.wide), ("sx", here.x_quarter), ("sy", here.y_quarter)):
            from_sib(kind, name, part)
        from_sib(kind, "sd", here.d_quarter)
    links.finish()
    for copy in (copy_e, copy_w, copy_a, *outs):
        copy.wait()


def gather_call(narrow, x, proj, wo, w1, w2, vec, segments, types):
    rows, width = x.shape
    share, deep, inner = proj.shape[0], w2.shape[0], w1.shape[1]
    ecols = inner + width + 2 * LANES
    heads = width // HEAD
    depth = narrow // 2
    count = 3 * (1 + 20 * (depth - 1)) + 1 + 4 * (depth - 1)
    vmem = pl.BlockSpec(memory_space=pltpu.VMEM)
    hbm = pl.BlockSpec(memory_space=pl.ANY)
    shape = jax.ShapeDtypeStruct
    part = heads // 4 * LANES
    return pl.pallas_call(
        functools.partial(gather_kernel, narrow),
        in_specs=[vmem] * 8,
        out_specs=[hbm] * 7 + [vmem] * 5,
        out_shape=[
            shape((rows, heads * LANES), BF16),
            shape((rows, heads * LANES), BF16),
            shape((rows, width), BF16),
            shape((rows, heads * LANES), BF16),
            shape((width, proj.shape[1]), BF16),
            shape((width, ecols), BF16),
            shape((deep * narrow, width), BF16),
            shape((16, width), F32),
            shape((rows, LANES), BF16),
            shape((rows, LANES), BF16),
            shape((rows, LANES), BF16),
            shape((width, rows), BF16),
        ],
        scratch_shapes=[
            pltpu.VMEM((width, proj.shape[1]), BF16),
            pltpu.VMEM((share, ecols), BF16),
            pltpu.VMEM((deep, width), BF16),
            pltpu.VMEM((narrow, 16, LANES), BF16),
            pltpu.VMEM((8, proj.shape[1]), F32),
            pltpu.VMEM((4, rows, part), BF16),
            pltpu.VMEM((4, rows, part), BF16),
            pltpu.VMEM((rows, width), BF16),
            pltpu.VMEM((rows, heads * LANES), BF16),
            pltpu.VMEM((rows, LANES), BF16),
            pltpu.SemaphoreType.DMA((count,)),
            pltpu.SemaphoreType.DMA((count,)),
            pltpu.SemaphoreType.DMA((11 + heads,)),
        ],
        compiler_params=pltpu.CompilerParams(
            vmem_limit_bytes=VMEM_LIMIT, collective_id=0, has_side_effects=True
        ),
        name="gather",
    )(x, proj, wo, w1, w2, vec, segments, types)


def key_pair(keyval, kmask, low):
    wide = keyval.astype(F32)
    return (jnp.where(low, wide, swap_halves(wide)) * kmask.astype(F32)).astype(BF16)


def attend_head(query, keyval, qaug, kaug, kmask):
    rows = query.shape[0]
    low = low_lanes(rows)
    lane = lax.broadcasted_iota(jnp.int32, (rows, LANES), 1)
    keys = jnp.concatenate([key_pair(keyval, kmask, low), kaug], axis=1)
    scores = mm_nt(jnp.concatenate([query, qaug], axis=1), keys)
    top = jnp.max(scores, axis=1, keepdims=True)
    weight = jnp.exp2((scores - top) * LOG2E).astype(BF16)
    ones_val = jnp.where(low, 1.0, keyval.astype(F32)).astype(BF16)
    both = mm(weight, ones_val)
    total = swap_halves(both)
    log_total = top + jnp.log(jnp.where(low, both, total))
    high, mid, rest = split_three(log_total)
    extra = jnp.where(lane == 8, -high, jnp.where(lane == 9, -mid, jnp.where(lane == 10, -rest, 0.0)))
    return both / total, jnp.where(lane < 8, qaug.astype(F32), extra).astype(BF16)


def attend_kernel(q_ref, kv_ref, qa_ref, ka_ref, km_ref, ctx_ref, aug_ref):
    outs = []
    for part in range(2):
        cols = slice(part * LANES, (part + 1) * LANES)
        out, aug_ref[:, cols] = attend_head(q_ref[:, cols], kv_ref[:, cols], qa_ref[...], ka_ref[...], km_ref[...])
        outs.append(out)
    ctx_ref[...] = jnp.where(low_lanes(q_ref.shape[0]), swap_halves(outs[0]), outs[1]).astype(BF16)


def attend_call(q, kv, qa, ka, km, length):
    rows, cols = q.shape
    seqs, steps = rows // length, cols // (2 * LANES)
    pair = pl.BlockSpec((length, 2 * LANES), lambda s, i: (s, i))
    one = pl.BlockSpec((length, LANES), lambda s, i: (s, 0))
    return pl.pallas_call(
        attend_kernel,
        grid=(seqs, steps),
        in_specs=[pair, pair, one, one, one],
        out_specs=[pl.BlockSpec((length, LANES), lambda s, i: (s, i)), pair],
        out_shape=[
            jax.ShapeDtypeStruct((rows, cols // 2), BF16),
            jax.ShapeDtypeStruct((rows, cols), BF16),
        ],
        compiler_params=pltpu.CompilerParams(vmem_limit_bytes=VMEM_LIMIT),
        name="attend",
    )(q, kv, qa, ka, km)


def attend_back_head(query, keyval, aug, gcon, con, kaug, kmask, word, odd, low, lane):
    keys = key_pair(keyval, kmask, low)
    scores_t = mm_nt(jnp.concatenate([keys, kaug], axis=1), jnp.concatenate([query, aug], axis=1))
    probs_t = jnp.exp2(scores_t * LOG2E)
    gwide = gcon.astype(F32)
    prod = gwide * con.astype(F32)
    prod = jnp.where(low, 0.0, prod) if odd else jnp.where(low, prod, 0.0)
    high, mid, rest = split_three(jnp.sum(prod, axis=1, keepdims=True))
    extra = jnp.where(lane == 0, -high, jnp.where(lane == 1, -mid, jnp.where(lane == 2, -rest, 0.0)))
    ghead = jnp.where(low, extra, gwide if odd else swap_halves(gwide)).astype(BF16)
    ones_val = jnp.where(low, jnp.where(lane < 3, 1.0, 0.0), keyval.astype(F32)).astype(BF16)
    gscores_t = (probs_t * mm_nt(ones_val, ghead)).astype(BF16)
    blank = jnp.zeros_like(ghead)
    both = mm(
        jnp.concatenate([probs_t.astype(BF16), gscores_t], axis=1),
        jnp.concatenate(
            [jnp.concatenate([ghead, blank], axis=1), jnp.concatenate([blank, query], axis=1)], axis=0
        ),
    )
    gval, gkey = both[:, 0:LANES], both[:, LANES:]
    gquery = (jnp.transpose(mm_tn(keys, gscores_t)) * (HEAD**-0.5)).astype(BF16)
    zero = jnp.zeros_like(gquery)
    gkey = jnp.where(kmask.astype(F32) > 0, gkey, 0.0)
    gkey = gkey + swap_halves(gkey)
    return (
        jnp.where(word, gquery, zero),
        jnp.where(word, zero, gquery),
        jnp.where(low, gkey, gval).astype(BF16),
    )


def attend_back_kernel(
    length, x_ref, q_ref, kv_ref, aug_ref, gc_ref, ctx_ref, ka_ref, km_ref, word_ref, gp_ref, gw_ref, sum_ref, xt
):
    rows = x_ref.shape[0]

    @pl.when(pl.program_id(0) == 0)
    def _():
        xt[...] = jnp.transpose(x_ref[...])

    low = low_lanes(length)
    lane = lax.broadcasted_iota(jnp.int32, (length, LANES), 1)
    for part in range(2):
        cols = slice(part * LANES, (part + 1) * LANES)
        for seq in range(rows // length):
            here = slice(seq * length, (seq + 1) * length)
            tiles = attend_back_head(
                q_ref[here, cols], kv_ref[here, cols], aug_ref[here, cols], gc_ref[here], ctx_ref[here],
                ka_ref[here], km_ref[here], word_ref[here] > 0, part == 1, low, lane,
            )
            for index, tile in enumerate(tiles):
                at = part * GROUP + index * LANES
                gp_ref[here, at : at + LANES] = tile
    grads = gp_ref[...]
    gw_ref[...] = mm(xt[...], grads).astype(BF16)
    sum_ref[...] = jnp.sum(fold(grads.astype(F32)), axis=0, keepdims=True)


def attend_back_call(x, q, kv, aug, gc, ctx, ka, km, word, length):
    rows, width = x.shape
    pairs = q.shape[1] // (2 * LANES)
    head = pl.BlockSpec((rows, 2 * LANES), lambda h: (0, h))
    pair = pl.BlockSpec((rows, LANES), lambda h: (0, h))
    one = pl.BlockSpec((rows, LANES), lambda h: (0, 0))
    return pl.pallas_call(
        functools.partial(attend_back_kernel, length),
        grid=(pairs,),
        in_specs=[pl.BlockSpec((rows, width), lambda h: (0, 0)), head, head, head, pair, pair, one, one, one],
        out_specs=[
            pl.BlockSpec((rows, 2 * GROUP), lambda h: (0, h)),
            pl.BlockSpec((width, 2 * GROUP), lambda h: (0, h)),
            pl.BlockSpec((1, 2 * GROUP), lambda h: (0, h)),
        ],
        out_shape=[
            jax.ShapeDtypeStruct((rows, pairs * 2 * GROUP), BF16),
            jax.ShapeDtypeStruct((width, pairs * 2 * GROUP), BF16),
            jax.ShapeDtypeStruct((1, pairs * 2 * GROUP), F32),
        ],
        scratch_shapes=[pltpu.VMEM((width, rows), BF16)],
        compiler_params=pltpu.CompilerParams(vmem_limit_bytes=VMEM_LIMIT),
        name="attend_back",
    )(x, q, kv, aug, gc, ctx, ka, km, word)


class Chunk:
    def __init__(self, name, shape, total, plane=(), end=None, via=None):
        self.name = name
        self.rows, self.cols = shape
        self.total, self.via = total, via
        for label, ref in zip(("r1a", "r1b", "r2a", "r2b"), plane):
            setattr(self, label, ref)
        if end is not None:
            self.rz, self.final = end

    def row_half(self, wide):
        return spot(wide // 2 * (self.rows // 2), self.rows // 2, 16)

    def col_half(self, wide):
        return spot(lax.rem(wide, 2) * (self.cols // 2), self.cols // 2, LANES)

    def quarter(self, wide):
        return self.row_half(wide), self.col_half(wide)

    def mine(self, z, wide):
        if self.total.shape[1:] != (self.rows, self.cols):
            return self.total.at[z]
        return self.total.at[(z, *self.quarter(wide))]


def plane_scratch(depth, rows, cols):
    half = depth // 2
    return [
        pltpu.VMEM((half, rows, cols // 2), BF16),
        pltpu.VMEM((half, rows // 2, cols), BF16),
        pltpu.VMEM((half, rows // 2, cols // 2), BF16),
        pltpu.VMEM((half, rows // 2, cols // 2), BF16),
    ]


def end_scratch(depth, rows, cols):
    return [pltpu.VMEM((depth - 1, rows // 2, cols // 2), BF16), pltpu.VMEM((rows, cols), BF16)]


class Reducer:
    def __init__(self, here, send, recv):
        self.here = here
        self.links = Links(send, recv)
        self.send, self.arrived, self.finish = self.links.send, self.links.arrived, self.links.finish

    def pair_send(self, chunk, sources, only=None):
        here = self.here
        for z in range(here.depth) if only is None else (only,):
            for part, (_, cols) in enumerate(sources(0)):

                def build(z=z, part=part, cols=cols):
                    owner = 2 * z + 1 - here.core
                    return sources(owner)[part][0], chunk.total.at[z, :, cols], here.sib_dev

                self.send((chunk.name, "s", z, part), build)

    def pair_wait(self, chunk, sources):
        for z in range(self.here.depth):
            for part, (_, cols) in enumerate(sources(0)):
                self.arrived((chunk.name, "s", z, part), chunk.total.at[z, :, cols], self.here.sib_dev)

    def lower(self):
        return slice(0, self.here.depth // 2)

    def upper(self):
        return slice(self.here.depth // 2, self.here.depth)

    def plane_send(self, chunk):
        here = self.here
        cols, rows = (lambda: chunk.col_half(here.x_quarter)), (lambda: chunk.row_half(here.y_quarter))
        self.send((chunk.name, "1a"), lambda: (chunk.total.at[self.lower(), :, cols()], chunk.r1a, here.x_dev))
        self.send((chunk.name, "1b"), lambda: (chunk.total.at[self.upper(), rows(), :], chunk.r1b, here.y_dev))

    def plane_add(self, chunk):
        here = self.here
        total = chunk.total
        self.arrived((chunk.name, "1a"), chunk.r1a, here.x_dev)
        self.arrived((chunk.name, "1b"), chunk.r1b, here.y_dev)
        rows, cols = chunk.quarter(here.wide)
        total[self.lower(), :, cols] = total[self.lower(), :, cols] + chunk.r1a[...]
        total[self.upper(), rows, :] = total[self.upper(), rows, :] + chunk.r1b[...]

    def plane_next(self, chunk):
        here = self.here
        total = chunk.total

        def first():
            return total.at[(self.lower(), *chunk.quarter(here.y_quarter))], chunk.r2a, here.y_dev

        def second():
            return total.at[(self.upper(), *chunk.quarter(here.x_quarter))], chunk.r2b, here.x_dev

        self.send((chunk.name, "2a"), first)
        self.send((chunk.name, "2b"), second)

    def plane_turn(self, chunk):
        self.plane_add(chunk)
        self.plane_next(chunk)

    def plane_done(self, chunk):
        here = self.here
        self.arrived((chunk.name, "2a"), chunk.r2a, here.y_dev)
        self.arrived((chunk.name, "2b"), chunk.r2b, here.x_dev)
        rows, cols = chunk.quarter(here.wide)
        for part, value in ((self.lower(), chunk.r2a), (self.upper(), chunk.r2b)):
            chunk.total[part, rows, cols] = chunk.total[part, rows, cols] + value[...]

    def depth_send(self, chunk):
        here = self.here
        for k in range(1, here.depth):

            def build(k=k):
                piece = chunk.mine(lax.rem(here.z + k, here.depth), here.wide)
                return piece, chunk.rz.at[k - 1], here.z_dev(k)

            self.send((chunk.name, "z", k), build)

    def share_send(self, chunk):
        here = self.here
        for k in range(1, here.depth):
            self.arrived((chunk.name, "z", k), chunk.rz.at[k - 1], here.z_dev(k))
        done = chunk.mine(here.z, here.wide)[...].astype(F32)
        for k in range(1, here.depth):
            done = done + chunk.rz[k - 1].astype(F32)
        done = done.astype(BF16)
        rows, cols = chunk.quarter(here.wide)
        chunk.final[rows, cols] = done

        ways = [("fx", here.x_dev), ("fy", here.y_dev)] + ([] if chunk.via else [("fd", here.d_dev)])
        for name, device in ways:
            self.send((chunk.name, name), lambda device=device: self.share_copy(chunk, here.wide, device))
        return squares(done)

    def share_copy(self, chunk, quarter, device):
        piece = chunk.final.at[chunk.quarter(quarter)]
        return piece, piece, device

    def share_pass(self, chunk):
        here = self.here
        by_x = chunk.via == "x"
        name, quarter, device = ("fy", here.y_quarter, here.x_dev) if by_x else ("fx", here.x_quarter, here.y_dev)
        self.arrived((chunk.name, name), chunk.final.at[chunk.quarter(quarter)], device)
        self.send((chunk.name, "fd"), lambda: self.share_copy(chunk, quarter, device))

    def share_wait(self, chunk):
        here = self.here
        ways = (("fx", here.x_quarter, here.x_dev), ("fy", here.y_quarter, here.y_dev), ("fd", here.d_quarter, here.d_dev))
        seen = {"x": "fy", "y": "fx"}.get(chunk.via)
        for name, quarter, device in ways:
            if name != seen:
                self.arrived((chunk.name, name), chunk.final.at[chunk.quarter(quarter)], device)


def squares(value):
    total = jnp.zeros((8, LANES), F32)
    rows, cols = value.shape
    for start in range(0, cols, LANES):
        tile = value[:, start : start + LANES].astype(F32)
        total = total + jnp.sum((tile * tile).reshape(rows // 8, 8, LANES), axis=0)
    return total


def pair_groups(pairs):
    return (pairs // 3, pairs // 3, pairs // 6, pairs // 6)


def reduce_kernel(
    narrow, length, groups, deep,
    xt, q_ref, kv_ref, aug_ref, gc_ref, ctx_ref, wp_ref, ka_ref, km_ref, word_ref, gvec_ref,
    gr1_ref, t1_ref, tw_ref, gwo_ref,
    ig_ref, f1_ref, fo_ref, fw_ref, fa_ref, v_ref, n_ref,
    gp, ig, *scratch,
):
    step = pl.program_id(0)
    width, rows = xt.shape
    pairs = sum(groups)
    _, _, share, part = t1_ref.shape
    here = Place(narrow)
    scratch = list(scratch)
    red = Reducer(here, scratch[-3], scratch[-2])
    local = scratch[-1]

    def take(count):
        taken, scratch[:count] = scratch[:count], []
        return taken

    chunk_w = Chunk("w", (deep, width), take(1)[0], (), take(2), "x")
    chunk_1 = [Chunk(("1", j), (share, part), take(1)[0], take(4), take(2), "yx"[j]) for j in range(2)]
    gw, chunk_a = [], []
    for j in range(len(groups)):
        gw += take(1)
        via = ("y", "x", None, None)[j]
        chunk_a.append(Chunk(("a", j), (share, gw[j].shape[1]), take(1)[0], take(4), take(2), via))
    v0, v1, v2, vs, vx, vy, vz, n0, np, n1, ns, nz = take(12)
    begin = [sum(groups[:j]) for j in range(len(groups) + 1)]
    both = 2 * GROUP
    wide = groups[0] * both

    def sources_a(j):
        return lambda owner: [(gw[j].at[spot(owner * share, share, 16), :], slice(0, gw[j].shape[1]))]

    def load(index):
        source, target = (
            (t1_ref.at[0], chunk_1[0].total),
            (t1_ref.at[1], chunk_1[1].total),
            (tw_ref, chunk_w.total),
            (gwo_ref, gw[0].at[:, wide : wide + width]),
            (gr1_ref, ig),
        )[index]
        return pltpu.make_async_copy(source, target, local.at[index])

    def stores():
        copies = [(chunk_w.final, fw_ref)]
        copies += [(chunk.final, f1_ref.at[:, j * part : (j + 1) * part]) for j, chunk in enumerate(chunk_1)]
        copies += [(chunk_a[0].final.at[:, wide : wide + width], fo_ref)]
        for j, chunk in enumerate(chunk_a):
            cols = slice(begin[j] * both, begin[j + 1] * both)
            copies.append((chunk.final.at[:, 0 : groups[j] * both], fa_ref.at[:, cols]))
        return [pltpu.make_async_copy(a, b, local.at[5 + i]) for i, (a, b) in enumerate(copies)]

    def merge(j):
        def one(z, carry):
            mine = spot((2 * z + here.core) * share, share, 16)
            chunk_a[j].total[z] = chunk_a[j].total[z] + gw[j][mine, :]
            return carry

        red.pair_wait(chunk_a[j], sources_a(j))
        lax.fori_loop(0, here.depth, one, 0)
        red.plane_send(chunk_a[j])

    def turn_z(chunk):
        red.plane_done(chunk)
        red.depth_send(chunk)

    @pl.when(step == 0)
    def _():
        for index in range(5):
            load(index).start()
        here.greet()
        load(0).wait()
        red.plane_next(chunk_1[0])
        load(1).wait()
        red.plane_send(chunk_1[1])
        load(2).wait()
        red.depth_send(chunk_w)
        v0[...] = gvec_ref[...]
        n0[...] = jnp.zeros_like(n0)

    def at(when):
        def run(action):
            def body():
                action()

            pl.when(step == when)(body)

        return run

    def finish(chunk):
        n0[...] += red.share_send(chunk)

    def vec_pair():
        red.arrived(("v", "s"), vs, here.sib_dev)
        v1[...] = v0[...] + vs[...]
        red.send(("v", "x"), lambda: (v1, vx, here.x_dev))

    def vec_plane():
        red.arrived(("v", "x"), vx, here.x_dev)
        v2[...] = v1[...] + vx[...]
        red.send(("v", "y"), lambda: (v2, vy, here.y_dev))

    def vec_depth():
        red.arrived(("v", "y"), vy, here.y_dev)
        vz[here.z] = v2[...] + vy[...]
        for k in range(1, here.depth):
            red.send(("v", "z", k), lambda k=k: (vz.at[here.z], vz.at[here.z], here.z_dev(k)))

    def vec_done():
        for k in range(1, here.depth):
            red.arrived(("v", "z", k), vz.at[here.behind(k) // 2], here.z_dev(k))
        vec = vz[0]
        for z in range(1, here.depth):
            vec = vec + vz[z]
        v_ref[...] = vec

    a = chunk_a
    last = len(groups) - 1
    plan = {
        2: [lambda: load(3).wait(), lambda: turn_z(chunk_1[0])],
        3: [lambda: red.plane_turn(chunk_1[1])],
        4: [lambda: finish(chunk_w)],
        5: [lambda: merge(0), lambda: turn_z(chunk_1[1])],
        6: [lambda: red.share_pass(chunk_w)],
        7: [lambda: finish(chunk_1[0])],
        8: [lambda: red.plane_turn(a[0])],
        9: [lambda: merge(1), lambda: finish(chunk_1[1]), lambda: red.share_pass(chunk_1[0])],
        10: [lambda: turn_z(a[0])],
        11: [lambda: red.plane_turn(a[1]), lambda: merge(2), lambda: red.share_pass(chunk_1[1])],
    }
    tail = [
        [lambda: turn_z(a[1])],
        [lambda: merge(3), vec_pair, lambda: red.plane_turn(a[2])],
        [lambda: turn_z(a[2]), lambda: finish(a[0])],
        [lambda: red.plane_turn(a[3]), vec_plane],
        [lambda: turn_z(a[3]), lambda: finish(a[1]), lambda: red.share_pass(a[0]), vec_depth],
        [lambda: finish(a[2]), vec_done, lambda: red.share_pass(a[1])],
    ]

    def advance(half):
        for when, actions in plan.items():
            if when % 2 == half:
                for action in actions:
                    at(when // 2)(action)

    for index, actions in enumerate(tail):
        for action in actions:
            at(pairs + index)(action)

    @pl.when(step < pairs)
    def _():
        low = low_lanes(length)
        lane = lax.broadcasted_iota(jnp.int32, (length, LANES), 1)
        for part in range(2):
            advance(part)
            cols = slice(part * LANES, (part + 1) * LANES)
            for seq in range(rows // length):
                mine = slice(seq * length, (seq + 1) * length)
                tiles = attend_back_head(
                    q_ref[mine, cols], kv_ref[mine, cols], aug_ref[mine, cols], gc_ref[mine], ctx_ref[mine],
                    ka_ref[mine], km_ref[mine], word_ref[mine] > 0, part == 1, low, lane,
                )
                for index, tile in enumerate(tiles):
                    start = part * GROUP + index * LANES
                    gp[step, mine, start : start + LANES] = tile
        grads = gp[step]
        product = mm(xt[...], grads).astype(BF16)
        for j in range(len(groups)):

            @pl.when((step >= begin[j]) & (step < begin[j + 1]))
            def _():
                gw[j][:, spot((step - begin[j]) * both, both, LANES)] = product

        sums = jnp.sum(fold(grads.astype(F32)), axis=0, keepdims=True)
        low1 = low_lanes(1)
        place = spot(step * LANES, LANES, LANES)
        for b in range(3):
            even = sums[:, b * LANES : (b + 1) * LANES]
            odd = sums[:, GROUP + b * LANES : GROUP + (b + 1) * LANES]
            second = jnp.where(low1, swap_halves(even), odd)
            if b < 2:
                v0[2 * b : 2 * b + 1, place] = jnp.where(low1, even, swap_halves(odd))
                v0[2 * b + 1 : 2 * b + 2, place] = second
            else:
                v0[4:5, place] = second

    for j in range(len(groups)):
        at(begin[j + 1] - 1)(lambda j=j: red.pair_send(chunk_a[j], sources_a(j)))

    at(pairs - 1)(lambda: red.send(("v", "s"), lambda: (v0, vs, here.sib_dev)))
    at(pairs)(lambda: load(4).wait())

    @pl.when(step >= pairs)
    def _():
        ig[...] += mm_nt(gp[step - pairs], wp_ref[...])

    @pl.when(step == 2 * pairs - 1)
    def _():
        finish(a[last])
        np[here.wide] = n0[...]
        for name, device in (("nx", here.x_dev), ("ny", here.y_dev), ("nd", here.d_dev)):
            red.send((name,), lambda device=device: (np.at[here.wide], np.at[here.wide], device))
        vec = v_ref[...]
        square = jnp.sum(jnp.sum(vec * vec, axis=0, keepdims=True), axis=1, keepdims=True)
        ig_ref[...] = ig[...].astype(BF16)
        ways = (("nx", here.x_quarter, here.x_dev), ("ny", here.y_quarter, here.y_dev), ("nd", here.d_quarter, here.d_dev))
        for name, quarter, device in ways:
            red.arrived((name,), np.at[quarter], device)
        n1[...] = (np[0] + np[1]) + (np[2] + np[3])
        red.send(("n", "s"), lambda: (n1, ns, here.sib_dev))
        for chunk in (chunk_w, *chunk_1, *a):
            red.share_wait(chunk)
        for copy in stores():
            copy.start()
        red.arrived(("n", "s"), ns, here.sib_dev)
        nz[here.z] = n1[...] + ns[...]
        for k in range(1, here.depth):
            red.send(("n", "z", k), lambda k=k: (nz.at[here.z], nz.at[here.z], here.z_dev(k)))
        for k in range(1, here.depth):
            red.arrived(("n", "z", k), nz.at[here.behind(k) // 2], here.z_dev(k))
        total = nz[0]
        for z in range(1, here.depth):
            total = total + nz[z]
        every = jnp.sum(jnp.sum(total, axis=0, keepdims=True), axis=1, keepdims=True)
        n_ref[...] = jnp.broadcast_to(every + square, n_ref.shape)
        red.finish()
        for copy in stores():
            copy.wait()


def reduce_call(narrow, xt, q, kv, aug, gc, ctx, wp, ka, km, word, gvec, gr1, t1, tw, gwo, deep, length):
    width, rows = xt.shape
    pairs = q.shape[1] // (2 * LANES)
    groups = pair_groups(pairs)
    _, depth, share, inner = t1.shape

    def now(h):
        return jnp.minimum(h, pairs - 1)

    def fixed(shape):
        return pl.BlockSpec(shape, lambda h: (0, 0), pipeline_mode=pl.Buffered(1))

    head = pl.BlockSpec((rows, 2 * LANES), lambda h: (0, now(h)))
    pair = pl.BlockSpec((rows, LANES), lambda h: (0, now(h)))
    later = pl.BlockSpec((width, 2 * GROUP), lambda h: (0, jnp.maximum(h - pairs, 0)))
    one = fixed((rows, LANES))
    hbm = pl.BlockSpec(memory_space=pl.ANY)
    shape = jax.ShapeDtypeStruct
    vec = pltpu.VMEM((16, width), F32)
    tile = pltpu.VMEM((8, LANES), F32)
    scratch = [pltpu.VMEM((pairs, rows, 2 * GROUP), BF16), pltpu.VMEM((rows, width), F32)]
    scratch += [pltpu.VMEM(tw.shape, BF16), *end_scratch(depth, deep, width)]
    for _ in range(2):
        scratch += [pltpu.VMEM((depth, share, inner), BF16)]
        scratch += [*plane_scratch(depth, share, inner), *end_scratch(depth, share, inner)]
    for j, size in enumerate(groups):
        cols = size * 2 * GROUP + (width if j == 0 else 0)
        scratch += [
            pltpu.VMEM((width, cols), BF16),
            pltpu.VMEM((depth, share, cols), BF16),
            *plane_scratch(depth, share, cols),
            *end_scratch(depth, share, cols),
        ]
    several = pltpu.VMEM((depth, 8, LANES), F32)
    scratch += [vec] * 6 + [pltpu.VMEM((depth, 16, width), F32), tile, pltpu.VMEM((4, 8, LANES), F32), tile, tile, several]
    count = (3 + len(groups)) * (2 * depth + 6) + 2 * (4 + depth)
    scratch += [pltpu.SemaphoreType.DMA((count,))] * 2 + [pltpu.SemaphoreType.DMA((9 + len(groups),))]
    return pl.pallas_call(
        functools.partial(reduce_kernel, narrow, length, groups, deep),
        grid=(2 * pairs,),
        in_specs=[
            fixed((width, rows)), head, head, head, pair, pair, later, one, one, one, fixed((16, width)),
            hbm, hbm, hbm, hbm,
        ],
        out_specs=[fixed((rows, width)), hbm, hbm, hbm, hbm, fixed((16, width)), fixed((8, LANES))],
        out_shape=[
            shape((rows, width), BF16),
            shape((share, 2 * inner), BF16),
            shape((share, width), BF16),
            shape((deep, width), BF16),
            shape((share, pairs * 2 * GROUP), BF16),
            shape((16, width), F32),
            shape((8, LANES), F32),
        ],
        scratch_shapes=scratch,
        compiler_params=pltpu.CompilerParams(
            vmem_limit_bytes=VMEM_LIMIT, collective_id=1, has_side_effects=True
        ),
        name="reduce",
    )(xt, q, kv, aug, gc, ctx, wp, ka, km, word, gvec, gr1, t1, tw, gwo)


def gelu_pair(pre):
    bell = jnp.exp2(pre * pre * (-0.5 * LOG2E))
    share = 0.5 + 0.5 * lax.erf(pre * (0.5**0.5))
    return pre * share, share + pre * bell * 0.3989422804014327


def fold(array_in):
    rows, cols = array_in.shape
    return jnp.sum(array_in.reshape(rows // 8, 8, cols), axis=0)


def middle_kernel(
    narrow, x_hbm, ctx_hbm, cot_hbm, vec_ref, e_hbm, w2_hbm,
    out_hbm, gr1_hbm, gctx_hbm, gw1_hbm, gwo_hbm, gw2_hbm, gvec_ref,
    wo, w1, w2, io, ctx, h1_s, n1_s, inv_s, act_s, slope_s, gb_s, sum_s, gw2_s, gwo_s, acc, sems, *scratch,
):
    rows, width = io.shape
    inner = w1.shape[1]
    blocks, size, block = inner // width, 256, 256
    red = None

    def load(index):
        source, target = (
            (x_hbm, io),
            (ctx_hbm, ctx),
            (e_hbm.at[:, inner : inner + width], wo),
            (e_hbm.at[:, 0:inner], w1),
            (w2_hbm, w2),
            (cot_hbm, io),
        )[index]
        return pltpu.make_async_copy(source, target, sems.at[index])

    def store(index):
        source, target = (
            (io, out_hbm),
            (sum_s, gr1_hbm),
            (io, gctx_hbm),
            (gwo_s, gwo_hbm),
            (gw2_s, gw2_hbm) if red is None else (chunk.total.at[(slice(None), *chunk.quarter(here.wide))], gw2_hbm),
            (act_s.at[0:width, :], gw1_hbm) if red is None else (chunk_1[0].total, gw1_hbm.at[0]),
            None if red is None else (chunk_1[1].total, gw1_hbm.at[1]),
        )[index]
        return pltpu.make_async_copy(source, target, sems.at[6 + index])

    def vec(row):
        return vec_ref[row : row + 1, :].astype(F32)

    def over_rows(step):
        def one(i, carry):
            step(spot(i * size, size, size))
            return carry

        lax.fori_loop(0, rows // size, one, 0)

    def over_cols(first, last, step):
        def one(i, carry):
            step(spot(i * block, block, block), i)
            return carry

        lax.fori_loop(first, last, one, 0)

    for index in (1, 2, 0, 3, 4):
        load(index).start()
    acc[...] = jnp.zeros_like(acc)
    if narrow is not None:
        here = Place(narrow)
        red = Reducer(here, scratch[0], scratch[1])
        deep, share = scratch[2].shape[1], scratch[7].shape[1]
        chunk = Chunk("w", (deep, width), scratch[2], scratch[3:7])
        part = inner // 2
        chunk_1 = [Chunk(("1", j), (share, part), scratch[7 + 3 * j], scratch[8:10] if j == 0 else ()) for j in range(2)]
        here.greet()

        def sources(owner):
            return [(gw2_s.at[spot(owner * deep, deep, 16), :], slice(0, width))]

        def sources_1(j):
            cols = slice(j * part, (j + 1) * part)
            return lambda owner: [(act_s.at[spot(owner * share, share, 16), cols], slice(0, part))]

    for index in (1, 2, 0):
        load(index).wait()

    def norm_one(at):
        resid = io[at, :].astype(F32) + mm(ctx[at, :], wo[...]) + vec(5)
        center = resid - jnp.mean(resid, axis=1, keepdims=True)
        inverse = lax.rsqrt(jnp.mean(center * center, axis=1, keepdims=True) + norm_eps)
        unit = center * inverse
        hidden = unit * vec(6) + vec(7)
        n1_s[at, :] = unit.astype(BF16)
        inv_s[at, :] = jnp.broadcast_to(inverse, (size, LANES))
        h1_s[at, :] = hidden.astype(BF16)
        sum_s[at, :] = hidden + vec(8)

    over_rows(norm_one)
    load(5).start()
    load(3).wait()
    per = width // block

    def expand(at, i):
        bias = vec_ref[11 + i // per, spot(lax.rem(i, per) * block, block, LANES)].astype(F32).reshape(1, block)
        act, slope = gelu_pair(mm(h1_s[...], w1[:, at]) + bias)
        act_s[:, at] = act.astype(BF16)
        slope_s[:, at] = slope.astype(BF16)

    over_cols(0, inner // block, expand)
    load(4).wait()

    def reduce(at, i):
        sum_s[:, at] += mm(act_s[...], w2[:, at])

    over_cols(0, per, reduce)
    load(5).wait()

    def norm_two(at):
        resid = sum_s[at, :]
        center = resid - jnp.mean(resid, axis=1, keepdims=True)
        inverse = lax.rsqrt(jnp.mean(center * center, axis=1, keepdims=True) + norm_eps)
        unit = center * inverse
        grad = io[at, :].astype(F32)
        io[at, :] = (unit * vec(9) + vec(10)).astype(BF16)
        acc[9] += fold(grad * unit)
        acc[10] += fold(grad)
        scaled = grad * vec(9)
        back = inverse * (
            scaled
            - jnp.mean(scaled, axis=1, keepdims=True)
            - unit * jnp.mean(scaled * unit, axis=1, keepdims=True)
        )
        sum_s[at, :] = back
        half = back.astype(BF16)
        gb_s[at, :] = half
        acc[8] += fold(half.astype(F32))

    over_rows(norm_two)
    store(0).start()
    for z in range(blocks):
        cols = slice(z * width, (z + 1) * width)
        gw2_s[cols, :] = mm_tn(act_s[:, cols], gb_s[...]).astype(BF16)
        if red is not None:
            red.pair_send(chunk, sources, z)

    def expand_back(at, i):
        grad = (mm_nt(gb_s[...], w2[at, :]) * slope_s[:, at].astype(F32)).astype(BF16)
        slope_s[:, at] = grad
        row = 11 + i // per
        cols = spot(lax.rem(i, per) * block, block, LANES)
        acc[row, :, cols] = acc[row, :, cols] + fold(grad.astype(F32))

    def hidden_back(at, i):
        sum_s[:, at] += mm_nt(slope_s[...], w1[at, :])

    def norm_one_back(at):
        grad, unit = sum_s[at, :], n1_s[at, :].astype(F32)
        acc[6] += fold(grad * unit)
        acc[7] += fold(grad)
        scaled = grad * vec(6)
        back = inv_s[at, 0:1] * (
            scaled
            - jnp.mean(scaled, axis=1, keepdims=True)
            - unit * jnp.mean(scaled * unit, axis=1, keepdims=True)
        )
        sum_s[at, :] = back
        half = back.astype(BF16)
        gb_s[at, :] = half
        acc[5] += fold(half.astype(F32))

    def merge(target, source, size):
        def one(z, carry):
            mine = spot((2 * z + here.core) * size, size, 16)
            target[z] = target[z] + source(mine)
            return carry

        lax.fori_loop(0, here.depth, one, 0)

    def merge_1(j):
        red.pair_wait(chunk_1[j], sources_1(j))
        merge(chunk_1[j].total, lambda mine: act_s[mine, j * part : (j + 1) * part], share)

    count = inner // block
    over_cols(0, count // 3, expand_back)
    if red is not None:
        red.pair_wait(chunk, sources)
        merge(chunk.total, lambda mine: gw2_s[mine, :], deep)
        red.plane_send(chunk)
    over_cols(count // 3, count, expand_back)
    for c in range(blocks):
        cols = slice(c * width, (c + 1) * width)
        act_s[0:width, cols] = mm_tn(h1_s[...], slope_s[:, cols]).astype(BF16)
        if red is not None and (c + 1) % (blocks // 2) == 0:
            red.pair_send(chunk_1[c // (blocks // 2)], sources_1(c // (blocks // 2)))
    over_cols(0, 1, hidden_back)
    if red is not None:
        merge_1(0)
        red.plane_send(chunk_1[0])
    over_cols(1, per, hidden_back)
    if red is not None:
        red.plane_turn(chunk)
        merge_1(1)
        store(6).start()
    else:
        store(5).start()
    over_rows(norm_one_back)
    store(1).start()
    store(0).wait()
    io[...] = mm_nt(gb_s[...], wo[...]).astype(BF16)
    store(2).start()
    gwo_s[...] = mm_tn(ctx[...], gb_s[...]).astype(BF16)
    store(3).start()
    for row in range(acc.shape[0]):
        gvec_ref[row : row + 1, :] = jnp.sum(acc[row], axis=0, keepdims=True)
    if red is not None:
        red.plane_done(chunk)
    store(4).start()
    if red is not None:
        red.plane_add(chunk_1[0])
        store(5).start()
        red.finish()
    for index in range(1, 6 if red is None else 7):
        store(index).wait()


def middle_call(narrow, x, ctx, cot, vec, e, w2):
    rows, width = x.shape
    inner = w2.shape[0]
    hbm, vmem = pl.BlockSpec(memory_space=pl.ANY), pl.BlockSpec(memory_space=pltpu.VMEM)
    shape = jax.ShapeDtypeStruct
    scratch, params = [], {}
    shape_w, shape_1 = (inner, width), (width, inner)
    if narrow is not None:
        depth, deep, share = narrow // 2, inner // narrow, width // narrow
        part = inner // 2
        shape_w, shape_1 = (depth, deep // 2, width // 2), (2, depth, share, part)
        scratch = [pltpu.SemaphoreType.DMA((3 * depth + 8,))] * 2
        scratch += [pltpu.VMEM((depth, deep, width), BF16), *plane_scratch(depth, deep, width)]
        scratch += [pltpu.VMEM((depth, share, part), BF16), *plane_scratch(depth, share, part)[0:2]]
        scratch += [pltpu.VMEM((depth, share, part), BF16)]
        params = dict(collective_id=2, has_side_effects=True)
    return pl.pallas_call(
        functools.partial(middle_kernel, narrow),
        in_specs=[hbm, hbm, hbm, vmem, hbm, hbm],
        out_specs=[hbm] * 6 + [vmem],
        out_shape=[
            shape((rows, width), BF16),
            shape((rows, width), F32),
            shape((rows, width), BF16),
            shape(shape_1, BF16),
            shape((width, width), BF16),
            shape(shape_w, BF16),
            shape(vec.shape, F32),
        ],
        scratch_shapes=[
            pltpu.VMEM((width, width), BF16),
            pltpu.VMEM((width, inner), BF16),
            pltpu.VMEM((inner, width), BF16),
            pltpu.VMEM((rows, width), BF16),
            pltpu.VMEM((rows, width), BF16),
            pltpu.VMEM((rows, width), BF16),
            pltpu.VMEM((rows, width), BF16),
            pltpu.VMEM((rows, LANES), F32),
            pltpu.VMEM((rows, inner), BF16),
            pltpu.VMEM((rows, inner), BF16),
            pltpu.VMEM((rows, width), BF16),
            pltpu.VMEM((rows, width), F32),
            pltpu.VMEM((inner, width), BF16),
            pltpu.VMEM((width, width), BF16),
            pltpu.VMEM((vec.shape[0], 8, width), F32),
            pltpu.SemaphoreType.DMA((13,)),
            *scratch,
        ],
        compiler_params=pltpu.CompilerParams(vmem_limit_bytes=VMEM_LIMIT, **params),
        name="middle",
    )(x, ctx, cot, vec, e, w2)


def input_grad_kernel(gp_ref, w_ref, gr1_ref, out_ref):
    out_ref[...] = (gr1_ref[...] + mm_nt(gp_ref[...], w_ref[...])).astype(BF16)


def input_grad_call(gp, w, gr1, size):
    rows, cols = gp.shape
    width = w.shape[0]
    return pl.pallas_call(
        input_grad_kernel,
        grid=(rows // size,),
        in_specs=[
            pl.BlockSpec((size, cols), lambda i: (i, 0)),
            pl.BlockSpec((width, cols), lambda i: (0, 0)),
            pl.BlockSpec((size, width), lambda i: (i, 0)),
        ],
        out_specs=pl.BlockSpec((size, width), lambda i: (i, 0)),
        out_shape=jax.ShapeDtypeStruct((rows, width), BF16),
        compiler_params=pltpu.CompilerParams(vmem_limit_bytes=VMEM_LIMIT),
        name="input_grad",
    )(gp, w, gr1)


def adam_update(master, first_old, second_old, grad_shard, factor, index):
    clipped = grad_shard * factor
    new_first = beta_one * first_old + (1.0 - beta_one) * clipped
    new_second = beta_two * second_old + (1.0 - beta_two) * clipped * clipped
    direction = (
        new_first
        / (1.0 - beta_one**STEP)
        / (jnp.sqrt(new_second / (1.0 - beta_two**STEP)) + adam_eps)
    )
    new_weight = master - rate_table[index] * (direction + decay_table[index] * master)
    return (new_weight, new_first, new_second)


def update_tile(master, first, second, grad, factor, index):
    weight, first, second = adam_update(master, first, second, grad.astype(F32), factor, index)
    return weight, first, second, weight.astype(BF16)


def update_kernel(narrow, n_ref, fa_ref, fo_ref, f1_ref, fw_ref, v_ref, *refs):
    ins, outs = refs[0:15], refs[15:35]
    heads = fa_ref.shape[1] // GROUP
    width = heads * HEAD
    norm = jnp.sqrt(n_ref[0:1, 0:1])
    factor = jnp.minimum(1.0, clip_limit / (norm + 1e-06))

    def store(index, rows, cols, grad):
        news = update_tile(*(ins[5 * t + index][rows, cols] for t in range(3)), grad, factor, index)
        for t, new in enumerate(news):
            outs[5 * t + index][rows, cols] = new

    every = slice(None)
    low = low_lanes(fa_ref.shape[0])
    for pair in range(heads // 2):
        at = 2 * pair * GROUP
        for b in range(3):
            even = fa_ref[:, at + b * LANES : at + (b + 1) * LANES].astype(F32)
            odd = fa_ref[:, at + GROUP + b * LANES : at + GROUP + (b + 1) * LANES].astype(F32)
            for second in range(2):
                if second:
                    grad = jnp.where(low, swap_halves(even), odd)
                else:
                    grad = jnp.where(low, even, swap_halves(odd))
                start = (2 * b + second) * width + pair * LANES
                store(0, every, slice(start, start + LANES), grad)
    store(1, every, every, fo_ref[...])
    store(2, every, every, f1_ref[...])
    store(3, every, every, fw_ref[...])

    @pl.when(pl.program_id(0) == 0)
    def _():
        count, span = ins[4].shape
        me = lax.axis_index("narrow")
        turned = pltpu.roll(v_ref[...], lax.rem(width - me * span, width), 1)
        store(4, every, every, turned[0:count, 0:span])


def update_call(narrow, norm, shards, vec, masters, firsts, seconds):
    share = shards[0].shape[0]
    steps = share // 48 if share % 48 == 0 else share // 16

    def rows_of(array_in):
        return pl.BlockSpec((array_in.shape[0] // steps, array_in.shape[1]), lambda i: (i, 0))

    def fixed(array_in):
        return pl.BlockSpec(array_in.shape, lambda i: (0, 0))

    def group(arrays):
        return [rows_of(a) for a in arrays[:4]] + [fixed(arrays[4])]

    def shapes(arrays, dtype):
        return [jax.ShapeDtypeStruct(a.shape, dtype) for a in arrays]

    return pl.pallas_call(
        functools.partial(update_kernel, narrow),
        grid=(steps,),
        in_specs=[fixed(norm), *(rows_of(a) for a in shards), fixed(vec)] + group(masters) * 3,
        out_specs=group(masters) * 4,
        out_shape=shapes(masters, F32) * 3 + shapes(masters, BF16),
        compiler_params=pltpu.CompilerParams(vmem_limit_bytes=VMEM_LIMIT),
        name="update",
    )(norm, *shards, vec, *masters, *firsts, *seconds)


def by_head(array_in):
    rows, cols = array_in.shape
    heads = cols // GROUP
    return array_in.reshape(rows, 6, heads, HEAD).transpose(0, 2, 1, 3).reshape(rows, cols)


def by_block(array_in):
    rows, cols = array_in.shape
    heads = cols // GROUP
    return array_in.reshape(rows, heads, 6, HEAD).transpose(0, 2, 1, 3).reshape(rows, cols)


def can_pass_pieces(wide, narrow, width, deep):
    share = width // narrow
    return wide == 4 and narrow % 2 == 0 and narrow > 2 and share % 32 == 0 and deep % 128 == 0 and 2 * deep == width


def body(
    x_in, cotangent, segment_ids, type_ids,
    projection, context_out, expand_weight, reduce_weight, vector_params,
    first_projection, first_context, first_expand, first_reduce, first_vectors,
    second_projection, second_context, second_expand, second_reduce, second_vectors,
):
    seq_count, seq_len, width = x_in.shape
    rows = seq_count * seq_len

    def gather(array_in, axis):
        return lax.all_gather(array_in.astype(BF16), "narrow", axis=axis, tiled=True)

    hidden = x_in.reshape(rows, width)
    cot = cotangent.reshape(rows, width)
    narrow = lax.axis_size("narrow")
    pieces = can_pass_pieces(lax.axis_size("wide"), narrow, width, reduce_weight.shape[0])
    if pieces:
        query, keyval, context, aug, proj_w, mid_w, reduce_w, vec_rows, word, kmask, kaug, turned = gather_call(
            narrow, hidden, projection, context_out, expand_weight, reduce_weight, vector_params,
            segment_ids, type_ids,
        )
    else:
        word_col = (type_ids == 0).reshape(rows, 1)
        lane = lax.broadcasted_iota(jnp.int32, (rows, LANES), 1)
        word = jnp.broadcast_to(word_col, (rows, LANES)).astype(BF16)
        kmask = ((lane < HEAD) == word_col).astype(BF16)
        same = segment_ids.reshape(rows, 1) == lane
        qaug = jnp.where(same & (lane < 8), 1.0, 0.0).astype(BF16)
        kaug = jnp.where(lane < 8, jnp.where(same, 0.0, FAR), jnp.where(lane < 11, 1.0, 0.0)).astype(BF16)
        proj_w, vec_half = gather(by_head(projection), 0), gather(vector_params, 1)
        reduce_w = gather(reduce_weight, 0)
        mid_w = jnp.concatenate(
            [gather(expand_weight, 0), gather(context_out, 0), jnp.zeros((width, 2 * LANES), BF16)], axis=1
        )
        zero_row = jnp.zeros((1, width), BF16)
        bias = by_head(jnp.concatenate([vec_half[0:4], zero_row, vec_half[4:5]]).reshape(1, -1)).astype(F32)
        vec_rows = jnp.pad(vec_half.astype(F32), ((0, 1), (0, 0)))
        query, keyval = qkv_call(hidden, proj_w, bias, word)
        context, aug = attend_call(query, keyval, qaug, kaug, kmask, seq_len)
    block_out, grad_r1, grad_context, grad_expand, grad_ctx_w, grad_reduce, grad_mid = middle_call(
        narrow if pieces else None, hidden, context, cot, vec_rows, mid_w, reduce_w
    )
    masters = (projection, context_out, expand_weight, reduce_weight, vector_params)
    firsts = (first_projection, first_context, first_expand, first_reduce, first_vectors)
    seconds = (second_projection, second_context, second_expand, second_reduce, second_vectors)
    out_shape = (seq_count, seq_len, width)
    if pieces:
        input_grad, shard_1, shard_o, shard_w, shard_a, grad_vectors, norm = reduce_call(
            narrow, turned, query, keyval, aug, grad_context, context, proj_w, kaug, kmask, word, grad_mid,
            grad_r1, grad_expand, grad_reduce, grad_ctx_w, reduce_weight.shape[0], seq_len,
        )
        shards = (shard_a, shard_o, shard_1, shard_w)
        updated = update_call(narrow, norm, shards, grad_vectors, masters, firsts, seconds)
        return (
            block_out.reshape(out_shape),
            input_grad.reshape(out_shape),
            jnp.sqrt(norm[0, 0]),
            *updated,
        )
    grad_proj, grad_proj_w, grad_sums = attend_back_call(
        hidden, query, keyval, aug, grad_context, context, kaug, kmask, word, seq_len
    )
    input_grad = input_grad_call(grad_proj, proj_w, grad_r1, 256)
    sum_rows = by_block(grad_sums).reshape(6, width)
    grad_vectors = jnp.concatenate([sum_rows[0:4], sum_rows[5:6], grad_mid[5:15]], axis=0)

    def scatter(array_in, axis):
        return lax.psum_scatter(array_in, "narrow", scatter_dimension=axis, tiled=True)

    def over_wide(array_in):
        return lax.psum(array_in.astype(BF16), "wide").astype(F32)

    shards = (
        by_block(over_wide(scatter(grad_proj_w, 0))),
        over_wide(scatter(grad_ctx_w, 0)),
        over_wide(scatter(grad_expand, 0)),
        over_wide(scatter(grad_reduce, 0)),
        over_wide(scatter(grad_vectors, 1)),
    )
    local_squares = sum((jnp.sum(shard_item * shard_item) for shard_item in shards))
    total_squares = lax.psum(local_squares, "narrow")
    grad_norm = jnp.sqrt(total_squares)
    factor = jnp.minimum(1.0, clip_limit / (grad_norm + 1e-06))
    results = [
        adam_update(masters[index], firsts[index], seconds[index], shards[index], factor, index)
        for index in range(5)
    ]
    return (
        block_out.reshape(out_shape),
        input_grad.reshape(out_shape),
        grad_norm,
        *(item[0] for item in results),
        *(item[1] for item in results),
        *(item[2] for item in results),
        *(item[0].astype(BF16) for item in results),
    )


def solution(mesh):
    shard, col = P("narrow", None), P(None, "narrow")
    seqs = P(("wide", "narrow"), None, None)
    group = (shard, shard, shard, shard, col)
    return jax.shard_map(
        body,
        mesh=mesh,
        in_specs=(seqs, seqs, P(("wide", "narrow"), None), P(("wide", "narrow"), None), *group, *group, *group),
        out_specs=(seqs, seqs, P(), *group, *group, *group, *group),
        check_vma=False,
    )
```

```python
import functools

import jax
import jax.numpy as jnp
from jax import lax
from jax.experimental import pallas as pl
from jax.experimental.pallas import tpu as pltpu
from jax.sharding import PartitionSpec as P

HEAD = 64
STEP = 10
LANES = 128
GROUP = 6 * HEAD
LOG2E = 1.4426950408889634
FAR = -1e30
VMEM_LIMIT = 60 * 1024 * 1024

beta_one = 0.9
beta_two = 0.999
adam_eps = 1e-08
norm_eps = 1e-05
clip_limit = 1.0
rate_table = (0.03, 0.3, 0.03, 0.015, 0.4)
decay_table = (0.01, 0.01, 0.01, 0.01, 0.0)

F32 = jnp.float32
BF16 = jnp.bfloat16


def mm(a, b):
    return lax.dot_general(a, b, (((1,), (0,)), ((), ())), preferred_element_type=F32)


def mm_nt(a, b):
    return lax.dot_general(a, b, (((1,), (1,)), ((), ())), preferred_element_type=F32)


def mm_tn(a, b):
    return lax.dot_general(a, b, (((0,), (0,)), ((), ())), preferred_element_type=F32)


def low_lanes(rows):
    return lax.broadcasted_iota(jnp.int32, (rows, LANES), 1) < HEAD


def swap_halves(tile):
    return pltpu.roll(tile, HEAD, 1)


def split_three(col):
    high = col.astype(BF16).astype(F32)
    rest = col - high
    mid = rest.astype(BF16).astype(F32)
    return high, mid, rest - mid


def qkv_tile(prod, bias, word):
    full = prod + bias
    query = jnp.where(word, full[:, 0:LANES], full[:, LANES : 2 * LANES])
    return (query.astype(BF16).astype(F32) * (HEAD**-0.5)).astype(BF16), full[
        :, 2 * LANES :
    ].astype(BF16)


def qkv_kernel(x_ref, w_ref, b_ref, word_ref, q_ref, kv_ref):
    word = word_ref[...] > 0
    for part in range(2):
        cols = slice(part * GROUP, (part + 1) * GROUP)
        query, keyval = qkv_tile(mm(x_ref[...], w_ref[:, cols]), b_ref[:, cols], word)
        out = slice(part * LANES, (part + 1) * LANES)
        q_ref[:, out] = query
        kv_ref[:, out] = keyval


def qkv_call(x, w, bias, word):
    rows, width = x.shape
    steps = w.shape[1] // (2 * GROUP)
    out = jax.ShapeDtypeStruct((rows, steps * 2 * LANES), BF16)
    return pl.pallas_call(
        qkv_kernel,
        grid=(steps,),
        in_specs=[
            pl.BlockSpec((rows, width), lambda i: (0, 0)),
            pl.BlockSpec((width, 2 * GROUP), lambda i: (0, i)),
            pl.BlockSpec((1, 2 * GROUP), lambda i: (0, i)),
            pl.BlockSpec((rows, LANES), lambda i: (0, 0)),
        ],
        out_specs=[pl.BlockSpec((rows, 2 * LANES), lambda i: (0, i))] * 2,
        out_shape=[out, out],
        compiler_params=pltpu.CompilerParams(vmem_limit_bytes=VMEM_LIMIT),
        name="qkv",
    )(x, w, bias, word)


class Links:
    def __init__(self, send, recv):
        self.send_sem, self.recv_sem = send, recv
        self.slots = {}
        self.sent = []

    def copy(self, key, src, dst, device):
        index = self.slots.setdefault(key, len(self.slots))
        return pltpu.make_async_remote_copy(
            src_ref=src,
            dst_ref=dst,
            send_sem=self.send_sem.at[index],
            recv_sem=self.recv_sem.at[index],
            device_id=device,
            device_id_type=pl.DeviceIdType.MESH,
        )

    def send(self, key, build, *guards):
        def start():
            self.copy(key, *build()).start()

        guarded(start, guards)
        self.sent.append((key, build, guards))

    def arrived(self, key, dst, device):
        self.copy(key, dst, dst, device).wait_recv()

    def finish(self):
        for key, build, guards in self.sent:

            def wait(key=key, build=build):
                self.copy(key, *build()).wait_send()

            guarded(wait, guards)


def guarded(action, guards):
    if not guards:
        action()
        return
    holds = guards[0]()
    for guard in guards[1:]:
        holds = jnp.logical_and(holds, guard())
    pl.when(holds)(action)


class Place:
    def __init__(self, narrow):
        self.wide, self.me = lax.axis_index("wide"), lax.axis_index("narrow")
        self.core = lax.rem(self.me, 2)
        self.z = self.me // 2
        self.depth = narrow // 2
        self.x_quarter = self.wide + 1 - 2 * lax.rem(self.wide, 2)
        self.y_quarter = lax.rem(self.wide + 2, 4)
        self.d_quarter = lax.rem(self.x_quarter + 2, 4)
        self.sib = self.me + 1 - 2 * self.core
        self.x_dev, self.y_dev = {"wide": self.x_quarter}, {"wide": self.y_quarter}
        self.d_dev = {"wide": self.d_quarter}
        self.sib_dev = {"narrow": self.sib}

    def ahead(self, k):
        return 2 * lax.rem(self.z + k, self.depth) + self.core

    def behind(self, k, other=False):
        core = 1 - self.core if other else self.core
        return 2 * lax.rem(self.z + self.depth - k, self.depth) + core

    def z_dev(self, k):
        return {"narrow": self.ahead(k)}

    def has_next(self, way):
        return lambda: self.z + 1 < self.depth if way == 0 else self.z > 0

    def comes(self, way, hop):
        return lambda: self.z >= hop if way == 0 else self.z + hop < self.depth

    def origin(self, way, hop, other=False):
        core = 1 - self.core if other else self.core
        return 2 * (self.z - hop if way == 0 else self.z + hop) + core

    def next_dev(self, way):
        return {"narrow": self.me + 2 if way == 0 else self.me - 2}

    def greet_near(self):
        barrier = pltpu.get_barrier_semaphore()

        def greet(device):
            pl.semaphore_signal(barrier, inc=1, device_id=device, device_id_type=pl.DeviceIdType.MESH)

        for device in (self.x_dev, self.y_dev, self.sib_dev):
            greet(device)
        for way in range(2):
            guarded(lambda way=way: greet(self.next_dev(way)), (self.has_next(way),))
        pl.semaphore_wait(barrier, 3 + jnp.minimum(self.z, 1) + jnp.minimum(self.depth - 1 - self.z, 1))

    def greet(self):
        barrier = pltpu.get_barrier_semaphore()
        partners = [self.x_dev, self.y_dev, self.d_dev, self.sib_dev] + [self.z_dev(k) for k in range(1, self.depth)]
        for device in partners:
            pl.semaphore_signal(barrier, inc=1, device_id=device, device_id_type=pl.DeviceIdType.MESH)
        pl.semaphore_wait(barrier, len(partners))


def spot(start, size, unit):
    return pl.ds(pl.multiple_of(start, unit), size)


def gather_kernel(
    narrow, proj_ref, vec_ref, seg_ref, type_ref, x_hbm, wo_hbm, w1_hbm, w2_hbm,
    q_out, kv_out, ctx_out, aug_out, a_out, e_out, w2_out, vec_out, word_ref, km_ref, ka_ref, xt_ref,
    a_full, e_own, w2_own, v_all, bias, q_s, kv_s, ctx_s, aug_s, qa_ref, x_ref, wo_ref, w1_ref, w2_ref, send, recv, local,
):
    rows, width = x_ref.shape
    share = proj_ref.shape[0]
    deep = w2_ref.shape[0]
    half, quarter, equarter, dquarter = share // 2, proj_ref.shape[1] // 4, e_own.shape[1] // 4, deep // 4
    heads = width // HEAD
    here = Place(narrow)
    links = Links(send, recv)
    last = local.shape[0]
    loads = [
        pltpu.make_async_copy(source, target, local.at[last - 4 + index])
        for index, (source, target) in enumerate(
            ((x_hbm, x_ref), (w1_hbm, w1_ref), (wo_hbm, wo_ref), (w2_hbm, w2_ref))
        )
    ]
    for copy in loads:
        copy.start()
    me, hops = here.me, range(1, here.depth)
    routes = [(way, hop) for hop in hops for way in range(2)]

    def region(kind, owner, part, side=None):
        size, start = (share, 0) if side is None else (half, side * half)
        if kind == "a":
            return a_full.at[spot(owner * share + start, size, 16), spot(part * quarter, quarter, LANES)]
        if kind == "e":
            return e_out.at[spot(owner * share + start, size, 16), spot(part * equarter, equarter, LANES)]
        size, start = (dquarter, 0) if side is None else (dquarter // 2, side * (dquarter // 2))
        return w2_out.at[spot(owner * deep + part * dquarter + start, size, 16), :]

    def whole(kind, owner):
        if kind == "a":
            return a_full.at[spot(owner * share, share, 16), :]
        if kind == "e":
            return e_out.at[spot(owner * share, share, 16), :]
        if kind == "w":
            return w2_out.at[spot(owner * deep, deep, 16), :]
        return v_all.at[owner]

    def own(kind):
        return {"a": whole("a", me), "e": e_own, "w": w2_own, "v": v_all.at[me]}[kind]

    def own_part(kind, part, side=None):
        if kind == "a":
            return region("a", me, part, side)
        if kind == "e":
            rows = slice(0, share) if side is None else slice(side * half, (side + 1) * half)
            return e_own.at[rows, spot(part * equarter, equarter, LANES)]
        size, start = (dquarter, 0) if side is None else (dquarter // 2, side * (dquarter // 2))
        return w2_own.at[spot(part * dquarter + start, size, 16), :]

    def send_own(kind):
        links.send((kind, "o"), lambda: (own(kind), whole(kind, me), here.sib_dev))

    def send_z(kind):
        for way in range(2):
            ahead = here.has_next(way)
            if kind == "v":
                links.send(("v", "z", way, 1), lambda way=way: (own("v"), own("v"), here.next_dev(way)), ahead)
                continue
            links.send(
                (kind, "z", way, 1),
                lambda way=way: (own_part(kind, here.wide), region(kind, me, here.wide), here.next_dev(way)),
                ahead,
            )
            if kind == "a":
                continue
            links.send(
                (kind, "h", way, 1),
                lambda way=way: (
                    own_part(kind, here.d_quarter, 0), region(kind, me, here.d_quarter, 0), here.next_dev(way)
                ),
                ahead,
            )

    def relay(key, target, device, *guards):
        links.send(key, lambda: (target(), target(), device()), *guards)

    def receive(key, target, guard):
        guarded(lambda: links.arrived(key, target(), here.sib_dev), (guard,))

    def pass_z(kind, hop):
        for way in range(2):
            comes, ahead = here.comes(way, hop), here.has_next(way)
            onward = lambda way=way: here.next_dev(way)
            if kind == "v":
                piece = lambda way=way: whole("v", here.origin(way, hop))
            else:
                piece = lambda way=way: region(kind, here.origin(way, hop), here.wide)
            receive((kind, "z", way, hop), piece, comes)
            if hop + 1 < here.depth:
                relay((kind, "z", way, hop + 1), piece, onward, comes, ahead)
            if kind != "v":
                relay((kind, "x", way, hop), piece, lambda: here.x_dev, comes)
                relay((kind, "y", way, hop), piece, lambda: here.y_dev, comes)
            relay((kind, "sz", way, hop), piece, lambda: here.sib_dev, comes)
            if kind not in "va":
                other = lambda way=way: region(kind, here.origin(way, hop), here.d_quarter, 0)
                receive((kind, "h", way, hop), other, comes)
                if hop + 1 < here.depth:
                    relay((kind, "h", way, hop + 1), other, onward, comes, ahead)
                relay((kind, "sh", way, hop), other, lambda: here.sib_dev, comes)

    def diagonal(kind, hop):
        by_y, by_x = ("x", 0 if kind == "a" else 1, here.y_dev), ("y", 1, here.x_dev)
        if kind == "a":
            return [by_y, by_x]
        return [by_x if (kind == "e") == (hop % 2 == 1) else by_y]

    def pass_xy(kind, hop):
        for way in range(2):
            comes = here.comes(way, hop)
            for name, part in (("x", here.x_quarter), ("y", here.y_quarter)):
                piece = lambda way=way, part=part: region(kind, here.origin(way, hop), part)
                receive((kind, name, way, hop), piece, comes)
                for back, side, device in diagonal(kind, hop):
                    if back == name:
                        rest = lambda way=way, part=part, side=side: region(kind, here.origin(way, hop), part, side)
                        relay((kind, "d", side, way, hop), rest, lambda device=device: device, comes)
                relay((kind, "s" + name, way, hop), piece, lambda: here.sib_dev, comes)

    def pass_d(kind, number):
        for way in range(2):
            comes = here.comes(way, number)
            for _, side, _ in diagonal(kind, number):
                rest = lambda way=way, side=side: region(kind, here.origin(way, number), here.d_quarter, side)
                receive((kind, "d", side, way, number), rest, comes)
                relay((kind, "sd", side, way, number), rest, lambda: here.sib_dev, comes)

    def from_sib(kind, name, part, side=None):
        if name == "sd":
            for side in range(2):
                if kind == "a" or side == 1:
                    from_sib(kind, ("sd", side), part, side)
                else:
                    from_sib(kind, "sh", part, side)
            return
        name = name if isinstance(name, tuple) else (name,)
        for way, hop in routes:
            piece = lambda way=way, hop=hop: region(kind, here.origin(way, hop, True), part, side)
            receive((kind, *name, way, hop), piece, here.comes(way, hop))

    low = low_lanes(share)
    for pair in range(heads // 2):
        tiles = [proj_ref[:, slice(b * width + pair * LANES, b * width + (pair + 1) * LANES)] for b in range(6)]
        turned = [swap_halves(tile) for tile in tiles]
        for odd in range(2):
            for b in range(3):
                left, right = (turned[2 * b], tiles[2 * b + 1]) if odd else (tiles[2 * b], turned[2 * b + 1])
                at = (2 * pair + odd) * GROUP + b * LANES
                a_full[spot(me * share, share, 16), at : at + LANES] = jnp.where(low, left, right).astype(BF16)
    v_all[me] = jnp.zeros_like(v_all[me])
    v_all[me, 0 : vec_ref.shape[0], 0 : vec_ref.shape[1]] = vec_ref[...].astype(BF16)

    here.greet_near()
    send_z("a")
    send_z("v")
    send_own("v")
    send_own("a")

    for copy in loads:
        copy.wait()
    inner = w1_ref.shape[1]
    e_own[:, 0:inner] = w1_ref[...].astype(BF16)
    e_own[:, inner : inner + width] = wo_ref[...].astype(BF16)
    e_own[:, inner + width :] = jnp.zeros((share, e_own.shape[1] - inner - width), BF16)
    w2_own[...] = w2_ref[...].astype(BF16)
    copy_e = pltpu.make_async_copy(e_own, whole("e", me), local.at[0])
    copy_w = pltpu.make_async_copy(w2_own, whole("w", me), local.at[1])
    copy_e.start()
    copy_w.start()

    xt_ref[...] = jnp.transpose(x_ref[...])

    length = seg_ref.shape[1]
    lane = lax.broadcasted_iota(jnp.int32, (length, LANES), 1)
    for seq in range(seg_ref.shape[0]):
        at = slice(seq * length, (seq + 1) * length)
        segment, kind = (
            jnp.transpose(jnp.broadcast_to(ref[seq : seq + 1, :].astype(F32), (LANES, length)))
            for ref in (seg_ref, type_ref)
        )
        same = segment == lane.astype(F32)
        word = jnp.where(kind == 0.0, 1.0, 0.0)
        word_ref[at] = word.astype(BF16)
        km_ref[at] = jnp.where(lane < HEAD, word, 1.0 - word).astype(BF16)
        qa_ref[at] = jnp.where(same & (lane < 8), 1.0, 0.0).astype(BF16)
        ka_ref[at] = jnp.where(
            lane < 8, jnp.where(same, 0.0, FAR), jnp.where(lane < 11, 1.0, 0.0)
        ).astype(BF16)

    def hop(kind, number):
        if number < here.depth:
            pass_z(kind, number)
            if kind == "a":
                pass_z("v", number)

    def turn(kind, number):
        if number < here.depth:
            pass_xy(kind, number)

    deeper = range(4, here.depth)
    hop("a", 1)
    hop("a", 2)
    send_z("e")
    send_own("e")
    turn("a", 1)
    hop("a", 3)
    turn("a", 2)
    for number in deeper:
        hop("a", number)
        turn("a", number - 1)

    links.arrived(("v", "o"), v_all.at[here.sib], here.sib_dev)
    for way, number in routes:
        receive(
            ("v", "sz", way, number),
            lambda way=way, number=number: v_all.at[here.origin(way, number, True)],
            here.comes(way, number),
        )
    span = vec_ref.shape[1]
    vec_out[...] = jnp.concatenate([v_all[n].astype(F32)[:, 0:span] for n in range(narrow)], axis=1)
    low1 = low_lanes(1)
    for head in range(heads):
        cols = slice((head // 2) * LANES, (head // 2 + 1) * LANES)
        row = [vec_out[r : r + 1, cols] for r in range(4)] + [jnp.zeros((1, LANES), F32), vec_out[4:5, cols]]
        for b in range(3):
            left, right = row[2 * b], row[2 * b + 1]
            left, right = (swap_halves(left), right) if head % 2 else (left, swap_halves(right))
            at = head * GROUP + b * LANES
            bias[0:1, at : at + LANES] = jnp.where(low1, left, right)

    links.arrived(("a", "o"), whole("a", here.sib), here.sib_dev)
    outs = []

    def project(index, part):
        size = 256
        cols = spot(part * quarter, quarter, LANES)
        add = bias[0:1, cols]

        def tile(i, carry):
            at = spot(i * size, size, size)
            prod = mm(x_ref[at, :], a_full[:, cols])
            word = word_ref[at, :] > 0
            for head in range(quarter // GROUP):
                group = slice(head * GROUP, (head + 1) * GROUP)
                out = slice(head * LANES, (head + 1) * LANES)
                query, keyval = qkv_tile(prod[:, group], add[:, group], word)
                q_s[part, at, out] = query
                kv_s[part, at, out] = keyval
            return carry

        lax.fori_loop(0, rows // size, tile, 0)
        wide = q_s.shape[2]
        for number, (source, target) in enumerate(((q_s, q_out), (kv_s, kv_out))):
            copy = pltpu.make_async_copy(
                source.at[part], target.at[:, spot(part * wide, wide, LANES)], local.at[2 + 2 * index + number]
            )
            copy.start()
            outs.append(copy)

    from_sib("a", "sz", here.wide)
    project(0, here.wide)
    hop("e", 1)
    turn("a", here.depth - 1)
    from_sib("a", "sx", here.x_quarter)
    project(1, here.x_quarter)
    for number in hops:
        pass_d("a", number)
    hop("e", 2)
    send_z("w")
    send_own("w")
    turn("e", 1)
    from_sib("a", "sy", here.y_quarter)
    project(2, here.y_quarter)
    hop("e", 3)
    from_sib("a", "sd", here.d_quarter)
    project(3, here.d_quarter)
    copy_a = pltpu.make_async_copy(a_full, a_out, local.at[10])
    copy_a.start()
    low_seq = low_lanes(length)
    per = quarter // GROUP

    def attend(pair, seq):
        at = slice(seq * length, (seq + 1) * length)
        contexts = []
        for head in (2 * pair, 2 * pair + 1):
            cols = slice(head % per * LANES, (head % per + 1) * LANES)
            context, extra = attend_head(
                q_s[head // per, at, cols], kv_s[head // per, at, cols], qa_ref[at], ka_ref[at], km_ref[at]
            )
            aug_s[at, head * LANES : (head + 1) * LANES] = extra
            contexts.append(context)
        both = jnp.where(low_seq, swap_halves(contexts[0]), contexts[1])
        ctx_s[at, pair * LANES : (pair + 1) * LANES] = both.astype(BF16)

    def attended(pair):
        for number, (source, target, wide) in enumerate(((ctx_s, ctx_out, LANES), (aug_s, aug_out, 2 * LANES))):
            cols = slice(pair * wide, (pair + 1) * wide)
            copy = pltpu.make_async_copy(source.at[:, cols], target.at[:, cols], local.at[11 + 2 * pair + number])
            copy.start()
            outs.append(copy)

    def later(kind, first, last):
        for number in range(first, last):
            turn(kind, number)

    between = [
        lambda: [turn("e", 2), pass_d("e", 1)],
        lambda: hop("w", 1),
        lambda: [turn("e", 3), pass_d("e", 2)],
        lambda: [hop("w", 2), [hop("e", number) for number in deeper], later("e", 4, here.depth)],
        lambda: [turn("w", 1), [pass_d("e", number) for number in range(3, here.depth)]],
        lambda: hop("w", 3),
        lambda: [turn("w", 2), pass_d("w", 1)],
        lambda: [hop("w", number) for number in deeper],
        lambda: [later("w", 3, here.depth), pass_d("w", 2)],
        lambda: [pass_d("w", number) for number in range(3, here.depth)],
    ]
    units = [(pair, seq) for pair in range(heads // 2) for seq in range(seg_ref.shape[0])]
    for index, (pair, seq) in enumerate(units):
        attend(pair, seq)
        if seq == seg_ref.shape[0] - 1:
            attended(pair)
        if index < len(between):
            between[index]()
    for action in between[len(units) :]:
        action()
    for kind in ("e", "w"):
        links.arrived((kind, "o"), whole(kind, here.sib), here.sib_dev)
        for name, part in (("sz", here.wide), ("sx", here.x_quarter), ("sy", here.y_quarter)):
            from_sib(kind, name, part)
        from_sib(kind, "sd", here.d_quarter)
    links.finish()
    for copy in (copy_e, copy_w, copy_a, *outs):
        copy.wait()


def gather_call(narrow, x, proj, wo, w1, w2, vec, segments, types):
    rows, width = x.shape
    share, deep, inner = proj.shape[0], w2.shape[0], w1.shape[1]
    ecols = inner + width + 2 * LANES
    heads = width // HEAD
    depth = narrow // 2
    count = 3 * (1 + 20 * (depth - 1)) + 1 + 4 * (depth - 1)
    vmem = pl.BlockSpec(memory_space=pltpu.VMEM)
    hbm = pl.BlockSpec(memory_space=pl.ANY)
    shape = jax.ShapeDtypeStruct
    part = heads // 4 * LANES
    return pl.pallas_call(
        functools.partial(gather_kernel, narrow),
        in_specs=[vmem] * 4 + [hbm] * 4,
        out_specs=[hbm] * 7 + [vmem] * 5,
        out_shape=[
            shape((rows, heads * LANES), BF16),
            shape((rows, heads * LANES), BF16),
            shape((rows, width), BF16),
            shape((rows, heads * LANES), BF16),
            shape((width, proj.shape[1]), BF16),
            shape((width, ecols), BF16),
            shape((deep * narrow, width), BF16),
            shape((16, width), F32),
            shape((rows, LANES), BF16),
            shape((rows, LANES), BF16),
            shape((rows, LANES), BF16),
            shape((width, rows), BF16),
        ],
        scratch_shapes=[
            pltpu.VMEM((width, proj.shape[1]), BF16),
            pltpu.VMEM((share, ecols), BF16),
            pltpu.VMEM((deep, width), BF16),
            pltpu.VMEM((narrow, 16, LANES), BF16),
            pltpu.VMEM((8, proj.shape[1]), F32),
            pltpu.VMEM((4, rows, part), BF16),
            pltpu.VMEM((4, rows, part), BF16),
            pltpu.VMEM((rows, width), BF16),
            pltpu.VMEM((rows, heads * LANES), BF16),
            pltpu.VMEM((rows, LANES), BF16),
            pltpu.VMEM(x.shape, x.dtype),
            pltpu.VMEM(wo.shape, F32),
            pltpu.VMEM(w1.shape, F32),
            pltpu.VMEM(w2.shape, F32),
            pltpu.SemaphoreType.DMA((count,)),
            pltpu.SemaphoreType.DMA((count,)),
            pltpu.SemaphoreType.DMA((15 + heads,)),
        ],
        compiler_params=pltpu.CompilerParams(
            vmem_limit_bytes=VMEM_LIMIT, collective_id=0, has_side_effects=True
        ),
        name="gather",
    )(proj, vec, segments, types, x, wo, w1, w2)


def key_pair(keyval, kmask, low):
    wide = keyval.astype(F32)
    return (jnp.where(low, wide, swap_halves(wide)) * kmask.astype(F32)).astype(BF16)


def attend_head(query, keyval, qaug, kaug, kmask):
    rows = query.shape[0]
    low = low_lanes(rows)
    lane = lax.broadcasted_iota(jnp.int32, (rows, LANES), 1)
    keys = jnp.concatenate([key_pair(keyval, kmask, low), kaug], axis=1)
    scores = mm_nt(jnp.concatenate([query, qaug], axis=1), keys)
    top = jnp.max(scores, axis=1, keepdims=True)
    weight = jnp.exp2((scores - top) * LOG2E).astype(BF16)
    ones_val = jnp.where(low, 1.0, keyval.astype(F32)).astype(BF16)
    both = mm(weight, ones_val)
    total = swap_halves(both)
    log_total = top + jnp.log(jnp.where(low, both, total))
    high, mid, rest = split_three(log_total)
    extra = jnp.where(lane == 8, -high, jnp.where(lane == 9, -mid, jnp.where(lane == 10, -rest, 0.0)))
    return both / total, jnp.where(lane < 8, qaug.astype(F32), extra).astype(BF16)


def attend_kernel(q_ref, kv_ref, qa_ref, ka_ref, km_ref, ctx_ref, aug_ref):
    outs = []
    for part in range(2):
        cols = slice(part * LANES, (part + 1) * LANES)
        out, aug_ref[:, cols] = attend_head(q_ref[:, cols], kv_ref[:, cols], qa_ref[...], ka_ref[...], km_ref[...])
        outs.append(out)
    ctx_ref[...] = jnp.where(low_lanes(q_ref.shape[0]), swap_halves(outs[0]), outs[1]).astype(BF16)


def attend_call(q, kv, qa, ka, km, length):
    rows, cols = q.shape
    seqs, steps = rows // length, cols // (2 * LANES)
    pair = pl.BlockSpec((length, 2 * LANES), lambda s, i: (s, i))
    one = pl.BlockSpec((length, LANES), lambda s, i: (s, 0))
    return pl.pallas_call(
        attend_kernel,
        grid=(seqs, steps),
        in_specs=[pair, pair, one, one, one],
        out_specs=[pl.BlockSpec((length, LANES), lambda s, i: (s, i)), pair],
        out_shape=[
            jax.ShapeDtypeStruct((rows, cols // 2), BF16),
            jax.ShapeDtypeStruct((rows, cols), BF16),
        ],
        compiler_params=pltpu.CompilerParams(vmem_limit_bytes=VMEM_LIMIT),
        name="attend",
    )(q, kv, qa, ka, km)


def attend_back_head(query, keyval, aug, gcon, con, kaug, kmask, word, odd, low, lane):
    keys = key_pair(keyval, kmask, low)
    scores_t = mm_nt(jnp.concatenate([keys, kaug], axis=1), jnp.concatenate([query, aug], axis=1))
    probs_t = jnp.exp2(scores_t * LOG2E)
    gwide = gcon.astype(F32)
    prod = gwide * con.astype(F32)
    prod = jnp.where(low, 0.0, prod) if odd else jnp.where(low, prod, 0.0)
    high, mid, rest = split_three(jnp.sum(prod, axis=1, keepdims=True))
    extra = jnp.where(lane == 0, -high, jnp.where(lane == 1, -mid, jnp.where(lane == 2, -rest, 0.0)))
    ghead = jnp.where(low, extra, gwide if odd else swap_halves(gwide)).astype(BF16)
    ones_val = jnp.where(low, jnp.where(lane < 3, 1.0, 0.0), keyval.astype(F32)).astype(BF16)
    gscores_t = (probs_t * mm_nt(ones_val, ghead)).astype(BF16)
    blank = jnp.zeros_like(ghead)
    both = mm(
        jnp.concatenate([probs_t.astype(BF16), gscores_t], axis=1),
        jnp.concatenate(
            [jnp.concatenate([ghead, blank], axis=1), jnp.concatenate([blank, query], axis=1)], axis=0
        ),
    )
    gval, gkey = both[:, 0:LANES], both[:, LANES:]
    gquery = (jnp.transpose(mm_tn(keys, gscores_t)) * (HEAD**-0.5)).astype(BF16)
    zero = jnp.zeros_like(gquery)
    gkey = jnp.where(kmask.astype(F32) > 0, gkey, 0.0)
    gkey = gkey + swap_halves(gkey)
    return (
        jnp.where(word, gquery, zero),
        jnp.where(word, zero, gquery),
        jnp.where(low, gkey, gval).astype(BF16),
    )


def attend_back_kernel(
    length, x_ref, q_ref, kv_ref, aug_ref, gc_ref, ctx_ref, ka_ref, km_ref, word_ref, gp_ref, gw_ref, sum_ref, xt
):
    rows = x_ref.shape[0]

    @pl.when(pl.program_id(0) == 0)
    def _():
        xt[...] = jnp.transpose(x_ref[...])

    low = low_lanes(length)
    lane = lax.broadcasted_iota(jnp.int32, (length, LANES), 1)
    for part in range(2):
        cols = slice(part * LANES, (part + 1) * LANES)
        for seq in range(rows // length):
            here = slice(seq * length, (seq + 1) * length)
            tiles = attend_back_head(
                q_ref[here, cols], kv_ref[here, cols], aug_ref[here, cols], gc_ref[here], ctx_ref[here],
                ka_ref[here], km_ref[here], word_ref[here] > 0, part == 1, low, lane,
            )
            for index, tile in enumerate(tiles):
                at = part * GROUP + index * LANES
                gp_ref[here, at : at + LANES] = tile
    grads = gp_ref[...]
    gw_ref[...] = mm(xt[...], grads).astype(BF16)
    sum_ref[...] = jnp.sum(fold(grads.astype(F32)), axis=0, keepdims=True)


def attend_back_call(x, q, kv, aug, gc, ctx, ka, km, word, length):
    rows, width = x.shape
    pairs = q.shape[1] // (2 * LANES)
    head = pl.BlockSpec((rows, 2 * LANES), lambda h: (0, h))
    pair = pl.BlockSpec((rows, LANES), lambda h: (0, h))
    one = pl.BlockSpec((rows, LANES), lambda h: (0, 0))
    return pl.pallas_call(
        functools.partial(attend_back_kernel, length),
        grid=(pairs,),
        in_specs=[pl.BlockSpec((rows, width), lambda h: (0, 0)), head, head, head, pair, pair, one, one, one],
        out_specs=[
            pl.BlockSpec((rows, 2 * GROUP), lambda h: (0, h)),
            pl.BlockSpec((width, 2 * GROUP), lambda h: (0, h)),
            pl.BlockSpec((1, 2 * GROUP), lambda h: (0, h)),
        ],
        out_shape=[
            jax.ShapeDtypeStruct((rows, pairs * 2 * GROUP), BF16),
            jax.ShapeDtypeStruct((width, pairs * 2 * GROUP), BF16),
            jax.ShapeDtypeStruct((1, pairs * 2 * GROUP), F32),
        ],
        scratch_shapes=[pltpu.VMEM((width, rows), BF16)],
        compiler_params=pltpu.CompilerParams(vmem_limit_bytes=VMEM_LIMIT),
        name="attend_back",
    )(x, q, kv, aug, gc, ctx, ka, km, word)


class Chunk:
    def __init__(self, name, shape, total, plane=(), end=None, via=None):
        self.name = name
        self.rows, self.cols = shape
        self.total, self.via = total, via
        for label, ref in zip(("r1a", "r1b", "r2a", "r2b"), plane):
            setattr(self, label, ref)
        if end is not None:
            self.rz, self.final = end

    def row_half(self, wide):
        return spot(wide // 2 * (self.rows // 2), self.rows // 2, 16)

    def col_half(self, wide):
        return spot(lax.rem(wide, 2) * (self.cols // 2), self.cols // 2, LANES)

    def quarter(self, wide):
        return self.row_half(wide), self.col_half(wide)

    def mine(self, z, wide):
        if self.total.shape[1:] != (self.rows, self.cols):
            return self.total.at[z]
        return self.total.at[(z, *self.quarter(wide))]


def plane_scratch(depth, rows, cols):
    half = depth // 2
    return [
        pltpu.VMEM((half, rows, cols // 2), BF16),
        pltpu.VMEM((half, rows // 2, cols), BF16),
        pltpu.VMEM((half, rows // 2, cols // 2), BF16),
        pltpu.VMEM((half, rows // 2, cols // 2), BF16),
    ]


def end_scratch(depth, rows, cols):
    return [pltpu.VMEM((depth - 1, rows // 2, cols // 2), BF16), pltpu.VMEM((rows, cols), BF16)]


class Reducer:
    def __init__(self, here, send, recv):
        self.here = here
        self.links = Links(send, recv)
        self.send, self.arrived, self.finish = self.links.send, self.links.arrived, self.links.finish

    def pair_send(self, chunk, sources, only=None):
        here = self.here
        for z in range(here.depth) if only is None else (only,):
            for part, (_, cols) in enumerate(sources(0)):

                def build(z=z, part=part, cols=cols):
                    owner = 2 * z + 1 - here.core
                    return sources(owner)[part][0], chunk.total.at[z, :, cols], here.sib_dev

                self.send((chunk.name, "s", z, part), build)

    def pair_wait(self, chunk, sources):
        for z in range(self.here.depth):
            for part, (_, cols) in enumerate(sources(0)):
                self.arrived((chunk.name, "s", z, part), chunk.total.at[z, :, cols], self.here.sib_dev)

    def lower(self):
        return slice(0, self.here.depth // 2)

    def upper(self):
        return slice(self.here.depth // 2, self.here.depth)

    def plane_send(self, chunk):
        here = self.here
        cols, rows = (lambda: chunk.col_half(here.x_quarter)), (lambda: chunk.row_half(here.y_quarter))
        self.send((chunk.name, "1a"), lambda: (chunk.total.at[self.lower(), :, cols()], chunk.r1a, here.x_dev))
        self.send((chunk.name, "1b"), lambda: (chunk.total.at[self.upper(), rows(), :], chunk.r1b, here.y_dev))

    def plane_add(self, chunk):
        here = self.here
        total = chunk.total
        self.arrived((chunk.name, "1a"), chunk.r1a, here.x_dev)
        self.arrived((chunk.name, "1b"), chunk.r1b, here.y_dev)
        rows, cols = chunk.quarter(here.wide)
        total[self.lower(), :, cols] = total[self.lower(), :, cols] + chunk.r1a[...]
        total[self.upper(), rows, :] = total[self.upper(), rows, :] + chunk.r1b[...]

    def plane_next(self, chunk):
        here = self.here
        total = chunk.total

        def first():
            return total.at[(self.lower(), *chunk.quarter(here.y_quarter))], chunk.r2a, here.y_dev

        def second():
            return total.at[(self.upper(), *chunk.quarter(here.x_quarter))], chunk.r2b, here.x_dev

        self.send((chunk.name, "2a"), first)
        self.send((chunk.name, "2b"), second)

    def plane_turn(self, chunk):
        self.plane_add(chunk)
        self.plane_next(chunk)

    def plane_done(self, chunk):
        here = self.here
        self.arrived((chunk.name, "2a"), chunk.r2a, here.y_dev)
        self.arrived((chunk.name, "2b"), chunk.r2b, here.x_dev)
        rows, cols = chunk.quarter(here.wide)
        for part, value in ((self.lower(), chunk.r2a), (self.upper(), chunk.r2b)):
            chunk.total[part, rows, cols] = chunk.total[part, rows, cols] + value[...]

    def depth_send(self, chunk):
        here = self.here
        for k in range(1, here.depth):

            def build(k=k):
                piece = chunk.mine(lax.rem(here.z + k, here.depth), here.wide)
                return piece, chunk.rz.at[k - 1], here.z_dev(k)

            self.send((chunk.name, "z", k), build)

    def share_send(self, chunk):
        here = self.here
        for k in range(1, here.depth):
            self.arrived((chunk.name, "z", k), chunk.rz.at[k - 1], here.z_dev(k))
        done = chunk.mine(here.z, here.wide)[...].astype(F32)
        for k in range(1, here.depth):
            done = done + chunk.rz[k - 1].astype(F32)
        done = done.astype(BF16)
        rows, cols = chunk.quarter(here.wide)
        chunk.final[rows, cols] = done

        ways = [("fx", here.x_dev), ("fy", here.y_dev)] + ([] if chunk.via else [("fd", here.d_dev)])
        for name, device in ways:
            self.send((chunk.name, name), lambda device=device: self.share_copy(chunk, here.wide, device))
        return squares(done)

    def share_copy(self, chunk, quarter, device):
        piece = chunk.final.at[chunk.quarter(quarter)]
        return piece, piece, device

    def share_pass(self, chunk):
        here = self.here
        by_x = chunk.via == "x"
        name, quarter, device = ("fy", here.y_quarter, here.x_dev) if by_x else ("fx", here.x_quarter, here.y_dev)
        self.arrived((chunk.name, name), chunk.final.at[chunk.quarter(quarter)], device)
        self.send((chunk.name, "fd"), lambda: self.share_copy(chunk, quarter, device))

    def share_wait(self, chunk):
        here = self.here
        ways = (("fx", here.x_quarter, here.x_dev), ("fy", here.y_quarter, here.y_dev), ("fd", here.d_quarter, here.d_dev))
        seen = {"x": "fy", "y": "fx"}.get(chunk.via)
        for name, quarter, device in ways:
            if name != seen:
                self.arrived((chunk.name, name), chunk.final.at[chunk.quarter(quarter)], device)


def squares(value):
    total = jnp.zeros((8, LANES), F32)
    rows, cols = value.shape
    for start in range(0, cols, LANES):
        tile = value[:, start : start + LANES].astype(F32)
        total = total + jnp.sum((tile * tile).reshape(rows // 8, 8, LANES), axis=0)
    return total


def pair_groups(pairs):
    return (pairs // 3, pairs // 3, pairs // 6, pairs // 6)


def reduce_kernel(
    narrow, length, groups, deep,
    xt, q_ref, kv_ref, aug_ref, gc_ref, ctx_ref, wp_ref, ka_ref, km_ref, word_ref, gvec_ref,
    gr1_ref, t1_ref, tw_ref, gwo_ref,
    ig_ref, f1_ref, fo_ref, fw_ref, fa_ref, v_ref, n_ref,
    gp, ig, *scratch,
):
    step = pl.program_id(0)
    width, rows = xt.shape
    pairs = sum(groups)
    _, _, share, part = t1_ref.shape
    here = Place(narrow)
    scratch = list(scratch)
    red = Reducer(here, scratch[-3], scratch[-2])
    local = scratch[-1]

    def take(count):
        taken, scratch[:count] = scratch[:count], []
        return taken

    chunk_w = Chunk("w", (deep, width), take(1)[0], (), take(2), "x")
    chunk_1 = [Chunk(("1", j), (share, part), take(1)[0], take(4), take(2), "yx"[j]) for j in range(2)]
    gw, chunk_a = [], []
    for j in range(len(groups)):
        gw += take(1)
        via = ("y", "x", None, None)[j]
        chunk_a.append(Chunk(("a", j), (share, gw[j].shape[1]), take(1)[0], take(4), take(2), via))
    v0, v1, v2, vs, vx, vy, vz, n0, np, n1, ns, nz = take(12)
    begin = [sum(groups[:j]) for j in range(len(groups) + 1)]
    both = 2 * GROUP
    wide = groups[0] * both

    def sources_a(j):
        return lambda owner: [(gw[j].at[spot(owner * share, share, 16), :], slice(0, gw[j].shape[1]))]

    def load(index):
        source, target = (
            (t1_ref.at[0], chunk_1[0].total),
            (t1_ref.at[1], chunk_1[1].total),
            (tw_ref, chunk_w.total),
            (gwo_ref, gw[0].at[:, wide : wide + width]),
            (gr1_ref, ig),
        )[index]
        return pltpu.make_async_copy(source, target, local.at[index])

    def stores():
        copies = [(chunk_w.final, fw_ref)]
        copies += [(chunk.final, f1_ref.at[:, j * part : (j + 1) * part]) for j, chunk in enumerate(chunk_1)]
        copies += [(chunk_a[0].final.at[:, wide : wide + width], fo_ref)]
        for j, chunk in enumerate(chunk_a):
            cols = slice(begin[j] * both, begin[j + 1] * both)
            copies.append((chunk.final.at[:, 0 : groups[j] * both], fa_ref.at[:, cols]))
        return [pltpu.make_async_copy(a, b, local.at[5 + i]) for i, (a, b) in enumerate(copies)]

    def merge(j):
        def one(z, carry):
            mine = spot((2 * z + here.core) * share, share, 16)
            chunk_a[j].total[z] = chunk_a[j].total[z] + gw[j][mine, :]
            return carry

        red.pair_wait(chunk_a[j], sources_a(j))
        lax.fori_loop(0, here.depth, one, 0)
        red.plane_send(chunk_a[j])

    def turn_z(chunk):
        red.plane_done(chunk)
        red.depth_send(chunk)

    @pl.when(step == 0)
    def _():
        for index in range(5):
            load(index).start()
        here.greet()
        load(0).wait()
        red.plane_next(chunk_1[0])
        load(1).wait()
        red.plane_send(chunk_1[1])
        load(2).wait()
        red.depth_send(chunk_w)
        v0[...] = gvec_ref[...]
        n0[...] = jnp.zeros_like(n0)

    def at(when):
        def run(action):
            def body():
                action()

            pl.when(step == when)(body)

        return run

    def finish(chunk):
        n0[...] += red.share_send(chunk)

    def vec_pair():
        red.arrived(("v", "s"), vs, here.sib_dev)
        v1[...] = v0[...] + vs[...]
        red.send(("v", "x"), lambda: (v1, vx, here.x_dev))

    def vec_plane():
        red.arrived(("v", "x"), vx, here.x_dev)
        v2[...] = v1[...] + vx[...]
        red.send(("v", "y"), lambda: (v2, vy, here.y_dev))

    def vec_depth():
        red.arrived(("v", "y"), vy, here.y_dev)
        vz[here.z] = v2[...] + vy[...]
        for k in range(1, here.depth):
            red.send(("v", "z", k), lambda k=k: (vz.at[here.z], vz.at[here.z], here.z_dev(k)))

    def vec_done():
        for k in range(1, here.depth):
            red.arrived(("v", "z", k), vz.at[here.behind(k) // 2], here.z_dev(k))
        vec = vz[0]
        for z in range(1, here.depth):
            vec = vec + vz[z]
        v_ref[...] = vec

    a = chunk_a
    last = len(groups) - 1
    plan = {
        2: [lambda: load(3).wait(), lambda: turn_z(chunk_1[0])],
        3: [lambda: red.plane_turn(chunk_1[1])],
        4: [lambda: finish(chunk_w)],
        5: [lambda: merge(0), lambda: turn_z(chunk_1[1])],
        6: [lambda: red.share_pass(chunk_w)],
        7: [lambda: finish(chunk_1[0])],
        8: [lambda: red.plane_turn(a[0])],
        9: [lambda: merge(1), lambda: finish(chunk_1[1]), lambda: red.share_pass(chunk_1[0])],
        10: [lambda: turn_z(a[0])],
        11: [lambda: red.plane_turn(a[1]), lambda: merge(2), lambda: red.share_pass(chunk_1[1])],
    }
    tail = [
        [lambda: turn_z(a[1])],
        [lambda: merge(3), vec_pair, lambda: red.plane_turn(a[2])],
        [lambda: turn_z(a[2]), lambda: finish(a[0])],
        [lambda: red.plane_turn(a[3]), vec_plane],
        [lambda: turn_z(a[3]), lambda: finish(a[1]), lambda: red.share_pass(a[0]), vec_depth],
        [lambda: finish(a[2]), vec_done, lambda: red.share_pass(a[1])],
    ]

    def advance(half):
        for when, actions in plan.items():
            if when % 2 == half:
                for action in actions:
                    at(when // 2)(action)

    for index, actions in enumerate(tail):
        for action in actions:
            at(pairs + index)(action)

    @pl.when(step < pairs)
    def _():
        low = low_lanes(length)
        lane = lax.broadcasted_iota(jnp.int32, (length, LANES), 1)
        for part in range(2):
            advance(part)
            cols = slice(part * LANES, (part + 1) * LANES)
            for seq in range(rows // length):
                mine = slice(seq * length, (seq + 1) * length)
                tiles = attend_back_head(
                    q_ref[mine, cols], kv_ref[mine, cols], aug_ref[mine, cols], gc_ref[mine], ctx_ref[mine],
                    ka_ref[mine], km_ref[mine], word_ref[mine] > 0, part == 1, low, lane,
                )
                for index, tile in enumerate(tiles):
                    start = part * GROUP + index * LANES
                    gp[step, mine, start : start + LANES] = tile
        grads = gp[step]
        product = mm(xt[...], grads).astype(BF16)
        for j in range(len(groups)):

            @pl.when((step >= begin[j]) & (step < begin[j + 1]))
            def _():
                gw[j][:, spot((step - begin[j]) * both, both, LANES)] = product

        sums = jnp.sum(fold(grads.astype(F32)), axis=0, keepdims=True)
        low1 = low_lanes(1)
        place = spot(step * LANES, LANES, LANES)
        for b in range(3):
            even = sums[:, b * LANES : (b + 1) * LANES]
            odd = sums[:, GROUP + b * LANES : GROUP + (b + 1) * LANES]
            second = jnp.where(low1, swap_halves(even), odd)
            if b < 2:
                v0[2 * b : 2 * b + 1, place] = jnp.where(low1, even, swap_halves(odd))
                v0[2 * b + 1 : 2 * b + 2, place] = second
            else:
                v0[4:5, place] = second

    for j in range(len(groups)):
        at(begin[j + 1] - 1)(lambda j=j: red.pair_send(chunk_a[j], sources_a(j)))

    at(pairs - 1)(lambda: red.send(("v", "s"), lambda: (v0, vs, here.sib_dev)))
    at(pairs)(lambda: load(4).wait())

    @pl.when(step >= pairs)
    def _():
        ig[...] += mm_nt(gp[step - pairs], wp_ref[...])

    @pl.when(step == 2 * pairs - 1)
    def _():
        finish(a[last])
        np[here.wide] = n0[...]
        for name, device in (("nx", here.x_dev), ("ny", here.y_dev), ("nd", here.d_dev)):
            red.send((name,), lambda device=device: (np.at[here.wide], np.at[here.wide], device))
        vec = v_ref[...]
        square = jnp.sum(jnp.sum(vec * vec, axis=0, keepdims=True), axis=1, keepdims=True)
        ig_ref[...] = ig[...].astype(BF16)
        ways = (("nx", here.x_quarter, here.x_dev), ("ny", here.y_quarter, here.y_dev), ("nd", here.d_quarter, here.d_dev))
        for name, quarter, device in ways:
            red.arrived((name,), np.at[quarter], device)
        n1[...] = (np[0] + np[1]) + (np[2] + np[3])
        red.send(("n", "s"), lambda: (n1, ns, here.sib_dev))
        for chunk in (chunk_w, *chunk_1, *a):
            red.share_wait(chunk)
        for copy in stores():
            copy.start()
        red.arrived(("n", "s"), ns, here.sib_dev)
        nz[here.z] = n1[...] + ns[...]
        for k in range(1, here.depth):
            red.send(("n", "z", k), lambda k=k: (nz.at[here.z], nz.at[here.z], here.z_dev(k)))
        for k in range(1, here.depth):
            red.arrived(("n", "z", k), nz.at[here.behind(k) // 2], here.z_dev(k))
        total = nz[0]
        for z in range(1, here.depth):
            total = total + nz[z]
        every = jnp.sum(jnp.sum(total, axis=0, keepdims=True), axis=1, keepdims=True)
        n_ref[...] = jnp.broadcast_to(every + square, n_ref.shape)
        red.finish()
        for copy in stores():
            copy.wait()


def reduce_call(narrow, xt, q, kv, aug, gc, ctx, wp, ka, km, word, gvec, gr1, t1, tw, gwo, deep, length):
    width, rows = xt.shape
    pairs = q.shape[1] // (2 * LANES)
    groups = pair_groups(pairs)
    _, depth, share, inner = t1.shape

    def now(h):
        return jnp.minimum(h, pairs - 1)

    def fixed(shape):
        return pl.BlockSpec(shape, lambda h: (0, 0), pipeline_mode=pl.Buffered(1))

    head = pl.BlockSpec((rows, 2 * LANES), lambda h: (0, now(h)))
    pair = pl.BlockSpec((rows, LANES), lambda h: (0, now(h)))
    later = pl.BlockSpec((width, 2 * GROUP), lambda h: (0, jnp.maximum(h - pairs, 0)))
    one = fixed((rows, LANES))
    hbm = pl.BlockSpec(memory_space=pl.ANY)
    shape = jax.ShapeDtypeStruct
    vec = pltpu.VMEM((16, width), F32)
    tile = pltpu.VMEM((8, LANES), F32)
    scratch = [pltpu.VMEM((pairs, rows, 2 * GROUP), BF16), pltpu.VMEM((rows, width), F32)]
    scratch += [pltpu.VMEM(tw.shape, BF16), *end_scratch(depth, deep, width)]
    for _ in range(2):
        scratch += [pltpu.VMEM((depth, share, inner), BF16)]
        scratch += [*plane_scratch(depth, share, inner), *end_scratch(depth, share, inner)]
    for j, size in enumerate(groups):
        cols = size * 2 * GROUP + (width if j == 0 else 0)
        scratch += [
            pltpu.VMEM((width, cols), BF16),
            pltpu.VMEM((depth, share, cols), BF16),
            *plane_scratch(depth, share, cols),
            *end_scratch(depth, share, cols),
        ]
    several = pltpu.VMEM((depth, 8, LANES), F32)
    scratch += [vec] * 6 + [pltpu.VMEM((depth, 16, width), F32), tile, pltpu.VMEM((4, 8, LANES), F32), tile, tile, several]
    count = (3 + len(groups)) * (2 * depth + 6) + 2 * (4 + depth)
    scratch += [pltpu.SemaphoreType.DMA((count,))] * 2 + [pltpu.SemaphoreType.DMA((9 + len(groups),))]
    return pl.pallas_call(
        functools.partial(reduce_kernel, narrow, length, groups, deep),
        grid=(2 * pairs,),
        in_specs=[
            fixed((width, rows)), head, head, head, pair, pair, later, one, one, one, fixed((16, width)),
            hbm, hbm, hbm, hbm,
        ],
        out_specs=[fixed((rows, width)), hbm, hbm, hbm, hbm, fixed((16, width)), fixed((8, LANES))],
        out_shape=[
            shape((rows, width), BF16),
            shape((share, 2 * inner), BF16),
            shape((share, width), BF16),
            shape((deep, width), BF16),
            shape((share, pairs * 2 * GROUP), BF16),
            shape((16, width), F32),
            shape((8, LANES), F32),
        ],
        scratch_shapes=scratch,
        compiler_params=pltpu.CompilerParams(
            vmem_limit_bytes=VMEM_LIMIT, collective_id=1, has_side_effects=True
        ),
        name="reduce",
    )(xt, q, kv, aug, gc, ctx, wp, ka, km, word, gvec, gr1, t1, tw, gwo)


def gelu_pair(pre):
    bell = jnp.exp2(pre * pre * (-0.5 * LOG2E))
    share = 0.5 + 0.5 * lax.erf(pre * (0.5**0.5))
    return pre * share, share + pre * bell * 0.3989422804014327


def fold(array_in):
    rows, cols = array_in.shape
    return jnp.sum(array_in.reshape(rows // 8, 8, cols), axis=0)


def middle_kernel(
    narrow, x_hbm, ctx_hbm, cot_hbm, vec_ref, e_hbm, w2_hbm,
    out_hbm, gr1_hbm, gctx_hbm, gw1_hbm, gwo_hbm, gw2_hbm, gvec_ref,
    wo, w1, w2, io, ctx, h1_s, n1_s, inv_s, act_s, slope_s, gb_s, sum_s, gw2_s, gwo_s, acc, sems, *scratch,
):
    rows, width = io.shape
    inner = w1.shape[1]
    blocks, size, block = inner // width, 256, 256
    red = None

    def load(index):
        source, target = (
            (x_hbm, io),
            (ctx_hbm, ctx),
            (e_hbm.at[:, inner : inner + width], wo),
            (e_hbm.at[:, 0:inner], w1),
            (w2_hbm, w2),
            (cot_hbm, io),
        )[index]
        return pltpu.make_async_copy(source, target, sems.at[index])

    def store(index):
        source, target = (
            (io, out_hbm),
            (sum_s, gr1_hbm),
            (io, gctx_hbm),
            (gwo_s, gwo_hbm),
            (gw2_s, gw2_hbm) if red is None else (chunk.total.at[(slice(None), *chunk.quarter(here.wide))], gw2_hbm),
            (act_s.at[0:width, :], gw1_hbm) if red is None else (chunk_1[0].total, gw1_hbm.at[0]),
            None if red is None else (chunk_1[1].total, gw1_hbm.at[1]),
        )[index]
        return pltpu.make_async_copy(source, target, sems.at[6 + index])

    def vec(row):
        return vec_ref[row : row + 1, :].astype(F32)

    def over_rows(step):
        def one(i, carry):
            step(spot(i * size, size, size))
            return carry

        lax.fori_loop(0, rows // size, one, 0)

    def over_cols(first, last, step):
        def one(i, carry):
            step(spot(i * block, block, block), i)
            return carry

        lax.fori_loop(first, last, one, 0)

    for index in (1, 2, 0, 3, 4):
        load(index).start()
    acc[...] = jnp.zeros_like(acc)
    if narrow is not None:
        here = Place(narrow)
        red = Reducer(here, scratch[0], scratch[1])
        deep, share = scratch[2].shape[1], scratch[7].shape[1]
        chunk = Chunk("w", (deep, width), scratch[2], scratch[3:7])
        part = inner // 2
        chunk_1 = [Chunk(("1", j), (share, part), scratch[7 + 3 * j], scratch[8:10] if j == 0 else ()) for j in range(2)]
        here.greet()

        def sources(owner):
            return [(gw2_s.at[spot(owner * deep, deep, 16), :], slice(0, width))]

        def sources_1(j):
            cols = slice(j * part, (j + 1) * part)
            return lambda owner: [(act_s.at[spot(owner * share, share, 16), cols], slice(0, part))]

    for index in (1, 2, 0):
        load(index).wait()

    def norm_one(at):
        resid = io[at, :].astype(F32) + mm(ctx[at, :], wo[...]) + vec(5)
        center = resid - jnp.mean(resid, axis=1, keepdims=True)
        inverse = lax.rsqrt(jnp.mean(center * center, axis=1, keepdims=True) + norm_eps)
        unit = center * inverse
        hidden = unit * vec(6) + vec(7)
        n1_s[at, :] = unit.astype(BF16)
        inv_s[at, :] = jnp.broadcast_to(inverse, (size, LANES))
        h1_s[at, :] = hidden.astype(BF16)
        sum_s[at, :] = hidden + vec(8)

    over_rows(norm_one)
    load(5).start()
    load(3).wait()
    per = width // block

    def expand(at, i):
        bias = vec_ref[11 + i // per, spot(lax.rem(i, per) * block, block, LANES)].astype(F32).reshape(1, block)
        act, slope = gelu_pair(mm(h1_s[...], w1[:, at]) + bias)
        act_s[:, at] = act.astype(BF16)
        slope_s[:, at] = slope.astype(BF16)

    over_cols(0, inner // block, expand)
    load(4).wait()

    def reduce(at, i):
        sum_s[:, at] += mm(act_s[...], w2[:, at])

    over_cols(0, per, reduce)
    load(5).wait()

    def norm_two(at):
        resid = sum_s[at, :]
        center = resid - jnp.mean(resid, axis=1, keepdims=True)
        inverse = lax.rsqrt(jnp.mean(center * center, axis=1, keepdims=True) + norm_eps)
        unit = center * inverse
        grad = io[at, :].astype(F32)
        io[at, :] = (unit * vec(9) + vec(10)).astype(BF16)
        acc[9] += fold(grad * unit)
        acc[10] += fold(grad)
        scaled = grad * vec(9)
        back = inverse * (
            scaled
            - jnp.mean(scaled, axis=1, keepdims=True)
            - unit * jnp.mean(scaled * unit, axis=1, keepdims=True)
        )
        sum_s[at, :] = back
        half = back.astype(BF16)
        gb_s[at, :] = half
        acc[8] += fold(half.astype(F32))

    over_rows(norm_two)
    store(0).start()
    for z in range(blocks):
        cols = slice(z * width, (z + 1) * width)
        gw2_s[cols, :] = mm_tn(act_s[:, cols], gb_s[...]).astype(BF16)
        if red is not None:
            red.pair_send(chunk, sources, z)

    def expand_back(at, i):
        grad = (mm_nt(gb_s[...], w2[at, :]) * slope_s[:, at].astype(F32)).astype(BF16)
        slope_s[:, at] = grad
        row = 11 + i // per
        cols = spot(lax.rem(i, per) * block, block, LANES)
        acc[row, :, cols] = acc[row, :, cols] + fold(grad.astype(F32))

    def hidden_back(at, i):
        sum_s[:, at] += mm_nt(slope_s[...], w1[at, :])

    def norm_one_back(at):
        grad, unit = sum_s[at, :], n1_s[at, :].astype(F32)
        acc[6] += fold(grad * unit)
        acc[7] += fold(grad)
        scaled = grad * vec(6)
        back = inv_s[at, 0:1] * (
            scaled
            - jnp.mean(scaled, axis=1, keepdims=True)
            - unit * jnp.mean(scaled * unit, axis=1, keepdims=True)
        )
        sum_s[at, :] = back
        half = back.astype(BF16)
        gb_s[at, :] = half
        acc[5] += fold(half.astype(F32))

    def merge(target, source, size):
        def one(z, carry):
            mine = spot((2 * z + here.core) * size, size, 16)
            target[z] = target[z] + source(mine)
            return carry

        lax.fori_loop(0, here.depth, one, 0)

    def merge_1(j):
        red.pair_wait(chunk_1[j], sources_1(j))
        merge(chunk_1[j].total, lambda mine: act_s[mine, j * part : (j + 1) * part], share)

    count = inner // block
    over_cols(0, count // 3, expand_back)
    if red is not None:
        red.pair_wait(chunk, sources)
        merge(chunk.total, lambda mine: gw2_s[mine, :], deep)
        red.plane_send(chunk)
    over_cols(count // 3, count, expand_back)
    for c in range(blocks):
        cols = slice(c * width, (c + 1) * width)
        act_s[0:width, cols] = mm_tn(h1_s[...], slope_s[:, cols]).astype(BF16)
        if red is not None and (c + 1) % (blocks // 2) == 0:
            red.pair_send(chunk_1[c // (blocks // 2)], sources_1(c // (blocks // 2)))
    over_cols(0, 1, hidden_back)
    if red is not None:
        merge_1(0)
        red.plane_send(chunk_1[0])
    over_cols(1, per, hidden_back)
    if red is not None:
        red.plane_turn(chunk)
        merge_1(1)
        store(6).start()
    else:
        store(5).start()
    over_rows(norm_one_back)
    store(1).start()
    store(0).wait()
    io[...] = mm_nt(gb_s[...], wo[...]).astype(BF16)
    store(2).start()
    gwo_s[...] = mm_tn(ctx[...], gb_s[...]).astype(BF16)
    store(3).start()
    for row in range(acc.shape[0]):
        gvec_ref[row : row + 1, :] = jnp.sum(acc[row], axis=0, keepdims=True)
    if red is not None:
        red.plane_done(chunk)
    store(4).start()
    if red is not None:
        red.plane_add(chunk_1[0])
        store(5).start()
        red.finish()
    for index in range(1, 6 if red is None else 7):
        store(index).wait()


def middle_call(narrow, x, ctx, cot, vec, e, w2):
    rows, width = x.shape
    inner = w2.shape[0]
    hbm, vmem = pl.BlockSpec(memory_space=pl.ANY), pl.BlockSpec(memory_space=pltpu.VMEM)
    shape = jax.ShapeDtypeStruct
    scratch, params = [], {}
    shape_w, shape_1 = (inner, width), (width, inner)
    if narrow is not None:
        depth, deep, share = narrow // 2, inner // narrow, width // narrow
        part = inner // 2
        shape_w, shape_1 = (depth, deep // 2, width // 2), (2, depth, share, part)
        scratch = [pltpu.SemaphoreType.DMA((3 * depth + 8,))] * 2
        scratch += [pltpu.VMEM((depth, deep, width), BF16), *plane_scratch(depth, deep, width)]
        scratch += [pltpu.VMEM((depth, share, part), BF16), *plane_scratch(depth, share, part)[0:2]]
        scratch += [pltpu.VMEM((depth, share, part), BF16)]
        params = dict(collective_id=2, has_side_effects=True)
    return pl.pallas_call(
        functools.partial(middle_kernel, narrow),
        in_specs=[hbm, hbm, hbm, vmem, hbm, hbm],
        out_specs=[hbm] * 6 + [vmem],
        out_shape=[
            shape((rows, width), BF16),
            shape((rows, width), F32),
            shape((rows, width), BF16),
            shape(shape_1, BF16),
            shape((width, width), BF16),
            shape(shape_w, BF16),
            shape(vec.shape, F32),
        ],
        scratch_shapes=[
            pltpu.VMEM((width, width), BF16),
            pltpu.VMEM((width, inner), BF16),
            pltpu.VMEM((inner, width), BF16),
            pltpu.VMEM((rows, width), BF16),
            pltpu.VMEM((rows, width), BF16),
            pltpu.VMEM((rows, width), BF16),
            pltpu.VMEM((rows, width), BF16),
            pltpu.VMEM((rows, LANES), F32),
            pltpu.VMEM((rows, inner), BF16),
            pltpu.VMEM((rows, inner), BF16),
            pltpu.VMEM((rows, width), BF16),
            pltpu.VMEM((rows, width), F32),
            pltpu.VMEM((inner, width), BF16),
            pltpu.VMEM((width, width), BF16),
            pltpu.VMEM((vec.shape[0], 8, width), F32),
            pltpu.SemaphoreType.DMA((13,)),
            *scratch,
        ],
        compiler_params=pltpu.CompilerParams(vmem_limit_bytes=VMEM_LIMIT, **params),
        name="middle",
    )(x, ctx, cot, vec, e, w2)


def input_grad_kernel(gp_ref, w_ref, gr1_ref, out_ref):
    out_ref[...] = (gr1_ref[...] + mm_nt(gp_ref[...], w_ref[...])).astype(BF16)


def input_grad_call(gp, w, gr1, size):
    rows, cols = gp.shape
    width = w.shape[0]
    return pl.pallas_call(
        input_grad_kernel,
        grid=(rows // size,),
        in_specs=[
            pl.BlockSpec((size, cols), lambda i: (i, 0)),
            pl.BlockSpec((width, cols), lambda i: (0, 0)),
            pl.BlockSpec((size, width), lambda i: (i, 0)),
        ],
        out_specs=pl.BlockSpec((size, width), lambda i: (i, 0)),
        out_shape=jax.ShapeDtypeStruct((rows, width), BF16),
        compiler_params=pltpu.CompilerParams(vmem_limit_bytes=VMEM_LIMIT),
        name="input_grad",
    )(gp, w, gr1)


def adam_update(master, first_old, second_old, grad_shard, factor, index):
    clipped = grad_shard * factor
    new_first = beta_one * first_old + (1.0 - beta_one) * clipped
    new_second = beta_two * second_old + (1.0 - beta_two) * clipped * clipped
    direction = (
        new_first
        / (1.0 - beta_one**STEP)
        / (jnp.sqrt(new_second / (1.0 - beta_two**STEP)) + adam_eps)
    )
    new_weight = master - rate_table[index] * (direction + decay_table[index] * master)
    return (new_weight, new_first, new_second)


def update_tile(master, first, second, grad, factor, index):
    weight, first, second = adam_update(master, first, second, grad.astype(F32), factor, index)
    return weight, first, second, weight.astype(BF16)


def update_kernel(narrow, n_ref, fa_ref, fo_ref, f1_ref, fw_ref, v_ref, *refs):
    ins, whole, outs, norm_ref, copied = refs[0:15], refs[15:17], refs[17:37], refs[37], refs[38:40]
    step = pl.program_id(0)
    for source, target in zip(whole, copied):
        target[...] = source[...]
    heads = fa_ref.shape[1] // GROUP
    width = heads * HEAD
    norm = jnp.sqrt(n_ref[0:1, 0:1])
    factor = jnp.minimum(1.0, clip_limit / (norm + 1e-06))
    norm_ref[...] = norm

    def store(index, rows, cols, grad):
        news = update_tile(*(ins[5 * t + index][rows, cols] for t in range(3)), grad, factor, index)
        for t, new in enumerate(news):
            outs[5 * t + index][rows, cols] = new

    every = slice(None)
    low = low_lanes(fa_ref.shape[0])
    for pair in range(heads // 2):
        at = 2 * pair * GROUP
        for b in range(3):
            even = fa_ref[:, at + b * LANES : at + (b + 1) * LANES].astype(F32)
            odd = fa_ref[:, at + GROUP + b * LANES : at + GROUP + (b + 1) * LANES].astype(F32)
            for second in range(2):
                if second:
                    grad = jnp.where(low, swap_halves(even), odd)
                else:
                    grad = jnp.where(low, even, swap_halves(odd))
                start = (2 * b + second) * width + pair * LANES
                store(0, every, slice(start, start + LANES), grad)
    store(1, every, every, fo_ref[...])
    store(2, every, every, f1_ref[...])
    store(3, every, every, fw_ref[...])

    @pl.when(step == 0)
    def _():
        count, span = ins[4].shape
        me = lax.axis_index("narrow")
        turned = pltpu.roll(v_ref[...], lax.rem(width - me * span, width), 1)
        store(4, every, every, turned[0:count, 0:span])


def update_call(narrow, norm, shards, vec, masters, firsts, seconds, whole):
    share = shards[0].shape[0]
    steps = share // 48 if share % 48 == 0 else share // 16

    def rows_of(array_in):
        return pl.BlockSpec((array_in.shape[0] // steps, array_in.shape[1]), lambda i: (i, 0))

    def fixed(array_in):
        return pl.BlockSpec(array_in.shape, lambda i: (0, 0))

    def group(arrays):
        return [rows_of(a) for a in arrays[:4]] + [fixed(arrays[4])]

    def shapes(arrays, dtype):
        return [jax.ShapeDtypeStruct(a.shape, dtype) for a in arrays]

    return pl.pallas_call(
        functools.partial(update_kernel, narrow),
        grid=(steps,),
        in_specs=[fixed(norm), *(rows_of(a) for a in shards), fixed(vec)] + group(masters) * 3 + [rows_of(a) for a in whole],
        out_specs=group(masters) * 4 + [pl.BlockSpec((1, 1), lambda i: (0, 0))] + [rows_of(a) for a in whole],
        out_shape=shapes(masters, F32) * 3
        + shapes(masters, BF16)
        + [jax.ShapeDtypeStruct((1, 1), F32)]
        + [jax.ShapeDtypeStruct(a.shape, a.dtype) for a in whole],
        compiler_params=pltpu.CompilerParams(vmem_limit_bytes=VMEM_LIMIT),
        name="update",
    )(norm, *shards, vec, *masters, *firsts, *seconds, *whole)


def by_head(array_in):
    rows, cols = array_in.shape
    heads = cols // GROUP
    return array_in.reshape(rows, 6, heads, HEAD).transpose(0, 2, 1, 3).reshape(rows, cols)


def by_block(array_in):
    rows, cols = array_in.shape
    heads = cols // GROUP
    return array_in.reshape(rows, heads, 6, HEAD).transpose(0, 2, 1, 3).reshape(rows, cols)


def can_pass_pieces(wide, narrow, width, deep):
    share = width // narrow
    return wide == 4 and narrow % 2 == 0 and narrow > 2 and share % 32 == 0 and deep % 128 == 0 and 2 * deep == width


def body(
    x_in, cotangent, segment_ids, type_ids,
    projection, context_out, expand_weight, reduce_weight, vector_params,
    first_projection, first_context, first_expand, first_reduce, first_vectors,
    second_projection, second_context, second_expand, second_reduce, second_vectors,
):
    seq_count, seq_len, width = x_in.shape
    rows = seq_count * seq_len

    def gather(array_in, axis):
        return lax.all_gather(array_in.astype(BF16), "narrow", axis=axis, tiled=True)

    hidden = x_in.reshape(rows, width)
    cot = cotangent.reshape(rows, width)
    narrow = lax.axis_size("narrow")
    pieces = can_pass_pieces(lax.axis_size("wide"), narrow, width, reduce_weight.shape[0])
    if pieces:
        query, keyval, context, aug, proj_w, mid_w, reduce_w, vec_rows, word, kmask, kaug, turned = gather_call(
            narrow, hidden, projection, context_out, expand_weight, reduce_weight, vector_params,
            segment_ids, type_ids,
        )
    else:
        word_col = (type_ids == 0).reshape(rows, 1)
        lane = lax.broadcasted_iota(jnp.int32, (rows, LANES), 1)
        word = jnp.broadcast_to(word_col, (rows, LANES)).astype(BF16)
        kmask = ((lane < HEAD) == word_col).astype(BF16)
        same = segment_ids.reshape(rows, 1) == lane
        qaug = jnp.where(same & (lane < 8), 1.0, 0.0).astype(BF16)
        kaug = jnp.where(lane < 8, jnp.where(same, 0.0, FAR), jnp.where(lane < 11, 1.0, 0.0)).astype(BF16)
        proj_w, vec_half = gather(by_head(projection), 0), gather(vector_params, 1)
        reduce_w = gather(reduce_weight, 0)
        mid_w = jnp.concatenate(
            [gather(expand_weight, 0), gather(context_out, 0), jnp.zeros((width, 2 * LANES), BF16)], axis=1
        )
        zero_row = jnp.zeros((1, width), BF16)
        bias = by_head(jnp.concatenate([vec_half[0:4], zero_row, vec_half[4:5]]).reshape(1, -1)).astype(F32)
        vec_rows = jnp.pad(vec_half.astype(F32), ((0, 1), (0, 0)))
        query, keyval = qkv_call(hidden, proj_w, bias, word)
        context, aug = attend_call(query, keyval, qaug, kaug, kmask, seq_len)
    block_out, grad_r1, grad_context, grad_expand, grad_ctx_w, grad_reduce, grad_mid = middle_call(
        narrow if pieces else None, hidden, context, cot, vec_rows, mid_w, reduce_w
    )
    masters = (projection, context_out, expand_weight, reduce_weight, vector_params)
    firsts = (first_projection, first_context, first_expand, first_reduce, first_vectors)
    seconds = (second_projection, second_context, second_expand, second_reduce, second_vectors)
    out_shape = (seq_count, seq_len, width)
    if pieces:
        input_grad, shard_1, shard_o, shard_w, shard_a, grad_vectors, norm = reduce_call(
            narrow, turned, query, keyval, aug, grad_context, context, proj_w, kaug, kmask, word, grad_mid,
            grad_r1, grad_expand, grad_reduce, grad_ctx_w, reduce_weight.shape[0], seq_len,
        )
        shards = (shard_a, shard_o, shard_1, shard_w)
        *updated, grad_norm, block_out, input_grad = update_call(
            narrow, norm, shards, grad_vectors, masters, firsts, seconds, (block_out, input_grad)
        )
        return (
            block_out.reshape(out_shape),
            input_grad.reshape(out_shape),
            grad_norm.reshape(()),
            *updated,
        )
    grad_proj, grad_proj_w, grad_sums = attend_back_call(
        hidden, query, keyval, aug, grad_context, context, kaug, kmask, word, seq_len
    )
    input_grad = input_grad_call(grad_proj, proj_w, grad_r1, 256)
    sum_rows = by_block(grad_sums).reshape(6, width)
    grad_vectors = jnp.concatenate([sum_rows[0:4], sum_rows[5:6], grad_mid[5:15]], axis=0)

    def scatter(array_in, axis):
        return lax.psum_scatter(array_in, "narrow", scatter_dimension=axis, tiled=True)

    def over_wide(array_in):
        return lax.psum(array_in.astype(BF16), "wide").astype(F32)

    shards = (
        by_block(over_wide(scatter(grad_proj_w, 0))),
        over_wide(scatter(grad_ctx_w, 0)),
        over_wide(scatter(grad_expand, 0)),
        over_wide(scatter(grad_reduce, 0)),
        over_wide(scatter(grad_vectors, 1)),
    )
    local_squares = sum((jnp.sum(shard_item * shard_item) for shard_item in shards))
    total_squares = lax.psum(local_squares, "narrow")
    grad_norm = jnp.sqrt(total_squares)
    factor = jnp.minimum(1.0, clip_limit / (grad_norm + 1e-06))
    results = [
        adam_update(masters[index], firsts[index], seconds[index], shards[index], factor, index)
        for index in range(5)
    ]
    return (
        block_out.reshape(out_shape),
        input_grad.reshape(out_shape),
        grad_norm,
        *(item[0] for item in results),
        *(item[1] for item in results),
        *(item[2] for item in results),
        *(item[0].astype(BF16) for item in results),
    )


def solution(mesh):
    shard, col = P("narrow", None), P(None, "narrow")
    seqs = P(("wide", "narrow"), None, None)
    group = (shard, shard, shard, shard, col)
    return jax.shard_map(
        body,
        mesh=mesh,
        in_specs=(seqs, seqs, P(("wide", "narrow"), None), P(("wide", "narrow"), None), *group, *group, *group),
        out_specs=(seqs, seqs, P(), *group, *group, *group, *group),
        check_vma=False,
    )
```

```python
import functools

import jax
import jax.numpy as jnp
from jax import lax
from jax.experimental import pallas as pl
from jax.experimental.pallas import tpu as pltpu
from jax.sharding import PartitionSpec as P

HEAD = 64
STEP = 10
LANES = 128
GROUP = 6 * HEAD
LOG2E = 1.4426950408889634
FAR = -1e30
VMEM_LIMIT = 60 * 1024 * 1024

beta_one = 0.9
beta_two = 0.999
adam_eps = 1e-08
norm_eps = 1e-05
clip_limit = 1.0
rate_table = (0.03, 0.3, 0.03, 0.015, 0.4)
decay_table = (0.01, 0.01, 0.01, 0.01, 0.0)

F32 = jnp.float32
BF16 = jnp.bfloat16


def mm(a, b):
    return lax.dot_general(a, b, (((1,), (0,)), ((), ())), preferred_element_type=F32)


def mm_nt(a, b):
    return lax.dot_general(a, b, (((1,), (1,)), ((), ())), preferred_element_type=F32)


def mm_tn(a, b):
    return lax.dot_general(a, b, (((0,), (0,)), ((), ())), preferred_element_type=F32)


def low_lanes(rows):
    return lax.broadcasted_iota(jnp.int32, (rows, LANES), 1) < HEAD


def swap_halves(tile):
    return pltpu.roll(tile, HEAD, 1)


def split_three(col):
    high = col.astype(BF16).astype(F32)
    rest = col - high
    mid = rest.astype(BF16).astype(F32)
    return high, mid, rest - mid


def qkv_tile(prod, bias, word):
    full = prod + bias
    query = jnp.where(word, full[:, 0:LANES], full[:, LANES : 2 * LANES])
    return (query.astype(BF16).astype(F32) * (HEAD**-0.5)).astype(BF16), full[
        :, 2 * LANES :
    ].astype(BF16)


def qkv_kernel(x_ref, w_ref, b_ref, word_ref, q_ref, kv_ref):
    word = word_ref[...] > 0
    for part in range(2):
        cols = slice(part * GROUP, (part + 1) * GROUP)
        query, keyval = qkv_tile(mm(x_ref[...], w_ref[:, cols]), b_ref[:, cols], word)
        out = slice(part * LANES, (part + 1) * LANES)
        q_ref[:, out] = query
        kv_ref[:, out] = keyval


def qkv_call(x, w, bias, word):
    rows, width = x.shape
    steps = w.shape[1] // (2 * GROUP)
    out = jax.ShapeDtypeStruct((rows, steps * 2 * LANES), BF16)
    return pl.pallas_call(
        qkv_kernel,
        grid=(steps,),
        in_specs=[
            pl.BlockSpec((rows, width), lambda i: (0, 0)),
            pl.BlockSpec((width, 2 * GROUP), lambda i: (0, i)),
            pl.BlockSpec((1, 2 * GROUP), lambda i: (0, i)),
            pl.BlockSpec((rows, LANES), lambda i: (0, 0)),
        ],
        out_specs=[pl.BlockSpec((rows, 2 * LANES), lambda i: (0, i))] * 2,
        out_shape=[out, out],
        compiler_params=pltpu.CompilerParams(vmem_limit_bytes=VMEM_LIMIT),
        name="qkv",
    )(x, w, bias, word)


class Links:
    def __init__(self, send, recv):
        self.send_sem, self.recv_sem = send, recv
        self.slots = {}
        self.sent = []

    def copy(self, key, src, dst, device):
        index = self.slots.setdefault(key, len(self.slots))
        return pltpu.make_async_remote_copy(
            src_ref=src,
            dst_ref=dst,
            send_sem=self.send_sem.at[index],
            recv_sem=self.recv_sem.at[index],
            device_id=device,
            device_id_type=pl.DeviceIdType.MESH,
        )

    def send(self, key, build, *guards):
        def start():
            self.copy(key, *build()).start()

        guarded(start, guards)
        self.sent.append((key, build, guards))

    def arrived(self, key, dst, device):
        self.copy(key, dst, dst, device).wait_recv()

    def finish(self):
        for key, build, guards in self.sent:

            def wait(key=key, build=build):
                self.copy(key, *build()).wait_send()

            guarded(wait, guards)


def guarded(action, guards):
    if not guards:
        action()
        return
    holds = guards[0]()
    for guard in guards[1:]:
        holds = jnp.logical_and(holds, guard())
    pl.when(holds)(action)


class Place:
    def __init__(self, narrow):
        self.wide, self.me = lax.axis_index("wide"), lax.axis_index("narrow")
        self.core = lax.rem(self.me, 2)
        self.z = self.me // 2
        self.depth = narrow // 2
        self.x_quarter = self.wide + 1 - 2 * lax.rem(self.wide, 2)
        self.y_quarter = lax.rem(self.wide + 2, 4)
        self.d_quarter = lax.rem(self.x_quarter + 2, 4)
        self.sib = self.me + 1 - 2 * self.core
        self.x_dev, self.y_dev = {"wide": self.x_quarter}, {"wide": self.y_quarter}
        self.d_dev = {"wide": self.d_quarter}
        self.sib_dev = {"narrow": self.sib}

    def ahead(self, k):
        return 2 * lax.rem(self.z + k, self.depth) + self.core

    def behind(self, k, other=False):
        core = 1 - self.core if other else self.core
        return 2 * lax.rem(self.z + self.depth - k, self.depth) + core

    def z_dev(self, k):
        return {"narrow": self.ahead(k)}

    def has_next(self, way):
        return lambda: self.z + 1 < self.depth if way == 0 else self.z > 0

    def comes(self, way, hop):
        return lambda: self.z >= hop if way == 0 else self.z + hop < self.depth

    def origin(self, way, hop, other=False):
        core = 1 - self.core if other else self.core
        return 2 * (self.z - hop if way == 0 else self.z + hop) + core

    def next_dev(self, way):
        return {"narrow": self.me + 2 if way == 0 else self.me - 2}

    def greet_near(self):
        barrier = pltpu.get_barrier_semaphore()

        def greet(device):
            pl.semaphore_signal(barrier, inc=1, device_id=device, device_id_type=pl.DeviceIdType.MESH)

        for device in (self.x_dev, self.y_dev, self.sib_dev):
            greet(device)
        for way in range(2):
            guarded(lambda way=way: greet(self.next_dev(way)), (self.has_next(way),))
        pl.semaphore_wait(barrier, 3 + jnp.minimum(self.z, 1) + jnp.minimum(self.depth - 1 - self.z, 1))

    def greet(self):
        barrier = pltpu.get_barrier_semaphore()
        partners = [self.x_dev, self.y_dev, self.d_dev, self.sib_dev] + [self.z_dev(k) for k in range(1, self.depth)]
        for device in partners:
            pl.semaphore_signal(barrier, inc=1, device_id=device, device_id_type=pl.DeviceIdType.MESH)
        pl.semaphore_wait(barrier, len(partners))


def spot(start, size, unit):
    return pl.ds(pl.multiple_of(start, unit), size)


def gather_kernel(
    narrow, proj_ref, vec_ref, seg_ref, type_ref, x_hbm, wo_hbm, w1_hbm, w2_hbm,
    q_out, kv_out, ctx_out, aug_out, a_out, e_out, w2_out, vec_out, word_ref, km_ref, ka_ref, xt_ref,
    a_full, e_own, w2_own, v_all, bias, q_s, kv_s, ctx_s, aug_s, qa_ref, x_ref, wo_ref, w1_ref, w2_ref, send, recv, local,
):
    rows, width = x_ref.shape
    share = proj_ref.shape[0]
    deep = w2_ref.shape[0]
    half, quarter, equarter, dquarter = share // 2, proj_ref.shape[1] // 4, e_own.shape[1] // 4, deep // 4
    heads = width // HEAD
    here = Place(narrow)
    links = Links(send, recv)
    last = local.shape[0]
    loads = [
        pltpu.make_async_copy(source, target, local.at[last - 4 + index])
        for index, (source, target) in enumerate(
            ((x_hbm, x_ref), (w1_hbm, w1_ref), (wo_hbm, wo_ref), (w2_hbm, w2_ref))
        )
    ]
    for copy in loads:
        copy.start()
    me, hops = here.me, range(1, here.depth)
    routes = [(way, hop) for hop in hops for way in range(2)]

    def region(kind, owner, part, side=None):
        size, start = (share, 0) if side is None else (half, side * half)
        if kind == "a":
            return a_full.at[spot(owner * share + start, size, 16), spot(part * quarter, quarter, LANES)]
        if kind == "e":
            return e_out.at[spot(owner * share + start, size, 16), spot(part * equarter, equarter, LANES)]
        size, start = (dquarter, 0) if side is None else (dquarter // 2, side * (dquarter // 2))
        return w2_out.at[spot(owner * deep + part * dquarter + start, size, 16), :]

    def whole(kind, owner):
        if kind == "a":
            return a_full.at[spot(owner * share, share, 16), :]
        if kind == "e":
            return e_out.at[spot(owner * share, share, 16), :]
        if kind == "w":
            return w2_out.at[spot(owner * deep, deep, 16), :]
        return v_all.at[owner]

    def own(kind):
        return {"a": whole("a", me), "e": e_own, "w": w2_own, "v": v_all.at[me]}[kind]

    def own_part(kind, part, side=None):
        if kind == "a":
            return region("a", me, part, side)
        if kind == "e":
            rows = slice(0, share) if side is None else slice(side * half, (side + 1) * half)
            return e_own.at[rows, spot(part * equarter, equarter, LANES)]
        size, start = (dquarter, 0) if side is None else (dquarter // 2, side * (dquarter // 2))
        return w2_own.at[spot(part * dquarter + start, size, 16), :]

    def send_own(kind):
        links.send((kind, "o"), lambda: (own(kind), whole(kind, me), here.sib_dev))

    def send_z(kind):
        for way in range(2):
            ahead = here.has_next(way)
            if kind == "v":
                links.send(("v", "z", way, 1), lambda way=way: (own("v"), own("v"), here.next_dev(way)), ahead)
                continue
            links.send(
                (kind, "z", way, 1),
                lambda way=way: (own_part(kind, here.wide), region(kind, me, here.wide), here.next_dev(way)),
                ahead,
            )
            if kind == "a":
                continue
            links.send(
                (kind, "h", way, 1),
                lambda way=way: (
                    own_part(kind, here.d_quarter, 0), region(kind, me, here.d_quarter, 0), here.next_dev(way)
                ),
                ahead,
            )

    def relay(key, target, device, *guards):
        links.send(key, lambda: (target(), target(), device()), *guards)

    def receive(key, target, guard):
        guarded(lambda: links.arrived(key, target(), here.sib_dev), (guard,))

    def pass_z(kind, hop):
        for way in range(2):
            comes, ahead = here.comes(way, hop), here.has_next(way)
            onward = lambda way=way: here.next_dev(way)
            if kind == "v":
                piece = lambda way=way: whole("v", here.origin(way, hop))
            else:
                piece = lambda way=way: region(kind, here.origin(way, hop), here.wide)
            receive((kind, "z", way, hop), piece, comes)
            if hop + 1 < here.depth:
                relay((kind, "z", way, hop + 1), piece, onward, comes, ahead)
            if kind != "v":
                relay((kind, "x", way, hop), piece, lambda: here.x_dev, comes)
                relay((kind, "y", way, hop), piece, lambda: here.y_dev, comes)
            relay((kind, "sz", way, hop), piece, lambda: here.sib_dev, comes)
            if kind not in "va":
                other = lambda way=way: region(kind, here.origin(way, hop), here.d_quarter, 0)
                receive((kind, "h", way, hop), other, comes)
                if hop + 1 < here.depth:
                    relay((kind, "h", way, hop + 1), other, onward, comes, ahead)
                relay((kind, "sh", way, hop), other, lambda: here.sib_dev, comes)

    def diagonal(kind, hop):
        by_y, by_x = ("x", 0 if kind == "a" else 1, here.y_dev), ("y", 1, here.x_dev)
        if kind == "a":
            return [by_y, by_x]
        return [by_x if (kind == "e") == (hop % 2 == 1) else by_y]

    def pass_xy(kind, hop):
        for way in range(2):
            comes = here.comes(way, hop)
            for name, part in (("x", here.x_quarter), ("y", here.y_quarter)):
                piece = lambda way=way, part=part: region(kind, here.origin(way, hop), part)
                receive((kind, name, way, hop), piece, comes)
                for back, side, device in diagonal(kind, hop):
                    if back == name:
                        rest = lambda way=way, part=part, side=side: region(kind, here.origin(way, hop), part, side)
                        relay((kind, "d", side, way, hop), rest, lambda device=device: device, comes)
                relay((kind, "s" + name, way, hop), piece, lambda: here.sib_dev, comes)

    def pass_d(kind, number):
        for way in range(2):
            comes = here.comes(way, number)
            for _, side, _ in diagonal(kind, number):
                rest = lambda way=way, side=side: region(kind, here.origin(way, number), here.d_quarter, side)
                receive((kind, "d", side, way, number), rest, comes)
                relay((kind, "sd", side, way, number), rest, lambda: here.sib_dev, comes)

    def from_sib(kind, name, part, side=None):
        if name == "sd":
            for side in range(2):
                if kind == "a" or side == 1:
                    from_sib(kind, ("sd", side), part, side)
                else:
                    from_sib(kind, "sh", part, side)
            return
        name = name if isinstance(name, tuple) else (name,)
        for way, hop in routes:
            piece = lambda way=way, hop=hop: region(kind, here.origin(way, hop, True), part, side)
            receive((kind, *name, way, hop), piece, here.comes(way, hop))

    low = low_lanes(share)
    for pair in range(heads // 2):
        tiles = [proj_ref[:, slice(b * width + pair * LANES, b * width + (pair + 1) * LANES)] for b in range(6)]
        turned = [swap_halves(tile) for tile in tiles]
        for odd in range(2):
            for b in range(3):
                left, right = (turned[2 * b], tiles[2 * b + 1]) if odd else (tiles[2 * b], turned[2 * b + 1])
                at = (2 * pair + odd) * GROUP + b * LANES
                a_full[spot(me * share, share, 16), at : at + LANES] = jnp.where(low, left, right).astype(BF16)
    v_all[me] = jnp.zeros_like(v_all[me])
    v_all[me, 0 : vec_ref.shape[0], 0 : vec_ref.shape[1]] = vec_ref[...].astype(BF16)

    here.greet_near()
    send_z("a")
    send_z("v")
    send_own("v")
    send_own("a")

    for copy in loads:
        copy.wait()
    inner = w1_ref.shape[1]
    e_own[:, 0:inner] = w1_ref[...].astype(BF16)
    e_own[:, inner : inner + width] = wo_ref[...].astype(BF16)
    e_own[:, inner + width :] = jnp.zeros((share, e_own.shape[1] - inner - width), BF16)
    w2_own[...] = w2_ref[...].astype(BF16)
    copy_e = pltpu.make_async_copy(e_own, whole("e", me), local.at[0])
    copy_w = pltpu.make_async_copy(w2_own, whole("w", me), local.at[1])
    copy_e.start()
    copy_w.start()

    xt_ref[...] = jnp.transpose(x_ref[...])

    length = seg_ref.shape[1]
    lane = lax.broadcasted_iota(jnp.int32, (length, LANES), 1)
    for seq in range(seg_ref.shape[0]):
        at = slice(seq * length, (seq + 1) * length)
        segment, kind = (
            jnp.transpose(jnp.broadcast_to(ref[seq : seq + 1, :].astype(F32), (LANES, length)))
            for ref in (seg_ref, type_ref)
        )
        same = segment == lane.astype(F32)
        word = jnp.where(kind == 0.0, 1.0, 0.0)
        word_ref[at] = word.astype(BF16)
        km_ref[at] = jnp.where(lane < HEAD, word, 1.0 - word).astype(BF16)
        qa_ref[at] = jnp.where(same & (lane < 8), 1.0, 0.0).astype(BF16)
        ka_ref[at] = jnp.where(
            lane < 8, jnp.where(same, 0.0, FAR), jnp.where(lane < 11, 1.0, 0.0)
        ).astype(BF16)

    def hop(kind, number):
        if number < here.depth:
            pass_z(kind, number)
            if kind == "a":
                pass_z("v", number)

    def turn(kind, number):
        if number < here.depth:
            pass_xy(kind, number)

    deeper = range(4, here.depth)
    hop("a", 1)
    hop("a", 2)
    send_z("e")
    send_own("e")
    turn("a", 1)
    hop("a", 3)
    turn("a", 2)
    for number in deeper:
        hop("a", number)
        turn("a", number - 1)

    links.arrived(("v", "o"), v_all.at[here.sib], here.sib_dev)
    for way, number in routes:
        receive(
            ("v", "sz", way, number),
            lambda way=way, number=number: v_all.at[here.origin(way, number, True)],
            here.comes(way, number),
        )
    span = vec_ref.shape[1]
    vec_out[...] = jnp.concatenate([v_all[n].astype(F32)[:, 0:span] for n in range(narrow)], axis=1)
    low1 = low_lanes(1)
    for head in range(heads):
        cols = slice((head // 2) * LANES, (head // 2 + 1) * LANES)
        row = [vec_out[r : r + 1, cols] for r in range(4)] + [jnp.zeros((1, LANES), F32), vec_out[4:5, cols]]
        for b in range(3):
            left, right = row[2 * b], row[2 * b + 1]
            left, right = (swap_halves(left), right) if head % 2 else (left, swap_halves(right))
            at = head * GROUP + b * LANES
            bias[0:1, at : at + LANES] = jnp.where(low1, left, right)

    links.arrived(("a", "o"), whole("a", here.sib), here.sib_dev)
    outs = []

    def project(index, part):
        size = 256
        cols = spot(part * quarter, quarter, LANES)
        add = bias[0:1, cols]

        def tile(i, carry):
            at = spot(i * size, size, size)
            prod = mm(x_ref[at, :], a_full[:, cols])
            word = word_ref[at, :] > 0
            for head in range(quarter // GROUP):
                group = slice(head * GROUP, (head + 1) * GROUP)
                out = slice(head * LANES, (head + 1) * LANES)
                query, keyval = qkv_tile(prod[:, group], add[:, group], word)
                q_s[part, at, out] = query
                kv_s[part, at, out] = keyval
            return carry

        lax.fori_loop(0, rows // size, tile, 0)
        wide = q_s.shape[2]
        for number, (source, target) in enumerate(((q_s, q_out), (kv_s, kv_out))):
            copy = pltpu.make_async_copy(
                source.at[part], target.at[:, spot(part * wide, wide, LANES)], local.at[2 + 2 * index + number]
            )
            copy.start()
            outs.append(copy)

    from_sib("a", "sz", here.wide)
    project(0, here.wide)
    hop("e", 1)
    turn("a", here.depth - 1)
    from_sib("a", "sx", here.x_quarter)
    project(1, here.x_quarter)
    for number in hops:
        pass_d("a", number)
    hop("e", 2)
    send_z("w")
    send_own("w")
    turn("e", 1)
    from_sib("a", "sy", here.y_quarter)
    project(2, here.y_quarter)
    hop("e", 3)
    from_sib("a", "sd", here.d_quarter)
    project(3, here.d_quarter)
    copy_a = pltpu.make_async_copy(a_full, a_out, local.at[10])
    copy_a.start()
    low_seq = low_lanes(length)
    per = quarter // GROUP

    def attend(pair, seq):
        at = slice(seq * length, (seq + 1) * length)
        contexts = []
        for head in (2 * pair, 2 * pair + 1):
            cols = slice(head % per * LANES, (head % per + 1) * LANES)
            context, extra = attend_head(
                q_s[head // per, at, cols], kv_s[head // per, at, cols], qa_ref[at], ka_ref[at], km_ref[at]
            )
            aug_s[at, head * LANES : (head + 1) * LANES] = extra
            contexts.append(context)
        both = jnp.where(low_seq, swap_halves(contexts[0]), contexts[1])
        ctx_s[at, pair * LANES : (pair + 1) * LANES] = both.astype(BF16)

    def attended(pair):
        for number, (source, target, wide) in enumerate(((ctx_s, ctx_out, LANES), (aug_s, aug_out, 2 * LANES))):
            cols = slice(pair * wide, (pair + 1) * wide)
            copy = pltpu.make_async_copy(source.at[:, cols], target.at[:, cols], local.at[11 + 2 * pair + number])
            copy.start()
            outs.append(copy)

    def later(kind, first, last):
        for number in range(first, last):
            turn(kind, number)

    between = [
        lambda: [turn("e", 2), pass_d("e", 1)],
        lambda: hop("w", 1),
        lambda: [turn("e", 3), pass_d("e", 2)],
        lambda: [hop("w", 2), [hop("e", number) for number in deeper], later("e", 4, here.depth)],
        lambda: [turn("w", 1), [pass_d("e", number) for number in range(3, here.depth)]],
        lambda: hop("w", 3),
        lambda: [turn("w", 2), pass_d("w", 1)],
        lambda: [hop("w", number) for number in deeper],
        lambda: [later("w", 3, here.depth), pass_d("w", 2)],
        lambda: [pass_d("w", number) for number in range(3, here.depth)],
    ]
    units = [(pair, seq) for pair in range(heads // 2) for seq in range(seg_ref.shape[0])]
    for index, (pair, seq) in enumerate(units):
        attend(pair, seq)
        if seq == seg_ref.shape[0] - 1:
            attended(pair)
        if index < len(between):
            between[index]()
    for action in between[len(units) :]:
        action()
    for kind in ("e", "w"):
        links.arrived((kind, "o"), whole(kind, here.sib), here.sib_dev)
        for name, part in (("sz", here.wide), ("sx", here.x_quarter), ("sy", here.y_quarter)):
            from_sib(kind, name, part)
        from_sib(kind, "sd", here.d_quarter)
    links.finish()
    for copy in (copy_e, copy_w, copy_a, *outs):
        copy.wait()


def gather_call(narrow, x, proj, wo, w1, w2, vec, segments, types):
    rows, width = x.shape
    share, deep, inner = proj.shape[0], w2.shape[0], w1.shape[1]
    ecols = inner + width + 2 * LANES
    heads = width // HEAD
    depth = narrow // 2
    count = 3 * (1 + 20 * (depth - 1)) + 1 + 4 * (depth - 1)
    vmem = pl.BlockSpec(memory_space=pltpu.VMEM)
    hbm = pl.BlockSpec(memory_space=pl.ANY)
    shape = jax.ShapeDtypeStruct
    part = heads // 4 * LANES
    return pl.pallas_call(
        functools.partial(gather_kernel, narrow),
        in_specs=[vmem] * 4 + [hbm] * 4,
        out_specs=[hbm] * 7 + [vmem] * 5,
        out_shape=[
            shape((rows, heads * LANES), BF16),
            shape((rows, heads * LANES), BF16),
            shape((rows, width), BF16),
            shape((rows, heads * LANES), BF16),
            shape((width, proj.shape[1]), BF16),
            shape((width, ecols), BF16),
            shape((deep * narrow, width), BF16),
            shape((16, width), F32),
            shape((rows, LANES), BF16),
            shape((rows, LANES), BF16),
            shape((rows, LANES), BF16),
            shape((width, rows), BF16),
        ],
        scratch_shapes=[
            pltpu.VMEM((width, proj.shape[1]), BF16),
            pltpu.VMEM((share, ecols), BF16),
            pltpu.VMEM((deep, width), BF16),
            pltpu.VMEM((narrow, 16, LANES), BF16),
            pltpu.VMEM((8, proj.shape[1]), F32),
            pltpu.VMEM((4, rows, part), BF16),
            pltpu.VMEM((4, rows, part), BF16),
            pltpu.VMEM((rows, width), BF16),
            pltpu.VMEM((rows, heads * LANES), BF16),
            pltpu.VMEM((rows, LANES), BF16),
            pltpu.VMEM(x.shape, x.dtype),
            pltpu.VMEM(wo.shape, F32),
            pltpu.VMEM(w1.shape, F32),
            pltpu.VMEM(w2.shape, F32),
            pltpu.SemaphoreType.DMA((count,)),
            pltpu.SemaphoreType.DMA((count,)),
            pltpu.SemaphoreType.DMA((15 + heads,)),
        ],
        compiler_params=pltpu.CompilerParams(
            vmem_limit_bytes=VMEM_LIMIT, collective_id=0, has_side_effects=True
        ),
        name="gather",
    )(proj, vec, segments, types, x, wo, w1, w2)


def key_pair(keyval, kmask, low):
    wide = keyval.astype(F32)
    return (jnp.where(low, wide, swap_halves(wide)) * kmask.astype(F32)).astype(BF16)


def attend_head(query, keyval, qaug, kaug, kmask):
    rows = query.shape[0]
    low = low_lanes(rows)
    lane = lax.broadcasted_iota(jnp.int32, (rows, LANES), 1)
    keys = jnp.concatenate([key_pair(keyval, kmask, low), kaug], axis=1)
    scores = mm_nt(jnp.concatenate([query, qaug], axis=1), keys)
    top = jnp.max(scores, axis=1, keepdims=True)
    weight = jnp.exp2((scores - top) * LOG2E).astype(BF16)
    ones_val = jnp.where(low, 1.0, keyval.astype(F32)).astype(BF16)
    both = mm(weight, ones_val)
    total = swap_halves(both)
    log_total = top + jnp.log(jnp.where(low, both, total))
    high, mid, rest = split_three(log_total)
    extra = jnp.where(lane == 8, -high, jnp.where(lane == 9, -mid, jnp.where(lane == 10, -rest, 0.0)))
    return both / total, jnp.where(lane < 8, qaug.astype(F32), extra).astype(BF16)


def attend_kernel(q_ref, kv_ref, qa_ref, ka_ref, km_ref, ctx_ref, aug_ref):
    outs = []
    for part in range(2):
        cols = slice(part * LANES, (part + 1) * LANES)
        out, aug_ref[:, cols] = attend_head(q_ref[:, cols], kv_ref[:, cols], qa_ref[...], ka_ref[...], km_ref[...])
        outs.append(out)
    ctx_ref[...] = jnp.where(low_lanes(q_ref.shape[0]), swap_halves(outs[0]), outs[1]).astype(BF16)


def attend_call(q, kv, qa, ka, km, length):
    rows, cols = q.shape
    seqs, steps = rows // length, cols // (2 * LANES)
    pair = pl.BlockSpec((length, 2 * LANES), lambda s, i: (s, i))
    one = pl.BlockSpec((length, LANES), lambda s, i: (s, 0))
    return pl.pallas_call(
        attend_kernel,
        grid=(seqs, steps),
        in_specs=[pair, pair, one, one, one],
        out_specs=[pl.BlockSpec((length, LANES), lambda s, i: (s, i)), pair],
        out_shape=[
            jax.ShapeDtypeStruct((rows, cols // 2), BF16),
            jax.ShapeDtypeStruct((rows, cols), BF16),
        ],
        compiler_params=pltpu.CompilerParams(vmem_limit_bytes=VMEM_LIMIT),
        name="attend",
    )(q, kv, qa, ka, km)


def attend_back_head(query, keyval, aug, gcon, con, kaug, kmask, word, odd, low, lane):
    keys = key_pair(keyval, kmask, low)
    scores_t = mm_nt(jnp.concatenate([keys, kaug], axis=1), jnp.concatenate([query, aug], axis=1))
    probs_t = jnp.exp2(scores_t * LOG2E)
    gwide = gcon.astype(F32)
    prod = gwide * con.astype(F32)
    prod = jnp.where(low, 0.0, prod) if odd else jnp.where(low, prod, 0.0)
    high, mid, rest = split_three(jnp.sum(prod, axis=1, keepdims=True))
    extra = jnp.where(lane == 0, -high, jnp.where(lane == 1, -mid, jnp.where(lane == 2, -rest, 0.0)))
    ghead = jnp.where(low, extra, gwide if odd else swap_halves(gwide)).astype(BF16)
    ones_val = jnp.where(low, jnp.where(lane < 3, 1.0, 0.0), keyval.astype(F32)).astype(BF16)
    gscores_t = (probs_t * mm_nt(ones_val, ghead)).astype(BF16)
    blank = jnp.zeros_like(ghead)
    both = mm(
        jnp.concatenate([probs_t.astype(BF16), gscores_t], axis=1),
        jnp.concatenate(
            [jnp.concatenate([ghead, blank], axis=1), jnp.concatenate([blank, query], axis=1)], axis=0
        ),
    )
    gval, gkey = both[:, 0:LANES], both[:, LANES:]
    gquery = (jnp.transpose(mm_tn(keys, gscores_t)) * (HEAD**-0.5)).astype(BF16)
    zero = jnp.zeros_like(gquery)
    gkey = jnp.where(kmask.astype(F32) > 0, gkey, 0.0)
    gkey = gkey + swap_halves(gkey)
    return (
        jnp.where(word, gquery, zero),
        jnp.where(word, zero, gquery),
        jnp.where(low, gkey, gval).astype(BF16),
    )


def attend_back_kernel(
    length, x_ref, q_ref, kv_ref, aug_ref, gc_ref, ctx_ref, ka_ref, km_ref, word_ref, gp_ref, gw_ref, sum_ref, xt
):
    rows = x_ref.shape[0]

    @pl.when(pl.program_id(0) == 0)
    def _():
        xt[...] = jnp.transpose(x_ref[...])

    low = low_lanes(length)
    lane = lax.broadcasted_iota(jnp.int32, (length, LANES), 1)
    for part in range(2):
        cols = slice(part * LANES, (part + 1) * LANES)
        for seq in range(rows // length):
            here = slice(seq * length, (seq + 1) * length)
            tiles = attend_back_head(
                q_ref[here, cols], kv_ref[here, cols], aug_ref[here, cols], gc_ref[here], ctx_ref[here],
                ka_ref[here], km_ref[here], word_ref[here] > 0, part == 1, low, lane,
            )
            for index, tile in enumerate(tiles):
                at = part * GROUP + index * LANES
                gp_ref[here, at : at + LANES] = tile
    grads = gp_ref[...]
    gw_ref[...] = mm(xt[...], grads).astype(BF16)
    sum_ref[...] = jnp.sum(fold(grads.astype(F32)), axis=0, keepdims=True)


def attend_back_call(x, q, kv, aug, gc, ctx, ka, km, word, length):
    rows, width = x.shape
    pairs = q.shape[1] // (2 * LANES)
    head = pl.BlockSpec((rows, 2 * LANES), lambda h: (0, h))
    pair = pl.BlockSpec((rows, LANES), lambda h: (0, h))
    one = pl.BlockSpec((rows, LANES), lambda h: (0, 0))
    return pl.pallas_call(
        functools.partial(attend_back_kernel, length),
        grid=(pairs,),
        in_specs=[pl.BlockSpec((rows, width), lambda h: (0, 0)), head, head, head, pair, pair, one, one, one],
        out_specs=[
            pl.BlockSpec((rows, 2 * GROUP), lambda h: (0, h)),
            pl.BlockSpec((width, 2 * GROUP), lambda h: (0, h)),
            pl.BlockSpec((1, 2 * GROUP), lambda h: (0, h)),
        ],
        out_shape=[
            jax.ShapeDtypeStruct((rows, pairs * 2 * GROUP), BF16),
            jax.ShapeDtypeStruct((width, pairs * 2 * GROUP), BF16),
            jax.ShapeDtypeStruct((1, pairs * 2 * GROUP), F32),
        ],
        scratch_shapes=[pltpu.VMEM((width, rows), BF16)],
        compiler_params=pltpu.CompilerParams(vmem_limit_bytes=VMEM_LIMIT),
        name="attend_back",
    )(x, q, kv, aug, gc, ctx, ka, km, word)


class Chunk:
    def __init__(self, name, shape, total, plane=(), end=None, via=None):
        self.name = name
        self.rows, self.cols = shape
        self.total, self.via = total, via
        for label, ref in zip(("r1a", "r1b", "r2a", "r2b"), plane):
            setattr(self, label, ref)
        if end is not None:
            self.rz, self.final = end

    def row_half(self, wide):
        return spot(wide // 2 * (self.rows // 2), self.rows // 2, 16)

    def col_half(self, wide):
        return spot(lax.rem(wide, 2) * (self.cols // 2), self.cols // 2, LANES)

    def quarter(self, wide):
        return self.row_half(wide), self.col_half(wide)

    def mine(self, z, wide):
        if self.total.shape[1:] != (self.rows, self.cols):
            return self.total.at[z]
        return self.total.at[(z, *self.quarter(wide))]


def plane_scratch(depth, rows, cols):
    half = depth // 2
    return [
        pltpu.VMEM((half, rows, cols // 2), BF16),
        pltpu.VMEM((half, rows // 2, cols), BF16),
        pltpu.VMEM((half, rows // 2, cols // 2), BF16),
        pltpu.VMEM((half, rows // 2, cols // 2), BF16),
    ]


def end_scratch(depth, rows, cols):
    return [pltpu.VMEM((depth - 1, rows // 2, cols // 2), BF16), pltpu.VMEM((rows, cols), BF16)]


class Reducer:
    def __init__(self, here, send, recv):
        self.here = here
        self.links = Links(send, recv)
        self.send, self.arrived, self.finish = self.links.send, self.links.arrived, self.links.finish

    def pair_send(self, chunk, sources, only=None):
        here = self.here
        for z in range(here.depth) if only is None else (only,):
            for part, (_, cols) in enumerate(sources(0)):

                def build(z=z, part=part, cols=cols):
                    owner = 2 * z + 1 - here.core
                    return sources(owner)[part][0], chunk.total.at[z, :, cols], here.sib_dev

                self.send((chunk.name, "s", z, part), build)

    def pair_wait(self, chunk, sources):
        for z in range(self.here.depth):
            for part, (_, cols) in enumerate(sources(0)):
                self.arrived((chunk.name, "s", z, part), chunk.total.at[z, :, cols], self.here.sib_dev)

    def lower(self):
        return slice(0, self.here.depth // 2)

    def upper(self):
        return slice(self.here.depth // 2, self.here.depth)

    def plane_send(self, chunk):
        here = self.here
        cols, rows = (lambda: chunk.col_half(here.x_quarter)), (lambda: chunk.row_half(here.y_quarter))
        self.send((chunk.name, "1a"), lambda: (chunk.total.at[self.lower(), :, cols()], chunk.r1a, here.x_dev))
        self.send((chunk.name, "1b"), lambda: (chunk.total.at[self.upper(), rows(), :], chunk.r1b, here.y_dev))

    def plane_add(self, chunk):
        here = self.here
        total = chunk.total
        self.arrived((chunk.name, "1a"), chunk.r1a, here.x_dev)
        self.arrived((chunk.name, "1b"), chunk.r1b, here.y_dev)
        rows, cols = chunk.quarter(here.wide)
        total[self.lower(), :, cols] = total[self.lower(), :, cols] + chunk.r1a[...]
        total[self.upper(), rows, :] = total[self.upper(), rows, :] + chunk.r1b[...]

    def plane_next(self, chunk):
        here = self.here
        total = chunk.total

        def first():
            return total.at[(self.lower(), *chunk.quarter(here.y_quarter))], chunk.r2a, here.y_dev

        def second():
            return total.at[(self.upper(), *chunk.quarter(here.x_quarter))], chunk.r2b, here.x_dev

        self.send((chunk.name, "2a"), first)
        self.send((chunk.name, "2b"), second)

    def plane_turn(self, chunk):
        self.plane_add(chunk)
        self.plane_next(chunk)

    def plane_done(self, chunk):
        here = self.here
        self.arrived((chunk.name, "2a"), chunk.r2a, here.y_dev)
        self.arrived((chunk.name, "2b"), chunk.r2b, here.x_dev)
        rows, cols = chunk.quarter(here.wide)
        for part, value in ((self.lower(), chunk.r2a), (self.upper(), chunk.r2b)):
            chunk.total[part, rows, cols] = chunk.total[part, rows, cols] + value[...]

    def depth_send(self, chunk):
        here = self.here
        for k in range(1, here.depth):

            def build(k=k):
                piece = chunk.mine(lax.rem(here.z + k, here.depth), here.wide)
                return piece, chunk.rz.at[k - 1], here.z_dev(k)

            self.send((chunk.name, "z", k), build)

    def share_send(self, chunk):
        here = self.here
        for k in range(1, here.depth):
            self.arrived((chunk.name, "z", k), chunk.rz.at[k - 1], here.z_dev(k))
        done = chunk.mine(here.z, here.wide)[...].astype(F32)
        for k in range(1, here.depth):
            done = done + chunk.rz[k - 1].astype(F32)
        done = done.astype(BF16)
        rows, cols = chunk.quarter(here.wide)
        chunk.final[rows, cols] = done

        ways = [("fx", here.x_dev), ("fy", here.y_dev)] + ([] if chunk.via else [("fd", here.d_dev)])
        for name, device in ways:
            self.send((chunk.name, name), lambda device=device: self.share_copy(chunk, here.wide, device))
        return squares(done)

    def share_copy(self, chunk, quarter, device):
        piece = chunk.final.at[chunk.quarter(quarter)]
        return piece, piece, device

    def share_pass(self, chunk):
        here = self.here
        by_x = chunk.via == "x"
        name, quarter, device = ("fy", here.y_quarter, here.x_dev) if by_x else ("fx", here.x_quarter, here.y_dev)
        self.arrived((chunk.name, name), chunk.final.at[chunk.quarter(quarter)], device)
        self.send((chunk.name, "fd"), lambda: self.share_copy(chunk, quarter, device))

    def share_wait(self, chunk):
        here = self.here
        ways = (("fx", here.x_quarter, here.x_dev), ("fy", here.y_quarter, here.y_dev), ("fd", here.d_quarter, here.d_dev))
        seen = {"x": "fy", "y": "fx"}.get(chunk.via)
        for name, quarter, device in ways:
            if name != seen:
                self.arrived((chunk.name, name), chunk.final.at[chunk.quarter(quarter)], device)


def squares(value):
    total = jnp.zeros((8, LANES), F32)
    rows, cols = value.shape
    for start in range(0, cols, LANES):
        tile = value[:, start : start + LANES].astype(F32)
        total = total + jnp.sum((tile * tile).reshape(rows // 8, 8, LANES), axis=0)
    return total


def pair_groups(pairs):
    return (pairs // 3, pairs // 3, pairs // 6, pairs // 6)


def reduce_kernel(
    narrow, length, groups, deep,
    xt, q_ref, kv_ref, aug_ref, gc_ref, ctx_ref, wp_ref, ka_ref, km_ref, word_ref, gvec_ref,
    gr1_ref, t1_ref, tw_ref, gwo_ref,
    ig_ref, f1_ref, fo_ref, fw_ref, fa_ref, v_ref, n_ref,
    gp, ig, *scratch,
):
    step = pl.program_id(0)
    width, rows = xt.shape
    pairs = sum(groups)
    _, _, share, part = t1_ref.shape
    here = Place(narrow)
    scratch = list(scratch)
    red = Reducer(here, scratch[-3], scratch[-2])
    local = scratch[-1]

    def take(count):
        taken, scratch[:count] = scratch[:count], []
        return taken

    chunk_w = Chunk("w", (deep, width), take(1)[0], (), take(2), "x")
    chunk_1 = [Chunk(("1", j), (share, part), take(1)[0], take(4), take(2), "yx"[j]) for j in range(2)]
    gw, chunk_a = [], []
    for j in range(len(groups)):
        gw += take(1)
        via = ("y", "x", None, None)[j]
        chunk_a.append(Chunk(("a", j), (share, gw[j].shape[1]), take(1)[0], take(4), take(2), via))
    v0, v1, v2, vs, vx, vy, vz, n0, np, n1, ns, nz = take(12)
    begin = [sum(groups[:j]) for j in range(len(groups) + 1)]
    both = 2 * GROUP
    wide = groups[0] * both

    def sources_a(j):
        return lambda owner: [(gw[j].at[spot(owner * share, share, 16), :], slice(0, gw[j].shape[1]))]

    def load(index):
        source, target = (
            (t1_ref.at[0], chunk_1[0].total),
            (t1_ref.at[1], chunk_1[1].total),
            (tw_ref, chunk_w.total),
            (gwo_ref, gw[0].at[:, wide : wide + width]),
            (gr1_ref, ig),
        )[index]
        return pltpu.make_async_copy(source, target, local.at[index])

    def stores():
        copies = [(chunk_w.final, fw_ref)]
        copies += [(chunk.final, f1_ref.at[:, j * part : (j + 1) * part]) for j, chunk in enumerate(chunk_1)]
        copies += [(chunk_a[0].final.at[:, wide : wide + width], fo_ref)]
        for j, chunk in enumerate(chunk_a):
            cols = slice(begin[j] * both, begin[j + 1] * both)
            copies.append((chunk.final.at[:, 0 : groups[j] * both], fa_ref.at[:, cols]))
        return [pltpu.make_async_copy(a, b, local.at[5 + i]) for i, (a, b) in enumerate(copies)]

    def merge(j):
        def one(z, carry):
            mine = spot((2 * z + here.core) * share, share, 16)
            chunk_a[j].total[z] = chunk_a[j].total[z] + gw[j][mine, :]
            return carry

        red.pair_wait(chunk_a[j], sources_a(j))
        lax.fori_loop(0, here.depth, one, 0)
        red.plane_send(chunk_a[j])

    def turn_z(chunk):
        red.plane_done(chunk)
        red.depth_send(chunk)

    @pl.when(step == 0)
    def _():
        for index in range(5):
            load(index).start()
        here.greet()
        load(0).wait()
        red.plane_next(chunk_1[0])
        load(1).wait()
        red.plane_send(chunk_1[1])
        load(2).wait()
        red.depth_send(chunk_w)
        v0[...] = gvec_ref[...]
        n0[...] = jnp.zeros_like(n0)

    def at(when):
        def run(action):
            def body():
                action()

            pl.when(step == when)(body)

        return run

    def finish(chunk):
        n0[...] += red.share_send(chunk)

    def vec_pair():
        red.arrived(("v", "s"), vs, here.sib_dev)
        v1[...] = v0[...] + vs[...]
        red.send(("v", "x"), lambda: (v1, vx, here.x_dev))

    def vec_plane():
        red.arrived(("v", "x"), vx, here.x_dev)
        v2[...] = v1[...] + vx[...]
        red.send(("v", "y"), lambda: (v2, vy, here.y_dev))

    def vec_depth():
        red.arrived(("v", "y"), vy, here.y_dev)
        vz[here.z] = v2[...] + vy[...]
        for k in range(1, here.depth):
            red.send(("v", "z", k), lambda k=k: (vz.at[here.z], vz.at[here.z], here.z_dev(k)))

    def vec_done():
        for k in range(1, here.depth):
            red.arrived(("v", "z", k), vz.at[here.behind(k) // 2], here.z_dev(k))
        vec = vz[0]
        for z in range(1, here.depth):
            vec = vec + vz[z]
        v_ref[...] = vec

    a = chunk_a
    last = len(groups) - 1
    plan = {
        2: [lambda: load(3).wait(), lambda: turn_z(chunk_1[0])],
        3: [lambda: red.plane_turn(chunk_1[1])],
        4: [lambda: finish(chunk_w)],
        5: [lambda: merge(0), lambda: turn_z(chunk_1[1])],
        6: [lambda: red.share_pass(chunk_w)],
        7: [lambda: finish(chunk_1[0])],
        8: [lambda: red.plane_turn(a[0])],
        9: [lambda: merge(1), lambda: red.share_pass(chunk_1[0])],
        10: [lambda: turn_z(a[0]), lambda: finish(chunk_1[1])],
        11: [lambda: merge(2), lambda: red.plane_turn(a[1]), lambda: red.share_pass(chunk_1[1])],
    }
    tail = [
        [lambda: turn_z(a[1])],
        [lambda: merge(3), vec_pair, lambda: red.plane_turn(a[2])],
        [lambda: turn_z(a[2])],
        [lambda: red.plane_turn(a[3]), lambda: finish(a[0]), vec_plane],
        [lambda: turn_z(a[3]), lambda: finish(a[1]), lambda: red.share_pass(a[0]), vec_depth],
        [lambda: finish(a[2]), vec_done, lambda: red.share_pass(a[1])],
    ]

    def advance(half):
        for when, actions in plan.items():
            if when % 2 == half:
                for action in actions:
                    at(when // 2)(action)

    for index, actions in enumerate(tail):
        for action in actions:
            at(pairs + index)(action)

    @pl.when(step < pairs)
    def _():
        low = low_lanes(length)
        lane = lax.broadcasted_iota(jnp.int32, (length, LANES), 1)
        for part in range(2):
            advance(part)
            cols = slice(part * LANES, (part + 1) * LANES)
            for seq in range(rows // length):
                mine = slice(seq * length, (seq + 1) * length)
                tiles = attend_back_head(
                    q_ref[mine, cols], kv_ref[mine, cols], aug_ref[mine, cols], gc_ref[mine], ctx_ref[mine],
                    ka_ref[mine], km_ref[mine], word_ref[mine] > 0, part == 1, low, lane,
                )
                for index, tile in enumerate(tiles):
                    start = part * GROUP + index * LANES
                    gp[step, mine, start : start + LANES] = tile
        grads = gp[step]
        product = mm(xt[...], grads).astype(BF16)
        for j in range(len(groups)):

            @pl.when((step >= begin[j]) & (step < begin[j + 1]))
            def _():
                gw[j][:, spot((step - begin[j]) * both, both, LANES)] = product

        sums = jnp.sum(fold(grads.astype(F32)), axis=0, keepdims=True)
        low1 = low_lanes(1)
        place = spot(step * LANES, LANES, LANES)
        for b in range(3):
            even = sums[:, b * LANES : (b + 1) * LANES]
            odd = sums[:, GROUP + b * LANES : GROUP + (b + 1) * LANES]
            second = jnp.where(low1, swap_halves(even), odd)
            if b < 2:
                v0[2 * b : 2 * b + 1, place] = jnp.where(low1, even, swap_halves(odd))
                v0[2 * b + 1 : 2 * b + 2, place] = second
            else:
                v0[4:5, place] = second

    for j in range(len(groups)):
        at(begin[j + 1] - 1)(lambda j=j: red.pair_send(chunk_a[j], sources_a(j)))

    at(pairs - 1)(lambda: red.send(("v", "s"), lambda: (v0, vs, here.sib_dev)))
    at(pairs)(lambda: load(4).wait())

    @pl.when(step >= pairs)
    def _():
        ig[...] += mm_nt(gp[step - pairs], wp_ref[...])

    @pl.when(step == 2 * pairs - 1)
    def _():
        finish(a[last])
        np[here.wide] = n0[...]
        for name, device in (("nx", here.x_dev), ("ny", here.y_dev), ("nd", here.d_dev)):
            red.send((name,), lambda device=device: (np.at[here.wide], np.at[here.wide], device))
        vec = v_ref[...]
        square = jnp.sum(jnp.sum(vec * vec, axis=0, keepdims=True), axis=1, keepdims=True)
        ig_ref[...] = ig[...].astype(BF16)
        ways = (("nx", here.x_quarter, here.x_dev), ("ny", here.y_quarter, here.y_dev), ("nd", here.d_quarter, here.d_dev))
        for name, quarter, device in ways:
            red.arrived((name,), np.at[quarter], device)
        n1[...] = (np[0] + np[1]) + (np[2] + np[3])
        red.send(("n", "s"), lambda: (n1, ns, here.sib_dev))
        for chunk in (chunk_w, *chunk_1, *a):
            red.share_wait(chunk)
        for copy in stores():
            copy.start()
        red.arrived(("n", "s"), ns, here.sib_dev)
        nz[here.z] = n1[...] + ns[...]
        for k in range(1, here.depth):
            red.send(("n", "z", k), lambda k=k: (nz.at[here.z], nz.at[here.z], here.z_dev(k)))
        for k in range(1, here.depth):
            red.arrived(("n", "z", k), nz.at[here.behind(k) // 2], here.z_dev(k))
        total = nz[0]
        for z in range(1, here.depth):
            total = total + nz[z]
        every = jnp.sum(jnp.sum(total, axis=0, keepdims=True), axis=1, keepdims=True)
        n_ref[...] = jnp.broadcast_to(every + square, n_ref.shape)
        red.finish()
        for copy in stores():
            copy.wait()


def reduce_call(narrow, xt, q, kv, aug, gc, ctx, wp, ka, km, word, gvec, gr1, t1, tw, gwo, deep, length):
    width, rows = xt.shape
    pairs = q.shape[1] // (2 * LANES)
    groups = pair_groups(pairs)
    _, depth, share, inner = t1.shape

    def now(h):
        return jnp.minimum(h, pairs - 1)

    def fixed(shape):
        return pl.BlockSpec(shape, lambda h: (0, 0), pipeline_mode=pl.Buffered(1))

    head = pl.BlockSpec((rows, 2 * LANES), lambda h: (0, now(h)))
    pair = pl.BlockSpec((rows, LANES), lambda h: (0, now(h)))
    later = pl.BlockSpec((width, 2 * GROUP), lambda h: (0, jnp.maximum(h - pairs, 0)))
    one = fixed((rows, LANES))
    hbm = pl.BlockSpec(memory_space=pl.ANY)
    shape = jax.ShapeDtypeStruct
    vec = pltpu.VMEM((16, width), F32)
    tile = pltpu.VMEM((8, LANES), F32)
    scratch = [pltpu.VMEM((pairs, rows, 2 * GROUP), BF16), pltpu.VMEM((rows, width), F32)]
    scratch += [pltpu.VMEM(tw.shape, BF16), *end_scratch(depth, deep, width)]
    for _ in range(2):
        scratch += [pltpu.VMEM((depth, share, inner), BF16)]
        scratch += [*plane_scratch(depth, share, inner), *end_scratch(depth, share, inner)]
    for j, size in enumerate(groups):
        cols = size * 2 * GROUP + (width if j == 0 else 0)
        scratch += [
            pltpu.VMEM((width, cols), BF16),
            pltpu.VMEM((depth, share, cols), BF16),
            *plane_scratch(depth, share, cols),
            *end_scratch(depth, share, cols),
        ]
    several = pltpu.VMEM((depth, 8, LANES), F32)
    scratch += [vec] * 6 + [pltpu.VMEM((depth, 16, width), F32), tile, pltpu.VMEM((4, 8, LANES), F32), tile, tile, several]
    count = (3 + len(groups)) * (2 * depth + 6) + 2 * (4 + depth)
    scratch += [pltpu.SemaphoreType.DMA((count,))] * 2 + [pltpu.SemaphoreType.DMA((9 + len(groups),))]
    return pl.pallas_call(
        functools.partial(reduce_kernel, narrow, length, groups, deep),
        grid=(2 * pairs,),
        in_specs=[
            fixed((width, rows)), head, head, head, pair, pair, later, one, one, one, fixed((16, width)),
            hbm, hbm, hbm, hbm,
        ],
        out_specs=[fixed((rows, width)), hbm, hbm, hbm, hbm, fixed((16, width)), fixed((8, LANES))],
        out_shape=[
            shape((rows, width), BF16),
            shape((share, 2 * inner), BF16),
            shape((share, width), BF16),
            shape((deep, width), BF16),
            shape((share, pairs * 2 * GROUP), BF16),
            shape((16, width), F32),
            shape((8, LANES), F32),
        ],
        scratch_shapes=scratch,
        compiler_params=pltpu.CompilerParams(
            vmem_limit_bytes=VMEM_LIMIT, collective_id=1, has_side_effects=True
        ),
        name="reduce",
    )(xt, q, kv, aug, gc, ctx, wp, ka, km, word, gvec, gr1, t1, tw, gwo)


def gelu_pair(pre):
    bell = jnp.exp2(pre * pre * (-0.5 * LOG2E))
    share = 0.5 + 0.5 * lax.erf(pre * (0.5**0.5))
    return pre * share, share + pre * bell * 0.3989422804014327


def fold(array_in):
    rows, cols = array_in.shape
    return jnp.sum(array_in.reshape(rows // 8, 8, cols), axis=0)


def middle_kernel(
    narrow, x_hbm, ctx_hbm, cot_hbm, vec_ref, e_hbm, w2_hbm,
    out_hbm, gr1_hbm, gctx_hbm, gw1_hbm, gwo_hbm, gw2_hbm, gvec_ref,
    wo, w1, w2, io, ctx, h1_s, n1_s, inv_s, act_s, slope_s, gb_s, sum_s, gw2_s, gwo_s, acc, sems, *scratch,
):
    rows, width = io.shape
    inner = w1.shape[1]
    blocks, size, block = inner // width, 256, 256
    red = None

    def load(index):
        source, target = (
            (x_hbm, io),
            (ctx_hbm, ctx),
            (e_hbm.at[:, inner : inner + width], wo),
            (e_hbm.at[:, 0:inner], w1),
            (w2_hbm, w2),
            (cot_hbm, io),
        )[index]
        return pltpu.make_async_copy(source, target, sems.at[index])

    def store(index):
        source, target = (
            (io, out_hbm),
            (sum_s, gr1_hbm),
            (io, gctx_hbm),
            (gwo_s, gwo_hbm),
            (gw2_s, gw2_hbm) if red is None else (chunk.total.at[(slice(None), *chunk.quarter(here.wide))], gw2_hbm),
            (act_s.at[0:width, :], gw1_hbm) if red is None else (chunk_1[0].total, gw1_hbm.at[0]),
            None if red is None else (chunk_1[1].total, gw1_hbm.at[1]),
        )[index]
        return pltpu.make_async_copy(source, target, sems.at[6 + index])

    def vec(row):
        return vec_ref[row : row + 1, :].astype(F32)

    def over_rows(step):
        def one(i, carry):
            step(spot(i * size, size, size))
            return carry

        lax.fori_loop(0, rows // size, one, 0)

    def over_cols(first, last, step):
        def one(i, carry):
            step(spot(i * block, block, block), i)
            return carry

        lax.fori_loop(first, last, one, 0)

    for index in (1, 2, 0, 3, 4):
        load(index).start()
    acc[...] = jnp.zeros_like(acc)
    if narrow is not None:
        here = Place(narrow)
        red = Reducer(here, scratch[0], scratch[1])
        deep, share = scratch[2].shape[1], scratch[7].shape[1]
        chunk = Chunk("w", (deep, width), scratch[2], scratch[3:7])
        part = inner // 2
        chunk_1 = [Chunk(("1", j), (share, part), scratch[7 + 3 * j], scratch[8:10] if j == 0 else ()) for j in range(2)]
        here.greet()

        def sources(owner):
            return [(gw2_s.at[spot(owner * deep, deep, 16), :], slice(0, width))]

        def sources_1(j):
            cols = slice(j * part, (j + 1) * part)
            return lambda owner: [(act_s.at[spot(owner * share, share, 16), cols], slice(0, part))]

    for index in (1, 2, 0):
        load(index).wait()

    def norm_one(at):
        resid = io[at, :].astype(F32) + mm(ctx[at, :], wo[...]) + vec(5)
        center = resid - jnp.mean(resid, axis=1, keepdims=True)
        inverse = lax.rsqrt(jnp.mean(center * center, axis=1, keepdims=True) + norm_eps)
        unit = center * inverse
        hidden = unit * vec(6) + vec(7)
        n1_s[at, :] = unit.astype(BF16)
        inv_s[at, :] = jnp.broadcast_to(inverse, (size, LANES))
        h1_s[at, :] = hidden.astype(BF16)
        sum_s[at, :] = hidden + vec(8)

    over_rows(norm_one)
    load(5).start()
    load(3).wait()
    per = width // block

    def expand(at, i):
        bias = vec_ref[11 + i // per, spot(lax.rem(i, per) * block, block, LANES)].astype(F32).reshape(1, block)
        act, slope = gelu_pair(mm(h1_s[...], w1[:, at]) + bias)
        act_s[:, at] = act.astype(BF16)
        slope_s[:, at] = slope.astype(BF16)

    over_cols(0, inner // block, expand)
    load(4).wait()

    def reduce(at, i):
        sum_s[:, at] += mm(act_s[...], w2[:, at])

    over_cols(0, per, reduce)
    load(5).wait()

    def norm_two(at):
        resid = sum_s[at, :]
        center = resid - jnp.mean(resid, axis=1, keepdims=True)
        inverse = lax.rsqrt(jnp.mean(center * center, axis=1, keepdims=True) + norm_eps)
        unit = center * inverse
        grad = io[at, :].astype(F32)
        io[at, :] = (unit * vec(9) + vec(10)).astype(BF16)
        acc[9] += fold(grad * unit)
        acc[10] += fold(grad)
        scaled = grad * vec(9)
        back = inverse * (
            scaled
            - jnp.mean(scaled, axis=1, keepdims=True)
            - unit * jnp.mean(scaled * unit, axis=1, keepdims=True)
        )
        sum_s[at, :] = back
        half = back.astype(BF16)
        gb_s[at, :] = half
        acc[8] += fold(half.astype(F32))

    over_rows(norm_two)
    store(0).start()
    for z in range(blocks):
        cols = slice(z * width, (z + 1) * width)
        gw2_s[cols, :] = mm_tn(act_s[:, cols], gb_s[...]).astype(BF16)
        if red is not None:
            red.pair_send(chunk, sources, z)

    def expand_back(at, i):
        grad = (mm_nt(gb_s[...], w2[at, :]) * slope_s[:, at].astype(F32)).astype(BF16)
        slope_s[:, at] = grad
        row = 11 + i // per
        cols = spot(lax.rem(i, per) * block, block, LANES)
        acc[row, :, cols] = acc[row, :, cols] + fold(grad.astype(F32))

    def hidden_back(at, i):
        sum_s[:, at] += mm_nt(slope_s[...], w1[at, :])

    def norm_one_back(at):
        grad, unit = sum_s[at, :], n1_s[at, :].astype(F32)
        acc[6] += fold(grad * unit)
        acc[7] += fold(grad)
        scaled = grad * vec(6)
        back = inv_s[at, 0:1] * (
            scaled
            - jnp.mean(scaled, axis=1, keepdims=True)
            - unit * jnp.mean(scaled * unit, axis=1, keepdims=True)
        )
        sum_s[at, :] = back
        half = back.astype(BF16)
        gb_s[at, :] = half
        acc[5] += fold(half.astype(F32))

    def merge(target, source, size):
        def one(z, carry):
            mine = spot((2 * z + here.core) * size, size, 16)
            target[z] = target[z] + source(mine)
            return carry

        lax.fori_loop(0, here.depth, one, 0)

    def merge_1(j):
        red.pair_wait(chunk_1[j], sources_1(j))
        merge(chunk_1[j].total, lambda mine: act_s[mine, j * part : (j + 1) * part], share)

    count = inner // block
    over_cols(0, count // 3, expand_back)
    if red is not None:
        red.pair_wait(chunk, sources)
        merge(chunk.total, lambda mine: gw2_s[mine, :], deep)
        red.plane_send(chunk)
    over_cols(count // 3, count, expand_back)
    for c in range(blocks):
        cols = slice(c * width, (c + 1) * width)
        act_s[0:width, cols] = mm_tn(h1_s[...], slope_s[:, cols]).astype(BF16)
        if red is not None and (c + 1) % (blocks // 2) == 0:
            red.pair_send(chunk_1[c // (blocks // 2)], sources_1(c // (blocks // 2)))
    over_cols(0, 1, hidden_back)
    if red is not None:
        merge_1(0)
        red.plane_send(chunk_1[0])
    over_cols(1, per, hidden_back)
    if red is not None:
        red.plane_turn(chunk)
        merge_1(1)
        store(6).start()
    else:
        store(5).start()
    over_rows(norm_one_back)
    store(1).start()
    store(0).wait()
    io[...] = mm_nt(gb_s[...], wo[...]).astype(BF16)
    store(2).start()
    gwo_s[...] = mm_tn(ctx[...], gb_s[...]).astype(BF16)
    store(3).start()
    for row in range(acc.shape[0]):
        gvec_ref[row : row + 1, :] = jnp.sum(acc[row], axis=0, keepdims=True)
    if red is not None:
        red.plane_done(chunk)
    store(4).start()
    if red is not None:
        red.plane_add(chunk_1[0])
        store(5).start()
        red.finish()
    for index in range(1, 6 if red is None else 7):
        store(index).wait()


def middle_call(narrow, x, ctx, cot, vec, e, w2):
    rows, width = x.shape
    inner = w2.shape[0]
    hbm, vmem = pl.BlockSpec(memory_space=pl.ANY), pl.BlockSpec(memory_space=pltpu.VMEM)
    shape = jax.ShapeDtypeStruct
    scratch, params = [], {}
    shape_w, shape_1 = (inner, width), (width, inner)
    if narrow is not None:
        depth, deep, share = narrow // 2, inner // narrow, width // narrow
        part = inner // 2
        shape_w, shape_1 = (depth, deep // 2, width // 2), (2, depth, share, part)
        scratch = [pltpu.SemaphoreType.DMA((3 * depth + 8,))] * 2
        scratch += [pltpu.VMEM((depth, deep, width), BF16), *plane_scratch(depth, deep, width)]
        scratch += [pltpu.VMEM((depth, share, part), BF16), *plane_scratch(depth, share, part)[0:2]]
        scratch += [pltpu.VMEM((depth, share, part), BF16)]
        params = dict(collective_id=2, has_side_effects=True)
    return pl.pallas_call(
        functools.partial(middle_kernel, narrow),
        in_specs=[hbm, hbm, hbm, vmem, hbm, hbm],
        out_specs=[hbm] * 6 + [vmem],
        out_shape=[
            shape((rows, width), BF16),
            shape((rows, width), F32),
            shape((rows, width), BF16),
            shape(shape_1, BF16),
            shape((width, width), BF16),
            shape(shape_w, BF16),
            shape(vec.shape, F32),
        ],
        scratch_shapes=[
            pltpu.VMEM((width, width), BF16),
            pltpu.VMEM((width, inner), BF16),
            pltpu.VMEM((inner, width), BF16),
            pltpu.VMEM((rows, width), BF16),
            pltpu.VMEM((rows, width), BF16),
            pltpu.VMEM((rows, width), BF16),
            pltpu.VMEM((rows, width), BF16),
            pltpu.VMEM((rows, LANES), F32),
            pltpu.VMEM((rows, inner), BF16),
            pltpu.VMEM((rows, inner), BF16),
            pltpu.VMEM((rows, width), BF16),
            pltpu.VMEM((rows, width), F32),
            pltpu.VMEM((inner, width), BF16),
            pltpu.VMEM((width, width), BF16),
            pltpu.VMEM((vec.shape[0], 8, width), F32),
            pltpu.SemaphoreType.DMA((13,)),
            *scratch,
        ],
        compiler_params=pltpu.CompilerParams(vmem_limit_bytes=VMEM_LIMIT, **params),
        name="middle",
    )(x, ctx, cot, vec, e, w2)


def input_grad_kernel(gp_ref, w_ref, gr1_ref, out_ref):
    out_ref[...] = (gr1_ref[...] + mm_nt(gp_ref[...], w_ref[...])).astype(BF16)


def input_grad_call(gp, w, gr1, size):
    rows, cols = gp.shape
    width = w.shape[0]
    return pl.pallas_call(
        input_grad_kernel,
        grid=(rows // size,),
        in_specs=[
            pl.BlockSpec((size, cols), lambda i: (i, 0)),
            pl.BlockSpec((width, cols), lambda i: (0, 0)),
            pl.BlockSpec((size, width), lambda i: (i, 0)),
        ],
        out_specs=pl.BlockSpec((size, width), lambda i: (i, 0)),
        out_shape=jax.ShapeDtypeStruct((rows, width), BF16),
        compiler_params=pltpu.CompilerParams(vmem_limit_bytes=VMEM_LIMIT),
        name="input_grad",
    )(gp, w, gr1)


def adam_update(master, first_old, second_old, grad_shard, factor, index):
    clipped = grad_shard * factor
    new_first = beta_one * first_old + (1.0 - beta_one) * clipped
    new_second = beta_two * second_old + (1.0 - beta_two) * clipped * clipped
    direction = (
        new_first
        / (1.0 - beta_one**STEP)
        / (jnp.sqrt(new_second / (1.0 - beta_two**STEP)) + adam_eps)
    )
    new_weight = master - rate_table[index] * (direction + decay_table[index] * master)
    return (new_weight, new_first, new_second)


def update_tile(master, first, second, grad, factor, index):
    weight, first, second = adam_update(master, first, second, grad.astype(F32), factor, index)
    return weight, first, second, weight.astype(BF16)


def update_kernel(narrow, n_ref, fa_ref, fo_ref, f1_ref, fw_ref, v_ref, *refs):
    ins, whole, outs, norm_ref, copied = refs[0:15], refs[15:17], refs[17:37], refs[37], refs[38:40]
    step = pl.program_id(0)
    for source, target in zip(whole, copied):
        target[...] = source[...]
    heads = fa_ref.shape[1] // GROUP
    width = heads * HEAD
    norm = jnp.sqrt(n_ref[0:1, 0:1])
    factor = jnp.minimum(1.0, clip_limit / (norm + 1e-06))
    norm_ref[...] = norm

    def store(index, rows, cols, grad):
        news = update_tile(*(ins[5 * t + index][rows, cols] for t in range(3)), grad, factor, index)
        for t, new in enumerate(news):
            outs[5 * t + index][rows, cols] = new

    every = slice(None)
    low = low_lanes(fa_ref.shape[0])
    for pair in range(heads // 2):
        at = 2 * pair * GROUP
        for b in range(3):
            even = fa_ref[:, at + b * LANES : at + (b + 1) * LANES].astype(F32)
            odd = fa_ref[:, at + GROUP + b * LANES : at + GROUP + (b + 1) * LANES].astype(F32)
            for second in range(2):
                if second:
                    grad = jnp.where(low, swap_halves(even), odd)
                else:
                    grad = jnp.where(low, even, swap_halves(odd))
                start = (2 * b + second) * width + pair * LANES
                store(0, every, slice(start, start + LANES), grad)
    store(1, every, every, fo_ref[...])
    store(2, every, every, f1_ref[...])
    store(3, every, every, fw_ref[...])

    @pl.when(step == 0)
    def _():
        count, span = ins[4].shape
        me = lax.axis_index("narrow")
        turned = pltpu.roll(v_ref[...], lax.rem(width - me * span, width), 1)
        store(4, every, every, turned[0:count, 0:span])


def update_call(narrow, norm, shards, vec, masters, firsts, seconds, whole):
    share = shards[0].shape[0]
    steps = share // 48 if share % 48 == 0 else share // 16

    def rows_of(array_in):
        return pl.BlockSpec((array_in.shape[0] // steps, array_in.shape[1]), lambda i: (i, 0))

    def fixed(array_in):
        return pl.BlockSpec(array_in.shape, lambda i: (0, 0))

    def group(arrays):
        return [rows_of(a) for a in arrays[:4]] + [fixed(arrays[4])]

    def shapes(arrays, dtype):
        return [jax.ShapeDtypeStruct(a.shape, dtype) for a in arrays]

    return pl.pallas_call(
        functools.partial(update_kernel, narrow),
        grid=(steps,),
        in_specs=[fixed(norm), *(rows_of(a) for a in shards), fixed(vec)] + group(masters) * 3 + [rows_of(a) for a in whole],
        out_specs=group(masters) * 4 + [pl.BlockSpec((1, 1), lambda i: (0, 0))] + [rows_of(a) for a in whole],
        out_shape=shapes(masters, F32) * 3
        + shapes(masters, BF16)
        + [jax.ShapeDtypeStruct((1, 1), F32)]
        + [jax.ShapeDtypeStruct(a.shape, a.dtype) for a in whole],
        compiler_params=pltpu.CompilerParams(vmem_limit_bytes=VMEM_LIMIT),
        name="update",
    )(norm, *shards, vec, *masters, *firsts, *seconds, *whole)


def by_head(array_in):
    rows, cols = array_in.shape
    heads = cols // GROUP
    return array_in.reshape(rows, 6, heads, HEAD).transpose(0, 2, 1, 3).reshape(rows, cols)


def by_block(array_in):
    rows, cols = array_in.shape
    heads = cols // GROUP
    return array_in.reshape(rows, heads, 6, HEAD).transpose(0, 2, 1, 3).reshape(rows, cols)


def can_pass_pieces(wide, narrow, width, deep):
    share = width // narrow
    return wide == 4 and narrow % 2 == 0 and narrow > 2 and share % 32 == 0 and deep % 128 == 0 and 2 * deep == width


def body(
    x_in, cotangent, segment_ids, type_ids,
    projection, context_out, expand_weight, reduce_weight, vector_params,
    first_projection, first_context, first_expand, first_reduce, first_vectors,
    second_projection, second_context, second_expand, second_reduce, second_vectors,
):
    seq_count, seq_len, width = x_in.shape
    rows = seq_count * seq_len

    def gather(array_in, axis):
        return lax.all_gather(array_in.astype(BF16), "narrow", axis=axis, tiled=True)

    hidden = x_in.reshape(rows, width)
    cot = cotangent.reshape(rows, width)
    narrow = lax.axis_size("narrow")
    pieces = can_pass_pieces(lax.axis_size("wide"), narrow, width, reduce_weight.shape[0])
    if pieces:
        query, keyval, context, aug, proj_w, mid_w, reduce_w, vec_rows, word, kmask, kaug, turned = gather_call(
            narrow, hidden, projection, context_out, expand_weight, reduce_weight, vector_params,
            segment_ids, type_ids,
        )
    else:
        word_col = (type_ids == 0).reshape(rows, 1)
        lane = lax.broadcasted_iota(jnp.int32, (rows, LANES), 1)
        word = jnp.broadcast_to(word_col, (rows, LANES)).astype(BF16)
        kmask = ((lane < HEAD) == word_col).astype(BF16)
        same = segment_ids.reshape(rows, 1) == lane
        qaug = jnp.where(same & (lane < 8), 1.0, 0.0).astype(BF16)
        kaug = jnp.where(lane < 8, jnp.where(same, 0.0, FAR), jnp.where(lane < 11, 1.0, 0.0)).astype(BF16)
        proj_w, vec_half = gather(by_head(projection), 0), gather(vector_params, 1)
        reduce_w = gather(reduce_weight, 0)
        mid_w = jnp.concatenate(
            [gather(expand_weight, 0), gather(context_out, 0), jnp.zeros((width, 2 * LANES), BF16)], axis=1
        )
        zero_row = jnp.zeros((1, width), BF16)
        bias = by_head(jnp.concatenate([vec_half[0:4], zero_row, vec_half[4:5]]).reshape(1, -1)).astype(F32)
        vec_rows = jnp.pad(vec_half.astype(F32), ((0, 1), (0, 0)))
        query, keyval = qkv_call(hidden, proj_w, bias, word)
        context, aug = attend_call(query, keyval, qaug, kaug, kmask, seq_len)
    block_out, grad_r1, grad_context, grad_expand, grad_ctx_w, grad_reduce, grad_mid = middle_call(
        narrow if pieces else None, hidden, context, cot, vec_rows, mid_w, reduce_w
    )
    masters = (projection, context_out, expand_weight, reduce_weight, vector_params)
    firsts = (first_projection, first_context, first_expand, first_reduce, first_vectors)
    seconds = (second_projection, second_context, second_expand, second_reduce, second_vectors)
    out_shape = (seq_count, seq_len, width)
    if pieces:
        input_grad, shard_1, shard_o, shard_w, shard_a, grad_vectors, norm = reduce_call(
            narrow, turned, query, keyval, aug, grad_context, context, proj_w, kaug, kmask, word, grad_mid,
            grad_r1, grad_expand, grad_reduce, grad_ctx_w, reduce_weight.shape[0], seq_len,
        )
        shards = (shard_a, shard_o, shard_1, shard_w)
        *updated, grad_norm, block_out, input_grad = update_call(
            narrow, norm, shards, grad_vectors, masters, firsts, seconds, (block_out, input_grad)
        )
        return (
            block_out.reshape(out_shape),
            input_grad.reshape(out_shape),
            grad_norm.reshape(()),
            *updated,
        )
    grad_proj, grad_proj_w, grad_sums = attend_back_call(
        hidden, query, keyval, aug, grad_context, context, kaug, kmask, word, seq_len
    )
    input_grad = input_grad_call(grad_proj, proj_w, grad_r1, 256)
    sum_rows = by_block(grad_sums).reshape(6, width)
    grad_vectors = jnp.concatenate([sum_rows[0:4], sum_rows[5:6], grad_mid[5:15]], axis=0)

    def scatter(array_in, axis):
        return lax.psum_scatter(array_in, "narrow", scatter_dimension=axis, tiled=True)

    def over_wide(array_in):
        return lax.psum(array_in.astype(BF16), "wide").astype(F32)

    shards = (
        by_block(over_wide(scatter(grad_proj_w, 0))),
        over_wide(scatter(grad_ctx_w, 0)),
        over_wide(scatter(grad_expand, 0)),
        over_wide(scatter(grad_reduce, 0)),
        over_wide(scatter(grad_vectors, 1)),
    )
    local_squares = sum((jnp.sum(shard_item * shard_item) for shard_item in shards))
    total_squares = lax.psum(local_squares, "narrow")
    grad_norm = jnp.sqrt(total_squares)
    factor = jnp.minimum(1.0, clip_limit / (grad_norm + 1e-06))
    results = [
        adam_update(masters[index], firsts[index], seconds[index], shards[index], factor, index)
        for index in range(5)
    ]
    return (
        block_out.reshape(out_shape),
        input_grad.reshape(out_shape),
        grad_norm,
        *(item[0] for item in results),
        *(item[1] for item in results),
        *(item[2] for item in results),
        *(item[0].astype(BF16) for item in results),
    )


def solution(mesh):
    shard, col = P("narrow", None), P(None, "narrow")
    seqs = P(("wide", "narrow"), None, None)
    group = (shard, shard, shard, shard, col)
    return jax.shard_map(
        body,
        mesh=mesh,
        in_specs=(seqs, seqs, P(("wide", "narrow"), None), P(("wide", "narrow"), None), *group, *group, *group),
        out_specs=(seqs, seqs, P(), *group, *group, *group, *group),
        check_vma=False,
    )
```
